32 devices in a mesh: lon: 2 (over y), batch: 16 (over z, x, core).
Axes of the slice: x: 2, y: 2, z: 4, core: 2. Of those that a mesh axis runs over, the one named last changes fastest.
Arguments:
- state: bfloat16 [16, 16, 64, 256], P('batch', None, 'lon'), may hold values from -8 to 8
- noise: float32 [16, 4, 16, 64, 32], P('batch', None, None, 'lon'), may hold values from -8 to 8
- samples: int32 [16], P('batch'), may hold values from 1 to 4, as said below
- step: int32 [], replicated, may hold values from 500 to 999
- kl_weight: float32 [], replicated, may hold values from 1 to 4
- floor: float32 [], replicated, may hold values from 0.2 to 0.6
- latent_weight: bfloat16 [256, 64], replicated, may hold values from -2 to 2
- state_weight: bfloat16 [256, 256], replicated, may hold values from -0.375 to 0.375
- noise_weight: bfloat16 [32, 512], replicated, may hold values from -1 to 1
- attention_gain: float32 [2, 256], replicated, may hold values from 0.1 to 1.9
- query_key_value: bfloat16 [2, 256, 768], replicated, may hold values from -0.375 to 0.375
- offset_bias: float32 [2, 8, 225], replicated, may hold values from -4 to 4
- output_weight: bfloat16 [2, 256, 256], replicated, may hold values from -3 to 3
- feedforward_gain: float32 [2, 256], replicated, may hold values from 0.1 to 1.9
- up_weight: bfloat16 [2, 256, 1024], replicated, may hold values from -0.375 to 0.375
- down_weight: bfloat16 [2, 1024, 256], replicated, may hold values from -0.1875 to 0.1875
- cotangent: bfloat16 [16, 4, 16, 64, 256], P('batch', None, None, 'lon'), may hold values from -6 to 6
Outputs:
- activations: bfloat16 [16, 4, 16, 64, 256], P('batch', None, None, 'lon')
- divergence: float32 [], replicated
- state_gradient: float32 [16, 16, 64, 256], P('batch', None, 'lon')
- latent_weight_gradient: float32 [256, 64], replicated
- state_weight_gradient: float32 [256, 256], replicated
- noise_weight_gradient: float32 [32, 512], replicated
- attention_gain_gradient: float32 [2, 256], replicated
- query_key_value_gradient: float32 [2, 256, 768], replicated
- offset_bias_gradient: float32 [2, 8, 225], replicated
- output_weight_gradient: float32 [2, 256, 256], replicated
- feedforward_gain_gradient: float32 [2, 256], replicated
- up_weight_gradient: float32 [2, 256, 1024], replicated
- down_weight_gradient: float32 [2, 1024, 256], replicated
The draws below stay inside these ranges and needn't reach their ends.
Inputs may be any that keep to these rules, and one draw needn't show every extreme that they name: At least one item has 4 live samples.
All inputs are finite; a program needn't handle non-finite values.
Results may differ from the reference program's by a relative error of at most 0.02.
Values may be sent and summed in bfloat16 or wider, within the bound.
No kernel may reach another device: no remote copies, remote signals or barrier semaphores. Data moves between devices by JAX's collectives and lax.ppermute only.
A program may use at most 256 MiB of HBM per device.

```python
import math
import jax
import jax.numpy as jnp
import numpy as np
from jax import lax

D = 256
HEADS = 8
HD = 32
FF = 1024
ZC = 32
WIN = 8
WARM = 1000
SLOTS = 4
LAT = 16
LON = 64
SHIFT = 4
RELS = 225
ITEMS = 16


def draw_samples(key, part):
    key = jax.random.fold_in(key, 11)
    counts_key, full_key = jax.random.split(key)
    counts = jax.random.randint(counts_key, (ITEMS,), 1, SLOTS + 1)
    chosen = jax.random.randint(full_key, (), 0, ITEMS)
    return jnp.where(jnp.arange(ITEMS) == chosen, SLOTS, counts).astype(jnp.int32)


def draw_state(key, part):
    key = jax.random.fold_in(key, 12)
    rising = jnp.arange(ITEMS, dtype=jnp.float32) / max(ITEMS - 1, 1)
    across = jnp.arange(LON, dtype=jnp.float32) / max(LON - 1, 1)
    position = across[None, :] + 0.5 * rising[:, None]
    entries = jnp.clip(jax.random.normal(key, (ITEMS, LAT, LON, D), jnp.float32), -3.0, 3.0)
    scale = 0.5 * 3.0 ** position
    return (entries * scale[:, None, :, None]).astype(jnp.bfloat16)


def draw_latent_weight(key, part):
    key = jax.random.fold_in(key, 13)
    entry_key, column_key = jax.random.split(key)
    column = jnp.exp(jax.random.uniform(column_key, (2 * ZC,), jnp.float32, math.log(0.3), math.log(1.5)))
    entries = jnp.clip(jax.random.normal(entry_key, (D, 2 * ZC), jnp.float32), -5.0, 5.0)
    return (entries * column[None, :] * D ** (-0.5)).astype(jnp.bfloat16)


def steps_of(own_key, dims, cuts, least, high):
    level, own = 1.0, jax.random.fold_in(own_key, 6)
    for axis_at, shards_of in cuts:
        heights = jnp.exp(jax.random.uniform(jax.random.fold_in(own, axis_at), (shards_of,), jnp.float32, least / len(cuts), high / len(cuts)))
        level = level * jnp.repeat(heights, dims[axis_at] // shards_of).reshape([-1 if axis == axis_at else 1 for axis in range(len(dims))])
    return level


def gaussian(rng, shape, scale, reach, cuts=(), held_as=jnp.bfloat16):
    factor_of = steps_of(rng, shape, cuts, -0.22, 0.18) if cuts else 1.0
    array = jax.random.normal(rng, shape, jnp.float32) * scale * factor_of
    return jnp.minimum(jnp.maximum(array, -reach), reach).astype(held_as)


def setup_inputs(seed: int = 0) -> dict:
    splits = jax.random.split(jax.random.key(seed), 18)
    state = draw_state(jax.random.fold_in(splits[17], 71), 0)
    noise = gaussian(splits[1], (ITEMS, SLOTS, LAT, LON, ZC), 1.0, 8.0, ((0, 16), (3, 2)), jnp.float32)
    samples = draw_samples(jax.random.fold_in(splits[17], 71), 0)
    step = jax.random.randint(splits[3], (), WARM // 2, WARM).astype(jnp.int32)
    kl_weight = jnp.clip(jnp.exp(jax.random.uniform(splits[4], (), jnp.float32, math.log(1.0), math.log(4.0))), 1.0, 4.0)
    floor = jnp.clip(jax.random.uniform(splits[5], (), jnp.float32, 0.2, 0.6), 0.2, 0.6)
    latent_weight = draw_latent_weight(jax.random.fold_in(splits[17], 71), 0)
    state_weight = gaussian(splits[7], (D, D), D ** -0.5, 0.375)
    noise_weight = gaussian(splits[8], (ZC, 2 * D), ZC ** -0.5, 1.0)
    attention_gain = jnp.clip(1.0 + 0.18 * jax.random.normal(splits[9], (2, D), jnp.float32), 0.1, 1.9)
    query_key_value = gaussian(splits[10], (2, D, 3 * D), D ** -0.5, 0.375)
    offset_bias = gaussian(splits[11], (2, HEADS, RELS), 1.0, 4.0, (), jnp.float32)
    output_weight = gaussian(splits[12], (2, D, D), (max(D // 64, 1)) ** -0.5, 3.0)
    feedforward_gain = jnp.clip(1.0 + 0.18 * jax.random.normal(splits[13], (2, D), jnp.float32), 0.1, 1.9)
    up_weight = gaussian(splits[14], (2, D, FF), D ** -0.5, 0.375)
    down_weight = gaussian(splits[15], (2, FF, D), FF ** -0.5, 0.1875)
    cotangent = gaussian(splits[16], (ITEMS, SLOTS, LAT, LON, D), 1.0, 6.0, ((0, 16), (3, 2)))
    return {"state": state, "noise": noise, "samples": samples, "step": step, "kl_weight": kl_weight, "floor": floor, "latent_weight": latent_weight, "state_weight": state_weight, "noise_weight": noise_weight, "attention_gain": attention_gain, "query_key_value": query_key_value, "offset_bias": offset_bias, "output_weight": output_weight, "feedforward_gain": feedforward_gain, "up_weight": up_weight, "down_weight": down_weight, "cotangent": cotangent}


eps_norm = 1e-05
sharpness = 8.0
spread_bound = 4.0

@jax.custom_vjp
def low(v):
    return lax.optimization_barrier(v.astype(jnp.bfloat16)).astype(jnp.float32)

@jax.custom_vjp
def low_back(v):
    return v

def low_keep(v):
    return (low(v), None)

def low_pass(kept, grad):
    return (grad,)

def back_keep(v):
    return (v, None)

def back_low(kept, grad):
    return (low(grad),)
low.defvjp(low_keep, low_pass)
low_back.defvjp(back_keep, back_low)

def product(left, right):
    return jnp.matmul(left, right, precision=lax.Precision.HIGHEST)

def layer_norm(values, gain):
    center = values - lax.optimization_barrier(jnp.mean(values, axis=-1, keepdims=True))
    scale = lax.rsqrt(lax.optimization_barrier(jnp.mean(center * center, axis=-1, keepdims=True)) + eps_norm)
    return center * scale * gain

def offsets(window):
    places = np.arange(window * window)
    rows_at = places // window
    cols_at = places % window
    return (rows_at[:, None] - rows_at[None, :] + window - 1) * (2 * window - 1) + cols_at[:, None] - cols_at[None, :] + window - 1

def to_windows(values, window):
    count, height, breadth, channels = values.shape
    values = values.reshape(count, height // window, window, breadth // window, window, channels)
    return values.transpose(0, 1, 3, 2, 4, 5).reshape(-1, window * window, channels)

def from_windows(values, count, height, breadth, window):
    channels = values.shape[-1]
    values = values.reshape(count, height // window, breadth // window, window, window, channels)
    return values.transpose(0, 1, 3, 2, 4, 5).reshape(count, height, breadth, channels)

def swin_block(hidden, gain_attention, packed_weight, table, out_weight, gain_forward, up_proj, down_proj, shifted):
    count, height, breadth, width = hidden.shape
    normed = low(layer_norm(hidden, gain_attention))
    if shifted:
        normed = low_back(jnp.roll(normed, -SHIFT, axis=2))
    windows = to_windows(normed, WIN)
    frames = windows.shape[0]
    packed = low(low_back(product(windows, packed_weight)))
    query = packed[..., :width].reshape(frames, WIN * WIN, HEADS, HD)
    keys = packed[..., width:2 * width].reshape(frames, WIN * WIN, HEADS, HD)
    values = packed[..., 2 * width:].reshape(frames, WIN * WIN, HEADS, HD)
    bias = table[:, offsets(WIN)]
    scores = jnp.einsum('wqhe,wkhe->whqk', query, keys, precision=lax.Precision.HIGHEST) * HD ** (-0.5) + bias[None]
    scores = low_back(scores)
    weights = low(jax.nn.softmax(scores, axis=-1))
    context = low(low_back(jnp.einsum('whqk,wkhe->wqhe', weights, values, precision=lax.Precision.HIGHEST)))
    context = from_windows(context.reshape(frames, WIN * WIN, width), count, height, breadth, WIN)
    if shifted:
        context = low_back(jnp.roll(context, SHIFT, axis=2))
    mixed = hidden + low_back(product(context, out_weight))
    normed_second = low(layer_norm(mixed, gain_forward))
    inner = low_back(product(normed_second, up_proj))
    active = low(jax.nn.gelu(inner, approximate=False))
    return mixed + low_back(product(active, down_proj))

def forward(state, params, noise, live, beta, floor):
    latent_weight, state_weight, noise_weight, attention_gain, query_key_value, offset_bias, output_weight, feedforward_gain, up_weight, down_weight = params
    linear = low_back(product(state, latent_weight))
    center = linear[..., :ZC]
    log_spread = spread_bound * jnp.tanh(linear[..., ZC:] / spread_bound)
    sigma = jnp.exp(0.5 * log_spread)
    terms = 0.5 * (center * center + sigma * sigma - 1.0 - log_spread)
    kl_mean = lax.optimization_barrier(jnp.sum(terms, axis=(0, 1, 2))) / (ITEMS * LAT * LON)
    divergence = beta * jnp.mean(floor + jax.nn.softplus(sharpness * (kl_mean - floor)) / sharpness)
    gate_state = low_back(product(state, state_weight))

    def one_item(pieces):
        item_state, item_gate, item_center, item_sigma, item_noise, item_live = pieces
        latent = low(item_center[None] + item_sigma[None] * item_noise)
        noise_mix = low_back(product(latent, noise_weight))
        gate = jax.nn.sigmoid(item_gate[None] + noise_mix[..., :D])
        hidden = gate * item_state[None] + (1.0 - gate) * jnp.tanh(noise_mix[..., D:])
        for layer in range(2):
            hidden = swin_block(hidden, attention_gain[layer], query_key_value[layer], offset_bias[layer], output_weight[layer], feedforward_gain[layer], up_weight[layer], down_weight[layer], layer == 1)
        return hidden * item_live[:, None, None, None]
    result = lax.map(jax.checkpoint(one_item), (state, gate_state, center, sigma, noise, live))
    return (result, divergence)

def reference(state, noise, samples, step, kl_weight, floor, latent_weight, state_weight, noise_weight, attention_gain, query_key_value, offset_bias, output_weight, feedforward_gain, up_weight, down_weight, cotangent):
    live = (jnp.arange(SLOTS)[None, :] < samples[:, None]).astype(jnp.float32)
    beta = kl_weight * (step + 1).astype(jnp.float32) / WARM
    params = (latent_weight.astype(jnp.float32), state_weight.astype(jnp.float32), noise_weight.astype(jnp.float32), attention_gain.astype(jnp.float32), query_key_value.astype(jnp.float32), offset_bias.astype(jnp.float32), output_weight.astype(jnp.float32), feedforward_gain.astype(jnp.float32), up_weight.astype(jnp.float32), down_weight.astype(jnp.float32))

    def objective(state_value, param_values):
        return forward(state_value, param_values, noise, live, beta, floor)
    (result, divergence), pullback = jax.vjp(objective, state.astype(jnp.float32), params)
    state_grads, param_grads = pullback((cotangent.astype(jnp.float32), jnp.ones((), divergence.dtype)))
    return (result.astype(jnp.bfloat16), divergence, state_grads, param_grads[0], param_grads[1], param_grads[2], param_grads[3], param_grads[4], param_grads[5], param_grads[6], param_grads[7], param_grads[8], param_grads[9])
```

```python
import jax
import jax.numpy as jnp
from jax import lax
from jax.experimental import pallas as pl
from jax.experimental.pallas import tpu as pltpu
from jax.sharding import PartitionSpec as P

HEADS = 8
HD = 32
WIN = 8
WARM = 1000
SLOTS = 4
D = 256
FF = 1024
ZC = 32
HALF = WIN // 2 * WIN
TILE = SLOTS * WIN * WIN

eps_norm = 1e-05
sharpness = 8.0
spread_bound = 4.0
LOG2E = 1.4426950408889634
f32 = jnp.float32
bf16 = jnp.bfloat16


def mm(a, b):
    return lax.dot_general(a, b, (((1,), (0,)), ((), ())), preferred_element_type=f32)


def mm_nt(a, b):
    return lax.dot_general(a, b, (((1,), (1,)), ((), ())), preferred_element_type=f32)


def mm_tn(a, b):
    return lax.dot_general(a, b, (((0,), (0,)), ((), ())), preferred_element_type=f32)


def low_sublanes(shape):
    return lax.broadcasted_iota(jnp.int32, shape, len(shape) - 2) < 4


def to_halves(x):
    rows, cols, ch = x.shape
    n = cols // 8
    v = x.reshape(4, 2, n, 8, ch)
    a, b = v[:, 0], v[:, 1]
    low = low_sublanes(a.shape)
    first = jnp.where(low, a, pltpu.roll(b, 4, 2))
    second = jnp.where(low, pltpu.roll(a, 4, 2), b)
    first = first.transpose(1, 0, 2, 3)
    second = second.transpose(1, 0, 2, 3)
    return jnp.stack([first, second], axis=1).reshape(2 * n, HALF, ch)


def from_halves(x):
    n = x.shape[0] // 2
    ch = x.shape[-1]
    v = x.reshape(n, 2, 4, 8, ch)
    first, second = v[:, 0].transpose(1, 0, 2, 3), v[:, 1].transpose(1, 0, 2, 3)
    low = low_sublanes(first.shape)
    a = jnp.where(low, first, pltpu.roll(second, 4, 2))
    b = jnp.where(low, pltpu.roll(first, 4, 2), second)
    return jnp.stack([a, b], axis=1).reshape(8, 8 * n, ch)


def tile_of(first, second):
    return jnp.stack([first, second], axis=1).reshape(TILE, first.shape[-1])


def halves_of(tile):
    v = tile.reshape(SLOTS, 2, HALF, tile.shape[-1])
    return v[:, 0], v[:, 1]


def norm(x):
    c = x - jnp.mean(x, axis=-1, keepdims=True)
    r = lax.rsqrt(jnp.mean(c * c, axis=-1, keepdims=True) + eps_norm)
    return c * r, r


def norm_back(dy, xhat, r, gain):
    along = dy * gain
    inward = r * (
        along
        - jnp.mean(along, axis=-1, keepdims=True)
        - xhat * jnp.mean(along * xhat, axis=-1, keepdims=True)
    )
    return inward, jnp.sum((dy * xhat).reshape(-1, 8, D), axis=0)


def gelu_parts(x, slope):
    a = jnp.abs(x)
    t = 1.0 / (1.0 + a * (0.3275911 * 0.7071067811865476))
    e = jnp.exp2(x * x * (-0.5 * LOG2E))
    poly = t * (
        0.5 * 0.254829592
        + t
        * (
            0.5 * -0.284496736
            + t * (0.5 * 1.421413741 + t * (0.5 * -1.453152027 + t * (0.5 * 1.061405429)))
        )
    )
    tail = poly * e
    dist = jnp.where(x >= 0.0, 1.0 - tail, tail)
    if not slope:
        return x * dist, None
    return x * dist, dist + x * e * 0.3989422804014327


def lane_masks():
    lane = lax.broadcasted_iota(jnp.int32, (1, 128), 1)
    return [(lane >= 32 * j) & (lane < 32 * j + 32) for j in range(4)]


def spread_heads(x, masks):
    return jnp.concatenate([x * m for m in masks], axis=0)


def gather_heads(x, masks):
    v = x.reshape(4, 64, 128)
    return jnp.where(masks[0], v[0], jnp.where(masks[1], v[1], jnp.where(masks[2], v[2], v[3])))


def attention(packed, bias_ref, p_ref, ctx_ref):
    sel = lane_masks()
    ones = [m.astype(f32).astype(bf16) for m in sel]
    scale = HD ** (-0.5) * LOG2E
    for w in range(SLOTS):
        rows = slice(64 * w, 64 * w + 64)
        for g in range(2):
            lanes = lambda part: slice(256 * part + 128 * g, 256 * part + 128 * g + 128)
            q, k, v = packed[rows, lanes(0)], packed[rows, lanes(1)], packed[rows, lanes(2)]
            s = mm_nt(k, spread_heads(q, ones)) * scale + bias_ref[g]
            s = jnp.exp2(s - jnp.max(s, axis=0, keepdims=True))
            p = (s * (1.0 / jnp.sum(s, axis=0, keepdims=True))).astype(bf16)
            p_ref[2 * w + g] = p
            ctx_ref[rows, 128 * g : 128 * g + 128] = gather_heads(mm_tn(p, v), sel).astype(bf16)


def attention_back(packed, dctx, p_ref, gp_ref, dbias_ref):
    sel = lane_masks()
    ones = [m.astype(f32).astype(bf16) for m in sel]
    scale = HD ** (-0.5)
    for g in range(2):
        total = None
        for w in range(SLOTS):
            rows = slice(64 * w, 64 * w + 64)
            lanes = lambda part: slice(256 * part + 128 * g, 256 * part + 128 * g + 128)
            q, k, v = packed[rows, lanes(0)], packed[rows, lanes(1)], packed[rows, lanes(2)]
            p = p_ref[2 * w + g]
            spread = spread_heads(dctx[rows, lanes(0)], ones)
            gp_ref[rows, lanes(2)] = mm(p, spread).astype(bf16)
            dp = mm_nt(v, spread)
            pf = p.astype(f32)
            t = pf * dp
            ds = t - pf * jnp.sum(t, axis=0, keepdims=True)
            total = ds if total is None else total + ds
            ds = ds.astype(bf16)
            gp_ref[rows, lanes(1)] = (mm(ds, spread_heads(q, ones)) * scale).astype(bf16)
            gp_ref[rows, lanes(0)] = (gather_heads(mm_tn(ds, k), sel) * scale).astype(bf16)
        dbias_ref[g] += total


def block_forward(x, w):
    xhat, _ = norm(x)
    w["packed"][...] = mm((xhat * w["gain1"][...]).astype(bf16), w["qkv"][...]).astype(bf16)
    attention(w["packed"], w["bias"], w["p"], w["ctx"])
    mixed = x + mm(w["ctx"][...], w["out"][...])
    xhat2, _ = norm(mixed)
    normed2 = (xhat2 * w["gain2"][...]).astype(bf16)
    out = mixed
    for c in range(FF // 256):
        cols = slice(256 * c, 256 * c + 256)
        active, _ = gelu_parts(mm(normed2, w["up"][:, cols]), False)
        out = out + mm(active.astype(bf16), w["down"][cols, :])
    return out


def block_both(x, g, w, want_out, round_dn):
    gain1, gain2 = w["gain1"][...], w["gain2"][...]
    xhat, r = norm(x)
    normed = (xhat * gain1).astype(bf16)
    w["packed"][...] = mm(normed, w["qkv"][...]).astype(bf16)
    attention(w["packed"], w["bias"], w["p"], w["ctx"])
    mixed = x + mm(w["ctx"][...], w["out"][...])
    xhat2, r2 = norm(mixed)
    normed2 = (xhat2 * gain2).astype(bf16)
    gb = g.astype(bf16)
    out = mixed
    dn2 = None
    for c in range(FF // 256):
        cols = slice(256 * c, 256 * c + 256)
        active, slope = gelu_parts(mm(normed2, w["up"][:, cols]), True)
        active = active.astype(bf16)
        if want_out:
            out = out + mm(active, w["down"][cols, :])
        w["d_ff"][1024 + 256 * c : 1280 + 256 * c, :] += mm_tn(active, gb)
        d_inner = (mm_nt(gb, w["down"][cols, :]) * slope).astype(bf16)
        w["d_ff"][cols, :] += mm_tn(normed2, d_inner)
        part = mm_nt(d_inner, w["up"][:, cols])
        dn2 = part if dn2 is None else dn2 + part
    inward, dgain2 = norm_back(dn2, xhat2, r2, gain2)
    w["d_small"][8:16, :] += dgain2
    d_mixed = g + inward
    g_out = d_mixed.astype(bf16)
    w["d_at"][768:1024, :] += mm_tn(w["ctx"][...], g_out)
    dctx = mm_nt(g_out, w["out"][...]).astype(bf16)
    attention_back(w["packed"], dctx, w["p"], w["gp"], w["d_bias"])
    gp = w["gp"][...]
    for c in range(3):
        cols = slice(256 * c, 256 * c + 256)
        w["d_at"][cols, :] += mm_tn(normed, gp[:, cols])
    dn = mm_nt(gp, w["qkv"][...])
    if round_dn:
        dn = dn.astype(bf16).astype(f32)
    inward, dgain1 = norm_back(dn, xhat, r, gain1)
    w["d_small"][0:8, :] += dgain1
    return out, d_mixed + inward


LIMIT = 56 * 1024 * 1024


def params(n):
    return pltpu.CompilerParams(
        dimension_semantics=("arbitrary",) * n, vmem_limit_bytes=LIMIT
    )


def prep_kernel(samples, cot, state, noise, cot_h, state_h, noise_h):
    live = samples[0]
    for s in range(SLOTS):
        factor = jnp.where(s < live, 1.0, 0.0).astype(f32)
        cot_h[0, :, s] = (to_halves(cot[0, s].astype(f32)) * factor).astype(bf16)
        noise_h[0, :, s] = to_halves(noise[0, s]).reshape(4, 64, ZC)
    state_h[0] = to_halves(state[0].astype(f32)).reshape(4, 64, D).astype(bf16)


def prep(samples, cot, state, noise):
    bands = state.shape[1] // WIN
    nw = state.shape[2] // WIN
    return pl.pallas_call(
        prep_kernel,
        grid=(bands,),
        in_specs=[
            pl.BlockSpec(memory_space=pltpu.SMEM),
            pl.BlockSpec((1, SLOTS, WIN, nw * WIN, D), lambda i: (0, 0, i, 0, 0)),
            pl.BlockSpec((1, WIN, nw * WIN, D), lambda i: (0, i, 0, 0)),
            pl.BlockSpec((1, SLOTS, WIN, nw * WIN, ZC), lambda i: (0, 0, i, 0, 0)),
        ],
        out_specs=[
            pl.BlockSpec((1, 2 * nw, SLOTS, HALF, D), lambda i: (i, 0, 0, 0, 0)),
            pl.BlockSpec((1, nw, 64, D), lambda i: (i, 0, 0, 0)),
            pl.BlockSpec((1, nw, SLOTS, 64, ZC), lambda i: (i, 0, 0, 0, 0)),
        ],
        out_shape=[
            jax.ShapeDtypeStruct((bands, 2 * nw, SLOTS, HALF, D), bf16),
            jax.ShapeDtypeStruct((bands, nw, 64, D), bf16),
            jax.ShapeDtypeStruct((bands, nw, SLOTS, 64, ZC), f32),
        ],
        compiler_params=params(1),
    )(samples, cot, state, noise)


def cell_forward(state, noise, wl_c, wl_r, ws, wn):
    center = mm(state, wl_c)
    squash = jnp.tanh(mm(state, wl_r) * (1.0 / spread_bound))
    sigma = jnp.exp((0.5 * spread_bound) * squash)
    latent = (center[None] + sigma[None] * noise).reshape(TILE, ZC).astype(bf16)
    mix = mm(latent, wn)
    gate = jax.nn.sigmoid(mm(state, ws)[None] + mix[:, :D].reshape(SLOTS, 64, D))
    cand = jnp.tanh(mix[:, D:].reshape(SLOTS, 64, D))
    wide = state.astype(f32)[None]
    hidden = gate * wide + (1.0 - gate) * cand
    return hidden.reshape(TILE, D), center, squash, sigma, latent, gate, cand


def full(a):
    return pl.BlockSpec(a.shape, lambda *_: (0,) * a.ndim)


def block_specs(k):
    return [
        pl.BlockSpec((1, 1, D), lambda *_: (k, 0, 0)),
        pl.BlockSpec((1, D, 3 * D), lambda *_: (k, 0, 0)),
        pl.BlockSpec((1, 2, 64, 256), lambda *_: (k, 0, 0, 0)),
        pl.BlockSpec((1, D, D), lambda *_: (k, 0, 0)),
        pl.BlockSpec((1, 1, D), lambda *_: (k, 0, 0)),
        pl.BlockSpec((1, D, FF), lambda *_: (k, 0, 0)),
        pl.BlockSpec((1, FF, D), lambda *_: (k, 0, 0)),
    ]


NAMES = ("gain1", "qkv", "bias", "out", "gain2", "up", "down")


def named(refs):
    return {n: r.at[0] for n, r in zip(NAMES, refs)}


FWD_SCRATCH = [
    pltpu.VMEM((TILE, 3 * D), bf16),
    pltpu.VMEM((2 * SLOTS, 64, 256), bf16),
    pltpu.VMEM((TILE, D), bf16),
]
BOTH_SCRATCH = FWD_SCRATCH + [pltpu.VMEM((TILE, 3 * D), bf16)]

GRAD_SHAPES = [(2048, D), (1024, D), (16, D), (2, 64, 256)]
GRAD_NAMES = ("d_ff", "d_at", "d_small", "d_bias")


def first_kernel(state, noise, wlc, wlr, ws, wn, *rest):
    w = named(rest[:7])
    h1, halo = rest[7:9]
    w["packed"], w["p"], w["ctx"] = rest[9:12]
    hidden = cell_forward(state[0, 0], noise[0, 0], wlc[...], wlr[...], ws[...], wn[...])[0]
    out = block_forward(hidden, w)
    a, b = halves_of(out)
    h1[0, 0, 0] = a
    h1[0, 0, 1] = b
    @pl.when(pl.program_id(1) == 0)
    def _():
        halo[0] = a.astype(bf16)


def first(state_h, noise_h, cell_w, block_w):
    bands, nw = state_h.shape[:2]
    return pl.pallas_call(
        first_kernel,
        grid=(bands, nw),
        in_specs=[
            pl.BlockSpec((1, 1, 64, D), lambda i, j: (i, j, 0, 0)),
            pl.BlockSpec((1, 1, SLOTS, 64, ZC), lambda i, j: (i, j, 0, 0, 0)),
        ]
        + [full(a) for a in cell_w]
        + block_specs(0),
        out_specs=[
            pl.BlockSpec((1, 1, 2, SLOTS, HALF, D), lambda i, j: (i, j, 0, 0, 0, 0)),
            pl.BlockSpec((1, SLOTS, HALF, D), lambda i, j: (i, 0, 0, 0)),
        ],
        out_shape=[
            jax.ShapeDtypeStruct((bands, nw, 2, SLOTS, HALF, D), f32),
            jax.ShapeDtypeStruct((bands, SLOTS, HALF, D), bf16),
        ],
        scratch_shapes=FWD_SCRATCH,
        compiler_params=params(2),
    )(state_h, noise_h, *cell_w, *block_w)


def zero_at_start(refs):
    @pl.when((pl.program_id(0) == 0) & (pl.program_id(1) == 0))
    def _():
        for r in refs:
            r[...] = jnp.zeros(r.shape, r.dtype)


def second_kernel(samples, ha, hb, hhalo, ca, cb, chalo, *rest):
    w = named(rest[:7])
    act, dh, act_halo, dh_halo = rest[7:11]
    grads = rest[11:15]
    w["packed"], w["p"], w["ctx"], w["gp"] = rest[15:19]
    w.update(zip(GRAD_NAMES, grads))
    zero_at_start(grads)
    last = pl.program_id(1) == pl.num_programs(1) - 1
    hb_v = jnp.where(last, hhalo[0].astype(f32), hb[0, 0, 0])
    cb_v = jnp.where(last, chalo[0].astype(f32), cb[0, 0].astype(f32))
    x = tile_of(ha[0, 0, 0], hb_v)
    g = tile_of(ca[0, 0].astype(f32), cb_v)
    out, dx = block_both(x, g, w, True, True)
    live = samples[0]
    a, b = halves_of(out)
    factor = jnp.concatenate(
        [jnp.where(s < live, 1.0, 0.0) * jnp.ones((1, 1, D), f32) for s in range(SLOTS)]
    )
    a, b = (a * factor).astype(bf16), (b * factor).astype(bf16)
    da, db = halves_of(dx)
    act[0, 0, 0] = a
    act[0, 0, 1] = b
    dh[0, 0, 0] = da
    dh[0, 0, 1] = db

    @pl.when(last)
    def _():
        act_halo[0] = b
        dh_halo[0] = db.astype(bf16)


def second(samples, h1, h1_halo, cot_h, cot_halo, block_w):
    bands, nw = h1.shape[:2]
    half = (SLOTS, HALF, D)
    return pl.pallas_call(
        second_kernel,
        grid=(bands, nw),
        in_specs=[
            pl.BlockSpec(memory_space=pltpu.SMEM),
            pl.BlockSpec((1, 1, 1) + half, lambda i, j: (i, j, 1, 0, 0, 0)),
            pl.BlockSpec((1, 1, 1) + half, lambda i, j: (i, jnp.minimum(j + 1, nw - 1), 0, 0, 0, 0)),
            pl.BlockSpec((1,) + half, lambda i, j: (i, 0, 0, 0)),
            pl.BlockSpec((1, 1) + half, lambda i, j: (i, 2 * j + 1, 0, 0, 0)),
            pl.BlockSpec((1, 1) + half, lambda i, j: (i, jnp.minimum(2 * j + 2, 2 * nw - 1), 0, 0, 0)),
            pl.BlockSpec((1,) + half, lambda i, j: (i, 0, 0, 0)),
        ]
        + block_specs(1),
        out_specs=[
            pl.BlockSpec((1, 1, 2) + half, lambda i, j: (i, j, 0, 0, 0, 0)),
            pl.BlockSpec((1, 1, 2) + half, lambda i, j: (i, j, 0, 0, 0, 0)),
            pl.BlockSpec((1,) + half, lambda i, j: (i, 0, 0, 0)),
            pl.BlockSpec((1,) + half, lambda i, j: (i, 0, 0, 0)),
        ]
        + [pl.BlockSpec(s, lambda *_, n=len(s): (0,) * n) for s in GRAD_SHAPES],
        out_shape=[
            jax.ShapeDtypeStruct((bands, nw, 2) + half, bf16),
            jax.ShapeDtypeStruct((bands, nw, 2) + half, f32),
            jax.ShapeDtypeStruct((bands,) + half, bf16),
            jax.ShapeDtypeStruct((bands,) + half, bf16),
        ]
        + [jax.ShapeDtypeStruct(s, f32) for s in GRAD_SHAPES],
        scratch_shapes=BOTH_SCRATCH,
        compiler_params=params(2),
    )(samples, h1, h1, h1_halo, cot_h, cot_h, cot_halo, *block_w)


CELL_SHAPES = [(D, D), (ZC, 2 * D), (2 * ZC, D)]


def third_kernel(amount, state, noise, da, db, dhalo, wlc, wlr, ws, wn, *rest):
    w = named(rest[:7])
    sg = rest[7]
    grads = rest[8:12]
    d_ws, d_wn, d_wl = rest[12:15]
    w["packed"], w["p"], w["ctx"], w["gp"] = rest[15:19]
    w.update(zip(GRAD_NAMES, grads))
    zero_at_start(rest[8:15])
    st = state[0, 0]
    nz = noise[0, 0]
    hidden, center, squash, sigma, latent, gate, cand = cell_forward(
        st, nz, wlc[...], wlr[...], ws[...], wn[...]
    )
    da_v = jnp.where(pl.program_id(1) == 0, dhalo[0].astype(f32), da[0, 0, 0])
    g = tile_of(da_v, db[0, 0, 0])
    _, dc = block_both(hidden, g, w, False, False)
    dc = dc.reshape(SLOTS, 64, D)
    wide = st.astype(f32)[None]
    rest_gate = 1.0 - gate
    d_pre = dc * (wide - cand) * gate * rest_gate
    d_cand = dc * rest_gate * (1.0 - cand * cand)
    direct = jnp.sum(dc * gate, axis=0)
    g_gate = jnp.sum(d_pre, axis=0).astype(bf16)
    d_ws[...] += mm_tn(st, g_gate)
    pre = d_pre.reshape(TILE, D).astype(bf16)
    cnd = d_cand.reshape(TILE, D).astype(bf16)
    d_wn[:, :D] += mm_tn(latent, pre)
    d_wn[:, D:] += mm_tn(latent, cnd)
    d_lat = mm_nt(pre, wn[:, :D]) + mm_nt(cnd, wn[:, D:])
    d_lat = d_lat.reshape(SLOTS, 64, ZC)
    amt = amount[...]
    d_center = jnp.sum(d_lat, axis=0) + amt * center
    d_sigma = jnp.sum(d_lat * nz, axis=0) + amt * sigma
    d_raw = (d_sigma * 0.5 * sigma - 0.5 * amt) * (1.0 - squash * squash)
    d_center, d_raw = d_center.astype(bf16), d_raw.astype(bf16)
    d_wl[:ZC] += mm_tn(d_center, st)
    d_wl[ZC:] += mm_tn(d_raw, st)
    total = direct + mm_nt(g_gate, ws[...]) + mm_nt(d_center, wlc[...]) + mm_nt(d_raw, wlr[...])
    sg[0] = from_halves(total.reshape(2, HALF, D))


def third(amount, state_h, noise_h, dh, dh_halo, cell_w, block_w):
    bands, nw = state_h.shape[:2]
    half = (SLOTS, HALF, D)
    return pl.pallas_call(
        third_kernel,
        grid=(bands, nw),
        in_specs=[
            full(amount),
            pl.BlockSpec((1, 1, 64, D), lambda i, j: (i, j, 0, 0)),
            pl.BlockSpec((1, 1, SLOTS, 64, ZC), lambda i, j: (i, j, 0, 0, 0)),
            pl.BlockSpec((1, 1, 1) + half, lambda i, j: (i, jnp.maximum(j - 1, 0), 1, 0, 0, 0)),
            pl.BlockSpec((1, 1, 1) + half, lambda i, j: (i, j, 0, 0, 0, 0)),
            pl.BlockSpec((1,) + half, lambda i, j: (i, 0, 0, 0)),
        ]
        + [full(a) for a in cell_w]
        + block_specs(0),
        out_specs=[pl.BlockSpec((1, WIN, WIN, D), lambda i, j: (0, i, j, 0))]
        + [pl.BlockSpec(s, lambda *_, n=len(s): (0,) * n) for s in GRAD_SHAPES + CELL_SHAPES],
        out_shape=[jax.ShapeDtypeStruct((1, bands * WIN, nw * WIN, D), f32)]
        + [jax.ShapeDtypeStruct(s, f32) for s in GRAD_SHAPES + CELL_SHAPES],
        scratch_shapes=BOTH_SCRATCH,
        compiler_params=params(2),
    )(amount, state_h, noise_h, dh, dh, dh_halo, *cell_w, *block_w)


def place_kernel(act, halo, out):
    nw = act.shape[1]
    for s in range(SLOTS):
        halves = [halo[0, s].astype(f32)]
        for j in range(nw):
            halves.append(act[0, j, 0, s].astype(f32))
            if j < nw - 1:
                halves.append(act[0, j, 1, s].astype(f32))
        out[0, s] = from_halves(jnp.stack(halves)).astype(bf16)


def place(act, halo):
    bands, nw = act.shape[:2]
    half = (SLOTS, HALF, D)
    return pl.pallas_call(
        place_kernel,
        grid=(bands,),
        in_specs=[
            pl.BlockSpec((1, nw, 2) + half, lambda i: (i, 0, 0, 0, 0, 0)),
            pl.BlockSpec((1,) + half, lambda i: (i, 0, 0, 0)),
        ],
        out_specs=pl.BlockSpec((1, SLOTS, WIN, nw * WIN, D), lambda i: (0, 0, i, 0, 0)),
        out_shape=jax.ShapeDtypeStruct((1, SLOTS, bands * WIN, nw * WIN, D), bf16),
        compiler_params=params(1),
    )(act, halo)


def shift_from(block, distance):
    n = lax.axis_size("lon")
    return lax.ppermute(block, "lon", [((i + distance) % n, i) for i in range(n)])


def offset_onehot():
    places = jnp.arange(WIN * WIN)
    row = places % HALF // 4
    col = places // HALF * 4 + places % 4
    target = (row[None, :] - row[:, None] + WIN - 1) * (2 * WIN - 1) + (
        col[None, :] - col[:, None] + WIN - 1
    )
    return (target[:, :, None] == jnp.arange((2 * WIN - 1) ** 2)).astype(f32)


def body(
    state,
    noise,
    samples,
    step,
    kl_weight,
    floor,
    latent_weight,
    state_weight,
    noise_weight,
    attention_gain,
    query_key_value,
    offset_bias,
    output_weight,
    feedforward_gain,
    up_weight,
    down_weight,
    cotangent,
):
    items, height, breadth, width = state.shape
    axes = ("lon", "batch")
    cells = items * height * breadth * lax.axis_size("lon") * lax.axis_size("batch")
    flat = state.reshape(-1, width)
    linear = jnp.dot(flat, latent_weight, preferred_element_type=f32)
    center = linear[:, :ZC]
    log_spread = spread_bound * jnp.tanh(linear[:, ZC:] / spread_bound)
    terms = 0.5 * (center * center + jnp.exp(log_spread) - 1.0 - log_spread)
    kl_mean = lax.psum(jnp.sum(terms, axis=0), axes) / cells
    beta = kl_weight * (step + 1).astype(f32) / WARM
    excess = sharpness * (kl_mean - floor)
    divergence = beta * jnp.mean(floor + jax.nn.softplus(excess) / sharpness)
    amount = (beta * jax.nn.sigmoid(excess) / (ZC * cells)).reshape(1, ZC)

    onehot = offset_onehot()
    bias = jnp.einsum(
        "bhr,kqr->bkhq", offset_bias * LOG2E, onehot, precision=lax.Precision.HIGHEST
    )
    bias = bias.reshape(2, 64, 2, 256).transpose(0, 2, 1, 3)
    cell_w = (latent_weight[:, :ZC], latent_weight[:, ZC:], state_weight, noise_weight)
    block_w = (
        attention_gain.reshape(2, 1, D),
        query_key_value,
        bias,
        output_weight,
        feedforward_gain.reshape(2, 1, D),
        up_weight,
        down_weight,
    )
    cot_h, state_h, noise_h = prep(samples, cotangent, state, noise)
    h1, h1_halo = first(state_h, noise_h, cell_w, block_w)
    halo = shift_from(jnp.stack([h1_halo, cot_h[:, 0]]), 1)
    act, dh, act_halo, dh_halo, *grads1 = second(samples, h1, halo[0], cot_h, halo[1], block_w)
    halo = shift_from(jnp.stack([dh_halo, act_halo]), -1)
    state_gradient, *grads0 = third(amount, state_h, noise_h, dh, halo[0], cell_w, block_w)
    activations = place(act, halo[1])
    d_ws, d_wn, d_wl = grads0[4:]

    def table(d):
        d = d.reshape(2, 64, 4, 64).transpose(0, 2, 1, 3).reshape(HEADS, -1)
        return jnp.dot(d, onehot.reshape(64 * 64, -1), precision=lax.Precision.HIGHEST)

    def wide(d):
        return jnp.concatenate([d[D * c : D * c + D] for c in range(d.shape[0] // D)], axis=1)

    parts = [(g[0], g[1], g[2], table(g[3])) for g in (grads0[:4], grads1)]
    parts, cell = lax.psum((parts, (d_ws, d_wn, d_wl)), axes)
    out = []
    for ff, at, small, tab in parts:
        out.append(
            (
                jnp.sum(small[:8], axis=0),
                wide(at[:768]),
                tab,
                at[768:],
                jnp.sum(small[8:], axis=0),
                wide(ff[:1024]),
                ff[1024:],
            )
        )
    stacked = [jnp.stack([a, b]) for a, b in zip(*out)]
    d_ws, d_wn, d_wl = cell
    return (activations, divergence, state_gradient, d_wl.T, d_ws, d_wn, *stacked)


def solution(mesh):
    return jax.shard_map(
        body,
        mesh=mesh,
        in_specs=(
            P("batch", None, "lon", None),
            P("batch", None, None, "lon", None),
            P("batch"),
            P(),
            P(),
            P(),
            P(),
            P(),
            P(),
            P(),
            P(),
            P(),
            P(),
            P(),
            P(),
            P(),
            P("batch", None, None, "lon", None),
        ),
        out_specs=(
            P("batch", None, None, "lon", None),
            P(),
            P("batch", None, "lon", None),
            P(),
            P(),
            P(),
            P(),
            P(),
            P(),
            P(),
            P(),
            P(),
            P(),
        ),
        check_vma=False,
    )
```

```python
import jax
import jax.numpy as jnp
from jax import lax
from jax.experimental import pallas as pl
from jax.experimental.pallas import tpu as pltpu
from jax.sharding import PartitionSpec as P

HEADS = 8
HD = 32
WIN = 8
WARM = 1000
SLOTS = 4
D = 256
FF = 1024
ZC = 32
HALF = WIN // 2 * WIN
TILE = SLOTS * WIN * WIN

eps_norm = 1e-05
sharpness = 8.0
spread_bound = 4.0
LOG2E = 1.4426950408889634
f32 = jnp.float32
bf16 = jnp.bfloat16


def mm(a, b):
    return lax.dot_general(a, b, (((1,), (0,)), ((), ())), preferred_element_type=f32)


def mm_nt(a, b):
    return lax.dot_general(a, b, (((1,), (1,)), ((), ())), preferred_element_type=f32)


def mm_tn(a, b):
    return lax.dot_general(a, b, (((0,), (0,)), ((), ())), preferred_element_type=f32)


def low_sublanes(shape):
    return lax.broadcasted_iota(jnp.int32, shape, len(shape) - 2) < 4


def to_halves(x):
    rows, cols, ch = x.shape
    n = cols // 8
    v = x.reshape(4, 2, n, 8, ch)
    a, b = v[:, 0], v[:, 1]
    low = low_sublanes(a.shape)
    first = jnp.where(low, a, pltpu.roll(b, 4, 2))
    second = jnp.where(low, pltpu.roll(a, 4, 2), b)
    first = first.transpose(1, 0, 2, 3)
    second = second.transpose(1, 0, 2, 3)
    return jnp.stack([first, second], axis=1).reshape(2 * n, HALF, ch)


def from_halves(x):
    n = x.shape[0] // 2
    ch = x.shape[-1]
    v = x.reshape(n, 2, 4, 8, ch)
    first, second = v[:, 0].transpose(1, 0, 2, 3), v[:, 1].transpose(1, 0, 2, 3)
    low = low_sublanes(first.shape)
    a = jnp.where(low, first, pltpu.roll(second, 4, 2))
    b = jnp.where(low, pltpu.roll(first, 4, 2), second)
    return jnp.stack([a, b], axis=1).reshape(8, 8 * n, ch)


def tile_of(first, second):
    return jnp.stack([first, second], axis=1).reshape(TILE, first.shape[-1])


def halves_of(tile):
    v = tile.reshape(SLOTS, 2, HALF, tile.shape[-1])
    return v[:, 0], v[:, 1]


def norm(x):
    c = x - jnp.mean(x, axis=-1, keepdims=True)
    r = lax.rsqrt(jnp.mean(c * c, axis=-1, keepdims=True) + eps_norm)
    return c * r, r


def norm_back(dy, xhat, r, gain):
    along = dy * gain
    inward = r * (
        along
        - jnp.mean(along, axis=-1, keepdims=True)
        - xhat * jnp.mean(along * xhat, axis=-1, keepdims=True)
    )
    return inward, jnp.sum((dy * xhat).reshape(-1, 8, D), axis=0)


def gelu_parts(x, slope):
    a = jnp.abs(x)
    t = 1.0 / (1.0 + a * (0.3275911 * 0.7071067811865476))
    e = jnp.exp2(x * x * (-0.5 * LOG2E))
    poly = t * (
        0.5 * 0.254829592
        + t
        * (
            0.5 * -0.284496736
            + t * (0.5 * 1.421413741 + t * (0.5 * -1.453152027 + t * (0.5 * 1.061405429)))
        )
    )
    tail = poly * e
    dist = jnp.where(x >= 0.0, 1.0 - tail, tail)
    if not slope:
        return x * dist, None
    return x * dist, dist + x * e * 0.3989422804014327


def lane_masks():
    lane = lax.broadcasted_iota(jnp.int32, (1, 128), 1)
    return [(lane >= 32 * j) & (lane < 32 * j + 32) for j in range(4)]


def spread_heads(x, masks):
    return jnp.concatenate([x * m for m in masks], axis=0)


def gather_heads(x, masks):
    v = x.reshape(4, 64, 128)
    return jnp.where(masks[0], v[0], jnp.where(masks[1], v[1], jnp.where(masks[2], v[2], v[3])))


def attention(packed, bias_ref, p_ref, ctx_ref):
    sel = lane_masks()
    ones = [m.astype(f32).astype(bf16) for m in sel]
    scale = HD ** (-0.5) * LOG2E
    for w in range(SLOTS):
        rows = slice(64 * w, 64 * w + 64)
        for g in range(2):
            lanes = lambda part: slice(256 * part + 128 * g, 256 * part + 128 * g + 128)
            q, k, v = packed[rows, lanes(0)], packed[rows, lanes(1)], packed[rows, lanes(2)]
            s = mm_nt(k, spread_heads(q, ones)) * scale + bias_ref[g]
            s = jnp.exp2(s - jnp.max(s, axis=0, keepdims=True))
            p = (s * (1.0 / jnp.sum(s, axis=0, keepdims=True))).astype(bf16)
            p_ref[2 * w + g] = p
            ctx_ref[rows, 128 * g : 128 * g + 128] = gather_heads(mm_tn(p, v), sel).astype(bf16)


def attention_back(packed, dctx, p_ref, gp_ref, dbias_ref):
    sel = lane_masks()
    ones = [m.astype(f32).astype(bf16) for m in sel]
    scale = HD ** (-0.5)
    for g in range(2):
        total = None
        for w in range(SLOTS):
            rows = slice(64 * w, 64 * w + 64)
            lanes = lambda part: slice(256 * part + 128 * g, 256 * part + 128 * g + 128)
            q, k, v = packed[rows, lanes(0)], packed[rows, lanes(1)], packed[rows, lanes(2)]
            p = p_ref[2 * w + g]
            spread = spread_heads(dctx[rows, lanes(0)], ones)
            gp_ref[rows, lanes(2)] = mm(p, spread).astype(bf16)
            dp = mm_nt(v, spread)
            pf = p.astype(f32)
            t = pf * dp
            ds = t - pf * jnp.sum(t, axis=0, keepdims=True)
            total = ds if total is None else total + ds
            ds = ds.astype(bf16)
            gp_ref[rows, lanes(1)] = (mm(ds, spread_heads(q, ones)) * scale).astype(bf16)
            gp_ref[rows, lanes(0)] = (gather_heads(mm_tn(ds, k), sel) * scale).astype(bf16)
        dbias_ref[g] += total


def block_forward(x, w):
    xhat, _ = norm(x)
    w["packed"][...] = mm((xhat * w["gain1"][...]).astype(bf16), w["qkv"][...]).astype(bf16)
    attention(w["packed"], w["bias"], w["p"], w["ctx"])
    mixed = x + mm(w["ctx"][...], w["out"][...])
    xhat2, _ = norm(mixed)
    normed2 = (xhat2 * w["gain2"][...]).astype(bf16)
    out = mixed
    for c in range(FF // 256):
        cols = slice(256 * c, 256 * c + 256)
        active, _ = gelu_parts(mm(normed2, w["up"][:, cols]), False)
        out = out + mm(active.astype(bf16), w["down"][cols, :])
    return out


def block_both(x, g, w, want_out, round_dn):
    gain1, gain2 = w["gain1"][...], w["gain2"][...]
    xhat, r = norm(x)
    normed = (xhat * gain1).astype(bf16)
    w["packed"][...] = mm(normed, w["qkv"][...]).astype(bf16)
    attention(w["packed"], w["bias"], w["p"], w["ctx"])
    mixed = x + mm(w["ctx"][...], w["out"][...])
    xhat2, r2 = norm(mixed)
    normed2 = (xhat2 * gain2).astype(bf16)
    gb = g.astype(bf16)
    out = mixed
    dn2 = None
    for c in range(FF // 256):
        cols = slice(256 * c, 256 * c + 256)
        active, slope = gelu_parts(mm(normed2, w["up"][:, cols]), True)
        active = active.astype(bf16)
        if want_out:
            out = out + mm(active, w["down"][cols, :])
        w["d_ff"][1024 + 256 * c : 1280 + 256 * c, :] += mm_tn(active, gb)
        d_inner = (mm_nt(gb, w["down"][cols, :]) * slope).astype(bf16)
        w["d_ff"][cols, :] += mm_tn(normed2, d_inner)
        part = mm_nt(d_inner, w["up"][:, cols])
        dn2 = part if dn2 is None else dn2 + part
    inward, dgain2 = norm_back(dn2, xhat2, r2, gain2)
    w["d_small"][8:16, :] += dgain2
    d_mixed = g + inward
    g_out = d_mixed.astype(bf16)
    w["d_at"][768:1024, :] += mm_tn(w["ctx"][...], g_out)
    dctx = mm_nt(g_out, w["out"][...]).astype(bf16)
    attention_back(w["packed"], dctx, w["p"], w["gp"], w["d_bias"])
    gp = w["gp"][...]
    for c in range(3):
        cols = slice(256 * c, 256 * c + 256)
        w["d_at"][cols, :] += mm_tn(normed, gp[:, cols])
    dn = mm_nt(gp, w["qkv"][...])
    if round_dn:
        dn = dn.astype(bf16).astype(f32)
    inward, dgain1 = norm_back(dn, xhat, r, gain1)
    w["d_small"][0:8, :] += dgain1
    return out, d_mixed + inward


LIMIT = 56 * 1024 * 1024


def params(n):
    return pltpu.CompilerParams(
        dimension_semantics=("arbitrary",) * n, vmem_limit_bytes=LIMIT
    )


def latent_head(state, wl_c, wl_r):
    center = mm(state, wl_c)
    squash = jnp.tanh(mm(state, wl_r) * (1.0 / spread_bound))
    return center, squash, jnp.exp((0.5 * spread_bound) * squash)


def prep_kernel(samples, cot, state, noise, wlc, wlr, cot_h, state_h, noise_h, kl):
    live = samples[0]
    for s in range(SLOTS):
        factor = jnp.where(s < live, 1.0, 0.0).astype(f32)
        cot_h[0, :, s] = (to_halves(cot[0, s].astype(f32)) * factor).astype(bf16)
        noise_h[0, :, s] = to_halves(noise[0, s]).reshape(4, 64, ZC)
    st = to_halves(state[0].astype(f32)).reshape(4, 64, D).astype(bf16)
    state_h[0] = st
    center, squash, sigma = latent_head(st.reshape(4 * 64, D), wlc[...], wlr[...])
    terms = 0.5 * (center * center + sigma * sigma - 1.0 - spread_bound * squash)

    @pl.when(pl.program_id(0) == 0)
    def _():
        kl[...] = jnp.zeros(kl.shape, f32)

    kl[:, :ZC] += jnp.sum(terms.reshape(-1, 8, ZC), axis=0)


def prep(samples, cot, state, noise, wlc, wlr):
    bands = state.shape[1] // WIN
    nw = state.shape[2] // WIN
    return pl.pallas_call(
        prep_kernel,
        grid=(bands,),
        in_specs=[
            pl.BlockSpec(memory_space=pltpu.SMEM),
            pl.BlockSpec((1, SLOTS, WIN, nw * WIN, D), lambda i: (0, 0, i, 0, 0)),
            pl.BlockSpec((1, WIN, nw * WIN, D), lambda i: (0, i, 0, 0)),
            pl.BlockSpec((1, SLOTS, WIN, nw * WIN, ZC), lambda i: (0, 0, i, 0, 0)),
            full(wlc),
            full(wlr),
        ],
        out_specs=[
            pl.BlockSpec((1, 2 * nw, SLOTS, HALF, D), lambda i: (i, 0, 0, 0, 0)),
            pl.BlockSpec((1, nw, 64, D), lambda i: (i, 0, 0, 0)),
            pl.BlockSpec((1, nw, SLOTS, 64, ZC), lambda i: (i, 0, 0, 0, 0)),
            pl.BlockSpec((8, D), lambda i: (0, 0)),
        ],
        out_shape=[
            jax.ShapeDtypeStruct((bands, 2 * nw, SLOTS, HALF, D), bf16),
            jax.ShapeDtypeStruct((bands, nw, 64, D), bf16),
            jax.ShapeDtypeStruct((bands, nw, SLOTS, 64, ZC), f32),
            jax.ShapeDtypeStruct((8, D), f32),
        ],
        compiler_params=params(1),
    )(samples, cot, state, noise, wlc, wlr)


def cell_forward(state, noise, wl_c, wl_r, ws, wn):
    center, squash, sigma = latent_head(state, wl_c, wl_r)
    latent = (center[None] + sigma[None] * noise).reshape(TILE, ZC).astype(bf16)
    mix = mm(latent, wn)
    gate = jax.nn.sigmoid(mm(state, ws)[None] + mix[:, :D].reshape(SLOTS, 64, D))
    cand = jnp.tanh(mix[:, D:].reshape(SLOTS, 64, D))
    wide = state.astype(f32)[None]
    hidden = gate * wide + (1.0 - gate) * cand
    return hidden.reshape(TILE, D), center, squash, sigma, latent, gate, cand


def full(a):
    return pl.BlockSpec(a.shape, lambda *_: (0,) * a.ndim)


def block_specs(k):
    return [
        pl.BlockSpec((1, 1, D), lambda *_: (k, 0, 0)),
        pl.BlockSpec((1, D, 3 * D), lambda *_: (k, 0, 0)),
        pl.BlockSpec((1, 2, 64, 256), lambda *_: (k, 0, 0, 0)),
        pl.BlockSpec((1, D, D), lambda *_: (k, 0, 0)),
        pl.BlockSpec((1, 1, D), lambda *_: (k, 0, 0)),
        pl.BlockSpec((1, D, FF), lambda *_: (k, 0, 0)),
        pl.BlockSpec((1, FF, D), lambda *_: (k, 0, 0)),
    ]


NAMES = ("gain1", "qkv", "bias", "out", "gain2", "up", "down")


def named(refs):
    return {n: r.at[0] for n, r in zip(NAMES, refs)}


FWD_SCRATCH = [
    pltpu.VMEM((TILE, 3 * D), bf16),
    pltpu.VMEM((2 * SLOTS, 64, 256), bf16),
    pltpu.VMEM((TILE, D), bf16),
]
BOTH_SCRATCH = FWD_SCRATCH + [pltpu.VMEM((TILE, 3 * D), bf16)]

GRAD_SHAPES = [(2048, D), (1024, D), (16, D), (2, 64, 256)]
GRAD_NAMES = ("d_ff", "d_at", "d_small", "d_bias")
GRAD_SCRATCH = [pltpu.VMEM(s, f32) for s in GRAD_SHAPES[:2]]
SMALL_SPECS = [pl.BlockSpec(s, lambda *_, n=len(s): (0,) * n) for s in GRAD_SHAPES[2:]]
SMALL_OUTS = [jax.ShapeDtypeStruct(s, f32) for s in GRAD_SHAPES[2:]]

ROWS_BLOCK = 3072
ROWS_CELL = 512


def first_kernel(state, noise, wlc, wlr, ws, wn, *rest):
    w = named(rest[:7])
    h1, halo = rest[7:9]
    w["packed"], w["p"], w["ctx"] = rest[9:12]
    hidden = cell_forward(state[0, 0], noise[0, 0], wlc[...], wlr[...], ws[...], wn[...])[0]
    out = block_forward(hidden, w)
    a, b = halves_of(out)
    h1[0, 0, 0] = a
    h1[0, 0, 1] = b
    @pl.when(pl.program_id(1) == 0)
    def _():
        halo[0] = a.astype(bf16)


def first(state_h, noise_h, cell_w, block_w):
    bands, nw = state_h.shape[:2]
    return pl.pallas_call(
        first_kernel,
        grid=(bands, nw),
        in_specs=[
            pl.BlockSpec((1, 1, 64, D), lambda i, j: (i, j, 0, 0)),
            pl.BlockSpec((1, 1, SLOTS, 64, ZC), lambda i, j: (i, j, 0, 0, 0)),
        ]
        + [full(a) for a in cell_w]
        + block_specs(0),
        out_specs=[
            pl.BlockSpec((1, 1, 2, SLOTS, HALF, D), lambda i, j: (i, j, 0, 0, 0, 0)),
            pl.BlockSpec((1, SLOTS, HALF, D), lambda i, j: (i, 0, 0, 0)),
        ],
        out_shape=[
            jax.ShapeDtypeStruct((bands, nw, 2, SLOTS, HALF, D), f32),
            jax.ShapeDtypeStruct((bands, SLOTS, HALF, D), bf16),
        ],
        scratch_shapes=FWD_SCRATCH,
        compiler_params=params(2),
    )(state_h, noise_h, *cell_w, *block_w)


def zero_at_start(refs):
    @pl.when((pl.program_id(0) == 0) & (pl.program_id(1) == 0))
    def _():
        for r in refs:
            r[...] = jnp.zeros(r.shape, r.dtype)


def at_end():
    return (pl.program_id(0) == pl.num_programs(0) - 1) & (
        pl.program_id(1) == pl.num_programs(1) - 1
    )


def second_kernel(samples, ha, hb, hhalo, ca, cb, chalo, *rest):
    w = named(rest[:7])
    act, dh, act_halo, dh_halo, packed_grads, d_small, d_bias = rest[7:14]
    w["packed"], w["p"], w["ctx"], w["gp"] = rest[14:18]
    grads = rest[18:20] + (d_small, d_bias)
    w.update(zip(GRAD_NAMES, grads))
    zero_at_start(grads)
    last = pl.program_id(1) == pl.num_programs(1) - 1
    hb_v = jnp.where(last, hhalo[0].astype(f32), hb[0, 0, 0])
    cb_v = jnp.where(last, chalo[0].astype(f32), cb[0, 0].astype(f32))
    x = tile_of(ha[0, 0, 0], hb_v)
    g = tile_of(ca[0, 0].astype(f32), cb_v)
    out, dx = block_both(x, g, w, True, True)
    live = samples[0]
    a, b = halves_of(out)
    factor = jnp.concatenate(
        [jnp.where(s < live, 1.0, 0.0) * jnp.ones((1, 1, D), f32) for s in range(SLOTS)]
    )
    a, b = (a * factor).astype(bf16), (b * factor).astype(bf16)
    da, db = halves_of(dx)
    act[0, 0, 0] = a
    act[0, 0, 1] = b
    dh[0, 0, 0] = da
    dh[0, 0, 1] = db

    @pl.when(last)
    def _():
        act_halo[0] = b
        dh_halo[0] = db.astype(bf16)

    @pl.when(at_end())
    def _():
        packed_grads[:2048] = grads[0][...].astype(bf16)
        packed_grads[2048:] = grads[1][...].astype(bf16)


def second(samples, h1, h1_halo, cot_h, cot_halo, block_w):
    bands, nw = h1.shape[:2]
    half = (SLOTS, HALF, D)
    return pl.pallas_call(
        second_kernel,
        grid=(bands, nw),
        in_specs=[
            pl.BlockSpec(memory_space=pltpu.SMEM),
            pl.BlockSpec((1, 1, 1) + half, lambda i, j: (i, j, 1, 0, 0, 0)),
            pl.BlockSpec((1, 1, 1) + half, lambda i, j: (i, jnp.minimum(j + 1, nw - 1), 0, 0, 0, 0)),
            pl.BlockSpec((1,) + half, lambda i, j: (i, 0, 0, 0)),
            pl.BlockSpec((1, 1) + half, lambda i, j: (i, 2 * j + 1, 0, 0, 0)),
            pl.BlockSpec((1, 1) + half, lambda i, j: (i, jnp.minimum(2 * j + 2, 2 * nw - 1), 0, 0, 0)),
            pl.BlockSpec((1,) + half, lambda i, j: (i, 0, 0, 0)),
        ]
        + block_specs(1),
        out_specs=[
            pl.BlockSpec((1, 1, 2) + half, lambda i, j: (i, j, 0, 0, 0, 0)),
            pl.BlockSpec((1, 1, 2) + half, lambda i, j: (i, j, 0, 0, 0, 0)),
            pl.BlockSpec((1,) + half, lambda i, j: (i, 0, 0, 0)),
            pl.BlockSpec((1,) + half, lambda i, j: (i, 0, 0, 0)),
        ]
        + [pl.BlockSpec((ROWS_BLOCK, D), lambda *_: (0, 0))]
        + SMALL_SPECS,
        out_shape=[
            jax.ShapeDtypeStruct((bands, nw, 2) + half, bf16),
            jax.ShapeDtypeStruct((bands, nw, 2) + half, f32),
            jax.ShapeDtypeStruct((bands,) + half, bf16),
            jax.ShapeDtypeStruct((bands,) + half, bf16),
        ]
        + [jax.ShapeDtypeStruct((ROWS_BLOCK, D), bf16)]
        + SMALL_OUTS,
        scratch_shapes=BOTH_SCRATCH + GRAD_SCRATCH,
        compiler_params=params(2),
    )(samples, h1, h1, h1_halo, cot_h, cot_h, cot_halo, *block_w)


CELL_SHAPES = [(D, D), (2 * ZC, D), (2 * ZC, D), (2 * ZC, D)]


def divergence_parts(center, squash, sigma):
    return center.astype(bf16), (
        0.5 * (sigma * sigma - 1.0) * (1.0 - squash * squash)
    ).astype(bf16)


def third_kernel(state, noise, da, db, dhalo, wlc, wlr, ws, wn, *rest):
    w = named(rest[:7])
    sg, packed_grads, d_small, d_bias = rest[7:11]
    w["packed"], w["p"], w["ctx"], w["gp"] = rest[11:15]
    grads = rest[15:17] + (d_small, d_bias)
    d_ws, d_wn, d_wl, d_kl = rest[17:21]
    w.update(zip(GRAD_NAMES, grads))
    zero_at_start(grads + rest[17:21])
    st = state[0, 0]
    nz = noise[0, 0]
    hidden, center, squash, sigma, latent, gate, cand = cell_forward(
        st, nz, wlc[...], wlr[...], ws[...], wn[...]
    )
    da_v = jnp.where(pl.program_id(1) == 0, dhalo[0].astype(f32), da[0, 0, 0])
    g = tile_of(da_v, db[0, 0, 0])
    _, dc = block_both(hidden, g, w, False, False)
    dc = dc.reshape(SLOTS, 64, D)
    wide = st.astype(f32)[None]
    rest_gate = 1.0 - gate
    d_pre = dc * (wide - cand) * gate * rest_gate
    d_cand = dc * rest_gate * (1.0 - cand * cand)
    direct = jnp.sum(dc * gate, axis=0)
    g_gate = jnp.sum(d_pre, axis=0).astype(bf16)
    d_ws[...] += mm_tn(st, g_gate)
    pre = d_pre.reshape(TILE, D).astype(bf16)
    cnd = d_cand.reshape(TILE, D).astype(bf16)
    d_wn[:ZC] += mm_tn(latent, pre)
    d_wn[ZC:] += mm_tn(latent, cnd)
    d_lat = mm_nt(pre, wn[:, :D]) + mm_nt(cnd, wn[:, D:])
    d_lat = d_lat.reshape(SLOTS, 64, ZC)
    d_center = jnp.sum(d_lat, axis=0)
    d_raw = jnp.sum(d_lat * nz, axis=0) * 0.5 * sigma * (1.0 - squash * squash)
    d_center, d_raw = d_center.astype(bf16), d_raw.astype(bf16)
    d_wl[:ZC] += mm_tn(d_center, st)
    d_wl[ZC:] += mm_tn(d_raw, st)
    kl_center, kl_raw = divergence_parts(center, squash, sigma)
    d_kl[:ZC] += mm_tn(kl_center, st)
    d_kl[ZC:] += mm_tn(kl_raw, st)
    total = direct + mm_nt(g_gate, ws[...]) + mm_nt(d_center, wlc[...]) + mm_nt(d_raw, wlr[...])
    sg[0] = from_halves(total.reshape(2, HALF, D))

    @pl.when(at_end())
    def _():
        packed_grads[:2048] = grads[0][...].astype(bf16)
        packed_grads[2048:3072] = grads[1][...].astype(bf16)
        packed_grads[3072:3328] = d_ws[...].astype(bf16)
        packed_grads[3328:3392] = d_wn[...].astype(bf16)
        packed_grads[3392:3456] = d_wl[...].astype(bf16)
        packed_grads[3456:3520] = d_kl[...].astype(bf16)
        packed_grads[3520:] = jnp.zeros((64, D), bf16)


def third(state_h, noise_h, dh, dh_halo, cell_w, block_w):
    bands, nw = state_h.shape[:2]
    half = (SLOTS, HALF, D)
    return pl.pallas_call(
        third_kernel,
        grid=(bands, nw),
        in_specs=[
            pl.BlockSpec((1, 1, 64, D), lambda i, j: (i, j, 0, 0)),
            pl.BlockSpec((1, 1, SLOTS, 64, ZC), lambda i, j: (i, j, 0, 0, 0)),
            pl.BlockSpec((1, 1, 1) + half, lambda i, j: (i, jnp.maximum(j - 1, 0), 1, 0, 0, 0)),
            pl.BlockSpec((1, 1, 1) + half, lambda i, j: (i, j, 0, 0, 0, 0)),
            pl.BlockSpec((1,) + half, lambda i, j: (i, 0, 0, 0)),
        ]
        + [full(a) for a in cell_w]
        + block_specs(0),
        out_specs=[pl.BlockSpec((1, WIN, WIN, D), lambda i, j: (0, i, j, 0))]
        + [pl.BlockSpec((ROWS_BLOCK + ROWS_CELL, D), lambda *_: (0, 0))]
        + SMALL_SPECS,
        out_shape=[jax.ShapeDtypeStruct((1, bands * WIN, nw * WIN, D), f32)]
        + [jax.ShapeDtypeStruct((ROWS_BLOCK + ROWS_CELL, D), bf16)]
        + SMALL_OUTS,
        scratch_shapes=BOTH_SCRATCH + GRAD_SCRATCH + [pltpu.VMEM(s, f32) for s in CELL_SHAPES],
        compiler_params=params(2),
    )(state_h, noise_h, dh, dh, dh_halo, *cell_w, *block_w)


def place_kernel(act, halo, out):
    nw = act.shape[1]
    for s in range(SLOTS):
        halves = [halo[0, s].astype(f32)]
        for j in range(nw):
            halves.append(act[0, j, 0, s].astype(f32))
            if j < nw - 1:
                halves.append(act[0, j, 1, s].astype(f32))
        out[0, s] = from_halves(jnp.stack(halves)).astype(bf16)


def place(act, halo):
    bands, nw = act.shape[:2]
    half = (SLOTS, HALF, D)
    return pl.pallas_call(
        place_kernel,
        grid=(bands,),
        in_specs=[
            pl.BlockSpec((1, nw, 2) + half, lambda i: (i, 0, 0, 0, 0, 0)),
            pl.BlockSpec((1,) + half, lambda i: (i, 0, 0, 0)),
        ],
        out_specs=pl.BlockSpec((1, SLOTS, WIN, nw * WIN, D), lambda i: (0, 0, i, 0, 0)),
        out_shape=jax.ShapeDtypeStruct((1, SLOTS, bands * WIN, nw * WIN, D), bf16),
        compiler_params=params(1),
    )(act, halo)


def finish_kernel(state, part, wlc, wlr, amount, out):
    rows = state.shape[1] * state.shape[2]
    center, squash, sigma = latent_head(state[0].reshape(rows, D), wlc[...], wlr[...])
    kl_center, kl_raw = divergence_parts(center, squash, sigma)
    amt = amount[...]
    g_center = (kl_center.astype(f32) * amt).astype(bf16)
    g_raw = (kl_raw.astype(f32) * amt).astype(bf16)
    add = mm_nt(g_center, wlc[...]) + mm_nt(g_raw, wlr[...])
    out[0] = part[0] + add.reshape(state.shape[1:])


def finish(state, part, wlc, wlr, amount):
    return pl.pallas_call(
        finish_kernel,
        out_shape=jax.ShapeDtypeStruct(part.shape, f32),
        compiler_params=pltpu.CompilerParams(vmem_limit_bytes=LIMIT),
    )(state, part, wlc, wlr, amount)


def shift_from(block, distance):
    n = lax.axis_size("lon")
    return lax.ppermute(block, "lon", [((i + distance) % n, i) for i in range(n)])


def summed(parts):
    n_lon, n_batch = lax.axis_size("lon"), lax.axis_size("batch")
    axes = ("lon", "batch")
    me = lax.axis_index("lon") * n_batch + lax.axis_index("batch")
    bits = [1 << i for i in range(1, (n_lon * n_batch).bit_length() - 1)]
    lon = bits.pop()
    near, far = bits[:1], bits[1:]
    orders = (near + [lon] + far, [lon] + far[:1] + near + far[1:])
    core = me & 1

    def swap(block, pick):
        return lax.ppermute(
            block, axes, [(i, i ^ pick(i & 1)) for i in range(n_lon * n_batch)]
        )

    steps = [(lambda c: 1, core)]
    for first, second in zip(*orders):
        bit = jnp.where(core == 0, first, second)
        steps.append(
            (lambda c, pair=(first, second): pair[c], (jnp.bitwise_and(me, bit) != 0).astype(jnp.int32))
        )

    def half(block, at):
        size = block.shape[0] // 2
        return lax.dynamic_slice_in_dim(block, at * size, size, 0)

    total, offset = None, 0
    size = sum(p.shape[0] for p in parts)
    for pick, bit in steps:
        if total is None:
            keep = jnp.concatenate([half(p, bit) for p in parts])
            send = jnp.concatenate([half(p, 1 - bit) for p in parts])
        else:
            keep, send = half(total, bit), half(total, 1 - bit)
        size //= 2
        offset = offset + bit * size
        total = (keep.astype(f32) + swap(send, pick).astype(f32)).astype(bf16)
    whole = jnp.zeros((sum(p.shape[0] for p in parts), parts[0].shape[1]), bf16)
    whole = lax.dynamic_update_slice_in_dim(whole, total, offset, 0)
    for pick, bit in reversed(steps):
        got = swap(lax.dynamic_slice_in_dim(whole, offset, size, 0), pick)
        whole = lax.dynamic_update_slice_in_dim(whole, got, offset + (1 - 2 * bit) * size, 0)
        offset = offset - bit * size
        size *= 2
    return whole


def offset_onehot():
    places = jnp.arange(WIN * WIN)
    row = places % HALF // 4
    col = places // HALF * 4 + places % 4
    target = (row[None, :] - row[:, None] + WIN - 1) * (2 * WIN - 1) + (
        col[None, :] - col[:, None] + WIN - 1
    )
    return (target[:, :, None] == jnp.arange((2 * WIN - 1) ** 2)).astype(f32)


def body(
    state,
    noise,
    samples,
    step,
    kl_weight,
    floor,
    latent_weight,
    state_weight,
    noise_weight,
    attention_gain,
    query_key_value,
    offset_bias,
    output_weight,
    feedforward_gain,
    up_weight,
    down_weight,
    cotangent,
):
    items, height, breadth, width = state.shape
    axes = ("lon", "batch")
    cells = items * height * breadth * lax.axis_size("lon") * lax.axis_size("batch")
    onehot = offset_onehot()
    bias = jnp.einsum(
        "bhr,kqr->bkhq", offset_bias * LOG2E, onehot, precision=lax.Precision.HIGHEST
    )
    bias = bias.reshape(2, 64, 2, 256).transpose(0, 2, 1, 3)
    cell_w = (latent_weight[:, :ZC], latent_weight[:, ZC:], state_weight, noise_weight)
    block_w = (
        attention_gain.reshape(2, 1, D),
        query_key_value,
        bias,
        output_weight,
        feedforward_gain.reshape(2, 1, D),
        up_weight,
        down_weight,
    )
    wlc, wlr = cell_w[:2]
    cot_h, state_h, noise_h, kl = prep(samples, cotangent, state, noise, wlc, wlr)
    h1, h1_halo = first(state_h, noise_h, cell_w, block_w)
    halo = shift_from(jnp.stack([h1_halo, cot_h[:, 0]]), 1)
    act, dh, act_halo, dh_halo, grads1, small1, bias1 = second(
        samples, h1, halo[0], cot_h, halo[1], block_w
    )
    halo = shift_from(jnp.stack([dh_halo, act_halo]), -1)
    part, grads0, small0, bias0 = third(state_h, noise_h, dh, halo[0], cell_w, block_w)
    activations = place(act, halo[1])

    table = jnp.stack([bias0, bias1]).reshape(2, 2, 64, 4, 64).transpose(0, 1, 3, 2, 4)
    table = jnp.dot(
        table.reshape(2 * HEADS, -1), onehot.reshape(64 * 64, -1), precision=lax.Precision.HIGHEST
    )
    gains = jnp.sum(jnp.stack([small0, small1]).reshape(4, 8, D), axis=1)
    small = jnp.concatenate(
        [jnp.pad(table, ((0, 0), (0, D - table.shape[1]))), gains, kl, jnp.zeros((36, D), f32)]
    ).astype(bf16)
    grads0 = lax.dynamic_update_slice_in_dim(grads0, small, ROWS_BLOCK + ROWS_CELL - 64, 0)
    whole = summed([grads1, grads0])

    ha, hb = ROWS_BLOCK // 2, (ROWS_BLOCK + ROWS_CELL) // 2
    g1 = jnp.concatenate([whole[:ha], whole[ha + hb : 2 * ha + hb]]).astype(f32)
    g0 = jnp.concatenate([whole[ha : ha + hb], whole[2 * ha + hb :]]).astype(f32)
    kl_mean = jnp.sum(g0[3540:3548, :ZC], axis=0) / cells
    beta = kl_weight * (step + 1).astype(f32) / WARM
    excess = sharpness * (kl_mean - floor)
    divergence = beta * jnp.mean(floor + jax.nn.softplus(excess) / sharpness)
    amount = (beta * jax.nn.sigmoid(excess) / (ZC * cells)).reshape(1, ZC)
    state_gradient = finish(state, part, wlc, wlr, amount)

    def wide(d):
        return jnp.concatenate([d[D * c : D * c + D] for c in range(d.shape[0] // D)], axis=1)

    def both(f):
        return jnp.stack([f(g0), f(g1)])

    table, gains = g0[3520:3536], g0[3536:3540].reshape(2, 2, D)
    weigh = jnp.concatenate([amount, amount], axis=1).reshape(2 * ZC, 1)
    d_wl = (g0[3392:3456] + weigh * g0[3456:3520]).T
    d_wn = jnp.concatenate([g0[3328:3360], g0[3360:3392]], axis=1)
    return (
        activations,
        divergence,
        state_gradient,
        d_wl,
        g0[3072:3328],
        d_wn,
        gains[:, 0],
        both(lambda g: wide(g[2048:2816])),
        table[:, : (2 * WIN - 1) ** 2].reshape(2, HEADS, -1),
        both(lambda g: g[2816:3072]),
        gains[:, 1],
        both(lambda g: wide(g[:1024])),
        both(lambda g: g[1024:2048]),
    )


def solution(mesh):
    return jax.shard_map(
        body,
        mesh=mesh,
        in_specs=(
            P("batch", None, "lon", None),
            P("batch", None, None, "lon", None),
            P("batch"),
            P(),
            P(),
            P(),
            P(),
            P(),
            P(),
            P(),
            P(),
            P(),
            P(),
            P(),
            P(),
            P(),
            P("batch", None, None, "lon", None),
        ),
        out_specs=(
            P("batch", None, None, "lon", None),
            P(),
            P("batch", None, "lon", None),
            P(),
            P(),
            P(),
            P(),
            P(),
            P(),
            P(),
            P(),
            P(),
            P(),
        ),
        check_vma=False,
    )
```

```python
import functools

import jax
import jax.numpy as jnp
from jax import lax
from jax.experimental import pallas as pl
from jax.experimental.pallas import tpu as pltpu
from jax.sharding import PartitionSpec as P

HEADS = 8
HD = 32
WIN = 8
WARM = 1000
SLOTS = 4
D = 256
FF = 1024
ZC = 32
HALF = WIN // 2 * WIN

eps_norm = 1e-05
sharpness = 8.0
spread_bound = 4.0
LOG2E = 1.4426950408889634
f32 = jnp.float32
bf16 = jnp.bfloat16


def mm(a, b):
    return lax.dot_general(a, b, (((1,), (0,)), ((), ())), preferred_element_type=f32)


def mm_nt(a, b):
    return lax.dot_general(a, b, (((1,), (1,)), ((), ())), preferred_element_type=f32)


def mm_tn(a, b):
    return lax.dot_general(a, b, (((0,), (0,)), ((), ())), preferred_element_type=f32)


def low_sublanes(shape):
    return lax.broadcasted_iota(jnp.int32, shape, len(shape) - 2) < 4


def to_halves(x):
    rows, cols, ch = x.shape
    n = cols // 8
    v = x.reshape(4, 2, n, 8, ch)
    a, b = v[:, 0], v[:, 1]
    low = low_sublanes(a.shape)
    first = jnp.where(low, a, pltpu.roll(b, 4, 2))
    second = jnp.where(low, pltpu.roll(a, 4, 2), b)
    first = first.transpose(1, 0, 2, 3)
    second = second.transpose(1, 0, 2, 3)
    return jnp.stack([first, second], axis=1).reshape(2 * n, HALF, ch)


def from_halves(x):
    n = x.shape[0] // 2
    ch = x.shape[-1]
    v = x.reshape(n, 2, 4, 8, ch)
    first, second = v[:, 0].transpose(1, 0, 2, 3), v[:, 1].transpose(1, 0, 2, 3)
    low = low_sublanes(first.shape)
    a = jnp.where(low, first, pltpu.roll(second, 4, 2))
    b = jnp.where(low, pltpu.roll(first, 4, 2), second)
    return jnp.stack([a, b], axis=1).reshape(8, 8 * n, ch)


def tile_of(first, second):
    return jnp.stack([first, second], axis=1).reshape(-1, first.shape[-1])


def halves_of(tile):
    v = tile.reshape(-1, 2, HALF, tile.shape[-1])
    return v[:, 0], v[:, 1]


def norm(x):
    c = x - jnp.mean(x, axis=-1, keepdims=True)
    r = lax.rsqrt(jnp.mean(c * c, axis=-1, keepdims=True) + eps_norm)
    return c * r, r


def norm_back(dy, xhat, r, gain):
    along = dy * gain
    inward = r * (
        along
        - jnp.mean(along, axis=-1, keepdims=True)
        - xhat * jnp.mean(along * xhat, axis=-1, keepdims=True)
    )
    return inward, jnp.sum((dy * xhat).reshape(-1, 8, D), axis=0)


def gelu_parts(x, slope):
    a = jnp.abs(x)
    t = 1.0 / (1.0 + a * (0.3275911 * 0.7071067811865476))
    e = jnp.exp2(x * x * (-0.5 * LOG2E))
    poly = t * (
        0.5 * 0.254829592
        + t
        * (
            0.5 * -0.284496736
            + t * (0.5 * 1.421413741 + t * (0.5 * -1.453152027 + t * (0.5 * 1.061405429)))
        )
    )
    tail = poly * e
    dist = jnp.where(x >= 0.0, 1.0 - tail, tail)
    if not slope:
        return x * dist, None
    return x * dist, dist + x * e * 0.3989422804014327


def lane_masks():
    lane = lax.broadcasted_iota(jnp.int32, (1, 128), 1)
    return [(lane >= 32 * j) & (lane < 32 * j + 32) for j in range(4)]


def spread_heads(x, masks):
    return jnp.concatenate([x * m for m in masks], axis=0)


def gather_heads(x, masks):
    v = x.reshape(4, 64, 128)
    return jnp.where(masks[0], v[0], jnp.where(masks[1], v[1], jnp.where(masks[2], v[2], v[3])))


def pieces(rows):
    return [slice(r, r + 64) for r in range(0, rows, 64)]


def staged(count, *stages):
    for n in range(count + len(stages) - 1):
        for late, stage in enumerate(stages):
            if 0 <= n - late < count:
                stage(n - late)


def unit_of(n):
    g = n % 2
    rows = slice(64 * (n // 2), 64 * (n // 2) + 64)
    return rows, lambda part: slice(256 * part + 128 * g, 256 * part + 128 * g + 128), g


def attention(w):
    sel = lane_masks()
    ones = [m.astype(f32).astype(bf16) for m in sel]
    scale = HD ** (-0.5) * LOG2E

    def scores(n):
        rows, lanes, g = unit_of(n)
        q, k = w["packed"][rows, lanes(0)], w["packed"][rows, lanes(1)]
        w["s"][n % 4] = mm_nt(k, spread_heads(q, ones))

    def softmax(n):
        s = w["s"][n % 4] * scale + w["bias"][n % 2]
        s = jnp.exp2(s - jnp.max(s, axis=0, keepdims=True))
        w["p"][n] = (s * (1.0 / jnp.sum(s, axis=0, keepdims=True))).astype(bf16)

    def values(n):
        rows, lanes, g = unit_of(n)
        found = gather_heads(mm_tn(w["p"][n], w["packed"][rows, lanes(2)]), sel)
        w["ctx"][rows, lanes(0)] = found.astype(bf16)

    staged(w["p"].shape[0], scores, softmax, values)


def attention_back(w):
    sel = lane_masks()
    ones = [m.astype(f32).astype(bf16) for m in sel]
    scale = HD ** (-0.5)

    def upstream(n):
        rows, lanes, g = unit_of(n)
        spread = spread_heads(w["dctx"][rows, lanes(0)], ones)
        w["gp"][rows, lanes(2)] = mm(w["p"][n], spread).astype(bf16)
        w["s"][n % 4] = mm_nt(w["packed"][rows, lanes(2)], spread)

    def inward(n):
        p = w["p"][n].astype(f32)
        t = p * w["s"][n % 4]
        ds = t - p * jnp.sum(t, axis=0, keepdims=True)
        w["d_bias"][n % 2] += ds
        w["ds"][n % 4] = ds.astype(bf16)

    def outer(n):
        rows, lanes, g = unit_of(n)
        ds = w["ds"][n % 4]
        q, k = w["packed"][rows, lanes(0)], w["packed"][rows, lanes(1)]
        w["gp"][rows, lanes(1)] = (mm(ds, spread_heads(q, ones)) * scale).astype(bf16)
        w["gp"][rows, lanes(0)] = (gather_heads(mm_tn(ds, k), sel) * scale).astype(bf16)

    staged(w["p"].shape[0], upstream, inward, outer)


def attend(x_ref, w):
    rows = x_ref.shape[0]
    gain1, gain2 = w["gain1"][...], w["gain2"][...]
    r1, r2 = [], []
    for at in pieces(rows):
        xhat, r = norm(x_ref[at])
        r1.append(r)
        w["normed"][at] = (xhat * gain1).astype(bf16)
    w["packed"][...] = mm(w["normed"][...], w["qkv"][...]).astype(bf16)
    attention(w)
    w["mixed"][...] = x_ref[...] + mm(w["ctx"][...], w["out"][...])
    for at in pieces(rows):
        xhat, r = norm(w["mixed"][at])
        r2.append(r)
        w["xhat"][at] = xhat
        w["normed2"][at] = (xhat * gain2).astype(bf16)
    return r1, r2


def block_forward(x_ref, w):
    attend(x_ref, w)
    rows = x_ref.shape[0]

    def start(c):
        w["a"][c % 2] = mm(w["normed2"][...], w["up"][:, 256 * c : 256 * c + 256])

    start(0)
    for c in range(FF // 256):
        cols = slice(256 * c, 256 * c + 256)
        if c < FF // 256 - 1:
            start(c + 1)
        for at in pieces(rows):
            w["active"][at, cols] = gelu_parts(w["a"][c % 2, at], False)[0].astype(bf16)
    return w["mixed"][...] + mm(w["active"][...], w["down"][...])


def block_both(x_ref, g_ref, w, want_out, round_dn):
    rows = x_ref.shape[0]
    gain1, gain2 = w["gain1"][...], w["gain2"][...]
    r1, r2 = attend(x_ref, w)
    normed2_t = w["normed2"][...].T
    gb = g_ref[...].astype(bf16)
    gb_t = gb.T

    def start(c):
        cols = slice(256 * c, 256 * c + 256)
        w["a"][c % 2] = mm(w["normed2"][...], w["up"][:, cols])
        w["b"][c % 2] = mm_nt(gb, w["down"][cols, :])

    start(0)
    for c in range(FF // 256):
        cols = slice(256 * c, 256 * c + 256)
        if c < FF // 256 - 1:
            start(c + 1)
        for at in pieces(rows):
            active, slope = gelu_parts(w["a"][c % 2, at], True)
            w["active"][at, cols] = active.astype(bf16)
            w["d_inner"][at, cols] = (w["b"][c % 2, at] * slope).astype(bf16)
        w["d_ff"][1024 + 256 * c : 1280 + 256 * c, :] += mm(gb_t, w["active"][:, cols])
        w["d_ff"][cols, :] += mm(normed2_t, w["d_inner"][:, cols])
        if c == FF // 512:
            w["dn"][...] = mm_nt(w["d_inner"][:, : FF // 2], w["up"][:, : FF // 2])
    w["dn"][...] += mm_nt(w["d_inner"][:, FF // 2 :], w["up"][:, FF // 2 :])
    out = None
    if want_out:
        out = w["mixed"][...] + mm(w["active"][...], w["down"][...])
    dgain = None
    for at, r in zip(pieces(rows), r2):
        inward, part = norm_back(w["dn"][at], w["xhat"][at], r, gain2)
        dgain = part if dgain is None else dgain + part
        d_mixed = g_ref[at] + inward
        g_ref[at] = d_mixed
        w["g_out"][at] = d_mixed.astype(bf16)
    w["d_small"][8:16, :] += dgain
    w["dctx"][...] = mm_nt(w["g_out"][...], w["out"][...]).astype(bf16)
    w["d_at"][768:1024, :] += mm_tn(w["ctx"][...], w["g_out"][...])
    attention_back(w)
    w["dn"][...] = mm_nt(w["gp"][...], w["qkv"][...])
    normed_t = w["normed"][...].T
    for c in range(3):
        cols = slice(256 * c, 256 * c + 256)
        w["d_at"][cols, :] += mm(normed_t, w["gp"][:, cols])
    dgain = None
    for at, r in zip(pieces(rows), r1):
        dn = w["dn"][at]
        if round_dn:
            dn = dn.astype(bf16).astype(f32)
        x = x_ref[at]
        xhat = (x - jnp.mean(x, axis=-1, keepdims=True)) * r
        inward, part = norm_back(dn, xhat, r, gain1)
        dgain = part if dgain is None else dgain + part
        g_ref[at] = g_ref[at] + inward
    w["d_small"][0:8, :] += dgain
    return out


LIMIT = 56 * 1024 * 1024


def params(n):
    return pltpu.CompilerParams(
        dimension_semantics=("arbitrary",) * n, vmem_limit_bytes=LIMIT
    )


def latent_head(state, wl_c, wl_r):
    center = mm(state, wl_c)
    squash = jnp.tanh(mm(state, wl_r) * (1.0 / spread_bound))
    return center, squash, jnp.exp((0.5 * spread_bound) * squash)


def prep_kernel(samples, cot, state, noise, wlc, wlr, cot_h, state_h, noise_h, kl):
    live = samples[0]
    for s in range(SLOTS):
        factor = jnp.where(s < live, 1.0, 0.0).astype(f32)
        cot_h[:, s] = (to_halves(cot[0, s].astype(f32)) * factor).astype(bf16)
        noise_h[:, 0, s] = to_halves(noise[0, s]).reshape(4, 64, ZC)
    st = to_halves(state[0].astype(f32)).reshape(4, 64, D).astype(bf16)
    state_h[:, 0] = st
    center, squash, sigma = latent_head(st.reshape(4 * 64, D), wlc[...], wlr[...])
    terms = 0.5 * (center * center + sigma * sigma - 1.0 - spread_bound * squash)

    @pl.when(pl.program_id(0) == 0)
    def _():
        kl[...] = jnp.zeros(kl.shape, f32)

    kl[:, :ZC] += jnp.sum(terms.reshape(-1, 8, ZC), axis=0)


def prep(samples, cot, state, noise, wlc, wlr):
    bands = state.shape[1] // WIN
    nw = state.shape[2] // WIN
    return pl.pallas_call(
        prep_kernel,
        grid=(bands,),
        in_specs=[
            pl.BlockSpec(memory_space=pltpu.SMEM),
            pl.BlockSpec((1, SLOTS, WIN, nw * WIN, D), lambda i: (0, 0, i, 0, 0)),
            pl.BlockSpec((1, WIN, nw * WIN, D), lambda i: (0, i, 0, 0)),
            pl.BlockSpec((1, SLOTS, WIN, nw * WIN, ZC), lambda i: (0, 0, i, 0, 0)),
            full(wlc),
            full(wlr),
        ],
        out_specs=[
            pl.BlockSpec((2 * nw, SLOTS, HALF, D), lambda i: (0, i, 0, 0)),
            pl.BlockSpec((nw, 1, 64, D), lambda i: (0, i, 0, 0)),
            pl.BlockSpec((nw, 1, SLOTS, 64, ZC), lambda i: (0, i, 0, 0, 0)),
            pl.BlockSpec((8, D), lambda i: (0, 0)),
        ],
        out_shape=[
            jax.ShapeDtypeStruct((2 * nw, bands * SLOTS, HALF, D), bf16),
            jax.ShapeDtypeStruct((nw, bands, 64, D), bf16),
            jax.ShapeDtypeStruct((nw, bands, SLOTS, 64, ZC), f32),
            jax.ShapeDtypeStruct((8, D), f32),
        ],
        compiler_params=params(1),
    )(samples, cot, state, noise, wlc, wlr)


def cell_forward(state, noise, wl_c, wl_r, ws, wn):
    bands = state.shape[0]
    flat = state.reshape(bands * 64, D)
    over = lambda x: x.reshape(bands, 1, 64, x.shape[-1])
    center, squash, sigma = latent_head(flat, wl_c, wl_r)
    latent = (over(center) + over(sigma) * noise).reshape(-1, ZC).astype(bf16)
    mix = mm(latent, wn)
    gate = jax.nn.sigmoid(over(mm(flat, ws)) + mix[:, :D].reshape(bands, SLOTS, 64, D))
    cand = jnp.tanh(mix[:, D:].reshape(bands, SLOTS, 64, D))
    hidden = gate * over(flat.astype(f32)) + (1.0 - gate) * cand
    return hidden.reshape(-1, D), center, squash, sigma, latent, gate, cand


def full(a):
    return pl.BlockSpec(a.shape, lambda *_: (0,) * a.ndim)


def block_specs(k):
    return [
        pl.BlockSpec((1, 1, D), lambda *_: (k, 0, 0)),
        pl.BlockSpec((1, D, 3 * D), lambda *_: (k, 0, 0)),
        pl.BlockSpec((1, 2, 64, 256), lambda *_: (k, 0, 0, 0)),
        pl.BlockSpec((1, D, D), lambda *_: (k, 0, 0)),
        pl.BlockSpec((1, 1, D), lambda *_: (k, 0, 0)),
        pl.BlockSpec((1, D, FF), lambda *_: (k, 0, 0)),
        pl.BlockSpec((1, FF, D), lambda *_: (k, 0, 0)),
    ]


NAMES = ("gain1", "qkv", "bias", "out", "gain2", "up", "down")


def named(refs):
    return {n: r.at[0] for n, r in zip(NAMES, refs)}


def tile_refs(rows, both):
    fwd = [
        ("x", (rows, D), f32),
        ("normed", (rows, D), bf16),
        ("packed", (rows, 3 * D), bf16),
        ("p", (rows // 32, 64, 256), bf16),
        ("s", (4, 64, 256), f32),
        ("ctx", (rows, D), bf16),
        ("mixed", (rows, D), f32),
        ("xhat", (rows, D), f32),
        ("normed2", (rows, D), bf16),
        ("a", (2, rows, 256), f32),
        ("active", (rows, FF), bf16),
    ]
    back = [
        ("g", (rows, D), f32),
        ("b", (2, rows, 256), f32),
        ("d_inner", (rows, FF), bf16),
        ("dn", (rows, D), f32),
        ("g_out", (rows, D), bf16),
        ("dctx", (rows, D), bf16),
        ("ds", (4, 64, 256), bf16),
        ("gp", (rows, 3 * D), bf16),
    ]
    return fwd + back if both else fwd


def tile_scratch(rows, both):
    return [pltpu.VMEM(shape, dtype) for _, shape, dtype in tile_refs(rows, both)]


def tile_names(both):
    return [name for name, _, _ in tile_refs(64, both)]


N_FWD, N_BOTH = len(tile_names(False)), len(tile_names(True))


GRAD_SHAPES = [(2048, D), (1024, D), (16, D), (2, 64, 256)]
GRAD_NAMES = ("d_ff", "d_at", "d_small", "d_bias")
GRAD_SCRATCH = [pltpu.VMEM(s, f32) for s in GRAD_SHAPES[:2]]
SMALL_SPECS = [pl.BlockSpec(s, lambda *_, n=len(s): (0,) * n) for s in GRAD_SHAPES[2:]]
SMALL_OUTS = [jax.ShapeDtypeStruct(s, f32) for s in GRAD_SHAPES[2:]]

ROWS_BLOCK = 3072
ROWS_CELL = 512


def first_kernel(state, noise, wlc, wlr, ws, wn, *rest):
    w = named(rest[:7])
    h1, halo = rest[7:9]
    w.update(zip(tile_names(False), rest[9:]))
    w["x"][...] = cell_forward(state[0], noise[0], wlc[...], wlr[...], ws[...], wn[...])[0]
    out = block_forward(w["x"], w)
    a, b = halves_of(out)
    h1[0, 0] = a
    h1[0, 1] = b

    @pl.when(pl.program_id(0) == 0)
    def _():
        halo[...] = a.astype(bf16)


def first(state_h, noise_h, cell_w, block_w):
    nw, bands = state_h.shape[:2]
    half = (bands * SLOTS, HALF, D)
    return pl.pallas_call(
        first_kernel,
        grid=(nw,),
        in_specs=[
            pl.BlockSpec((1, bands, 64, D), lambda j: (j, 0, 0, 0)),
            pl.BlockSpec((1, bands, SLOTS, 64, ZC), lambda j: (j, 0, 0, 0, 0)),
        ]
        + [full(a) for a in cell_w]
        + block_specs(0),
        out_specs=[
            pl.BlockSpec((1, 2) + half, lambda j: (j, 0, 0, 0, 0)),
            pl.BlockSpec(half, lambda j: (0, 0, 0)),
        ],
        out_shape=[
            jax.ShapeDtypeStruct((nw, 2) + half, f32),
            jax.ShapeDtypeStruct(half, bf16),
        ],
        scratch_shapes=tile_scratch(64 * bands * SLOTS, False),
        compiler_params=params(1),
    )(state_h, noise_h, *cell_w, *block_w)


def zero_at_start(refs):
    @pl.when(pl.program_id(0) == 0)
    def _():
        for r in refs:
            r[...] = jnp.zeros(r.shape, r.dtype)


def at_end():
    return pl.program_id(0) == pl.num_programs(0) - 1


def second_kernel(samples, ha, hb, hhalo, ca, cb, chalo, *rest):
    w = named(rest[:7])
    act, dh, act_halo, dh_halo, packed_grads, d_small, d_bias = rest[7:14]
    w.update(zip(tile_names(True), rest[14:]))
    grads = rest[14 + N_BOTH : 16 + N_BOTH] + (d_small, d_bias)
    w.update(zip(GRAD_NAMES, grads))
    zero_at_start(grads)
    last = at_end()
    hb_v = jnp.where(last, hhalo[...].astype(f32), hb[0, 0])
    cb_v = jnp.where(last, chalo[...].astype(f32), cb[0].astype(f32))
    w["x"][...] = tile_of(ha[0, 0], hb_v)
    w["g"][...] = tile_of(ca[0].astype(f32), cb_v)
    out = block_both(w["x"], w["g"], w, True, True)
    live = samples[0]
    a, b = halves_of(out)
    factor = jnp.concatenate(
        [jnp.where(s % SLOTS < live, 1.0, 0.0) * jnp.ones((1, 1, D), f32) for s in range(a.shape[0])]
    )
    a, b = (a * factor).astype(bf16), (b * factor).astype(bf16)
    da, db = halves_of(w["g"][...])
    act[0, 0] = a
    act[0, 1] = b
    dh[0, 0] = da
    dh[0, 1] = db

    @pl.when(last)
    def _():
        act_halo[...] = b
        dh_halo[...] = db.astype(bf16)
        packed_grads[:2048] = grads[0][...].astype(bf16)
        packed_grads[2048:] = grads[1][...].astype(bf16)


def second(samples, h1, h1_halo, cot_h, cot_halo, block_w):
    nw = h1.shape[0]
    half = h1.shape[2:]
    return pl.pallas_call(
        second_kernel,
        grid=(nw,),
        in_specs=[
            pl.BlockSpec(memory_space=pltpu.SMEM),
            pl.BlockSpec((1, 1) + half, lambda j: (j, 1, 0, 0, 0)),
            pl.BlockSpec((1, 1) + half, lambda j: (jnp.minimum(j + 1, nw - 1), 0, 0, 0, 0)),
            pl.BlockSpec(half, lambda j: (0, 0, 0)),
            pl.BlockSpec((1,) + half, lambda j: (2 * j + 1, 0, 0, 0)),
            pl.BlockSpec((1,) + half, lambda j: (jnp.minimum(2 * j + 2, 2 * nw - 1), 0, 0, 0)),
            pl.BlockSpec(half, lambda j: (0, 0, 0)),
        ]
        + block_specs(1),
        out_specs=[
            pl.BlockSpec((1, 2) + half, lambda j: (j, 0, 0, 0, 0)),
            pl.BlockSpec((1, 2) + half, lambda j: (j, 0, 0, 0, 0)),
            pl.BlockSpec(half, lambda j: (0, 0, 0)),
            pl.BlockSpec(half, lambda j: (0, 0, 0)),
        ]
        + [pl.BlockSpec((ROWS_BLOCK, D), lambda *_: (0, 0))]
        + SMALL_SPECS,
        out_shape=[
            jax.ShapeDtypeStruct((nw, 2) + half, bf16),
            jax.ShapeDtypeStruct((nw, 2) + half, f32),
            jax.ShapeDtypeStruct(half, bf16),
            jax.ShapeDtypeStruct(half, bf16),
        ]
        + [jax.ShapeDtypeStruct((ROWS_BLOCK, D), bf16)]
        + SMALL_OUTS,
        scratch_shapes=tile_scratch(64 * half[0], True) + GRAD_SCRATCH,
        compiler_params=params(1),
    )(samples, h1, h1, h1_halo, cot_h, cot_h, cot_halo, *block_w)


CELL_SHAPES = [(D, D), (2 * ZC, D), (2 * ZC, D), (2 * ZC, D)]


def divergence_parts(center, squash, sigma):
    return center.astype(bf16), (
        0.5 * (sigma * sigma - 1.0) * (1.0 - squash * squash)
    ).astype(bf16)


def third_kernel(state, noise, da, db, dhalo, wlc, wlr, ws, wn, *rest):
    w = named(rest[:7])
    sg, packed_grads, d_small, d_bias = rest[7:11]
    w.update(zip(tile_names(True), rest[11:]))
    grads = rest[11 + N_BOTH : 13 + N_BOTH] + (d_small, d_bias)
    d_ws, d_wn, d_wl, d_kl = cell_grads = rest[13 + N_BOTH :]
    w.update(zip(GRAD_NAMES, grads))
    zero_at_start(grads + cell_grads)
    st = state[0]
    nz = noise[0]
    bands = st.shape[0]
    hidden, center, squash, sigma, latent, gate, cand = cell_forward(
        st, nz, wlc[...], wlr[...], ws[...], wn[...]
    )
    da_v = jnp.where(pl.program_id(0) == 0, dhalo[...].astype(f32), da[0, 0])
    w["x"][...] = hidden
    w["g"][...] = tile_of(da_v, db[0, 0])
    block_both(w["x"], w["g"], w, False, False)
    dc = w["g"][...]
    over = lambda x: x.reshape(bands, 1, 64, x.shape[-1])
    flat = st.reshape(bands * 64, D)
    dc = dc.reshape(bands, SLOTS, 64, D)
    rest_gate = 1.0 - gate
    d_pre = dc * (over(flat.astype(f32)) - cand) * gate * rest_gate
    d_cand = dc * rest_gate * (1.0 - cand * cand)
    direct = jnp.sum(dc * gate, axis=1).reshape(-1, D)
    g_gate = jnp.sum(d_pre, axis=1).reshape(-1, D).astype(bf16)
    d_ws[...] += mm_tn(flat, g_gate)
    pre = d_pre.reshape(-1, D).astype(bf16)
    cnd = d_cand.reshape(-1, D).astype(bf16)
    d_wn[:ZC] += mm_tn(latent, pre)
    d_wn[ZC:] += mm_tn(latent, cnd)
    d_lat = mm_nt(pre, wn[:, :D]) + mm_nt(cnd, wn[:, D:])
    d_lat = d_lat.reshape(bands, SLOTS, 64, ZC)
    d_center = jnp.sum(d_lat, axis=1).reshape(-1, ZC)
    d_raw = jnp.sum(d_lat * nz, axis=1).reshape(-1, ZC) * 0.5 * sigma * (1.0 - squash * squash)
    d_center, d_raw = d_center.astype(bf16), d_raw.astype(bf16)
    d_wl[:ZC] += mm_tn(d_center, flat)
    d_wl[ZC:] += mm_tn(d_raw, flat)
    kl_center, kl_raw = divergence_parts(center, squash, sigma)
    d_kl[:ZC] += mm_tn(kl_center, flat)
    d_kl[ZC:] += mm_tn(kl_raw, flat)
    total = direct + mm_nt(g_gate, ws[...]) + mm_nt(d_center, wlc[...]) + mm_nt(d_raw, wlr[...])
    for b in range(bands):
        sg[0, WIN * b : WIN * b + WIN] = from_halves(
            total[64 * b : 64 * b + 64].reshape(2, HALF, D)
        )

    @pl.when(at_end())
    def _():
        packed_grads[:2048] = grads[0][...].astype(bf16)
        packed_grads[2048:3072] = grads[1][...].astype(bf16)
        packed_grads[3072:3328] = d_ws[...].astype(bf16)
        packed_grads[3328:3392] = d_wn[...].astype(bf16)
        packed_grads[3392:3456] = d_wl[...].astype(bf16)
        packed_grads[3456:3520] = d_kl[...].astype(bf16)


def third(state_h, noise_h, dh, dh_halo, cell_w, block_w):
    nw, bands = state_h.shape[:2]
    half = dh.shape[2:]
    return pl.pallas_call(
        third_kernel,
        grid=(nw,),
        in_specs=[
            pl.BlockSpec((1, bands, 64, D), lambda j: (j, 0, 0, 0)),
            pl.BlockSpec((1, bands, SLOTS, 64, ZC), lambda j: (j, 0, 0, 0, 0)),
            pl.BlockSpec((1, 1) + half, lambda j: (jnp.maximum(j - 1, 0), 1, 0, 0, 0)),
            pl.BlockSpec((1, 1) + half, lambda j: (j, 0, 0, 0, 0)),
            pl.BlockSpec(half, lambda j: (0, 0, 0)),
        ]
        + [full(a) for a in cell_w]
        + block_specs(0),
        out_specs=[pl.BlockSpec((1, bands * WIN, WIN, D), lambda j: (0, 0, j, 0))]
        + [pl.BlockSpec((ROWS_BLOCK + ROWS_CELL, D), lambda *_: (0, 0))]
        + SMALL_SPECS,
        out_shape=[jax.ShapeDtypeStruct((1, bands * WIN, nw * WIN, D), f32)]
        + [jax.ShapeDtypeStruct((ROWS_BLOCK + ROWS_CELL, D), bf16)]
        + SMALL_OUTS,
        scratch_shapes=tile_scratch(64 * half[0], True)
        + GRAD_SCRATCH
        + [pltpu.VMEM(s, f32) for s in CELL_SHAPES],
        compiler_params=params(1),
    )(state_h, noise_h, dh, dh, dh_halo, *cell_w, *block_w)


def place_kernel(act, halo, out):
    nw = act.shape[0]
    for s in range(SLOTS):
        halves = [halo[s].astype(f32)]
        for j in range(nw):
            halves.append(act[j, 0, s].astype(f32))
            if j < nw - 1:
                halves.append(act[j, 1, s].astype(f32))
        out[0, s] = from_halves(jnp.stack(halves)).astype(bf16)


def place(act, halo):
    nw = act.shape[0]
    bands = act.shape[2] // SLOTS
    return pl.pallas_call(
        place_kernel,
        grid=(bands,),
        in_specs=[
            pl.BlockSpec((nw, 2, SLOTS, HALF, D), lambda i: (0, 0, i, 0, 0)),
            pl.BlockSpec((SLOTS, HALF, D), lambda i: (i, 0, 0)),
        ],
        out_specs=pl.BlockSpec((1, SLOTS, WIN, nw * WIN, D), lambda i: (0, 0, i, 0, 0)),
        out_shape=jax.ShapeDtypeStruct((1, SLOTS, bands * WIN, nw * WIN, D), bf16),
        compiler_params=params(1),
    )(act, halo)


def finish_kernel(
    order, scalars, state, part, wlc, wlr, mine1, got1, mine0, got0,
    sg, div, o_wl, o_ws, o_wn, o_gain1, o_qkv, o_table, o_out, o_gain2, o_up, o_down,
    full1, full0, *, cells, devices,
):
    for mine, got, whole in ((mine1, got1, full1), (mine0, got0, full0)):
        count = whole.shape[0] // devices
        n = devices // 2
        for at, block in ((0, mine), (1, got)):
            for i in range(n):
                to = order[0, at] * n + jnp.bitwise_xor(order[1, at], i)
                whole[pl.ds(pl.multiple_of(to * count, 16), count)] = block[
                    count * i : count * i + count
                ]
    kl = full0[3536:3552].astype(f32)[4:12, :ZC]
    kl_mean = jnp.sum(kl, axis=0, keepdims=True) * (1.0 / cells)
    beta, floor = scalars[0], scalars[1]
    excess = sharpness * (kl_mean - floor)
    soft = jnp.maximum(excess, 0.0) + jnp.log(1.0 + jnp.exp(-jnp.abs(excess)))
    div[...] = beta * jnp.mean(floor + soft * (1.0 / sharpness), axis=-1, keepdims=True)
    amt = beta * jax.nn.sigmoid(excess) * (1.0 / (ZC * cells))

    rows = state.shape[1] * state.shape[2]
    center, squash, sigma = latent_head(state[0].reshape(rows, D), wlc[...], wlr[...])
    kl_center, kl_raw = divergence_parts(center, squash, sigma)
    g_center = (kl_center.astype(f32) * amt).astype(bf16)
    g_raw = (kl_raw.astype(f32) * amt).astype(bf16)
    add = mm_nt(g_center, wlc[...]) + mm_nt(g_raw, wlr[...])
    sg[0] = part[0] + add.reshape(state.shape[1:])

    for k, whole in ((0, full0), (1, full1)):
        for c in range(FF // 256):
            cols = slice(256 * c, 256 * c + 256)
            o_up[k, :, cols] = whole[cols].astype(f32)
            o_down[k, cols] = whole[FF + 256 * c : FF + 256 * c + 256].astype(f32).T
        for c in range(3):
            cols = slice(256 * c, 256 * c + 256)
            o_qkv[k, :, cols] = whole[2048 + 256 * c : 2304 + 256 * c].astype(f32)
        o_out[k] = whole[2816:3072].astype(f32)
    o_ws[...] = full0[3072:3328].astype(f32)
    wn = full0[3328:3392].astype(f32)
    o_wn[:, :D] = wn[:ZC]
    o_wn[:, D:] = wn[ZC:]
    o_wl[...] = full0[3392:3456].astype(f32).T + full0[3456:3520].astype(f32).T * jnp.concatenate(
        [amt, amt], axis=1
    )
    table = full0[3520:3536].astype(f32)
    o_table[0] = table[:HEADS, : (2 * WIN - 1) ** 2]
    o_table[1] = table[HEADS:, : (2 * WIN - 1) ** 2]
    gains = full0[3536:3552].astype(f32)
    for k in range(2):
        o_gain1[k : k + 1] = gains[2 * k : 2 * k + 1]
        o_gain2[k : k + 1] = gains[2 * k + 1 : 2 * k + 2]


def finish(order, scalars, state, part, wlc, wlr, *blocks, cells, devices):
    outs = [
        part.shape, (1, 1), (D, 2 * ZC), (D, D), (ZC, 2 * D), (2, D), (2, D, 3 * D),
        (2, HEADS, (2 * WIN - 1) ** 2), (2, D, D), (2, D), (2, D, FF), (2, FF, D),
    ]
    smem, vmem = pl.BlockSpec(memory_space=pltpu.SMEM), pl.BlockSpec(memory_space=pltpu.VMEM)
    return pl.pallas_call(
        functools.partial(finish_kernel, cells=cells, devices=devices),
        in_specs=[smem, smem] + [vmem] * 8,
        out_specs=[vmem] * len(outs),
        out_shape=[jax.ShapeDtypeStruct(o, f32) for o in outs],
        scratch_shapes=[pltpu.VMEM((2 * b.shape[0], D), bf16) for b in (blocks[0], blocks[2])],
        compiler_params=pltpu.CompilerParams(vmem_limit_bytes=LIMIT),
    )(order, scalars, state, part, wlc, wlr, *blocks)


def shift_from(block, distance):
    n = lax.axis_size("lon")
    return lax.ppermute(block, "lon", [((i + distance) % n, i) for i in range(n)])


class Summation:
    def __init__(self):
        n_lon, n_batch = lax.axis_size("lon"), lax.axis_size("batch")
        self.n = n = n_lon * n_batch
        me = lax.axis_index("lon") * n_batch + lax.axis_index("batch")
        bits = [1 << i for i in range(1, n.bit_length() - 1)]
        lon = bits.pop()
        near, far = bits[:1], bits[1:]
        self.pairs = list(zip(near + [lon] + far, [lon] + far[:1] + near + far[1:]))
        self.core = me & 1
        self.bits = [self.core] + self.bits_of(me)
        places = [self.place(self.bits[1:]), self.place(self.bits_of(me ^ 1))]
        self.order = jnp.stack([jnp.stack([self.core, 1 - self.core]), jnp.stack(places)])

    def bits_of(self, device):
        return [
            (jnp.bitwise_and(device, jnp.where(device & 1 == 0, a, b)) != 0).astype(jnp.int32)
            for a, b in self.pairs
        ]

    def place(self, bits):
        at = jnp.zeros((), jnp.int32)
        for bit in bits:
            at = 2 * at + bit
        return at

    def swap(self, block, step):
        pair = self.pairs[step - 1] if step else (1, 1)
        return lax.ppermute(
            block, ("lon", "batch"), [(i, i ^ pair[i & 1]) for i in range(self.n)]
        )

    def __call__(self, total):
        rows = total.shape[0]
        total = jnp.pad(total, ((0, -rows % (16 * self.n)), (0, 0)))
        for step, bit in enumerate(self.bits):
            size = total.shape[0] // 2
            keep = lax.dynamic_slice_in_dim(total, bit * size, size, 0)
            send = lax.dynamic_slice_in_dim(total, (1 - bit) * size, size, 0)
            total = (keep.astype(f32) + self.swap(send, step).astype(f32)).astype(bf16)
        for step in range(len(self.bits) - 1, 0, -1):
            total = jnp.concatenate([total, self.swap(total, step)])
        return total, self.swap(total, 0)


def offset_onehot():
    places = jnp.arange(WIN * WIN)
    row = places % HALF // 4
    col = places // HALF * 4 + places % 4
    target = (row[None, :] - row[:, None] + WIN - 1) * (2 * WIN - 1) + (
        col[None, :] - col[:, None] + WIN - 1
    )
    return (target[:, :, None] == jnp.arange((2 * WIN - 1) ** 2)).astype(f32)


def body(
    state,
    noise,
    samples,
    step,
    kl_weight,
    floor,
    latent_weight,
    state_weight,
    noise_weight,
    attention_gain,
    query_key_value,
    offset_bias,
    output_weight,
    feedforward_gain,
    up_weight,
    down_weight,
    cotangent,
):
    items, height, breadth, width = state.shape
    cells = items * height * breadth * lax.axis_size("lon") * lax.axis_size("batch")
    onehot = offset_onehot()
    bias = jnp.einsum(
        "bhr,kqr->bkhq", offset_bias * LOG2E, onehot, precision=lax.Precision.HIGHEST
    )
    bias = bias.reshape(2, 64, 2, 256).transpose(0, 2, 1, 3)
    cell_w = (latent_weight[:, :ZC], latent_weight[:, ZC:], state_weight, noise_weight)
    block_w = (
        attention_gain.reshape(2, 1, D),
        query_key_value,
        bias,
        output_weight,
        feedforward_gain.reshape(2, 1, D),
        up_weight,
        down_weight,
    )
    wlc, wlr = cell_w[:2]
    cot_h, state_h, noise_h, kl = prep(samples, cotangent, state, noise, wlc, wlr)
    h1, h1_halo = first(state_h, noise_h, cell_w, block_w)
    halo = shift_from(jnp.stack([h1_halo, cot_h[0]]), 1)
    act, dh, act_halo, dh_halo, grads1, small1, bias1 = second(
        samples, h1, halo[0], cot_h, halo[1], block_w
    )
    halo = shift_from(jnp.stack([dh_halo, act_halo]), -1)
    part, grads0, small0, bias0 = third(state_h, noise_h, dh, halo[0], cell_w, block_w)
    activations = place(act, halo[1])

    table = jnp.stack([bias0, bias1]).reshape(2, 2, 64, 4, 64).transpose(0, 1, 3, 2, 4)
    table = jnp.dot(
        table.reshape(2 * HEADS, -1), onehot.reshape(64 * 64, -1), precision=lax.Precision.HIGHEST
    )
    gains = jnp.sum(jnp.stack([small0, small1]).reshape(4, 8, D), axis=1)
    small = jnp.concatenate(
        [jnp.pad(table, ((0, 0), (0, D - table.shape[1]))), gains, kl, jnp.zeros((36, D), f32)]
    ).astype(bf16)
    grads0 = lax.dynamic_update_slice_in_dim(grads0, small, ROWS_BLOCK + ROWS_CELL - 64, 0)
    add_up = Summation()
    beta = kl_weight * (step + 1).astype(f32) / WARM
    scalars = jnp.stack([beta, floor])
    blocks = add_up(grads1) + add_up(grads0)
    state_gradient, divergence, *weights = finish(
        add_up.order, scalars, state, part, wlc, wlr, *blocks, cells=cells, devices=add_up.n
    )
    return (activations, divergence.reshape(()), state_gradient, *weights)


def solution(mesh):
    return jax.shard_map(
        body,
        mesh=mesh,
        in_specs=(
            P("batch", None, "lon", None),
            P("batch", None, None, "lon", None),
            P("batch"),
            P(),
            P(),
            P(),
            P(),
            P(),
            P(),
            P(),
            P(),
            P(),
            P(),
            P(),
            P(),
            P(),
            P("batch", None, None, "lon", None),
        ),
        out_specs=(
            P("batch", None, None, "lon", None),
            P(),
            P("batch", None, "lon", None),
            P(),
            P(),
            P(),
            P(),
            P(),
            P(),
            P(),
            P(),
            P(),
            P(),
        ),
        check_vma=False,
    )
```

```python
import functools

import jax
import jax.numpy as jnp
from jax import lax
from jax.experimental import pallas as pl
from jax.experimental.pallas import tpu as pltpu
from jax.sharding import PartitionSpec as P

HEADS = 8
HD = 32
WIN = 8
WARM = 1000
SLOTS = 4
D = 256
FF = 1024
ZC = 32
HALF = WIN // 2 * WIN

eps_norm = 1e-05
sharpness = 8.0
spread_bound = 4.0
LOG2E = 1.4426950408889634
f32 = jnp.float32
bf16 = jnp.bfloat16


def mm(a, b):
    return lax.dot_general(a, b, (((1,), (0,)), ((), ())), preferred_element_type=f32)


def mm_nt(a, b):
    return lax.dot_general(a, b, (((1,), (1,)), ((), ())), preferred_element_type=f32)


def mm_tn(a, b):
    return lax.dot_general(a, b, (((0,), (0,)), ((), ())), preferred_element_type=f32)


def low_sublanes(shape):
    return lax.broadcasted_iota(jnp.int32, shape, len(shape) - 2) < 4


def to_halves(x):
    rows, cols, ch = x.shape
    n = cols // 8
    v = x.reshape(4, 2, n, 8, ch)
    a, b = v[:, 0], v[:, 1]
    low = low_sublanes(a.shape)
    first = jnp.where(low, a, pltpu.roll(b, 4, 2))
    second = jnp.where(low, pltpu.roll(a, 4, 2), b)
    first = first.transpose(1, 0, 2, 3)
    second = second.transpose(1, 0, 2, 3)
    return jnp.stack([first, second], axis=1).reshape(2 * n, HALF, ch)


def from_halves(x):
    n = x.shape[0] // 2
    ch = x.shape[-1]
    v = x.reshape(n, 2, 4, 8, ch)
    first, second = v[:, 0].transpose(1, 0, 2, 3), v[:, 1].transpose(1, 0, 2, 3)
    low = low_sublanes(first.shape)
    a = jnp.where(low, first, pltpu.roll(second, 4, 2))
    b = jnp.where(low, pltpu.roll(first, 4, 2), second)
    return jnp.stack([a, b], axis=1).reshape(8, 8 * n, ch)


def tile_of(first, second):
    return jnp.stack([first, second], axis=1).reshape(-1, first.shape[-1])


def halves_of(tile):
    v = tile.reshape(-1, 2, HALF, tile.shape[-1])
    return v[:, 0], v[:, 1]


def norm(x):
    c = x - jnp.mean(x, axis=-1, keepdims=True)
    r = lax.rsqrt(jnp.mean(c * c, axis=-1, keepdims=True) + eps_norm)
    return c * r, r


def norm_back(dy, xhat, r, gain):
    along = dy * gain
    inward = r * (
        along
        - jnp.mean(along, axis=-1, keepdims=True)
        - xhat * jnp.mean(along * xhat, axis=-1, keepdims=True)
    )
    return inward, jnp.sum((dy * xhat).reshape(-1, 8, D), axis=0)


ERF = (0.7978697122393114, 0.036392286377165226, -8.78266605765619e-05,
       -3.669342209361701e-05, 1.425004260912749e-06)


def gelu_parts(x):
    square = x * x
    p = ERF[-1]
    for c in ERF[-2::-1]:
        p = p * square + c
    erf = jnp.tanh(x * p)
    half = 0.5 * x
    density = jnp.exp2(square * (-0.5 * LOG2E))
    return half + half * erf, 0.5 + 0.5 * erf + x * density * 0.3989422804014327


def lane_masks():
    lane = lax.broadcasted_iota(jnp.int32, (1, 128), 1)
    return [(lane >= 32 * j) & (lane < 32 * j + 32) for j in range(4)]


def spread_heads(x, masks):
    return jnp.concatenate([x * m for m in masks], axis=0)


def gather_heads(x, masks):
    v = x.reshape(4, 64, 128)
    return jnp.where(masks[0], v[0], jnp.where(masks[1], v[1], jnp.where(masks[2], v[2], v[3])))


def pieces(rows):
    return [slice(r, r + 64) for r in range(0, rows, 64)]


def staged(count, *stages):
    for n in range(count + len(stages) - 1):
        for late, stage in enumerate(stages):
            if 0 <= n - late < count:
                stage(n - late)


def unit_of(n):
    g = n % 2
    rows = slice(64 * (n // 2), 64 * (n // 2) + 64)
    return rows, lambda part: slice(256 * part + 128 * g, 256 * part + 128 * g + 128), g


def attention(w):
    sel = lane_masks()
    ones = [m.astype(f32).astype(bf16) for m in sel]
    scale = HD ** (-0.5) * LOG2E

    def scores(n):
        rows, lanes, g = unit_of(n)
        q, k = w["packed"][rows, lanes(0)], w["packed"][rows, lanes(1)]
        w["s"][n % 4] = mm_nt(k, spread_heads(q, ones))

    def softmax(n):
        s = w["s"][n % 4] * scale + w["bias"][n % 2]
        s = jnp.exp2(s - jnp.max(s, axis=0, keepdims=True))
        w["p"][n] = (s * (1.0 / jnp.sum(s, axis=0, keepdims=True))).astype(bf16)

    def values(n):
        rows, lanes, g = unit_of(n)
        found = gather_heads(mm_tn(w["p"][n], w["packed"][rows, lanes(2)]), sel)
        w["ctx"][rows, lanes(0)] = found.astype(bf16)

    staged(w["p"].shape[0], scores, softmax, values)


def attention_back(w):
    sel = lane_masks()
    ones = [m.astype(f32).astype(bf16) for m in sel]
    scale = HD ** (-0.5)

    def upstream(n):
        rows, lanes, g = unit_of(n)
        spread = spread_heads(w["dctx"][rows, lanes(0)], ones)
        w["gp"][rows, lanes(2)] = mm(w["p"][n], spread).astype(bf16)
        w["s"][n % 4] = mm_nt(w["packed"][rows, lanes(2)], spread)

    def inward(n):
        p = w["p"][n].astype(f32)
        t = p * w["s"][n % 4]
        ds = t - p * jnp.sum(t, axis=0, keepdims=True)
        w["d_bias"][n % 2] += ds
        w["ds"][n % 4] = ds.astype(bf16)

    def outer(n):
        rows, lanes, g = unit_of(n)
        ds = w["ds"][n % 4]
        q, k = w["packed"][rows, lanes(0)], w["packed"][rows, lanes(1)]
        w["gp"][rows, lanes(1)] = (mm(ds, spread_heads(q, ones)) * scale).astype(bf16)
        w["gp"][rows, lanes(0)] = (gather_heads(mm_tn(ds, k), sel) * scale).astype(bf16)

    staged(w["p"].shape[0], upstream, inward, outer)


def attend(x_ref, w):
    rows = x_ref.shape[0]
    gain1, gain2 = w["gain1"][...], w["gain2"][...]
    r1, r2 = [], []
    for at in pieces(rows):
        xhat, r = norm(x_ref[at])
        r1.append(r)
        w["normed"][at] = (xhat * gain1).astype(bf16)
    w["packed"][...] = mm(w["normed"][...], w["qkv"][...]).astype(bf16)
    attention(w)
    w["mixed"][...] = x_ref[...] + mm(w["ctx"][...], w["out"][...])
    for at in pieces(rows):
        xhat, r = norm(w["mixed"][at])
        r2.append(r)
        w["xhat"][at] = xhat
        w["normed2"][at] = (xhat * gain2).astype(bf16)
    return r1, r2


def block_forward(x_ref, w):
    attend(x_ref, w)
    rows = x_ref.shape[0]

    def start(c):
        w["a"][c % 2] = mm(w["normed2"][...], w["up"][:, 256 * c : 256 * c + 256])

    start(0)
    for c in range(FF // 256):
        cols = slice(256 * c, 256 * c + 256)
        if c < FF // 256 - 1:
            start(c + 1)
        for at in pieces(rows):
            active, slope = gelu_parts(w["a"][c % 2, at])
            w["active"][at, cols] = active.astype(bf16)
            w["slope"][at, cols] = slope.astype(bf16)
    return w["mixed"][...] + mm(w["active"][...], w["down"][...])


def block_backward(x_ref, g_ref, w, fused, round_dn):
    rows = x_ref.shape[0]
    gain1, gain2 = w["gain1"][...], w["gain2"][...]
    if fused:
        r1, r2 = attend(x_ref, w)
    normed2_t = w["normed2"][...].T
    gb = g_ref[...].astype(bf16)
    gb_t = gb.T

    def start(c):
        cols = slice(256 * c, 256 * c + 256)
        if fused:
            w["a"][c % 2] = mm(w["normed2"][...], w["up"][:, cols])
        w["b"][c % 2] = mm_nt(gb, w["down"][cols, :])

    start(0)
    for c in range(FF // 256):
        cols = slice(256 * c, 256 * c + 256)
        if c < FF // 256 - 1:
            start(c + 1)
        for at in pieces(rows):
            if fused:
                active, slope = gelu_parts(w["a"][c % 2, at])
                w["active"][at, cols] = active.astype(bf16)
            else:
                slope = w["slope"][at, cols].astype(f32)
            w["d_inner"][at, cols] = (w["b"][c % 2, at] * slope).astype(bf16)
        w["d_ff"][1024 + 256 * c : 1280 + 256 * c, :] += mm(gb_t, w["active"][:, cols])
        w["d_ff"][cols, :] += mm(normed2_t, w["d_inner"][:, cols])
        if c == FF // 512:
            w["dn"][...] = mm_nt(w["d_inner"][:, : FF // 2], w["up"][:, : FF // 2])
    w["dn"][...] += mm_nt(w["d_inner"][:, FF // 2 :], w["up"][:, FF // 2 :])
    out = None
    if fused:
        out = w["mixed"][...] + mm(w["active"][...], w["down"][...])
    dgain = None
    for n, at in enumerate(pieces(rows)):
        xhat, r = (w["xhat"][at], r2[n]) if fused else norm(w["mixed"][at])
        inward, part = norm_back(w["dn"][at], xhat, r, gain2)
        dgain = part if dgain is None else dgain + part
        d_mixed = g_ref[at] + inward
        g_ref[at] = d_mixed
        w["g_out"][at] = d_mixed.astype(bf16)
    w["d_small"][8:16, :] += dgain
    w["dctx"][...] = mm_nt(w["g_out"][...], w["out"][...]).astype(bf16)
    w["d_at"][768:1024, :] += mm_tn(w["ctx"][...], w["g_out"][...])
    attention_back(w)
    w["dn"][...] = mm_nt(w["gp"][...], w["qkv"][...])
    normed_t = w["normed"][...].T
    for c in range(3):
        cols = slice(256 * c, 256 * c + 256)
        w["d_at"][cols, :] += mm(normed_t, w["gp"][:, cols])
    dgain = None
    for at in pieces(rows):
        dn = w["dn"][at]
        if round_dn:
            dn = dn.astype(bf16).astype(f32)
        xhat, r = norm(x_ref[at])
        inward, part = norm_back(dn, xhat, r, gain1)
        dgain = part if dgain is None else dgain + part
        g_ref[at] = g_ref[at] + inward
    w["d_small"][0:8, :] += dgain
    return out


LIMIT = 56 * 1024 * 1024


def params(n):
    return pltpu.CompilerParams(
        dimension_semantics=("arbitrary",) * n, vmem_limit_bytes=LIMIT
    )


def latent_head(state, wl):
    center = mm_nt(state, wl[:ZC])
    squash = jnp.tanh(mm_nt(state, wl[ZC:]) * (1.0 / spread_bound))
    return center, squash, jnp.exp((0.5 * spread_bound) * squash)


def lanes_of_patch(width, back):
    lane = lax.broadcasted_iota(jnp.int32, (4 * 256, 4 * 64), 0)
    at = lax.broadcasted_iota(jnp.int32, (4 * 256, 4 * 64), 1)
    row, col = query_place(at & 63)
    want = 16 * (7 - row) + 7 - col if back else 16 * row + col
    return jnp.where(lane == (at >> 6) * 256 + want, 1.0, 0.0).astype(bf16)


def query_place(q):
    return (q >> 2) & 7, ((q >> 5) << 2) + (q & 3)


def table_lanes(back):
    a = lax.broadcasted_iota(jnp.int32, (256, 256), 0)
    b = lax.broadcasted_iota(jnp.int32, (256, 256), 1)
    side = 2 * WIN - 1
    if back:
        mirrored = 16 * (14 - (a >> 4)) + 14 - (a & 15)
        hit = ((a & 15) < side) & ((a >> 4) < side) & (b == (14 - (a >> 4)) * side + 14 - (a & 15))
    else:
        hit = ((b & 15) < side) & ((b >> 4) < side) & (a == (b >> 4) * side + (b & 15))
    return jnp.where(hit, 1.0, 0.0).astype(bf16)


def exactly(a, onehot):
    total = None
    for _ in range(3):
        term = a.astype(bf16)
        a = a - term.astype(f32)
        part = mm(term, onehot)
        total = part if total is None else total + part
    return total


def expand_bias(tables):
    spread = exactly(tables, table_lanes(False))
    choose = lanes_of_patch(64, False)
    out = []
    for n in range(4):
        heads = []
        for h in range(4 * n, 4 * n + 4):
            one = jnp.broadcast_to(spread[h : h + 1], (8, 256))
            heads.append(
                jnp.concatenate(
                    [
                        pltpu.roll(one, (16 * r + 137) % 256, 1, stride=1, stride_axis=0)
                        for r in range(WIN)
                    ]
                )
            )
        rows = exactly(jnp.concatenate(heads, axis=1), choose)
        out.append(to_halves(rows.reshape(WIN, WIN, 256)).reshape(64, 256))
    return out


def reduce_bias(grads):
    rows = from_halves(grads.reshape(2, HALF, 256)).reshape(64, 256).astype(bf16)
    lanes = lax.dot_general(
        rows, lanes_of_patch(64, True), (((1,), (1,)), ((), ())), preferred_element_type=f32
    )
    out = []
    for h in range(4):
        total = None
        for r in range(WIN):
            one = pltpu.roll(
                lanes[8 * r : 8 * r + 8, 256 * h : 256 * h + 256], 16 * r, 1, stride=1, stride_axis=0
            )
            total = one if total is None else total + one
        out.append(jnp.sum(total, axis=0, keepdims=True))
    return jnp.concatenate(out)


def prep_kernel(samples, cot, state, noise, wl, tables, cot_h, state_h, noise_h, kl, bias):
    @pl.when(pl.program_id(0) == 0)
    def _():
        padded = jnp.concatenate(
            [tables[...], jnp.zeros((16, 256 - tables.shape[1]), f32)], axis=1
        )
        for n, part in enumerate(expand_bias(padded * LOG2E)):
            bias[n // 2, n % 2] = part

    live = samples[0]
    for s in range(SLOTS):
        factor = jnp.where(s < live, 1.0, 0.0).astype(f32)
        cot_h[:, s] = (to_halves(cot[0, s].astype(f32)) * factor).astype(bf16)
        noise_h[:, 0, s] = to_halves(noise[0, s]).reshape(4, 64, ZC)
    st = to_halves(state[0].astype(f32)).reshape(4, 64, D).astype(bf16)
    state_h[:, 0] = st
    center, squash, sigma = latent_head(st.reshape(4 * 64, D), wl[...])
    terms = 0.5 * (center * center + sigma * sigma - 1.0 - spread_bound * squash)

    @pl.when(pl.program_id(0) == 0)
    def _():
        kl[...] = jnp.zeros(kl.shape, f32)

    kl[:, :ZC] += jnp.sum(terms.reshape(-1, 8, ZC), axis=0)


def prep(samples, cot, state, noise, wl, tables):
    bands = state.shape[1] // WIN
    nw = state.shape[2] // WIN
    return pl.pallas_call(
        prep_kernel,
        grid=(bands,),
        in_specs=[
            pl.BlockSpec(memory_space=pltpu.SMEM),
            pl.BlockSpec((1, SLOTS, WIN, nw * WIN, D), lambda i: (0, 0, i, 0, 0)),
            pl.BlockSpec((1, WIN, nw * WIN, D), lambda i: (0, i, 0, 0)),
            pl.BlockSpec((1, SLOTS, WIN, nw * WIN, ZC), lambda i: (0, 0, i, 0, 0)),
            full(wl),
            full(tables),
        ],
        out_specs=[
            pl.BlockSpec((2 * nw, SLOTS, HALF, D), lambda i: (0, i, 0, 0)),
            pl.BlockSpec((nw, 1, 64, D), lambda i: (0, i, 0, 0)),
            pl.BlockSpec((nw, 1, SLOTS, 64, ZC), lambda i: (0, i, 0, 0, 0)),
            pl.BlockSpec((8, D), lambda i: (0, 0)),
            pl.BlockSpec((2, 2, 64, 256), lambda i: (0, 0, 0, 0)),
        ],
        out_shape=[
            jax.ShapeDtypeStruct((2 * nw, bands * SLOTS, HALF, D), bf16),
            jax.ShapeDtypeStruct((nw, bands, 64, D), bf16),
            jax.ShapeDtypeStruct((nw, bands, SLOTS, 64, ZC), f32),
            jax.ShapeDtypeStruct((8, D), f32),
            jax.ShapeDtypeStruct((2, 2, 64, 256), f32),
        ],
        compiler_params=params(1),
    )(samples, cot, state, noise, wl, tables)


def cell_forward(state, noise, wl, ws, wn):
    bands = state.shape[0]
    flat = state.reshape(bands * 64, D)
    over = lambda x: x.reshape(bands, 1, 64, x.shape[-1])
    center, squash, sigma = latent_head(flat, wl)
    latent = (over(center) + over(sigma) * noise).reshape(-1, ZC).astype(bf16)
    mix = mm(latent, wn)
    gate = jax.nn.sigmoid(over(mm(flat, ws)) + mix[:, :D].reshape(bands, SLOTS, 64, D))
    cand = jnp.tanh(mix[:, D:].reshape(bands, SLOTS, 64, D))
    hidden = gate * over(flat.astype(f32)) + (1.0 - gate) * cand
    return hidden.reshape(-1, D), center, squash, sigma, latent, gate, cand


def full(a):
    return pl.BlockSpec(a.shape, lambda *_: (0,) * a.ndim)


def block_specs(k):
    return [
        pl.BlockSpec((2, D), lambda *_: (0, 0)),
        pl.BlockSpec((1, D, 3 * D), lambda *_: (k, 0, 0)),
        pl.BlockSpec((1, 2, 64, 256), lambda *_: (k, 0, 0, 0)),
        pl.BlockSpec((1, D, D), lambda *_: (k, 0, 0)),
        pl.BlockSpec((2, D), lambda *_: (0, 0)),
        pl.BlockSpec((1, D, FF), lambda *_: (k, 0, 0)),
        pl.BlockSpec((1, FF, D), lambda *_: (k, 0, 0)),
    ]


NAMES = ("gain1", "qkv", "bias", "out", "gain2", "up", "down")


def named(refs, k):
    return {
        n: r.at[k : k + 1] if n.startswith("gain") else r.at[0] for n, r in zip(NAMES, refs)
    }


def saved_refs(rows):
    return [
        ("normed", (rows, D), bf16),
        ("packed", (rows, 3 * D), bf16),
        ("p", (rows // 32, 64, 256), bf16),
        ("ctx", (rows, D), bf16),
        ("mixed", (rows, D), f32),
        ("normed2", (rows, D), bf16),
        ("active", (rows, FF), bf16),
        ("slope", (rows, FF), bf16),
    ]


def forward_refs(rows):
    return [
        ("x", (rows, D), f32),
        ("s", (4, 64, 256), f32),
        ("xhat", (rows, D), f32),
        ("a", (2, rows, 256), f32),
    ]


def backward_refs(rows):
    return [
        ("x", (rows, D), f32),
        ("g", (rows, D), f32),
        ("s", (4, 64, 256), f32),
        ("b", (2, rows, 256), f32),
        ("d_inner", (rows, FF), bf16),
        ("dn", (rows, D), f32),
        ("g_out", (rows, D), bf16),
        ("dctx", (rows, D), bf16),
        ("ds", (4, 64, 256), bf16),
        ("gp", (rows, 3 * D), bf16),
    ]


def both_refs(rows):
    return saved_refs(rows) + forward_refs(rows)[2:] + backward_refs(rows)


def scratch(refs):
    return [pltpu.VMEM(shape, dtype) for _, shape, dtype in refs]


def names(refs):
    return [name for name, _, _ in refs]


def saved_specs(rows):
    return [
        pl.BlockSpec((1,) + shape, lambda j, n=len(shape): (j,) + (0,) * n)
        for _, shape, _ in saved_refs(rows)
    ]


N_SAVED, N_BACK, N_BOTH = len(saved_refs(64)), len(backward_refs(64)), len(both_refs(64))


GRAD_SHAPES = [(2048, D), (1024, D), (16, D), (2, 64, 256)]
GRAD_NAMES = ("d_ff", "d_at", "d_small", "d_bias")
GRAD_SCRATCH = [pltpu.VMEM(s, f32) for s in GRAD_SHAPES[:2]]
SMALL_SPECS = [pl.BlockSpec(s, lambda *_, n=len(s): (0,) * n) for s in GRAD_SHAPES[2:]]
SMALL_OUTS = [jax.ShapeDtypeStruct(s, f32) for s in GRAD_SHAPES[2:]]

ROWS_BLOCK = 3072
ROWS_CELL = 512


def first_kernel(state, noise, cot, wl, ws, wn, *rest):
    w = named(rest[:7], 0)
    h1, halo = rest[7:9]
    w.update((n, r.at[0]) for n, r in zip(names(saved_refs(64)), rest[9:]))
    w.update(zip(names(forward_refs(64)), rest[9 + N_SAVED :]))
    w["x"][...] = cell_forward(state[0], noise[0], wl[...], ws[...], wn[...])[0]
    out = block_forward(w["x"], w)
    a, b = halves_of(out)
    h1[0, 0] = a
    h1[0, 1] = b

    @pl.when(pl.program_id(0) == 0)
    def _():
        halo[0] = a.astype(bf16)
        halo[1] = cot[0]


def first(state_h, noise_h, cot_h, cell_w, block_w):
    nw, bands = state_h.shape[:2]
    half = (bands * SLOTS, HALF, D)
    rows = 64 * bands * SLOTS
    return pl.pallas_call(
        first_kernel,
        grid=(nw,),
        in_specs=[
            pl.BlockSpec((1, bands, 64, D), lambda j: (j, 0, 0, 0)),
            pl.BlockSpec((1, bands, SLOTS, 64, ZC), lambda j: (j, 0, 0, 0, 0)),
            pl.BlockSpec((1,) + half, lambda j: (0, 0, 0, 0)),
        ]
        + [full(a) for a in cell_w]
        + block_specs(0),
        out_specs=[
            pl.BlockSpec((1, 2) + half, lambda j: (j, 0, 0, 0, 0)),
            pl.BlockSpec((2,) + half, lambda j: (0, 0, 0, 0)),
        ]
        + saved_specs(rows),
        out_shape=[
            jax.ShapeDtypeStruct((nw, 2) + half, f32),
            jax.ShapeDtypeStruct((2,) + half, bf16),
        ]
        + [jax.ShapeDtypeStruct((nw,) + shape, dtype) for _, shape, dtype in saved_refs(rows)],
        scratch_shapes=scratch(forward_refs(rows)),
        compiler_params=params(1),
    )(state_h, noise_h, cot_h, *cell_w, *block_w)


def zero_at_start(refs):
    @pl.when(pl.program_id(0) == 0)
    def _():
        for r in refs:
            r[...] = jnp.zeros(r.shape, r.dtype)


def at_end():
    return pl.program_id(0) == pl.num_programs(0) - 1


def second_kernel(samples, ha, hb, ca, cb, halo, *rest):
    w = named(rest[:7], 1)
    act, dh, back_halo, packed_grads, d_small, d_bias = rest[7:13]
    w.update(zip(names(both_refs(64)), rest[13:]))
    grads = rest[13 + N_BOTH : 15 + N_BOTH] + (d_small, d_bias)
    w.update(zip(GRAD_NAMES, grads))
    zero_at_start(grads)
    last = at_end()
    hb_v = jnp.where(last, halo[0].astype(f32), hb[0, 0])
    cb_v = jnp.where(last, halo[1].astype(f32), cb[0].astype(f32))
    w["x"][...] = tile_of(ha[0, 0], hb_v)
    w["g"][...] = tile_of(ca[0].astype(f32), cb_v)
    out = block_backward(w["x"], w["g"], w, True, True)
    live = samples[0]
    a, b = halves_of(out)
    factor = jnp.concatenate(
        [jnp.where(s % SLOTS < live, 1.0, 0.0) * jnp.ones((1, 1, D), f32) for s in range(a.shape[0])]
    )
    a, b = (a * factor).astype(bf16), (b * factor).astype(bf16)
    da, db = halves_of(w["g"][...])
    act[0, 0] = a
    act[0, 1] = b
    dh[0, 0] = da
    dh[0, 1] = db

    @pl.when(last)
    def _():
        back_halo[0] = db.astype(bf16)
        back_halo[1] = b
        packed_grads[:2048] = grads[0][...].astype(bf16)
        packed_grads[2048:] = grads[1][...].astype(bf16)


def second(samples, h1, cot_h, halo, block_w):
    nw = h1.shape[0]
    half = h1.shape[2:]
    return pl.pallas_call(
        second_kernel,
        grid=(nw,),
        in_specs=[
            pl.BlockSpec(memory_space=pltpu.SMEM),
            pl.BlockSpec((1, 1) + half, lambda j: (j, 1, 0, 0, 0)),
            pl.BlockSpec((1, 1) + half, lambda j: (jnp.minimum(j + 1, nw - 1), 0, 0, 0, 0)),
            pl.BlockSpec((1,) + half, lambda j: (2 * j + 1, 0, 0, 0)),
            pl.BlockSpec((1,) + half, lambda j: (jnp.minimum(2 * j + 2, 2 * nw - 1), 0, 0, 0)),
            pl.BlockSpec((2,) + half, lambda j: (0, 0, 0, 0)),
        ]
        + block_specs(1),
        out_specs=[
            pl.BlockSpec((1, 2) + half, lambda j: (j, 0, 0, 0, 0)),
            pl.BlockSpec((1, 2) + half, lambda j: (j, 0, 0, 0, 0)),
            pl.BlockSpec((2,) + half, lambda j: (0, 0, 0, 0)),
        ]
        + [pl.BlockSpec((ROWS_BLOCK, D), lambda *_: (0, 0))]
        + SMALL_SPECS,
        out_shape=[
            jax.ShapeDtypeStruct((nw, 2) + half, bf16),
            jax.ShapeDtypeStruct((nw, 2) + half, f32),
            jax.ShapeDtypeStruct((2,) + half, bf16),
        ]
        + [jax.ShapeDtypeStruct((ROWS_BLOCK, D), bf16)]
        + SMALL_OUTS,
        scratch_shapes=scratch(both_refs(64 * half[0])) + GRAD_SCRATCH,
        compiler_params=params(1),
    )(samples, h1, h1, cot_h, cot_h, halo, *block_w)


CELL_SHAPES = [(D, D), (2 * ZC, D), (2 * ZC, D), (2 * ZC, D)]


def divergence_parts(center, squash, sigma):
    return center.astype(bf16), (
        0.5 * (sigma * sigma - 1.0) * (1.0 - squash * squash)
    ).astype(bf16)


def third_kernel(state, noise, da, db, dhalo, small1, bias1, kl, wl, ws, wn, *rest):
    w = named(rest[:7], 0)
    w.update((n, r.at[0]) for n, r in zip(names(saved_refs(64)), rest[7:]))
    rest = rest[N_SAVED:]
    sg, packed_grads = rest[7:9]
    w.update(zip(names(backward_refs(64)), rest[9:]))
    grads = rest[9 + N_BACK : 13 + N_BACK]
    d_ws, d_wn, d_wl, d_kl = cell_grads = rest[13 + N_BACK :]
    w.update(zip(GRAD_NAMES, grads))
    zero_at_start(grads + cell_grads)
    st = state[0]
    nz = noise[0]
    bands = st.shape[0]
    hidden, center, squash, sigma, latent, gate, cand = cell_forward(
        st, nz, wl[...], ws[...], wn[...]
    )
    da_v = jnp.where(pl.program_id(0) == 0, dhalo[0].astype(f32), da[0, 0])
    w["x"][...] = hidden
    w["g"][...] = tile_of(da_v, db[0, 0])
    block_backward(w["x"], w["g"], w, False, False)
    dc = w["g"][...]
    over = lambda x: x.reshape(bands, 1, 64, x.shape[-1])
    flat = st.reshape(bands * 64, D)
    dc = dc.reshape(bands, SLOTS, 64, D)
    rest_gate = 1.0 - gate
    d_pre = dc * (over(flat.astype(f32)) - cand) * gate * rest_gate
    d_cand = dc * rest_gate * (1.0 - cand * cand)
    direct = jnp.sum(dc * gate, axis=1).reshape(-1, D)
    g_gate = jnp.sum(d_pre, axis=1).reshape(-1, D).astype(bf16)
    d_ws[...] += mm_tn(flat, g_gate)
    pre = d_pre.reshape(-1, D).astype(bf16)
    cnd = d_cand.reshape(-1, D).astype(bf16)
    d_wn[:ZC] += mm_tn(latent, pre)
    d_wn[ZC:] += mm_tn(latent, cnd)
    d_lat = mm_nt(pre, wn[:, :D]) + mm_nt(cnd, wn[:, D:])
    d_lat = d_lat.reshape(bands, SLOTS, 64, ZC)
    d_center = jnp.sum(d_lat, axis=1).reshape(-1, ZC)
    d_raw = jnp.sum(d_lat * nz, axis=1).reshape(-1, ZC) * 0.5 * sigma * (1.0 - squash * squash)
    d_center, d_raw = d_center.astype(bf16), d_raw.astype(bf16)
    d_wl[:ZC] += mm_tn(d_center, flat)
    d_wl[ZC:] += mm_tn(d_raw, flat)
    kl_center, kl_raw = divergence_parts(center, squash, sigma)
    d_kl[:ZC] += mm_tn(kl_center, flat)
    d_kl[ZC:] += mm_tn(kl_raw, flat)
    total = direct + mm_nt(g_gate, ws[...])
    total = total + mm(d_center, wl[:ZC]) + mm(d_raw, wl[ZC:])
    for b in range(bands):
        sg[0, WIN * b : WIN * b + WIN] = from_halves(
            total[64 * b : 64 * b + 64].reshape(2, HALF, D)
        )

    @pl.when(at_end())
    def _():
        packed_grads[:2048] = grads[0][...].astype(bf16)
        packed_grads[2048:3072] = grads[1][...].astype(bf16)
        packed_grads[3072:3328] = d_ws[...].astype(bf16)
        packed_grads[3328:3392] = d_wn[...].astype(bf16)
        packed_grads[3392:3456] = d_wl[...].astype(bf16)
        packed_grads[3456:3520] = d_kl[...].astype(bf16)
        d_small, d_bias = grads[2:]
        packed_grads[3520:3536] = jnp.concatenate(
            [reduce_bias(b) for b in (d_bias[0], d_bias[1], bias1[0], bias1[1])]
        ).astype(bf16)
        total = lambda x: jnp.sum(x, axis=0, keepdims=True)
        packed_grads[3536:3584] = jnp.concatenate(
            [total(d_small[:8]), total(d_small[8:]), total(small1[:8]), total(small1[8:])]
            + [total(kl[...]), jnp.zeros((43, D), f32)]
        ).astype(bf16)


def third(state_h, noise_h, dh, halo, small1, bias1, kl, cell_w, block_w, saved):
    nw, bands = state_h.shape[:2]
    rows = 64 * bands * SLOTS
    half = dh.shape[2:]
    return pl.pallas_call(
        third_kernel,
        grid=(nw,),
        in_specs=[
            pl.BlockSpec((1, bands, 64, D), lambda j: (j, 0, 0, 0)),
            pl.BlockSpec((1, bands, SLOTS, 64, ZC), lambda j: (j, 0, 0, 0, 0)),
            pl.BlockSpec((1, 1) + half, lambda j: (jnp.maximum(j - 1, 0), 1, 0, 0, 0)),
            pl.BlockSpec((1, 1) + half, lambda j: (j, 0, 0, 0, 0)),
            pl.BlockSpec((1,) + half, lambda j: (0, 0, 0, 0)),
        ]
        + [full(a) for a in (small1, bias1, kl)]
        + [full(a) for a in cell_w]
        + block_specs(0)
        + saved_specs(rows),
        out_specs=[pl.BlockSpec((1, bands * WIN, WIN, D), lambda j: (0, 0, j, 0))]
        + [pl.BlockSpec((ROWS_BLOCK + ROWS_CELL, D), lambda *_: (0, 0))],
        out_shape=[jax.ShapeDtypeStruct((1, bands * WIN, nw * WIN, D), f32)]
        + [jax.ShapeDtypeStruct((ROWS_BLOCK + ROWS_CELL, D), bf16)],
        scratch_shapes=scratch(backward_refs(rows))
        + [pltpu.VMEM(s, f32) for s in GRAD_SHAPES + CELL_SHAPES],
        compiler_params=params(1),
    )(state_h, noise_h, dh, dh, halo, small1, bias1, kl, *cell_w, *block_w, *saved)


def place_kernel(act, halo, out):
    nw = act.shape[0]
    for s in range(SLOTS):
        halves = [halo[0, s].astype(f32)]
        for j in range(nw):
            halves.append(act[j, 0, s].astype(f32))
            if j < nw - 1:
                halves.append(act[j, 1, s].astype(f32))
        out[0, s] = from_halves(jnp.stack(halves)).astype(bf16)


def place(act, halo):
    nw = act.shape[0]
    bands = act.shape[2] // SLOTS
    return pl.pallas_call(
        place_kernel,
        grid=(bands,),
        in_specs=[
            pl.BlockSpec((nw, 2, SLOTS, HALF, D), lambda i: (0, 0, i, 0, 0)),
            pl.BlockSpec((1, SLOTS, HALF, D), lambda i: (1, i, 0, 0)),
        ],
        out_specs=pl.BlockSpec((1, SLOTS, WIN, nw * WIN, D), lambda i: (0, 0, i, 0, 0)),
        out_shape=jax.ShapeDtypeStruct((1, SLOTS, bands * WIN, nw * WIN, D), bf16),
        compiler_params=params(1),
        cost_estimate=pl.CostEstimate(flops=1 << 23, bytes_accessed=1 << 22, transcendentals=0),
    )(act, halo)


def finish_kernel(
    order, scalars, state, part, wl, mine1, got1, mine0, got0,
    sg, div, o_wl, o_ws, o_wn, o_gain1, o_qkv, o_table, o_out, o_gain2, o_up, o_down,
    full1, full0, *, cells, devices,
):
    for mine, got, whole in ((mine1, got1, full1), (mine0, got0, full0)):
        count = whole.shape[0] // devices
        n = devices // 2
        for at, block in ((0, mine), (1, got)):
            for i in range(n):
                to = order[0, at] * n + jnp.bitwise_xor(order[1, at], i)
                whole[pl.ds(pl.multiple_of(to * count, 16), count)] = block[
                    count * i : count * i + count
                ]
    kl_mean = full0[3536:3552].astype(f32)[4:5, :ZC] * (1.0 / cells)
    beta, floor = scalars[0], scalars[1]
    excess = sharpness * (kl_mean - floor)
    soft = jnp.maximum(excess, 0.0) + jnp.log(1.0 + jnp.exp(-jnp.abs(excess)))
    div[...] = beta * jnp.mean(floor + soft * (1.0 / sharpness), axis=-1, keepdims=True)
    amt = beta * jax.nn.sigmoid(excess) * (1.0 / (ZC * cells))

    rows = state.shape[1] * state.shape[2]
    center, squash, sigma = latent_head(state[0].reshape(rows, D), wl[...])
    kl_center, kl_raw = divergence_parts(center, squash, sigma)
    g_center = (kl_center.astype(f32) * amt).astype(bf16)
    g_raw = (kl_raw.astype(f32) * amt).astype(bf16)
    add = mm(g_center, wl[:ZC]) + mm(g_raw, wl[ZC:])
    sg[0] = part[0] + add.reshape(state.shape[1:])

    for k, whole in ((0, full0), (1, full1)):
        for c in range(FF // 256):
            cols = slice(256 * c, 256 * c + 256)
            o_up[k, :, cols] = whole[cols].astype(f32)
            o_down[k, cols] = whole[FF + 256 * c : FF + 256 * c + 256].astype(f32).T
        for c in range(3):
            cols = slice(256 * c, 256 * c + 256)
            o_qkv[k, :, cols] = whole[2048 + 256 * c : 2304 + 256 * c].astype(f32)
        o_out[k] = whole[2816:3072].astype(f32)
    o_ws[...] = full0[3072:3328].astype(f32)
    wn = full0[3328:3392].astype(f32)
    o_wn[:, :D] = wn[:ZC]
    o_wn[:, D:] = wn[ZC:]
    at = lambda axis: lax.broadcasted_iota(jnp.int32, (ZC, ZC), axis)
    column = jnp.sum(jnp.where(at(0) == at(1), amt, 0.0), axis=1, keepdims=True)
    for h in range(2):
        rows = 3392 + ZC * h
        o_wl[ZC * h : ZC * h + ZC] = (
            full0[rows : rows + ZC].astype(f32) + full0[rows + 64 : rows + 64 + ZC].astype(f32) * column
        )
    table = mm(full0[3520:3536], table_lanes(True))
    o_table[0] = table[:HEADS, : (2 * WIN - 1) ** 2]
    o_table[1] = table[HEADS:, : (2 * WIN - 1) ** 2]
    gains = full0[3536:3552].astype(f32)
    for k in range(2):
        o_gain1[k : k + 1] = gains[2 * k : 2 * k + 1]
        o_gain2[k : k + 1] = gains[2 * k + 1 : 2 * k + 2]


def finish(order, scalars, state, part, wl, *blocks, cells, devices):
    outs = [
        part.shape, (1, 1), (2 * ZC, D), (D, D), (ZC, 2 * D), (2, D), (2, D, 3 * D),
        (2, HEADS, (2 * WIN - 1) ** 2), (2, D, D), (2, D), (2, D, FF), (2, FF, D),
    ]
    smem, vmem = pl.BlockSpec(memory_space=pltpu.SMEM), pl.BlockSpec(memory_space=pltpu.VMEM)
    return pl.pallas_call(
        functools.partial(finish_kernel, cells=cells, devices=devices),
        in_specs=[smem, smem] + [vmem] * 7,
        out_specs=[vmem] * len(outs),
        out_shape=[jax.ShapeDtypeStruct(o, f32) for o in outs],
        scratch_shapes=[pltpu.VMEM((2 * b.shape[0], D), bf16) for b in (blocks[0], blocks[2])],
        compiler_params=pltpu.CompilerParams(vmem_limit_bytes=LIMIT),
    )(order, scalars, state, part, wl, *blocks)


def shift_from(block, distance):
    n = lax.axis_size("lon")
    return lax.ppermute(block, "lon", [((i + distance) % n, i) for i in range(n)])


class Summation:
    def __init__(self):
        n_lon, n_batch = lax.axis_size("lon"), lax.axis_size("batch")
        self.n = n = n_lon * n_batch
        me = lax.axis_index("lon") * n_batch + lax.axis_index("batch")
        bits = [1 << i for i in range(1, n.bit_length() - 1)]
        lon = bits.pop()
        near, far = bits[:1], bits[1:]
        self.pairs = list(zip(near + [lon] + far, [lon] + far[:1] + near + far[1:]))
        self.core = me & 1
        self.bits = [self.core] + self.bits_of(me)
        places = [self.place(self.bits[1:]), self.place(self.bits_of(me ^ 1))]
        self.order = jnp.stack([jnp.stack([self.core, 1 - self.core]), jnp.stack(places)])

    def bits_of(self, device):
        return [
            (jnp.bitwise_and(device, jnp.where(device & 1 == 0, a, b)) != 0).astype(jnp.int32)
            for a, b in self.pairs
        ]

    def place(self, bits):
        at = jnp.zeros((), jnp.int32)
        for bit in bits:
            at = 2 * at + bit
        return at

    def swap(self, block, step):
        pair = self.pairs[step - 1] if step else (1, 1)
        return lax.ppermute(
            block, ("lon", "batch"), [(i, i ^ pair[i & 1]) for i in range(self.n)]
        )

    def __call__(self, total):
        rows = total.shape[0]
        total = jnp.pad(total, ((0, -rows % (16 * self.n)), (0, 0)))
        for step, bit in enumerate(self.bits):
            size = total.shape[0] // 2
            keep = lax.dynamic_slice_in_dim(total, bit * size, size, 0)
            send = lax.dynamic_slice_in_dim(total, (1 - bit) * size, size, 0)
            total = (keep.astype(f32) + self.swap(send, step).astype(f32)).astype(bf16)
        for step in range(len(self.bits) - 1, 0, -1):
            total = jnp.concatenate([total, self.swap(total, step)])
        return total, self.swap(total, 0)


def body(
    state,
    noise,
    samples,
    step,
    kl_weight,
    floor,
    latent_weight,
    state_weight,
    noise_weight,
    attention_gain,
    query_key_value,
    offset_bias,
    output_weight,
    feedforward_gain,
    up_weight,
    down_weight,
    cotangent,
):
    items, height, breadth, width = state.shape
    cells = items * height * breadth * lax.axis_size("lon") * lax.axis_size("batch")
    cell_w = (latent_weight.T, state_weight, noise_weight)
    cot_h, state_h, noise_h, kl, bias = prep(
        samples, cotangent, state, noise, cell_w[0], offset_bias.reshape(2 * HEADS, -1)
    )
    block_w = (
        attention_gain,
        query_key_value,
        bias,
        output_weight,
        feedforward_gain,
        up_weight,
        down_weight,
    )
    add_up = Summation()
    beta = kl_weight * (step + 1).astype(f32) / WARM
    scalars = jnp.stack([beta, floor])
    h1, halo, *saved = first(state_h, noise_h, cot_h, cell_w, block_w)
    halo, order, scalars = lax.optimization_barrier((halo, add_up.order, scalars))
    halo = shift_from(halo, 1)
    act, dh, halo, grads1, small1, bias1 = second(samples, h1, cot_h, halo, block_w)
    halo = shift_from(halo, -1)
    part, grads0 = third(
        state_h, noise_h, dh, halo, small1, bias1, kl, cell_w, block_w, saved
    )
    activations = place(act, halo)
    blocks = add_up(grads1) + add_up(grads0)
    state_gradient, divergence, *weights = finish(
        order, scalars, state, part, cell_w[0], *blocks, cells=cells, devices=add_up.n
    )
    return (activations, divergence.reshape(()), state_gradient, weights[0].T, *weights[1:])


def solution(mesh):
    return jax.shard_map(
        body,
        mesh=mesh,
        in_specs=(
            P("batch", None, "lon", None),
            P("batch", None, None, "lon", None),
            P("batch"),
            P(),
            P(),
            P(),
            P(),
            P(),
            P(),
            P(),
            P(),
            P(),
            P(),
            P(),
            P(),
            P(),
            P("batch", None, None, "lon", None),
        ),
        out_specs=(
            P("batch", None, None, "lon", None),
            P(),
            P("batch", None, "lon", None),
            P(),
            P(),
            P(),
            P(),
            P(),
            P(),
            P(),
            P(),
            P(),
            P(),
        ),
        check_vma=False,
    )
```

```python
import functools

import jax
import jax.numpy as jnp
from jax import lax
from jax.experimental import pallas as pl
from jax.experimental.pallas import tpu as pltpu
from jax.sharding import PartitionSpec as P

HEADS = 8
HD = 32
WIN = 8
WARM = 1000
SLOTS = 4
D = 256
FF = 1024
ZC = 32
HALF = WIN // 2 * WIN

eps_norm = 1e-05
sharpness = 8.0
spread_bound = 4.0
LOG2E = 1.4426950408889634
f32 = jnp.float32
bf16 = jnp.bfloat16


def mm(a, b):
    return lax.dot_general(a, b, (((1,), (0,)), ((), ())), preferred_element_type=f32)


def mm_nt(a, b):
    return lax.dot_general(a, b, (((1,), (1,)), ((), ())), preferred_element_type=f32)


def mm_tn(a, b):
    return lax.dot_general(a, b, (((0,), (0,)), ((), ())), preferred_element_type=f32)


def low_sublanes(shape):
    return lax.broadcasted_iota(jnp.int32, shape, len(shape) - 2) < 4


def to_halves(x):
    rows, cols, ch = x.shape
    n = cols // 8
    v = x.reshape(4, 2, n, 8, ch)
    a, b = v[:, 0], v[:, 1]
    low = low_sublanes(a.shape)
    first = jnp.where(low, a, pltpu.roll(b, 4, 2))
    second = jnp.where(low, pltpu.roll(a, 4, 2), b)
    first = first.transpose(1, 0, 2, 3)
    second = second.transpose(1, 0, 2, 3)
    return jnp.stack([first, second], axis=1).reshape(2 * n, HALF, ch)


def from_halves(x):
    n = x.shape[0] // 2
    ch = x.shape[-1]
    v = x.reshape(n, 2, 4, 8, ch)
    first, second = v[:, 0].transpose(1, 0, 2, 3), v[:, 1].transpose(1, 0, 2, 3)
    low = low_sublanes(first.shape)
    a = jnp.where(low, first, pltpu.roll(second, 4, 2))
    b = jnp.where(low, pltpu.roll(first, 4, 2), second)
    return jnp.stack([a, b], axis=1).reshape(8, 8 * n, ch)


def tile_of(first, second):
    return jnp.stack([first, second], axis=1).reshape(-1, first.shape[-1])


def halves_of(tile):
    v = tile.reshape(-1, 2, HALF, tile.shape[-1])
    return v[:, 0], v[:, 1]


def norm(x):
    c = x - jnp.mean(x, axis=-1, keepdims=True)
    r = lax.rsqrt(jnp.mean(c * c, axis=-1, keepdims=True) + eps_norm)
    return c * r, r


def norm_back(dy, xhat, r, gain):
    along = dy * gain
    inward = r * (
        along
        - jnp.mean(along, axis=-1, keepdims=True)
        - xhat * jnp.mean(along * xhat, axis=-1, keepdims=True)
    )
    return inward, jnp.sum((dy * xhat).reshape(-1, 8, D), axis=0)


ERF = (0.7978697122393114, 0.036392286377165226, -8.78266605765619e-05,
       -3.669342209361701e-05, 1.425004260912749e-06)


def gelu_parts(x):
    square = x * x
    p = ERF[-1]
    for c in ERF[-2::-1]:
        p = p * square + c
    erf = jnp.tanh(x * p)
    half = 0.5 * x
    density = jnp.exp2(square * (-0.5 * LOG2E))
    return half + half * erf, 0.5 + 0.5 * erf + x * density * 0.3989422804014327


def lane_masks():
    lane = lax.broadcasted_iota(jnp.int32, (1, 128), 1)
    return [(lane >= 32 * j) & (lane < 32 * j + 32) for j in range(4)]


def spread_heads(x, masks):
    return jnp.concatenate([x * m for m in masks], axis=0)


def gather_heads(x, masks):
    v = x.reshape(4, 64, 128)
    return jnp.where(masks[0], v[0], jnp.where(masks[1], v[1], jnp.where(masks[2], v[2], v[3])))


def pieces(rows):
    return [slice(r, r + 64) for r in range(0, rows, 64)]


def staged(count, *stages, beside):
    for n in range(count + len(stages) - 1):
        for work in beside.get(n, ()):
            work()
        for late, stage in enumerate(stages):
            if 0 <= n - late < count:
                stage(n - late)


def unit_of(n):
    g = n % 2
    rows = slice(64 * (n // 2), 64 * (n // 2) + 64)
    return rows, lambda part: slice(256 * part + 128 * g, 256 * part + 128 * g + 128), g


def attention(w, beside):
    sel = lane_masks()
    ones = [m.astype(f32).astype(bf16) for m in sel]
    scale = HD ** (-0.5) * LOG2E

    def scores(n):
        rows, lanes, g = unit_of(n)
        q, k = w["packed"][rows, lanes(0)], w["packed"][rows, lanes(1)]
        w["s"][n % 4] = mm_nt(k, spread_heads(q, ones))

    def softmax(n):
        s = w["s"][n % 4] * scale + w["bias"][n % 2]
        s = jnp.exp2(s - jnp.max(s, axis=0, keepdims=True))
        w["p"][n] = (s * (1.0 / jnp.sum(s, axis=0, keepdims=True))).astype(bf16)

    def values(n):
        rows, lanes, g = unit_of(n)
        found = gather_heads(mm_tn(w["p"][n], w["packed"][rows, lanes(2)]), sel)
        w["ctx"][rows, lanes(0)] = found.astype(bf16)

    staged(w["p"].shape[0], scores, softmax, values, beside=beside)


def attention_back(w, beside):
    sel = lane_masks()
    ones = [m.astype(f32).astype(bf16) for m in sel]
    scale = HD ** (-0.5)

    def upstream(n):
        rows, lanes, g = unit_of(n)
        spread = spread_heads(w["dctx"][rows, lanes(0)], ones)
        w["gp"][rows, lanes(2)] = mm(w["p"][n], spread).astype(bf16)
        w["s"][n % 4] = mm_nt(w["packed"][rows, lanes(2)], spread)

    def inward(n):
        p = w["p"][n].astype(f32)
        t = p * w["s"][n % 4]
        ds = t - p * jnp.sum(t, axis=0, keepdims=True)
        w["d_bias"][n % 2] += ds
        w["ds"][n % 4] = ds.astype(bf16)

    def outer(n):
        rows, lanes, g = unit_of(n)
        ds = w["ds"][n % 4]
        q, k = w["packed"][rows, lanes(0)], w["packed"][rows, lanes(1)]
        w["gp"][rows, lanes(1)] = (mm(ds, spread_heads(q, ones)) * scale).astype(bf16)
        w["gp"][rows, lanes(0)] = (gather_heads(mm_tn(ds, k), sel) * scale).astype(bf16)

    staged(w["p"].shape[0], upstream, inward, outer, beside=beside)


def halves(rows):
    return slice(0, rows // 2), slice(rows // 2, rows)


def pieces_of(half):
    return [slice(r, r + 64) for r in range(half.start, half.stop, 64)]


def attend(x_ref, w):
    rows = x_ref.shape[0]
    gain1, gain2 = w["gain1"][...], w["gain2"][...]
    scales = {}

    def project(half):
        for at in pieces_of(half):
            w["normed"][at] = (norm(x_ref[at])[0] * gain1).astype(bf16)
        w["packed"][half] = mm(w["normed"][half], w["qkv"][...]).astype(bf16)

    def join(half):
        w["mixed"][half] = x_ref[half] + mm(w["ctx"][half], w["out"][...])
        for at in pieces_of(half):
            xhat, scales[at.start] = norm(w["mixed"][at])
            w["xhat"][at] = xhat
            w["normed2"][at] = (xhat * gain2).astype(bf16)

    one, two = halves(rows)
    units = rows // 64
    project(one)
    beside = {2: [functools.partial(project, two)], units + 3: [functools.partial(join, one)]}
    attention(w, beside)
    join(two)
    return scales


def block_forward(x_ref, w):
    attend(x_ref, w)
    rows = x_ref.shape[0]

    def start(c):
        w["a"][c % 2] = mm(w["normed2"][...], w["up"][:, 256 * c : 256 * c + 256])

    start(0)
    for c in range(FF // 256):
        cols = slice(256 * c, 256 * c + 256)
        if c < FF // 256 - 1:
            start(c + 1)
        for at in pieces(rows):
            active, slope = gelu_parts(w["a"][c % 2, at])
            w["active"][at, cols] = active.astype(bf16)
            w["slope"][at, cols] = slope.astype(bf16)
        before = w["mixed"] if c == 0 else w["xhat"]
        w["xhat"][...] = before[...] + mm(w["active"][:, cols], w["down"][cols, :])


def block_backward(x_ref, g_ref, w, fused, round_dn):
    rows = x_ref.shape[0]
    gain1, gain2 = w["gain1"][...], w["gain2"][...]
    if fused:
        scales = attend(x_ref, w)
    normed2_t = w["normed2"][...].T
    gb = g_ref[...].astype(bf16)
    gb_t = gb.T

    def start(c):
        cols = slice(256 * c, 256 * c + 256)
        if fused:
            w["a"][c % 2] = mm(w["normed2"][...], w["up"][:, cols])
        w["b"][c % 2] = mm_nt(gb, w["down"][cols, :])

    start(0)
    for c in range(FF // 256):
        cols = slice(256 * c, 256 * c + 256)
        if c < FF // 256 - 1:
            start(c + 1)
        for at in pieces(rows):
            if fused:
                active, slope = gelu_parts(w["a"][c % 2, at])
                w["active"][at, cols] = active.astype(bf16)
            else:
                slope = w["slope"][at, cols].astype(f32)
            w["d_inner"][at, cols] = (w["b"][c % 2, at] * slope).astype(bf16)
        part = mm_nt(w["d_inner"][:, cols], w["up"][:, cols])
        w["dn"][...] = part if c == 0 else w["dn"][...] + part
        w["d_ff"][1024 + 256 * c : 1280 + 256 * c, :] += mm(gb_t, w["active"][:, cols])
        w["d_ff"][cols, :] += mm(normed2_t, w["d_inner"][:, cols])
        if fused:
            w["mixed"][...] += mm(w["active"][:, cols], w["down"][cols, :])

    def into_heads(half):
        dgain = None
        for at in pieces_of(half):
            xhat, r = (w["xhat"][at], scales[at.start]) if fused else norm(w["mixed"][at])
            inward, part = norm_back(w["dn"][at], xhat, r, gain2)
            dgain = part if dgain is None else dgain + part
            d_mixed = g_ref[at] + inward
            g_ref[at] = d_mixed
            w["g_out"][at] = d_mixed.astype(bf16)
        w["d_small"][8:16, :] += dgain
        w["dctx"][half] = mm_nt(w["g_out"][half], w["out"][...]).astype(bf16)

    def d_out():
        w["d_at"][768:1024, :] += mm_tn(w["ctx"][...], w["g_out"][...])

    def out_of_heads(half):
        gp = w["gp"][half]
        w["dn"][half] = mm_nt(gp, w["qkv"][...])
        normed_t = w["normed"][half].T
        for c in range(3):
            cols = slice(256 * c, 256 * c + 256)
            w["d_at"][cols, :] += mm(normed_t, gp[:, cols])
        dgain = None
        for at in pieces_of(half):
            dn = w["dn"][at]
            if round_dn:
                dn = dn.astype(bf16).astype(f32)
            xhat, r = norm(x_ref[at])
            inward, part = norm_back(dn, xhat, r, gain1)
            dgain = part if dgain is None else dgain + part
            g_ref[at] = g_ref[at] + inward
        w["d_small"][0:8, :] += dgain

    one, two = halves(rows)
    units = rows // 64
    into_heads(one)
    beside = {
        2: [functools.partial(into_heads, two)],
        units: [d_out],
        units + 3: [functools.partial(out_of_heads, one)],
    }
    attention_back(w, beside)
    out_of_heads(two)


LIMIT = 56 * 1024 * 1024


def cost(us):
    return pl.CostEstimate(flops=int(us * 1.1e9), bytes_accessed=int(us * 3.6e6), transcendentals=0)


def params(n):
    return pltpu.CompilerParams(
        dimension_semantics=("arbitrary",) * n, vmem_limit_bytes=LIMIT
    )


def latent_head(state, wl):
    center = mm_nt(state, wl[:ZC])
    squash = jnp.tanh(mm_nt(state, wl[ZC:]) * (1.0 / spread_bound))
    return center, squash, jnp.exp((0.5 * spread_bound) * squash)


def lanes_of_patch(width, back):
    lane = lax.broadcasted_iota(jnp.int32, (4 * 256, 4 * 64), 0)
    at = lax.broadcasted_iota(jnp.int32, (4 * 256, 4 * 64), 1)
    row, col = query_place(at & 63)
    want = 16 * (7 - row) + 7 - col if back else 16 * row + col
    return jnp.where(lane == (at >> 6) * 256 + want, 1.0, 0.0).astype(bf16)


def query_place(q):
    return (q >> 2) & 7, ((q >> 5) << 2) + (q & 3)


def table_lanes(back):
    a = lax.broadcasted_iota(jnp.int32, (256, 256), 0)
    b = lax.broadcasted_iota(jnp.int32, (256, 256), 1)
    side = 2 * WIN - 1
    if back:
        mirrored = 16 * (14 - (a >> 4)) + 14 - (a & 15)
        hit = ((a & 15) < side) & ((a >> 4) < side) & (b == (14 - (a >> 4)) * side + 14 - (a & 15))
    else:
        hit = ((b & 15) < side) & ((b >> 4) < side) & (a == (b >> 4) * side + (b & 15))
    return jnp.where(hit, 1.0, 0.0).astype(bf16)


def exactly(a, onehot):
    total = None
    for _ in range(3):
        term = a.astype(bf16)
        a = a - term.astype(f32)
        part = mm(term, onehot)
        total = part if total is None else total + part
    return total


def expand_bias(tables):
    spread = exactly(tables, table_lanes(False))
    choose = lanes_of_patch(64, False)
    out = []
    for n in range(4):
        heads = []
        for h in range(4 * n, 4 * n + 4):
            one = jnp.broadcast_to(spread[h : h + 1], (8, 256))
            heads.append(
                jnp.concatenate(
                    [
                        pltpu.roll(one, (16 * r + 137) % 256, 1, stride=1, stride_axis=0)
                        for r in range(WIN)
                    ]
                )
            )
        rows = exactly(jnp.concatenate(heads, axis=1), choose)
        out.append(to_halves(rows.reshape(WIN, WIN, 256)).reshape(64, 256))
    return out


def reduce_bias(grads):
    rows = from_halves(grads.reshape(2, HALF, 256)).reshape(64, 256).astype(bf16)
    lanes = lax.dot_general(
        rows, lanes_of_patch(64, True), (((1,), (1,)), ((), ())), preferred_element_type=f32
    )
    out = []
    for h in range(4):
        total = None
        for r in range(WIN):
            one = pltpu.roll(
                lanes[8 * r : 8 * r + 8, 256 * h : 256 * h + 256], 16 * r, 1, stride=1, stride_axis=0
            )
            total = one if total is None else total + one
        out.append(jnp.sum(total, axis=0, keepdims=True))
    return jnp.concatenate(out)


def prep_kernel(samples, cot, state, noise, wl, tables, cot_h, state_h, noise_h, kl, bias):
    @pl.when(pl.program_id(0) == 0)
    def _():
        padded = jnp.concatenate(
            [tables[...], jnp.zeros((16, 256 - tables.shape[1]), f32)], axis=1
        )
        for n, part in enumerate(expand_bias(padded * LOG2E)):
            bias[n // 2, n % 2] = part

    live = samples[0]
    for s in range(SLOTS):
        factor = jnp.where(s < live, 1.0, 0.0).astype(f32)
        cot_h[:, s] = (to_halves(cot[0, s].astype(f32)) * factor).astype(bf16)
        noise_h[:, 0, s] = to_halves(noise[0, s]).reshape(4, 64, ZC)
    st = to_halves(state[0].astype(f32)).reshape(4, 64, D).astype(bf16)
    state_h[:, 0] = st
    center, squash, sigma = latent_head(st.reshape(4 * 64, D), wl[...])
    terms = 0.5 * (center * center + sigma * sigma - 1.0 - spread_bound * squash)

    @pl.when(pl.program_id(0) == 0)
    def _():
        kl[...] = jnp.zeros(kl.shape, f32)

    kl[:, :ZC] += jnp.sum(terms.reshape(-1, 8, ZC), axis=0)


def prep(samples, cot, state, noise, wl, tables):
    bands = state.shape[1] // WIN
    nw = state.shape[2] // WIN
    return pl.pallas_call(
        prep_kernel,
        grid=(bands,),
        in_specs=[
            pl.BlockSpec(memory_space=pltpu.SMEM),
            pl.BlockSpec((1, SLOTS, WIN, nw * WIN, D), lambda i: (0, 0, i, 0, 0)),
            pl.BlockSpec((1, WIN, nw * WIN, D), lambda i: (0, i, 0, 0)),
            pl.BlockSpec((1, SLOTS, WIN, nw * WIN, ZC), lambda i: (0, 0, i, 0, 0)),
            full(wl),
            full(tables),
        ],
        out_specs=[
            pl.BlockSpec((2 * nw, SLOTS, HALF, D), lambda i: (0, i, 0, 0)),
            pl.BlockSpec((nw, 1, 64, D), lambda i: (0, i, 0, 0)),
            pl.BlockSpec((nw, 1, SLOTS, 64, ZC), lambda i: (0, i, 0, 0, 0)),
            pl.BlockSpec((8, D), lambda i: (0, 0)),
            pl.BlockSpec((2, 2, 64, 256), lambda i: (0, 0, 0, 0)),
        ],
        out_shape=[
            jax.ShapeDtypeStruct((2 * nw, bands * SLOTS, HALF, D), bf16),
            jax.ShapeDtypeStruct((nw, bands, 64, D), bf16),
            jax.ShapeDtypeStruct((nw, bands, SLOTS, 64, ZC), f32),
            jax.ShapeDtypeStruct((8, D), f32),
            jax.ShapeDtypeStruct((2, 2, 64, 256), f32),
        ],
        compiler_params=params(1),
        cost_estimate=cost(4),
    )(samples, cot, state, noise, wl, tables)


def cell_forward(state, noise, wl, ws, wn):
    bands = state.shape[0]
    flat = state.reshape(bands * 64, D)
    over = lambda x: x.reshape(bands, 1, 64, x.shape[-1])
    center, squash, sigma = latent_head(flat, wl)
    latent = (over(center) + over(sigma) * noise).reshape(-1, ZC).astype(bf16)
    mix = mm(latent, wn)
    gate = jax.nn.sigmoid(over(mm(flat, ws)) + mix[:, :D].reshape(bands, SLOTS, 64, D))
    cand = jnp.tanh(mix[:, D:].reshape(bands, SLOTS, 64, D))
    hidden = gate * over(flat.astype(f32)) + (1.0 - gate) * cand
    return hidden.reshape(-1, D), center, squash, sigma, latent, gate, cand


def full(a):
    return pl.BlockSpec(a.shape, lambda *_: (0,) * a.ndim)


def block_specs(k):
    return [
        pl.BlockSpec((2, D), lambda *_: (0, 0)),
        pl.BlockSpec((1, D, 3 * D), lambda *_: (k, 0, 0)),
        pl.BlockSpec((1, 2, 64, 256), lambda *_: (k, 0, 0, 0)),
        pl.BlockSpec((1, D, D), lambda *_: (k, 0, 0)),
        pl.BlockSpec((2, D), lambda *_: (0, 0)),
        pl.BlockSpec((1, D, FF), lambda *_: (k, 0, 0)),
        pl.BlockSpec((1, FF, D), lambda *_: (k, 0, 0)),
    ]


NAMES = ("gain1", "qkv", "bias", "out", "gain2", "up", "down")


def named(refs, k):
    return {
        n: r.at[k : k + 1] if n.startswith("gain") else r.at[0] for n, r in zip(NAMES, refs)
    }


def saved_refs(rows):
    return [
        ("normed", (rows, D), bf16),
        ("packed", (rows, 3 * D), bf16),
        ("p", (rows // 32, 64, 256), bf16),
        ("ctx", (rows, D), bf16),
        ("mixed", (rows, D), f32),
        ("normed2", (rows, D), bf16),
        ("active", (rows, FF), bf16),
        ("slope", (rows, FF), bf16),
    ]


def forward_refs(rows):
    return [
        ("x", (rows, D), f32),
        ("s", (4, 64, 256), f32),
        ("xhat", (rows, D), f32),
        ("a", (2, rows, 256), f32),
    ]


def backward_refs(rows):
    return [
        ("x", (rows, D), f32),
        ("g", (rows, D), f32),
        ("s", (4, 64, 256), f32),
        ("b", (2, rows, 256), f32),
        ("d_inner", (rows, FF), bf16),
        ("dn", (rows, D), f32),
        ("g_out", (rows, D), bf16),
        ("dctx", (rows, D), bf16),
        ("ds", (4, 64, 256), bf16),
        ("gp", (rows, 3 * D), bf16),
    ]


def both_refs(rows):
    return saved_refs(rows) + forward_refs(rows)[2:] + backward_refs(rows)


def scratch(refs):
    return [pltpu.VMEM(shape, dtype) for _, shape, dtype in refs]


def names(refs):
    return [name for name, _, _ in refs]


def saved_specs(rows, skip):
    return [
        pl.BlockSpec((1,) + shape, lambda j, n=len(shape): (j + skip,) + (0,) * n)
        for _, shape, _ in saved_refs(rows)
    ]


N_SAVED, N_BACK, N_BOTH = len(saved_refs(64)), len(backward_refs(64)), len(both_refs(64))


GRAD_SHAPES = [(2048, D), (1024, D), (16, D), (2, 64, 256)]
GRAD_NAMES = ("d_ff", "d_at", "d_small", "d_bias")
GRAD_SCRATCH = [pltpu.VMEM(s, f32) for s in GRAD_SHAPES[:2]]
SMALL_SPECS = [pl.BlockSpec(s, lambda *_, n=len(s): (0,) * n) for s in GRAD_SHAPES[2:]]
SMALL_OUTS = [jax.ShapeDtypeStruct(s, f32) for s in GRAD_SHAPES[2:]]

ROWS_BLOCK = 3072
ROWS_CELL = 512


def first_kernel(state, noise, cot, wl, ws, wn, *rest, lead):
    w = named(rest[:7], 0)
    rest = rest[7:] if lead else rest[7 + 1 + N_SAVED :]
    h1, rest = rest[0], rest[1:]
    w.update((n, r.at[0]) for n, r in zip(names(saved_refs(64)), rest))
    rest = rest[N_SAVED:]
    if lead:
        halo, rest = rest[0], rest[1:]
    w.update(zip(names(forward_refs(64)), rest))
    w["x"][...] = cell_forward(state[0], noise[0], wl[...], ws[...], wn[...])[0]
    block_forward(w["x"], w)
    a, b = halves_of(w["xhat"][...])
    h1[0, 0] = a
    h1[0, 1] = b
    if lead:
        halo[0] = a.astype(bf16)
        halo[1] = cot[0]


def first(state_h, noise_h, cot_h, cell_w, block_w, before=None):
    nw, bands = state_h.shape[:2]
    half = (bands * SLOTS, HALF, D)
    rows = 64 * bands * SLOTS
    lead = before is None
    skip = 0 if lead else 1
    specs = [pl.BlockSpec((1, 2) + half, lambda j: (j + skip, 0, 0, 0, 0))] + saved_specs(rows, skip)
    shapes = [jax.ShapeDtypeStruct((nw, 2) + half, f32)] + [
        jax.ShapeDtypeStruct((nw,) + shape, dtype) for _, shape, dtype in saved_refs(rows)
    ]
    inputs = [state_h, noise_h, cot_h, *cell_w, *block_w]
    in_specs = [
        pl.BlockSpec((1, bands, 64, D), lambda j: (j + skip, 0, 0, 0)),
        pl.BlockSpec((1, bands, SLOTS, 64, ZC), lambda j: (j + skip, 0, 0, 0, 0)),
        pl.BlockSpec((1,) + half, lambda j: (0, 0, 0, 0)),
    ]
    in_specs += [full(a) for a in cell_w] + block_specs(0)
    aliases = {}
    if lead:
        specs.append(pl.BlockSpec((2,) + half, lambda j: (0, 0, 0, 0)))
        shapes.append(jax.ShapeDtypeStruct((2,) + half, bf16))
    else:
        aliases = {len(inputs) + n: n for n in range(len(before))}
        inputs += before
        in_specs += [pl.BlockSpec(memory_space=pl.ANY)] * len(before)
    return pl.pallas_call(
        functools.partial(first_kernel, lead=lead),
        grid=(1 if lead else nw - 1,),
        in_specs=in_specs,
        out_specs=specs,
        out_shape=shapes,
        input_output_aliases=aliases,
        scratch_shapes=scratch(forward_refs(rows)),
        compiler_params=params(1),
        cost_estimate=cost(6 if lead else 16),
    )(*inputs)


def zero_at_start(refs):
    @pl.when(pl.program_id(0) == 0)
    def _():
        for r in refs:
            r[...] = jnp.zeros(r.shape, r.dtype)


def halves_out(core, keep, send, parts):
    size = keep.shape[0]

    def write(low, high):
        first = 0
        for ref in parts:
            rows = ref.shape[0]
            cut = min(max(size - first, 0), rows)
            if cut:
                low[first : first + cut] = ref[:cut].astype(bf16)
            if cut < rows:
                high[first + cut - size : first + rows - size] = ref[cut:rows].astype(bf16)
            first += rows

    @pl.when(core == 0)
    def _():
        write(keep, send)

    @pl.when(core != 0)
    def _():
        write(send, keep)


def at_end():
    return pl.program_id(0) == pl.num_programs(0) - 1


def second_kernel(numbers, ha, hb, ca, cb, *rest, lead):
    w = named(rest[:7], 1)
    grads1, small1, bias1 = (None,) * 3 if lead else rest[7:10]
    rest = rest[7:] if lead else rest[12:]
    act, dh, d_small, d_bias = rest[:4]
    if lead:
        packed_grads, back_halo = rest[4:6]
    else:
        keep, send = rest[4:6]
    rest = rest[6:]
    w.update(zip(names(both_refs(64)), rest))
    grads = rest[N_BOTH : N_BOTH + 2] + (d_small, d_bias)
    w.update(zip(GRAD_NAMES, grads))
    if lead:
        zero_at_start(grads)
    else:

        @pl.when(pl.program_id(0) == 0)
        def _():
            grads[0][...] = grads1[:2048].astype(f32)
            grads[1][...] = grads1[2048:].astype(f32)
            d_small[...] = small1[...]
            d_bias[...] = bias1[...]

    w["x"][...] = tile_of(ha[0, 0], hb[0].astype(f32) if lead else hb[0, 0])
    w["g"][...] = tile_of(ca[0].astype(f32), cb[0].astype(f32))
    block_backward(w["x"], w["g"], w, True, True)
    live = numbers[0]
    a, b = halves_of(w["mixed"][...])
    factor = jnp.concatenate(
        [jnp.where(s % SLOTS < live, 1.0, 0.0) * jnp.ones((1, 1, D), f32) for s in range(a.shape[0])]
    )
    a, b = (a * factor).astype(bf16), (b * factor).astype(bf16)
    da, db = halves_of(w["g"][...])
    act[0, 0] = a
    act[0, 1] = b
    dh[0, 0] = da
    dh[0, 1] = db
    if lead:
        back_halo[0] = db.astype(bf16)
        back_halo[1] = b
        packed_grads[:2048] = grads[0][...].astype(bf16)
        packed_grads[2048:] = grads[1][...].astype(bf16)
    else:

        @pl.when(at_end())
        def _():
            halves_out(numbers[1], keep, send, [grads[0], grads[1]])


def second(numbers, h1, cot_h, block_w, halo=None, before=None):
    nw = h1.shape[0]
    half = h1.shape[2:]
    lead = before is None
    if lead:
        tile, other = (lambda j: nw - 1), halo
        wide = [pl.BlockSpec((1,) + half, lambda j, n=n: (n, 0, 0, 0)) for n in range(2)]
    else:
        tile, other = (lambda j: j), cot_h
        wide = [
            pl.BlockSpec((1, 1) + half, lambda j: (j + 1, 0, 0, 0, 0)),
            pl.BlockSpec((1,) + half, lambda j: (2 * j + 2, 0, 0, 0)),
        ]
    inputs = [numbers, h1, halo if lead else h1, cot_h, other, *block_w]
    in_specs = [
        pl.BlockSpec(memory_space=pltpu.SMEM),
        pl.BlockSpec((1, 1) + half, lambda j: (tile(j), 1, 0, 0, 0)),
        wide[0],
        pl.BlockSpec((1,) + half, lambda j: (2 * tile(j) + 1, 0, 0, 0)),
        wide[1],
    ]
    in_specs += block_specs(1)
    out_specs = [
        pl.BlockSpec((1, 2) + half, lambda j: (tile(j), 0, 0, 0, 0)),
        pl.BlockSpec((1, 2) + half, lambda j: (tile(j), 0, 0, 0, 0)),
    ] + SMALL_SPECS
    out_shape = [
        jax.ShapeDtypeStruct((nw, 2) + half, bf16),
        jax.ShapeDtypeStruct((nw, 2) + half, f32),
    ] + SMALL_OUTS
    aliases = {}
    if lead:
        out_specs.append(pl.BlockSpec((ROWS_BLOCK, D), lambda *_: (0, 0)))
        out_specs.append(pl.BlockSpec((2,) + half, lambda j: (0, 0, 0, 0)))
        out_shape.append(jax.ShapeDtypeStruct((ROWS_BLOCK, D), bf16))
        out_shape.append(jax.ShapeDtypeStruct((2,) + half, bf16))
    else:
        out_specs += [pl.BlockSpec((ROWS_BLOCK // 2, D), lambda *_: (0, 0))] * 2
        out_shape += [jax.ShapeDtypeStruct((ROWS_BLOCK // 2, D), bf16)] * 2
        act, dh, small1, bias1, grads1 = before
        sums = [grads1, small1, bias1]
        aliases = {len(inputs) + 3: 0, len(inputs) + 4: 1}
        inputs += sums + [act, dh]
        in_specs += [full(a) for a in sums] + [pl.BlockSpec(memory_space=pl.ANY)] * 2
    return pl.pallas_call(
        functools.partial(second_kernel, lead=lead),
        grid=(1 if lead else nw - 1,),
        in_specs=in_specs,
        out_specs=out_specs,
        out_shape=out_shape,
        input_output_aliases=aliases,
        scratch_shapes=scratch(both_refs(64 * half[0])) + GRAD_SCRATCH,
        compiler_params=params(1),
        cost_estimate=cost(9 if lead else 24),
    )(*inputs)


CELL_SHAPES = [(D, D), (2 * ZC, D), (2 * ZC, D), (2 * ZC, D)]


def divergence_parts(center, squash, sigma):
    return center.astype(bf16), (
        0.5 * (sigma * sigma - 1.0) * (1.0 - squash * squash)
    ).astype(bf16)


def third_kernel(numbers, state, noise, da, db, dhalo, small1, bias1, kl, wl, ws, wn, *rest):
    w = named(rest[:7], 0)
    w.update((n, r.at[0]) for n, r in zip(names(saved_refs(64)), rest[7:]))
    rest = rest[N_SAVED:]
    sg, keep, send = rest[7:10]
    w.update(zip(names(backward_refs(64)), rest[10:]))
    grads = rest[10 + N_BACK : 14 + N_BACK]
    d_ws, d_wn, d_wl, d_kl, d_rest = rest[14 + N_BACK :]
    cell_grads = (d_ws, d_wn, d_wl, d_kl)
    w.update(zip(GRAD_NAMES, grads))
    zero_at_start(grads + cell_grads)
    st = state[0]
    nz = noise[0]
    bands = st.shape[0]
    hidden, center, squash, sigma, latent, gate, cand = cell_forward(
        st, nz, wl[...], ws[...], wn[...]
    )
    da_v = jnp.where(pl.program_id(0) == 0, dhalo[0].astype(f32), da[0, 0])
    w["x"][...] = hidden
    w["g"][...] = tile_of(da_v, db[0, 0])
    block_backward(w["x"], w["g"], w, False, False)
    dc = w["g"][...]
    over = lambda x: x.reshape(bands, 1, 64, x.shape[-1])
    flat = st.reshape(bands * 64, D)
    dc = dc.reshape(bands, SLOTS, 64, D)
    rest_gate = 1.0 - gate
    d_pre = dc * (over(flat.astype(f32)) - cand) * gate * rest_gate
    d_cand = dc * rest_gate * (1.0 - cand * cand)
    direct = jnp.sum(dc * gate, axis=1).reshape(-1, D)
    g_gate = jnp.sum(d_pre, axis=1).reshape(-1, D).astype(bf16)
    d_ws[...] += mm_tn(flat, g_gate)
    pre = d_pre.reshape(-1, D).astype(bf16)
    cnd = d_cand.reshape(-1, D).astype(bf16)
    d_wn[:ZC] += mm_tn(latent, pre)
    d_wn[ZC:] += mm_tn(latent, cnd)
    d_lat = mm_nt(pre, wn[:, :D]) + mm_nt(cnd, wn[:, D:])
    d_lat = d_lat.reshape(bands, SLOTS, 64, ZC)
    d_center = jnp.sum(d_lat, axis=1).reshape(-1, ZC)
    d_raw = jnp.sum(d_lat * nz, axis=1).reshape(-1, ZC) * 0.5 * sigma * (1.0 - squash * squash)
    d_center, d_raw = d_center.astype(bf16), d_raw.astype(bf16)
    d_wl[:ZC] += mm_tn(d_center, flat)
    d_wl[ZC:] += mm_tn(d_raw, flat)
    kl_center, kl_raw = divergence_parts(center, squash, sigma)
    d_kl[:ZC] += mm_tn(kl_center, flat)
    d_kl[ZC:] += mm_tn(kl_raw, flat)
    total = direct + mm_nt(g_gate, ws[...])
    total = total + mm(d_center, wl[:ZC]) + mm(d_raw, wl[ZC:])
    for b in range(bands):
        sg[0, WIN * b : WIN * b + WIN] = from_halves(
            total[64 * b : 64 * b + 64].reshape(2, HALF, D)
        )

    @pl.when(at_end())
    def _():
        d_small, d_bias = grads[2:]
        d_rest[:16] = jnp.concatenate(
            [reduce_bias(b) for b in (d_bias[0], d_bias[1], bias1[0], bias1[1])]
        )
        total = lambda x: jnp.sum(x, axis=0, keepdims=True)
        d_rest[16:] = jnp.concatenate(
            [total(d_small[:8]), total(d_small[8:]), total(small1[:8]), total(small1[8:])]
            + [total(kl[...]), jnp.zeros((43, D), f32)]
        )
        halves_out(numbers[1], keep, send, [grads[0], grads[1], *cell_grads, d_rest])


def third(numbers, state_h, noise_h, dh, halo, small1, bias1, kl, cell_w, block_w, saved):
    nw, bands = state_h.shape[:2]
    rows = 64 * bands * SLOTS
    half = dh.shape[2:]
    return pl.pallas_call(
        third_kernel,
        grid=(nw,),
        in_specs=[
            pl.BlockSpec(memory_space=pltpu.SMEM),
            pl.BlockSpec((1, bands, 64, D), lambda j: (j, 0, 0, 0)),
            pl.BlockSpec((1, bands, SLOTS, 64, ZC), lambda j: (j, 0, 0, 0, 0)),
            pl.BlockSpec((1, 1) + half, lambda j: (jnp.maximum(j - 1, 0), 1, 0, 0, 0)),
            pl.BlockSpec((1, 1) + half, lambda j: (j, 0, 0, 0, 0)),
            pl.BlockSpec((1,) + half, lambda j: (0, 0, 0, 0)),
        ]
        + [full(a) for a in (small1, bias1, kl)]
        + [full(a) for a in cell_w]
        + block_specs(0)
        + saved_specs(rows, 0),
        out_specs=[pl.BlockSpec((1, bands * WIN, WIN, D), lambda j: (0, 0, j, 0))]
        + [pl.BlockSpec(((ROWS_BLOCK + ROWS_CELL) // 2, D), lambda *_: (0, 0))] * 2,
        out_shape=[jax.ShapeDtypeStruct((1, bands * WIN, nw * WIN, D), f32)]
        + [jax.ShapeDtypeStruct(((ROWS_BLOCK + ROWS_CELL) // 2, D), bf16)] * 2,
        scratch_shapes=scratch(backward_refs(rows))
        + [pltpu.VMEM(s, f32) for s in GRAD_SHAPES + CELL_SHAPES + [(64, D)]],
        compiler_params=params(1),
        cost_estimate=cost(26),
    )(numbers, state_h, noise_h, dh, dh, halo, small1, bias1, kl, *cell_w, *block_w, *saved)


def place_kernel(act, halo, out):
    nw = act.shape[0]
    for s in range(SLOTS):
        halves = [halo[0, s].astype(f32)]
        for j in range(nw):
            halves.append(act[j, 0, s].astype(f32))
            if j < nw - 1:
                halves.append(act[j, 1, s].astype(f32))
        out[0, s] = from_halves(jnp.stack(halves)).astype(bf16)


def place(act, halo):
    nw = act.shape[0]
    bands = act.shape[2] // SLOTS
    return pl.pallas_call(
        place_kernel,
        grid=(bands,),
        in_specs=[
            pl.BlockSpec((nw, 2, SLOTS, HALF, D), lambda i: (0, 0, i, 0, 0)),
            pl.BlockSpec((1, SLOTS, HALF, D), lambda i: (1, i, 0, 0)),
        ],
        out_specs=pl.BlockSpec((1, SLOTS, WIN, nw * WIN, D), lambda i: (0, 0, i, 0, 0)),
        out_shape=jax.ShapeDtypeStruct((1, SLOTS, bands * WIN, nw * WIN, D), bf16),
        compiler_params=params(1),
        cost_estimate=cost(2),
    )(act, halo)


def finish_kernel(
    order, scalars, state, part, wl, mine1, got1, mine0, got0,
    sg, div, o_wl, o_ws, o_wn, o_gain1, o_qkv, o_table, o_out, o_gain2, o_up, o_down,
    full1, full0, *, cells, devices,
):
    for mine, got, whole in ((mine1, got1, full1), (mine0, got0, full0)):
        n = devices // 4
        count = mine.shape[0] // n
        for at, block in ((0, mine), (1, got)):
            for i in range(n):
                to = order[0, at] * n + jnp.bitwise_xor(order[1, at], i)
                whole[pl.ds(pl.multiple_of(to * count, 16), count)] = block[
                    count * i : count * i + count
                ]

    def rows_of(whole, first, count):
        half = (ROWS_BLOCK if whole is full1 else ROWS_BLOCK + ROWS_CELL) // 2
        if first >= half:
            first += whole.shape[0] // 2 - half
        return whole[first : first + count]

    cell_rows = lambda first, count: rows_of(full0, ROWS_BLOCK + first, count)
    small = cell_rows(464, 16).astype(f32)
    kl_mean = small[4:5, :ZC] * (1.0 / cells)
    beta, floor = scalars[0], scalars[1]
    excess = sharpness * (kl_mean - floor)
    soft = jnp.maximum(excess, 0.0) + jnp.log(1.0 + jnp.exp(-jnp.abs(excess)))
    div[...] = beta * jnp.mean(floor + soft * (1.0 / sharpness), axis=-1, keepdims=True)
    amt = beta * jax.nn.sigmoid(excess) * (1.0 / (ZC * cells))

    rows = state.shape[1] * state.shape[2]
    center, squash, sigma = latent_head(state[0].reshape(rows, D), wl[...])
    kl_center, kl_raw = divergence_parts(center, squash, sigma)
    g_center = (kl_center.astype(f32) * amt).astype(bf16)
    g_raw = (kl_raw.astype(f32) * amt).astype(bf16)
    add = mm(g_center, wl[:ZC]) + mm(g_raw, wl[ZC:])
    sg[0] = part[0] + add.reshape(state.shape[1:])

    for k, whole in ((0, full0), (1, full1)):
        for c in range(FF // 256):
            cols = slice(256 * c, 256 * c + 256)
            o_up[k, :, cols] = rows_of(whole, 256 * c, 256).astype(f32)
            o_down[k, cols] = rows_of(whole, FF + 256 * c, 256).astype(f32).T
        for c in range(3):
            cols = slice(256 * c, 256 * c + 256)
            o_qkv[k, :, cols] = rows_of(whole, 2 * FF + 256 * c, 256).astype(f32)
        o_out[k] = rows_of(whole, 2816, 256).astype(f32)
    o_ws[...] = cell_rows(0, 256).astype(f32)
    wn = cell_rows(256, 64).astype(f32)
    o_wn[:, :D] = wn[:ZC]
    o_wn[:, D:] = wn[ZC:]
    at = lambda axis: lax.broadcasted_iota(jnp.int32, (ZC, ZC), axis)
    column = jnp.sum(jnp.where(at(0) == at(1), amt, 0.0), axis=1, keepdims=True)
    for h in range(2):
        o_wl[ZC * h : ZC * h + ZC] = (
            cell_rows(320 + ZC * h, ZC).astype(f32) + cell_rows(384 + ZC * h, ZC).astype(f32) * column
        )
    table = mm(cell_rows(448, 16), table_lanes(True))
    o_table[0] = table[:HEADS, : (2 * WIN - 1) ** 2]
    o_table[1] = table[HEADS:, : (2 * WIN - 1) ** 2]
    for k in range(2):
        o_gain1[k : k + 1] = small[2 * k : 2 * k + 1]
        o_gain2[k : k + 1] = small[2 * k + 1 : 2 * k + 2]


def finish(order, scalars, state, part, wl, *blocks, cells, devices):
    outs = [
        part.shape, (1, 1), (2 * ZC, D), (D, D), (ZC, 2 * D), (2, D), (2, D, 3 * D),
        (2, HEADS, (2 * WIN - 1) ** 2), (2, D, D), (2, D), (2, D, FF), (2, FF, D),
    ]
    smem, vmem = pl.BlockSpec(memory_space=pltpu.SMEM), pl.BlockSpec(memory_space=pltpu.VMEM)
    return pl.pallas_call(
        functools.partial(finish_kernel, cells=cells, devices=devices),
        in_specs=[smem, smem] + [vmem] * 7,
        out_specs=[vmem] * len(outs),
        out_shape=[jax.ShapeDtypeStruct(o, f32) for o in outs],
        scratch_shapes=[pltpu.VMEM((2 * b.shape[0], D), bf16) for b in (blocks[0], blocks[2])],
        compiler_params=pltpu.CompilerParams(vmem_limit_bytes=LIMIT),
    )(order, scalars, state, part, wl, *blocks)


def shift_from(block, distance):
    n = lax.axis_size("lon")
    return lax.ppermute(block, "lon", [((i + distance) % n, i) for i in range(n)])


class Summation:
    def __init__(self):
        n_lon, n_batch = lax.axis_size("lon"), lax.axis_size("batch")
        self.n = n = n_lon * n_batch
        me = lax.axis_index("lon") * n_batch + lax.axis_index("batch")
        bits = [1 << i for i in range(1, n.bit_length() - 1)]
        lon = bits.pop()
        near, far = bits[:1], bits[1:]
        self.pairs = list(zip(near + [lon] + far, [lon] + far[:1] + near + far[1:]))
        self.core = me & 1
        self.bits = [self.core] + self.bits_of(me)
        places = [self.place(self.bits[1:-1]), self.place(self.bits_of(me ^ 1)[:-1])]
        self.order = jnp.stack([jnp.stack([self.core, 1 - self.core]), jnp.stack(places)])

    def bits_of(self, device):
        return [
            (jnp.bitwise_and(device, jnp.where(device & 1 == 0, a, b)) != 0).astype(jnp.int32)
            for a, b in self.pairs
        ]

    def place(self, bits):
        at = jnp.zeros((), jnp.int32)
        for bit in bits:
            at = 2 * at + bit
        return at

    def swap(self, block, step):
        pair = self.pairs[step - 1] if step else (1, 1)
        return lax.ppermute(
            block, ("lon", "batch"), [(i, i ^ pair[i & 1]) for i in range(self.n)]
        )

    def begin(self, keep, send):
        return self.add(keep, self.swap(send, 0))

    def add(self, a, b):
        return (a.astype(f32) + b.astype(f32)).astype(bf16)

    def end(self, total):
        last = len(self.bits) - 1
        total = jnp.pad(total, ((0, -total.shape[0] % (4 * self.n)), (0, 0)))
        for step in range(1, last):
            size = total.shape[0] // 2
            keep = lax.dynamic_slice_in_dim(total, self.bits[step] * size, size, 0)
            send = lax.dynamic_slice_in_dim(total, (1 - self.bits[step]) * size, size, 0)
            total = self.add(keep, self.swap(send, step))
        total = self.add(total, self.swap(total, last))
        for step in range(last - 1, 0, -1):
            total = jnp.concatenate([total, self.swap(total, step)])
        return total, self.swap(total, 0)


def body(
    state,
    noise,
    samples,
    step,
    kl_weight,
    floor,
    latent_weight,
    state_weight,
    noise_weight,
    attention_gain,
    query_key_value,
    offset_bias,
    output_weight,
    feedforward_gain,
    up_weight,
    down_weight,
    cotangent,
):
    items, height, breadth, width = state.shape
    cells = items * height * breadth * lax.axis_size("lon") * lax.axis_size("batch")
    cell_w = (latent_weight.T, state_weight, noise_weight)
    cot_h, state_h, noise_h, kl, bias = prep(
        samples, cotangent, state, noise, cell_w[0], offset_bias.reshape(2 * HEADS, -1)
    )
    block_w = (
        attention_gain,
        query_key_value,
        bias,
        output_weight,
        feedforward_gain,
        up_weight,
        down_weight,
    )
    add_up = Summation()
    beta = kl_weight * (step + 1).astype(f32) / WARM
    scalars = jnp.stack([beta, floor])
    *ahead, halo = first(state_h, noise_h, cot_h, cell_w, block_w)
    numbers = jnp.stack([samples[0], add_up.core])
    halo, order, scalars, numbers = lax.optimization_barrier((halo, add_up.order, scalars, numbers))
    halo = shift_from(halo, 1)
    h1, *saved = first(state_h, noise_h, cot_h, cell_w, block_w, ahead)
    *ahead, halo = second(numbers, h1, cot_h, block_w, halo=halo)
    halo = shift_from(halo, -1)
    act, dh, small1, bias1, *grads1 = second(numbers, h1, cot_h, block_w, before=ahead)
    part, *grads0 = third(
        numbers, state_h, noise_h, dh, halo, small1, bias1, kl, cell_w, block_w, saved
    )
    activations = place(act, halo)
    sum1 = add_up.begin(*grads1)
    sum0 = add_up.begin(*grads0)
    sum1, activations = lax.optimization_barrier((sum1, activations))
    blocks = add_up.end(sum1) + add_up.end(sum0)
    state_gradient, divergence, *weights = finish(
        order, scalars, state, part, cell_w[0], *blocks, cells=cells, devices=add_up.n
    )
    return (activations, divergence.reshape(()), state_gradient, weights[0].T, *weights[1:])


def solution(mesh):
    return jax.shard_map(
        body,
        mesh=mesh,
        in_specs=(
            P("batch", None, "lon", None),
            P("batch", None, None, "lon", None),
            P("batch"),
            P(),
            P(),
            P(),
            P(),
            P(),
            P(),
            P(),
            P(),
            P(),
            P(),
            P(),
            P(),
            P(),
            P("batch", None, None, "lon", None),
        ),
        out_specs=(
            P("batch", None, None, "lon", None),
            P(),
            P("batch", None, "lon", None),
            P(),
            P(),
            P(),
            P(),
            P(),
            P(),
            P(),
            P(),
            P(),
            P(),
        ),
        check_vma=False,
    )
```

```python
import functools

import jax
import jax.numpy as jnp
from jax import lax
from jax.experimental import pallas as pl
from jax.experimental.pallas import tpu as pltpu
from jax.sharding import PartitionSpec as P

HEADS = 8
HD = 32
WIN = 8
WARM = 1000
SLOTS = 4
D = 256
FF = 1024
ZC = 32
HALF = WIN // 2 * WIN

eps_norm = 1e-05
sharpness = 8.0
spread_bound = 4.0
LOG2E = 1.4426950408889634
f32 = jnp.float32
bf16 = jnp.bfloat16


def mm(a, b):
    return lax.dot_general(a, b, (((1,), (0,)), ((), ())), preferred_element_type=f32)


def mm_nt(a, b):
    return lax.dot_general(a, b, (((1,), (1,)), ((), ())), preferred_element_type=f32)


def mm_tn(a, b):
    return lax.dot_general(a, b, (((0,), (0,)), ((), ())), preferred_element_type=f32)


def low_sublanes(shape):
    return lax.broadcasted_iota(jnp.int32, shape, len(shape) - 2) < 4


def to_halves(x):
    rows, cols, ch = x.shape
    n = cols // 8
    v = x.reshape(4, 2, n, 8, ch)
    a, b = v[:, 0], v[:, 1]
    low = low_sublanes(a.shape)
    first = jnp.where(low, a, pltpu.roll(b, 4, 2))
    second = jnp.where(low, pltpu.roll(a, 4, 2), b)
    first = first.transpose(1, 0, 2, 3)
    second = second.transpose(1, 0, 2, 3)
    return jnp.stack([first, second], axis=1).reshape(2 * n, HALF, ch)


def from_halves(x):
    n = x.shape[0] // 2
    ch = x.shape[-1]
    v = x.reshape(n, 2, 4, 8, ch)
    first, second = v[:, 0].transpose(1, 0, 2, 3), v[:, 1].transpose(1, 0, 2, 3)
    low = low_sublanes(first.shape)
    a = jnp.where(low, first, pltpu.roll(second, 4, 2))
    b = jnp.where(low, pltpu.roll(first, 4, 2), second)
    return jnp.stack([a, b], axis=1).reshape(8, 8 * n, ch)


def tile_of(first, second):
    return jnp.stack([first, second], axis=1).reshape(-1, first.shape[-1])


def halves_of(tile):
    v = tile.reshape(-1, 2, HALF, tile.shape[-1])
    return v[:, 0], v[:, 1]


def norm(x):
    c = x - jnp.mean(x, axis=-1, keepdims=True)
    r = lax.rsqrt(jnp.mean(c * c, axis=-1, keepdims=True) + eps_norm)
    return c * r, r


def norm_back(dy, xhat, r, gain):
    along = dy * gain
    inward = r * (
        along
        - jnp.mean(along, axis=-1, keepdims=True)
        - xhat * jnp.mean(along * xhat, axis=-1, keepdims=True)
    )
    return inward, jnp.sum((dy * xhat).reshape(-1, 8, D), axis=0)


ERF = (0.7978697122393114, 0.036392286377165226, -8.78266605765619e-05,
       -3.669342209361701e-05, 1.425004260912749e-06)


def gelu_parts(x):
    square = x * x
    p = ERF[-1]
    for c in ERF[-2::-1]:
        p = p * square + c
    erf = jnp.tanh(x * p)
    half = 0.5 * x
    density = jnp.exp2(square * (-0.5 * LOG2E))
    return half + half * erf, 0.5 + 0.5 * erf + x * density * 0.3989422804014327


def lane_masks():
    lane = lax.broadcasted_iota(jnp.int32, (1, 128), 1)
    return [(lane >= 32 * j) & (lane < 32 * j + 32) for j in range(4)]


def spread_heads(x, masks):
    return jnp.concatenate([x * m for m in masks], axis=0)


def gather_heads(x, masks):
    v = x.reshape(4, 64, 128)
    return jnp.where(masks[0], v[0], jnp.where(masks[1], v[1], jnp.where(masks[2], v[2], v[3])))


def pieces(rows):
    return [slice(r, r + 64) for r in range(0, rows, 64)]


def staged(count, *stages, beside):
    for n in range(count + len(stages) - 1):
        for work in beside.get(n, ()):
            work()
        for late, stage in enumerate(stages):
            if 0 <= n - late < count:
                stage(n - late)


def unit_of(n):
    g = n % 2
    rows = slice(64 * (n // 2), 64 * (n // 2) + 64)
    return rows, lambda part: slice(256 * part + 128 * g, 256 * part + 128 * g + 128), g


def attention(w, beside):
    sel = lane_masks()
    ones = [m.astype(f32).astype(bf16) for m in sel]
    scale = HD ** (-0.5) * LOG2E

    def scores(n):
        rows, lanes, g = unit_of(n)
        q, k = w["packed"][rows, lanes(0)], w["packed"][rows, lanes(1)]
        w["s"][n % 4] = mm_nt(k, spread_heads(q, ones))

    def softmax(n):
        s = w["s"][n % 4] * scale + w["bias"][n % 2]
        s = jnp.exp2(s - jnp.max(s, axis=0, keepdims=True))
        w["p"][n] = (s * (1.0 / jnp.sum(s, axis=0, keepdims=True))).astype(bf16)

    def values(n):
        rows, lanes, g = unit_of(n)
        found = gather_heads(mm_tn(w["p"][n], w["packed"][rows, lanes(2)]), sel)
        w["ctx"][rows, lanes(0)] = found.astype(bf16)

    staged(w["p"].shape[0], scores, softmax, values, beside=beside)


def attention_back(w, beside):
    sel = lane_masks()
    ones = [m.astype(f32).astype(bf16) for m in sel]
    scale = HD ** (-0.5)

    def upstream(n):
        rows, lanes, g = unit_of(n)
        spread = spread_heads(w["dctx"][rows, lanes(0)], ones)
        w["gp"][rows, lanes(2)] = mm(w["p"][n], spread).astype(bf16)
        w["s"][n % 4] = mm_nt(w["packed"][rows, lanes(2)], spread)

    def inward(n):
        p = w["p"][n].astype(f32)
        t = p * w["s"][n % 4]
        ds = t - p * jnp.sum(t, axis=0, keepdims=True)
        w["d_bias"][n % 2] += ds
        w["ds"][n % 4] = ds.astype(bf16)

    def outer(n):
        rows, lanes, g = unit_of(n)
        ds = w["ds"][n % 4]
        q, k = w["packed"][rows, lanes(0)], w["packed"][rows, lanes(1)]
        w["gp"][rows, lanes(1)] = (mm(ds, spread_heads(q, ones)) * scale).astype(bf16)
        w["gp"][rows, lanes(0)] = (gather_heads(mm_tn(ds, k), sel) * scale).astype(bf16)

    staged(w["p"].shape[0], upstream, inward, outer, beside=beside)


def halves(rows):
    return slice(0, rows // 2), slice(rows // 2, rows)


def pieces_of(half):
    return [slice(r, r + 64) for r in range(half.start, half.stop, 64)]


def attend(x_ref, w):
    rows = x_ref.shape[0]
    gain1, gain2 = w["gain1"][...], w["gain2"][...]
    scales = {}

    def project(half):
        for at in pieces_of(half):
            w["normed"][at] = (norm(x_ref[at])[0] * gain1).astype(bf16)
        w["packed"][half] = mm(w["normed"][half], w["qkv"][...]).astype(bf16)

    def join(half):
        w["mixed"][half] = x_ref[half] + mm(w["ctx"][half], w["out"][...])
        for at in pieces_of(half):
            xhat, scales[at.start] = norm(w["mixed"][at])
            w["xhat"][at] = xhat
            w["normed2"][at] = (xhat * gain2).astype(bf16)

    one, two = halves(rows)
    units = rows // 64
    project(one)
    beside = {2: [functools.partial(project, two)], units + 3: [functools.partial(join, one)]}
    attention(w, beside)
    join(two)
    return scales


def block_forward(x_ref, w):
    attend(x_ref, w)
    rows = x_ref.shape[0]

    def start(c):
        w["a"][c % 2] = mm(w["normed2"][...], w["up"][:, 256 * c : 256 * c + 256])

    start(0)
    for c in range(FF // 256):
        cols = slice(256 * c, 256 * c + 256)
        if c < FF // 256 - 1:
            start(c + 1)
        for at in pieces(rows):
            active, slope = gelu_parts(w["a"][c % 2, at])
            w["active"][at, cols] = active.astype(bf16)
            w["slope"][at, cols] = slope.astype(bf16)
        before = w["mixed"] if c == 0 else w["xhat"]
        w["xhat"][...] = before[...] + mm(w["active"][:, cols], w["down"][cols, :])


def block_backward(x_ref, g_ref, w, fused, round_dn):
    rows = x_ref.shape[0]
    gain1, gain2 = w["gain1"][...], w["gain2"][...]
    if fused:
        scales = attend(x_ref, w)
    normed2_t = w["normed2"][...].T
    gb = g_ref[...].astype(bf16)
    gb_t = gb.T

    def start(c):
        cols = slice(256 * c, 256 * c + 256)
        if fused:
            w["a"][c % 2] = mm(w["normed2"][...], w["up"][:, cols])
        w["b"][c % 2] = mm_nt(gb, w["down"][cols, :])

    start(0)
    for c in range(FF // 256):
        cols = slice(256 * c, 256 * c + 256)
        if c < FF // 256 - 1:
            start(c + 1)
        for at in pieces(rows):
            if fused:
                active, slope = gelu_parts(w["a"][c % 2, at])
                w["active"][at, cols] = active.astype(bf16)
            else:
                slope = w["slope"][at, cols].astype(f32)
            w["d_inner"][at, cols] = (w["b"][c % 2, at] * slope).astype(bf16)
        part = mm_nt(w["d_inner"][:, cols], w["up"][:, cols])
        w["dn"][...] = part if c == 0 else w["dn"][...] + part
        w["d_ff"][1024 + 256 * c : 1280 + 256 * c, :] += mm(gb_t, w["active"][:, cols])
        w["d_ff"][cols, :] += mm(normed2_t, w["d_inner"][:, cols])
        if fused:
            w["mixed"][...] += mm(w["active"][:, cols], w["down"][cols, :])

    def into_heads(half):
        dgain = None
        for at in pieces_of(half):
            xhat, r = (w["xhat"][at], scales[at.start]) if fused else norm(w["mixed"][at])
            inward, part = norm_back(w["dn"][at], xhat, r, gain2)
            dgain = part if dgain is None else dgain + part
            d_mixed = g_ref[at] + inward
            g_ref[at] = d_mixed
            w["g_out"][at] = d_mixed.astype(bf16)
        w["d_small"][8:16, :] += dgain
        w["dctx"][half] = mm_nt(w["g_out"][half], w["out"][...]).astype(bf16)

    def d_out():
        w["d_at"][768:1024, :] += mm_tn(w["ctx"][...], w["g_out"][...])

    def out_of_heads(half):
        gp = w["gp"][half]
        w["dn"][half] = mm_nt(gp, w["qkv"][...])
        normed_t = w["normed"][half].T
        for c in range(3):
            cols = slice(256 * c, 256 * c + 256)
            w["d_at"][cols, :] += mm(normed_t, gp[:, cols])
        dgain = None
        for at in pieces_of(half):
            dn = w["dn"][at]
            if round_dn:
                dn = dn.astype(bf16).astype(f32)
            xhat, r = norm(x_ref[at])
            inward, part = norm_back(dn, xhat, r, gain1)
            dgain = part if dgain is None else dgain + part
            g_ref[at] = g_ref[at] + inward
        w["d_small"][0:8, :] += dgain

    one, two = halves(rows)
    units = rows // 64
    into_heads(one)
    beside = {
        2: [functools.partial(into_heads, two)],
        units: [d_out],
        units + 3: [functools.partial(out_of_heads, one)],
    }
    attention_back(w, beside)
    out_of_heads(two)


LIMIT = 56 * 1024 * 1024


def cost(us):
    return pl.CostEstimate(flops=int(us * 1.1e9), bytes_accessed=int(us * 3.6e6), transcendentals=0)


ANY = pl.BlockSpec(memory_space=pl.ANY)


def params(n):
    return pltpu.CompilerParams(
        dimension_semantics=("arbitrary",) * n, vmem_limit_bytes=LIMIT
    )


def latent_head(state, wl):
    center = mm_nt(state, wl[:ZC])
    squash = jnp.tanh(mm_nt(state, wl[ZC:]) * (1.0 / spread_bound))
    return center, squash, jnp.exp((0.5 * spread_bound) * squash)


def lanes_of_patch(width, back):
    lane = lax.broadcasted_iota(jnp.int32, (4 * 256, 4 * 64), 0)
    at = lax.broadcasted_iota(jnp.int32, (4 * 256, 4 * 64), 1)
    row, col = query_place(at & 63)
    want = 16 * (7 - row) + 7 - col if back else 16 * row + col
    return jnp.where(lane == (at >> 6) * 256 + want, 1.0, 0.0).astype(bf16)


def query_place(q):
    return (q >> 2) & 7, ((q >> 5) << 2) + (q & 3)


def table_lanes(back):
    a = lax.broadcasted_iota(jnp.int32, (256, 256), 0)
    b = lax.broadcasted_iota(jnp.int32, (256, 256), 1)
    side = 2 * WIN - 1
    if back:
        mirrored = 16 * (14 - (a >> 4)) + 14 - (a & 15)
        hit = ((a & 15) < side) & ((a >> 4) < side) & (b == (14 - (a >> 4)) * side + 14 - (a & 15))
    else:
        hit = ((b & 15) < side) & ((b >> 4) < side) & (a == (b >> 4) * side + (b & 15))
    return jnp.where(hit, 1.0, 0.0).astype(bf16)


def exactly(a, onehot):
    total = None
    for _ in range(3):
        term = a.astype(bf16)
        a = a - term.astype(f32)
        part = mm(term, onehot)
        total = part if total is None else total + part
    return total


def expand_bias(tables):
    spread = exactly(tables, table_lanes(False))
    choose = lanes_of_patch(64, False)
    out = []
    for n in range(4):
        heads = []
        for h in range(4 * n, 4 * n + 4):
            one = jnp.broadcast_to(spread[h : h + 1], (8, 256))
            heads.append(
                jnp.concatenate(
                    [
                        pltpu.roll(one, (16 * r + 137) % 256, 1, stride=1, stride_axis=0)
                        for r in range(WIN)
                    ]
                )
            )
        rows = exactly(jnp.concatenate(heads, axis=1), choose)
        out.append(to_halves(rows.reshape(WIN, WIN, 256)).reshape(64, 256))
    return out


def reduce_bias(grads):
    rows = from_halves(grads.reshape(2, HALF, 256)).reshape(64, 256).astype(bf16)
    lanes = lax.dot_general(
        rows, lanes_of_patch(64, True), (((1,), (1,)), ((), ())), preferred_element_type=f32
    )
    out = []
    for h in range(4):
        total = None
        for r in range(WIN):
            one = pltpu.roll(
                lanes[8 * r : 8 * r + 8, 256 * h : 256 * h + 256], 16 * r, 1, stride=1, stride_axis=0
            )
            total = one if total is None else total + one
        out.append(jnp.sum(total, axis=0, keepdims=True))
    return jnp.concatenate(out)


def prep_kernel(samples, cot, state, wl, tables, cot_h, state_h, kl, bias):
    @pl.when(pl.program_id(0) == 0)
    def _():
        padded = jnp.concatenate(
            [tables[...], jnp.zeros((16, 256 - tables.shape[1]), f32)], axis=1
        )
        for n, part in enumerate(expand_bias(padded * LOG2E)):
            bias[n // 2, n % 2] = part

    live = samples[0]
    for s in range(SLOTS):
        factor = jnp.where(s < live, 1.0, 0.0).astype(f32)
        cot_h[:, s] = (to_halves(cot[0, s].astype(f32)) * factor).astype(bf16)
    st = to_halves(state[0].astype(f32)).reshape(4, 64, D).astype(bf16)
    state_h[:, 0] = st
    center, squash, sigma = latent_head(st.reshape(4 * 64, D), wl[...])
    terms = 0.5 * (center * center + sigma * sigma - 1.0 - spread_bound * squash)

    @pl.when(pl.program_id(0) == 0)
    def _():
        kl[...] = jnp.zeros(kl.shape, f32)

    kl[:, :ZC] += jnp.sum(terms.reshape(-1, 8, ZC), axis=0)


def prep(samples, cot, state, wl, tables):
    bands = state.shape[1] // WIN
    nw = state.shape[2] // WIN
    return pl.pallas_call(
        prep_kernel,
        grid=(bands,),
        in_specs=[
            pl.BlockSpec(memory_space=pltpu.SMEM),
            pl.BlockSpec((1, SLOTS, WIN, nw * WIN, D), lambda i: (0, 0, i, 0, 0)),
            pl.BlockSpec((1, WIN, nw * WIN, D), lambda i: (0, i, 0, 0)),
            full(wl),
            full(tables),
        ],
        out_specs=[
            pl.BlockSpec((2 * nw, SLOTS, HALF, D), lambda i: (0, i, 0, 0)),
            pl.BlockSpec((nw, 1, 64, D), lambda i: (0, i, 0, 0)),
            pl.BlockSpec((8, D), lambda i: (0, 0)),
            pl.BlockSpec((2, 2, 64, 256), lambda i: (0, 0, 0, 0)),
        ],
        out_shape=[
            jax.ShapeDtypeStruct((2 * nw, bands * SLOTS, HALF, D), bf16),
            jax.ShapeDtypeStruct((nw, bands, 64, D), bf16),
            jax.ShapeDtypeStruct((8, D), f32),
            jax.ShapeDtypeStruct((2, 2, 64, 256), f32),
        ],
        compiler_params=params(1),
        cost_estimate=cost(4),
    )(samples, cot, state, wl, tables)


def noise_of(block):
    bands = block.shape[1] // WIN
    return jnp.stack(
        [
            jnp.stack(
                [to_halves(block[s, WIN * b : WIN * b + WIN]).reshape(64, ZC) for s in range(SLOTS)]
            )
            for b in range(bands)
        ]
    )


def noise_spec(bands, skip):
    return pl.BlockSpec((1, SLOTS, bands * WIN, WIN, ZC), lambda j: (0, 0, 0, j + skip, 0))


def cell_forward(state, noise, wl, ws, wn):
    bands = state.shape[0]
    flat = state.reshape(bands * 64, D)
    over = lambda x: x.reshape(bands, 1, 64, x.shape[-1])
    center, squash, sigma = latent_head(flat, wl)
    latent = (over(center) + over(sigma) * noise).reshape(-1, ZC).astype(bf16)
    mix = mm(latent, wn)
    half = 0.5 * (over(mm(flat, ws)) + mix[:, :D].reshape(bands, SLOTS, 64, D))
    gate = 0.5 + 0.5 * jnp.tanh(half)
    cand = jnp.tanh(mix[:, D:].reshape(bands, SLOTS, 64, D))
    hidden = gate * over(flat.astype(f32)) + (1.0 - gate) * cand
    return hidden.reshape(-1, D), center, squash, sigma, latent, gate, cand


def full(a):
    return pl.BlockSpec(a.shape, lambda *_: (0,) * a.ndim)


def block_specs(k):
    return [
        pl.BlockSpec((2, D), lambda *_: (0, 0)),
        pl.BlockSpec((1, D, 3 * D), lambda *_: (k, 0, 0)),
        pl.BlockSpec((1, 2, 64, 256), lambda *_: (k, 0, 0, 0)),
        pl.BlockSpec((1, D, D), lambda *_: (k, 0, 0)),
        pl.BlockSpec((2, D), lambda *_: (0, 0)),
        pl.BlockSpec((1, D, FF), lambda *_: (k, 0, 0)),
        pl.BlockSpec((1, FF, D), lambda *_: (k, 0, 0)),
    ]


NAMES = ("gain1", "qkv", "bias", "out", "gain2", "up", "down")


def named(refs, k):
    return {
        n: r.at[k : k + 1] if n.startswith("gain") else r.at[0] for n, r in zip(NAMES, refs)
    }


def saved_refs(rows):
    return [
        ("normed", (rows, D), bf16),
        ("packed", (rows, 3 * D), bf16),
        ("p", (rows // 32, 64, 256), bf16),
        ("ctx", (rows, D), bf16),
        ("mixed", (rows, D), f32),
        ("normed2", (rows, D), bf16),
        ("active", (rows, FF), bf16),
        ("slope", (rows, FF), bf16),
    ]


def forward_refs(rows):
    return [
        ("x", (rows, D), f32),
        ("s", (4, 64, 256), f32),
        ("xhat", (rows, D), f32),
        ("a", (2, rows, 256), f32),
    ]


def backward_refs(rows):
    return [
        ("x", (rows, D), f32),
        ("g", (rows, D), f32),
        ("s", (4, 64, 256), f32),
        ("b", (2, rows, 256), f32),
        ("d_inner", (rows, FF), bf16),
        ("dn", (rows, D), f32),
        ("g_out", (rows, D), bf16),
        ("dctx", (rows, D), bf16),
        ("ds", (4, 64, 256), bf16),
        ("gp", (rows, 3 * D), bf16),
    ]


def both_refs(rows):
    return saved_refs(rows) + forward_refs(rows)[2:] + backward_refs(rows)


def scratch(refs):
    return [pltpu.VMEM(shape, dtype) for _, shape, dtype in refs]


def names(refs):
    return [name for name, _, _ in refs]


def saved_specs(rows, skip):
    return [
        pl.BlockSpec((1,) + shape, lambda j, n=len(shape): (j + skip,) + (0,) * n)
        for _, shape, _ in saved_refs(rows)
    ]


N_SAVED, N_BACK, N_BOTH = len(saved_refs(64)), len(backward_refs(64)), len(both_refs(64))


GRAD_SHAPES = [(2048, D), (1024, D), (16, D), (2, 64, 256)]
GRAD_NAMES = ("d_ff", "d_at", "d_small", "d_bias")
GRAD_SCRATCH = [pltpu.VMEM(s, f32) for s in GRAD_SHAPES[:2]]
SMALL_SPECS = [pl.BlockSpec(s, lambda *_, n=len(s): (0,) * n) for s in GRAD_SHAPES[2:]]
SMALL_OUTS = [jax.ShapeDtypeStruct(s, f32) for s in GRAD_SHAPES[2:]]

ROWS_BLOCK = 3072
ROWS_CELL = 512
CHAINS = (((0, (ROWS_BLOCK + ROWS_CELL) // 2),), ((0, ROWS_BLOCK // 2),))
ALL_CHAINS = [(k, chain) for k in range(2) for chain in CHAINS[k]]


def first_kernel(state, noise, cot, wl, ws, wn, *rest, lead):
    w = named(rest[:7], 0)
    rest = rest[7:] if lead else rest[7 + 1 + N_SAVED :]
    h1, rest = rest[0], rest[1:]
    w.update((n, r.at[0]) for n, r in zip(names(saved_refs(64)), rest))
    rest = rest[N_SAVED:]
    if lead:
        halo, rest = rest[0], rest[1:]
    w.update(zip(names(forward_refs(64)), rest))
    w["x"][...] = cell_forward(state[0], noise_of(noise[0]), wl[...], ws[...], wn[...])[0]
    block_forward(w["x"], w)
    a, b = halves_of(w["xhat"][...])
    h1[0, 0] = a
    h1[0, 1] = b
    if lead:
        halo[0] = a.astype(bf16)
        halo[1] = cot[0]


def first(state_h, noise, cot_h, cell_w, block_w, before=None):
    nw, bands = state_h.shape[:2]
    half = (bands * SLOTS, HALF, D)
    rows = 64 * bands * SLOTS
    lead = before is None
    skip = 0 if lead else 1
    specs = [pl.BlockSpec((1, 2) + half, lambda j: (j + skip, 0, 0, 0, 0))] + saved_specs(rows, skip)
    shapes = [jax.ShapeDtypeStruct((nw, 2) + half, f32)] + [
        jax.ShapeDtypeStruct((nw,) + shape, dtype) for _, shape, dtype in saved_refs(rows)
    ]
    inputs = [state_h, noise, cot_h, *cell_w, *block_w]
    in_specs = [
        pl.BlockSpec((1, bands, 64, D), lambda j: (j + skip, 0, 0, 0)),
        noise_spec(bands, skip),
        pl.BlockSpec((1,) + half, lambda j: (0, 0, 0, 0)),
    ]
    in_specs += [full(a) for a in cell_w] + block_specs(0)
    aliases = {}
    if lead:
        specs.append(pl.BlockSpec((2,) + half, lambda j: (0, 0, 0, 0)))
        shapes.append(jax.ShapeDtypeStruct((2,) + half, bf16))
    else:
        aliases = {len(inputs) + n: n for n in range(len(before))}
        inputs += before
        in_specs += [pl.BlockSpec(memory_space=pl.ANY)] * len(before)
    return pl.pallas_call(
        functools.partial(first_kernel, lead=lead),
        grid=(1 if lead else nw - 1,),
        in_specs=in_specs,
        out_specs=specs,
        out_shape=shapes,
        input_output_aliases=aliases,
        scratch_shapes=scratch(forward_refs(rows)),
        compiler_params=params(1),
        cost_estimate=cost(6 if lead else 16),
    )(*inputs)


def zero_at_start(refs):
    @pl.when(pl.program_id(0) == 0)
    def _():
        for r in refs:
            r[...] = jnp.zeros(r.shape, r.dtype)


def halves_out(keep, send, parts):
    size = keep.shape[0]
    core = lax.axis_index("batch") & 1

    def write(low, high):
        first = 0
        for ref in parts:
            rows = ref.shape[0]
            cut = min(max(size - first, 0), rows)
            if cut:
                low[first : first + cut] = ref[:cut].astype(bf16)
            if cut < rows:
                high[first + cut - size : first + rows - size] = ref[cut:rows].astype(bf16)
            first += rows

    @pl.when(core == 0)
    def _():
        write(keep, send)

    @pl.when(core != 0)
    def _():
        write(send, keep)


def at_end():
    return pl.program_id(0) == pl.num_programs(0) - 1


def second_kernel(samples, ha, hb, ca, cb, *rest, lead):
    w = named(rest[:7], 1)
    grads1, small1, bias1 = (None,) * 3 if lead else rest[7:10]
    rest = rest[7:] if lead else rest[12:]
    act, dh, d_small, d_bias = rest[:4]
    if lead:
        packed_grads, back_halo = rest[4:6]
    else:
        keep, send = rest[4:6]
    rest = rest[6:]
    w.update(zip(names(both_refs(64)), rest))
    grads = rest[N_BOTH : N_BOTH + 2] + (d_small, d_bias)
    w.update(zip(GRAD_NAMES, grads))
    if lead:
        zero_at_start(grads)
    else:

        @pl.when(pl.program_id(0) == 0)
        def _():
            grads[0][...] = grads1[:2048].astype(f32)
            grads[1][...] = grads1[2048:].astype(f32)
            d_small[...] = small1[...]
            d_bias[...] = bias1[...]

    w["x"][...] = tile_of(ha[0, 0], hb[0].astype(f32) if lead else hb[0, 0])
    w["g"][...] = tile_of(ca[0].astype(f32), cb[0].astype(f32))
    block_backward(w["x"], w["g"], w, True, True)
    live = samples[0]
    a, b = halves_of(w["mixed"][...])
    factor = jnp.concatenate(
        [jnp.where(s % SLOTS < live, 1.0, 0.0) * jnp.ones((1, 1, D), f32) for s in range(a.shape[0])]
    )
    a, b = (a * factor).astype(bf16), (b * factor).astype(bf16)
    da, db = halves_of(w["g"][...])
    act[0, 0] = a
    act[0, 1] = b
    dh[0, 0] = da
    dh[0, 1] = db
    if lead:
        back_halo[0] = db.astype(bf16)
        back_halo[1] = b
        packed_grads[:2048] = grads[0][...].astype(bf16)
        packed_grads[2048:] = grads[1][...].astype(bf16)
    else:

        @pl.when(at_end())
        def _():
            halves_out(keep, send, [grads[0], grads[1]])


def second(samples, h1, cot_h, block_w, halo=None, before=None):
    nw = h1.shape[0]
    half = h1.shape[2:]
    lead = before is None
    if lead:
        tile, other = (lambda j: nw - 1), halo
        wide = [pl.BlockSpec((1,) + half, lambda j, n=n: (n, 0, 0, 0)) for n in range(2)]
    else:
        tile, other = (lambda j: j), cot_h
        wide = [
            pl.BlockSpec((1, 1) + half, lambda j: (j + 1, 0, 0, 0, 0)),
            pl.BlockSpec((1,) + half, lambda j: (2 * j + 2, 0, 0, 0)),
        ]
    inputs = [samples, h1, halo if lead else h1, cot_h, other, *block_w]
    in_specs = [
        pl.BlockSpec(memory_space=pltpu.SMEM),
        pl.BlockSpec((1, 1) + half, lambda j: (tile(j), 1, 0, 0, 0)),
        wide[0],
        pl.BlockSpec((1,) + half, lambda j: (2 * tile(j) + 1, 0, 0, 0)),
        wide[1],
    ]
    in_specs += block_specs(1)
    out_specs = [
        pl.BlockSpec((1, 2) + half, lambda j: (tile(j), 0, 0, 0, 0)),
        pl.BlockSpec((1, 2) + half, lambda j: (tile(j), 0, 0, 0, 0)),
    ] + SMALL_SPECS
    out_shape = [
        jax.ShapeDtypeStruct((nw, 2) + half, bf16),
        jax.ShapeDtypeStruct((nw, 2) + half, f32),
    ] + SMALL_OUTS
    aliases = {}
    if lead:
        out_specs.append(pl.BlockSpec((ROWS_BLOCK, D), lambda *_: (0, 0)))
        out_specs.append(pl.BlockSpec((2,) + half, lambda j: (0, 0, 0, 0)))
        out_shape.append(jax.ShapeDtypeStruct((ROWS_BLOCK, D), bf16))
        out_shape.append(jax.ShapeDtypeStruct((2,) + half, bf16))
    else:
        out_specs += [pl.BlockSpec((ROWS_BLOCK // 2, D), lambda *_: (0, 0))] * 2
        out_shape += [jax.ShapeDtypeStruct((ROWS_BLOCK // 2, D), bf16)] * 2
        act, dh, small1, bias1, grads1 = before
        sums = [grads1, small1, bias1]
        aliases = {len(inputs) + 3: 0, len(inputs) + 4: 1}
        inputs += sums + [act, dh]
        in_specs += [full(a) for a in sums] + [pl.BlockSpec(memory_space=pl.ANY)] * 2
    return pl.pallas_call(
        functools.partial(second_kernel, lead=lead),
        grid=(1 if lead else nw - 1,),
        in_specs=in_specs,
        out_specs=out_specs,
        out_shape=out_shape,
        input_output_aliases=aliases,
        scratch_shapes=scratch(both_refs(64 * half[0])) + GRAD_SCRATCH,
        compiler_params=params(1),
        cost_estimate=cost(9 if lead else 24),
    )(*inputs)


CELL_SHAPES = [(D, D), (2 * ZC, D), (2 * ZC, D), (2 * ZC, D)]


def divergence_parts(center, squash, sigma):
    return center.astype(bf16), (
        0.5 * (sigma * sigma - 1.0) * (1.0 - squash * squash)
    ).astype(bf16)


def third_kernel(state, noise, da, db, dhalo, small1, bias1, kl, wl, ws, wn, *rest):
    w = named(rest[:7], 0)
    w.update((n, r.at[0]) for n, r in zip(names(saved_refs(64)), rest[7:]))
    rest = rest[N_SAVED:]
    sg, keep, send = rest[7:10]
    w.update(zip(names(backward_refs(64)), rest[10:]))
    grads = rest[10 + N_BACK : 14 + N_BACK]
    d_ws, d_wn, d_wl, d_kl, d_rest = rest[14 + N_BACK :]
    cell_grads = (d_ws, d_wn, d_wl, d_kl)
    w.update(zip(GRAD_NAMES, grads))
    zero_at_start(grads + cell_grads)
    st = state[0]
    nz = noise_of(noise[0])
    bands = st.shape[0]
    hidden, center, squash, sigma, latent, gate, cand = cell_forward(
        st, nz, wl[...], ws[...], wn[...]
    )
    da_v = jnp.where(pl.program_id(0) == 0, dhalo[0].astype(f32), da[0, 0])
    w["x"][...] = hidden
    w["g"][...] = tile_of(da_v, db[0, 0])
    block_backward(w["x"], w["g"], w, False, False)
    dc = w["g"][...]
    over = lambda x: x.reshape(bands, 1, 64, x.shape[-1])
    flat = st.reshape(bands * 64, D)
    dc = dc.reshape(bands, SLOTS, 64, D)
    rest_gate = 1.0 - gate
    d_pre = dc * (over(flat.astype(f32)) - cand) * gate * rest_gate
    d_cand = dc * rest_gate * (1.0 - cand * cand)
    direct = jnp.sum(dc * gate, axis=1).reshape(-1, D)
    g_gate = jnp.sum(d_pre, axis=1).reshape(-1, D).astype(bf16)
    d_ws[...] += mm_tn(flat, g_gate)
    pre = d_pre.reshape(-1, D).astype(bf16)
    cnd = d_cand.reshape(-1, D).astype(bf16)
    d_wn[:ZC] += mm_tn(latent, pre)
    d_wn[ZC:] += mm_tn(latent, cnd)
    d_lat = mm_nt(pre, wn[:, :D]) + mm_nt(cnd, wn[:, D:])
    d_lat = d_lat.reshape(bands, SLOTS, 64, ZC)
    d_center = jnp.sum(d_lat, axis=1).reshape(-1, ZC)
    d_raw = jnp.sum(d_lat * nz, axis=1).reshape(-1, ZC) * 0.5 * sigma * (1.0 - squash * squash)
    d_center, d_raw = d_center.astype(bf16), d_raw.astype(bf16)
    d_wl[:ZC] += mm_tn(d_center, flat)
    d_wl[ZC:] += mm_tn(d_raw, flat)
    kl_center, kl_raw = divergence_parts(center, squash, sigma)
    d_kl[:ZC] += mm_tn(kl_center, flat)
    d_kl[ZC:] += mm_tn(kl_raw, flat)
    total = direct + mm_nt(g_gate, ws[...])
    total = total + mm(d_center, wl[:ZC]) + mm(d_raw, wl[ZC:])
    for b in range(bands):
        sg[0, WIN * b : WIN * b + WIN] = from_halves(
            total[64 * b : 64 * b + 64].reshape(2, HALF, D)
        )

    @pl.when(at_end())
    def _():
        d_small, d_bias = grads[2:]
        d_rest[:16] = jnp.concatenate(
            [reduce_bias(b) for b in (d_bias[0], d_bias[1], bias1[0], bias1[1])]
        )
        total = lambda x: jnp.sum(x, axis=0, keepdims=True)
        d_rest[16:] = jnp.concatenate(
            [total(d_small[:8]), total(d_small[8:]), total(small1[:8]), total(small1[8:])]
            + [total(kl[...]), jnp.zeros((43, D), f32)]
        )
        halves_out(keep, send, [grads[0], grads[1], *cell_grads, d_rest])


def third(state_h, noise, dh, halo, small1, bias1, kl, cell_w, block_w, saved):
    nw, bands = state_h.shape[:2]
    rows = 64 * bands * SLOTS
    half = dh.shape[2:]
    return pl.pallas_call(
        third_kernel,
        grid=(nw,),
        in_specs=[
            pl.BlockSpec((1, bands, 64, D), lambda j: (j, 0, 0, 0)),
            noise_spec(bands, 0),
            pl.BlockSpec((1, 1) + half, lambda j: (jnp.maximum(j - 1, 0), 1, 0, 0, 0)),
            pl.BlockSpec((1, 1) + half, lambda j: (j, 0, 0, 0, 0)),
            pl.BlockSpec((1,) + half, lambda j: (0, 0, 0, 0)),
        ]
        + [full(a) for a in (small1, bias1, kl)]
        + [full(a) for a in cell_w]
        + block_specs(0)
        + saved_specs(rows, 0),
        out_specs=[pl.BlockSpec((1, bands * WIN, WIN, D), lambda j: (0, 0, j, 0))]
        + [pl.BlockSpec(((ROWS_BLOCK + ROWS_CELL) // 2, D), lambda *_: (0, 0))] * 2,
        out_shape=[jax.ShapeDtypeStruct((1, bands * WIN, nw * WIN, D), f32)]
        + [jax.ShapeDtypeStruct(((ROWS_BLOCK + ROWS_CELL) // 2, D), bf16)] * 2,
        scratch_shapes=scratch(backward_refs(rows))
        + [pltpu.VMEM(s, f32) for s in GRAD_SHAPES + CELL_SHAPES + [(64, D)]],
        compiler_params=params(1),
        cost_estimate=cost(26),
    )(state_h, noise, dh, dh, halo, small1, bias1, kl, *cell_w, *block_w, *saved)


def place_kernel(act, halo, out):
    nw = act.shape[0]
    for s in range(SLOTS):
        halves = [halo[0, s].astype(f32)]
        for j in range(nw):
            halves.append(act[j, 0, s].astype(f32))
            if j < nw - 1:
                halves.append(act[j, 1, s].astype(f32))
        out[0, s] = from_halves(jnp.stack(halves)).astype(bf16)


def place(act, halo):
    nw = act.shape[0]
    bands = act.shape[2] // SLOTS
    return pl.pallas_call(
        place_kernel,
        grid=(bands,),
        in_specs=[
            pl.BlockSpec((nw, 2, SLOTS, HALF, D), lambda i: (0, 0, i, 0, 0)),
            pl.BlockSpec((1, SLOTS, HALF, D), lambda i: (1, i, 0, 0)),
        ],
        out_specs=pl.BlockSpec((1, SLOTS, WIN, nw * WIN, D), lambda i: (0, 0, i, 0, 0)),
        out_shape=jax.ShapeDtypeStruct((1, SLOTS, bands * WIN, nw * WIN, D), bf16),
        compiler_params=params(1),
        cost_estimate=cost(4),
    )(act, halo)


def finish_kernel(
    order, scalars, state, part, wl, *rest, cells, devices,
):
    n_blocks = 2 * len(ALL_CHAINS)
    blocks, rest = rest[:n_blocks], rest[n_blocks:]
    sg, div, o_wl, o_ws, o_wn, o_gain1, o_table, o_gain2, *large = rest[:12]
    sums, held = rest[12 : 12 + len(ALL_CHAINS)], rest[12 + len(ALL_CHAINS) : -6]
    o_qkv, o_out, o_up, o_down = stage = rest[-6:-2]
    in_sems, out_sems = rest[-2:]
    arrive = [pltpu.make_async_copy(b, h, in_sems.at[n]) for n, (b, h) in enumerate(zip(blocks, held))]
    leave = [
        [pltpu.make_async_copy(a.at[k], b.at[k], out_sems.at[4 * k + n]) for n, (a, b) in enumerate(zip(stage, large))]
        for k in range(2)
    ]
    for copy in arrive:
        copy.start()

    def assemble(k):
        for chain, (where, _) in enumerate(ALL_CHAINS):
            if where != k:
                continue
            whole = sums[chain]
            n = devices // 4
            count = whole.shape[0] // (2 * n)
            for at in range(2):
                arrive[2 * chain + at].wait()
                block = held[2 * chain + at]
                for i in range(n):
                    to = order[2 * chain, at] * n + jnp.bitwise_xor(order[2 * chain + 1, at], i)
                    whole[pl.ds(pl.multiple_of(to * count, 16), count)] = block[
                        count * i : count * i + count
                    ]

    def rows_of(k, first, count):
        size = CHAINS[k][-1][1]
        side, first = divmod(first, size)
        for (where, (low, high)), whole in zip(ALL_CHAINS, sums):
            if where == k and low <= first < high:
                first += side * whole.shape[0] // 2 - low
                return whole[first : first + count]

    def unpack(k):
        assemble(k)
        for c in range(3):
            cols = slice(256 * c, 256 * c + 256)
            o_qkv[k, :, cols] = rows_of(k, 2 * FF + 256 * c, 256).astype(f32)
        o_out[k] = rows_of(k, 2816, 256).astype(f32)
        leave[k][0].start()
        leave[k][1].start()
        for c in range(FF // 256):
            cols = slice(256 * c, 256 * c + 256)
            o_up[k, :, cols] = rows_of(k, 256 * c, 256).astype(f32)
        leave[k][2].start()
        for c in range(FF // 256):
            cols = slice(256 * c, 256 * c + 256)
            o_down[k, cols] = rows_of(k, FF + 256 * c, 256).astype(f32).T
        leave[k][3].start()

    unpack(0)
    unpack(1)
    cell_rows = lambda first, count: rows_of(0, ROWS_BLOCK + first, count)
    small = cell_rows(464, 16).astype(f32)
    kl_mean = small[4:5, :ZC] * (1.0 / cells)
    beta, floor = scalars[0], scalars[1]
    excess = sharpness * (kl_mean - floor)
    soft = jnp.maximum(excess, 0.0) + jnp.log(1.0 + jnp.exp(-jnp.abs(excess)))
    div[...] = beta * jnp.mean(floor + soft * (1.0 / sharpness), axis=-1, keepdims=True)
    amt = beta * jax.nn.sigmoid(excess) * (1.0 / (ZC * cells))

    rows = state.shape[1] * state.shape[2]
    center, squash, sigma = latent_head(state[0].reshape(rows, D), wl[...])
    kl_center, kl_raw = divergence_parts(center, squash, sigma)
    g_center = (kl_center.astype(f32) * amt).astype(bf16)
    g_raw = (kl_raw.astype(f32) * amt).astype(bf16)
    add = mm(g_center, wl[:ZC]) + mm(g_raw, wl[ZC:])
    sg[0] = part[0] + add.reshape(state.shape[1:])

    o_ws[...] = cell_rows(0, 256).astype(f32)
    wn = cell_rows(256, 64).astype(f32)
    o_wn[:, :D] = wn[:ZC]
    o_wn[:, D:] = wn[ZC:]
    at = lambda axis: lax.broadcasted_iota(jnp.int32, (ZC, ZC), axis)
    column = jnp.sum(jnp.where(at(0) == at(1), amt, 0.0), axis=1, keepdims=True)
    for h in range(2):
        o_wl[ZC * h : ZC * h + ZC] = (
            cell_rows(320 + ZC * h, ZC).astype(f32) + cell_rows(384 + ZC * h, ZC).astype(f32) * column
        )
    table = mm(cell_rows(448, 16), table_lanes(True))
    o_table[0] = table[:HEADS, : (2 * WIN - 1) ** 2]
    o_table[1] = table[HEADS:, : (2 * WIN - 1) ** 2]
    for k in range(2):
        o_gain1[k : k + 1] = small[2 * k : 2 * k + 1]
        o_gain2[k : k + 1] = small[2 * k + 1 : 2 * k + 2]
    for k in range(2):
        for copy in leave[k]:
            copy.wait()


def finish(order, scalars, state, part, wl, *blocks, cells, devices):
    small = [
        part.shape, (1, 1), (2 * ZC, D), (D, D), (ZC, 2 * D), (2, D),
        (2, HEADS, (2 * WIN - 1) ** 2), (2, D),
    ]
    large = [(2, D, 3 * D), (2, D, D), (2, D, FF), (2, FF, D)]
    smem, vmem = pl.BlockSpec(memory_space=pltpu.SMEM), pl.BlockSpec(memory_space=pltpu.VMEM)
    sg, div, wl, ws, wn, gain1, table, gain2, qkv, out, up, down = pl.pallas_call(
        functools.partial(finish_kernel, cells=cells, devices=devices),
        in_specs=[smem, smem] + [vmem] * 3 + [ANY] * len(blocks),
        out_specs=[vmem] * len(small) + [ANY] * len(large),
        out_shape=[jax.ShapeDtypeStruct(o, f32) for o in small + large],
        scratch_shapes=[pltpu.VMEM((2 * b.shape[0], D), bf16) for b in blocks[::2]]
        + [pltpu.VMEM(b.shape, bf16) for b in blocks]
        + [pltpu.VMEM(o, f32) for o in large]
        + [pltpu.SemaphoreType.DMA((len(blocks),)), pltpu.SemaphoreType.DMA((8,))],
        compiler_params=pltpu.CompilerParams(vmem_limit_bytes=40 * 1024 * 1024),
    )(order, scalars, state, part, wl, *blocks)
    return sg, div, wl, ws, wn, gain1, qkv, table, out, gain2, up, down


def shift_from(block, distance):
    n = lax.axis_size("lon")
    return lax.ppermute(block, "lon", [((i + distance) % n, i) for i in range(n)])


class Summation:
    def __init__(self, turn):
        n_lon, n_batch = lax.axis_size("lon"), lax.axis_size("batch")
        self.n = n = n_lon * n_batch
        me = lax.axis_index("lon") * n_batch + lax.axis_index("batch")
        bits = [1 << i for i in range(1, n.bit_length() - 1)]
        axes, rest = [bits[0], bits[-1]] + bits[1:2], bits[2:-1]
        axes = axes[: len(bits)]
        turned = lambda by: axes[by % len(axes) :] + axes[: by % len(axes)] + rest
        self.pairs = list(zip(turned(turn), turned(turn + 1)))
        self.core = me & 1
        self.bits = [self.core] + self.bits_of(me)
        places = [self.place(self.bits[1:-1]), self.place(self.bits_of(me ^ 1)[:-1])]
        self.order = jnp.stack([jnp.stack([self.core, 1 - self.core]), jnp.stack(places)])

    def bits_of(self, device):
        return [
            (jnp.bitwise_and(device, jnp.where(device & 1 == 0, a, b)) != 0).astype(jnp.int32)
            for a, b in self.pairs
        ]

    def place(self, bits):
        at = jnp.zeros((), jnp.int32)
        for bit in bits:
            at = 2 * at + bit
        return at

    def swap(self, block, step):
        pair = self.pairs[step - 1] if step else (1, 1)
        return lax.ppermute(
            block, ("lon", "batch"), [(i, i ^ pair[i & 1]) for i in range(self.n)]
        )

    def begin(self, keep, send):
        return self.add(keep, self.swap(send, 0))

    def add(self, a, b):
        return (a.astype(f32) + b.astype(f32)).astype(bf16)

    def plan(self):
        last = len(self.bits) - 1
        down, up = range(1, last), range(last - 1, 0, -1)
        return [("halve", n) for n in down] + [("both", last)] + [("double", n) for n in up]

    def pad(self, total):
        return jnp.pad(total, ((0, -total.shape[0] % (4 * self.n)), (0, 0)))

    def half(self, total, at):
        size = total.shape[0] // 2
        return lax.dynamic_slice_in_dim(total, at * size, size, 0)

    def exchange(self, total, kind, step):
        if kind == "halve":
            total = self.half(total, 1 - self.bits[step])
        return self.swap(total, step)

    def join(self, total, got, kind, step):
        if kind == "halve":
            total = self.half(total, self.bits[step])
        return jnp.concatenate([total, got]) if kind == "double" else self.add(total, got)


def in_turn(adders, totals, beside):
    tie = lax.optimization_barrier
    plain = [adder.pad(total) for adder, total in zip(adders, totals)]
    tied = list(plain)
    for n, move in enumerate(adders[0].plan()):
        got = [adder.exchange(total, *move) for adder, total in zip(adders, plain)]
        if n == 0:
            got[0], *beside = tie((got[0], *beside))
        got[0], tied[1] = tie((got[0], tied[1]))
        plain[0] = adders[0].join(tied[0], got[0], *move)
        got[1], tied[0] = tie((got[1], plain[0]))
        plain[1] = tied[1] = adders[1].join(tied[1], got[1], *move)
    blocks = []
    for adder, total in zip(adders, plain):
        blocks += [total, adder.swap(total, 0)]
    return blocks, beside


def body(
    state,
    noise,
    samples,
    step,
    kl_weight,
    floor,
    latent_weight,
    state_weight,
    noise_weight,
    attention_gain,
    query_key_value,
    offset_bias,
    output_weight,
    feedforward_gain,
    up_weight,
    down_weight,
    cotangent,
):
    items, height, breadth, width = state.shape
    cells = items * height * breadth * lax.axis_size("lon") * lax.axis_size("batch")
    cell_w = (latent_weight.T, state_weight, noise_weight)
    cot_h, state_h, kl, bias = prep(
        samples, cotangent, state, cell_w[0], offset_bias.reshape(2 * HEADS, -1)
    )
    block_w = (
        attention_gain,
        query_key_value,
        bias,
        output_weight,
        feedforward_gain,
        up_weight,
        down_weight,
    )
    adders = [Summation(turn) for turn in range(len(ALL_CHAINS))]
    add_up = adders[0]
    order = jnp.concatenate([adder.order for adder in adders])
    beta = kl_weight * (step + 1).astype(f32) / WARM
    scalars = jnp.stack([beta, floor])
    *ahead, halo = first(state_h, noise, cot_h, cell_w, block_w)
    halo = shift_from(halo, 1)
    h1, *saved = first(state_h, noise, cot_h, cell_w, block_w, ahead)
    *ahead, halo = second(samples, h1, cot_h, block_w, halo=halo)
    halo = shift_from(halo, -1)
    act, dh, small1, bias1, *grads1 = second(samples, h1, cot_h, block_w, before=ahead)
    part, *grads0 = third(
        state_h, noise, dh, halo, small1, bias1, kl, cell_w, block_w, saved
    )
    activations = place(act, halo)
    sum1 = add_up.begin(*grads1)
    sum0 = add_up.begin(*grads0)
    sum1, sum0 = lax.optimization_barrier((sum1, sum0))
    blocks, beside = in_turn(adders, (sum0, sum1), (activations, order, scalars))
    activations, order, scalars = beside
    state_gradient, divergence, *weights = finish(
        order, scalars, state, part, cell_w[0], *blocks, cells=cells, devices=add_up.n
    )
    return (activations, divergence.reshape(()), state_gradient, weights[0].T, *weights[1:])


def solution(mesh):
    return jax.shard_map(
        body,
        mesh=mesh,
        in_specs=(
            P("batch", None, "lon", None),
            P("batch", None, None, "lon", None),
            P("batch"),
            P(),
            P(),
            P(),
            P(),
            P(),
            P(),
            P(),
            P(),
            P(),
            P(),
            P(),
            P(),
            P(),
            P("batch", None, None, "lon", None),
        ),
        out_specs=(
            P("batch", None, None, "lon", None),
            P(),
            P("batch", None, "lon", None),
            P(),
            P(),
            P(),
            P(),
            P(),
            P(),
            P(),
            P(),
            P(),
            P(),
        ),
        check_vma=False,
    )
```

```python
import functools

import jax
import jax.numpy as jnp
from jax import lax
from jax.experimental import pallas as pl
from jax.experimental.pallas import tpu as pltpu
from jax.sharding import PartitionSpec as P

HEADS = 8
HD = 32
WIN = 8
WARM = 1000
SLOTS = 4
D = 256
FF = 1024
ZC = 32
HALF = WIN // 2 * WIN

eps_norm = 1e-05
sharpness = 8.0
spread_bound = 4.0
LOG2E = 1.4426950408889634
f32 = jnp.float32
bf16 = jnp.bfloat16


def mm(a, b):
    return lax.dot_general(a, b, (((1,), (0,)), ((), ())), preferred_element_type=f32)


def mm_nt(a, b):
    return lax.dot_general(a, b, (((1,), (1,)), ((), ())), preferred_element_type=f32)


def mm_tn(a, b):
    return lax.dot_general(a, b, (((0,), (0,)), ((), ())), preferred_element_type=f32)


def low_sublanes(shape):
    return lax.broadcasted_iota(jnp.int32, shape, len(shape) - 2) < 4


def to_halves(x):
    rows, cols, ch = x.shape
    n = cols // 8
    v = x.reshape(4, 2, n, 8, ch)
    a, b = v[:, 0], v[:, 1]
    low = low_sublanes(a.shape)
    first = jnp.where(low, a, pltpu.roll(b, 4, 2))
    second = jnp.where(low, pltpu.roll(a, 4, 2), b)
    first = first.transpose(1, 0, 2, 3)
    second = second.transpose(1, 0, 2, 3)
    return jnp.stack([first, second], axis=1).reshape(2 * n, HALF, ch)


def from_halves(x):
    n = x.shape[0] // 2
    ch = x.shape[-1]
    v = x.reshape(n, 2, 4, 8, ch)
    first, second = v[:, 0].transpose(1, 0, 2, 3), v[:, 1].transpose(1, 0, 2, 3)
    low = low_sublanes(first.shape)
    a = jnp.where(low, first, pltpu.roll(second, 4, 2))
    b = jnp.where(low, pltpu.roll(first, 4, 2), second)
    return jnp.stack([a, b], axis=1).reshape(8, 8 * n, ch)


def tile_of(first, second):
    return jnp.stack([first, second], axis=1).reshape(-1, first.shape[-1])


def halves_of(tile):
    v = tile.reshape(-1, 2, HALF, tile.shape[-1])
    return v[:, 0], v[:, 1]


def norm(x):
    c = x - jnp.mean(x, axis=-1, keepdims=True)
    r = lax.rsqrt(jnp.mean(c * c, axis=-1, keepdims=True) + eps_norm)
    return c * r, r


def norm_back(dy, xhat, r, gain):
    along = dy * gain
    inward = r * (
        along
        - jnp.mean(along, axis=-1, keepdims=True)
        - xhat * jnp.mean(along * xhat, axis=-1, keepdims=True)
    )
    return inward, jnp.sum((dy * xhat).reshape(-1, 8, D), axis=0)


ERF = (0.7978697122393114, 0.036392286377165226, -8.78266605765619e-05,
       -3.669342209361701e-05, 1.425004260912749e-06)


def gelu_parts(x):
    square = x * x
    p = ERF[-1]
    for c in ERF[-2::-1]:
        p = p * square + c
    erf = jnp.tanh(x * p)
    half = 0.5 * x
    density = jnp.exp2(square * (-0.5 * LOG2E))
    return half + half * erf, 0.5 + 0.5 * erf + x * density * 0.3989422804014327


def lane_masks():
    lane = lax.broadcasted_iota(jnp.int32, (1, 128), 1)
    return [(lane >= 32 * j) & (lane < 32 * j + 32) for j in range(4)]


def spread_heads(x, masks):
    return jnp.concatenate([x * m for m in masks], axis=0)


def gather_heads(x, masks):
    v = x.reshape(4, 64, 128)
    return jnp.where(masks[0], v[0], jnp.where(masks[1], v[1], jnp.where(masks[2], v[2], v[3])))


def pieces(rows):
    return [slice(r, r + 64) for r in range(0, rows, 64)]


LAG = 4
SLOTS_HELD = 2 * LAG


def staged(count, *stages, beside={}):
    for n in range(count + LAG * (len(stages) - 1)):
        for work in beside.get(n, ()):
            work()
        for late, stage in enumerate(stages):
            if 0 <= n - LAG * late < count:
                stage(n - LAG * late)


def unit_of(n):
    g = n % 2
    rows = slice(64 * (n // 2), 64 * (n // 2) + 64)
    return rows, lambda part: slice(256 * part + 128 * g, 256 * part + 128 * g + 128), g


def attention(w):
    sel = lane_masks()
    ones = [m.astype(f32).astype(bf16) for m in sel]
    scale = HD ** (-0.5) * LOG2E

    def scores(n):
        rows, lanes, g = unit_of(n)
        q, k = w["packed"][rows, lanes(0)], w["packed"][rows, lanes(1)]
        w["s"][n % SLOTS_HELD] = mm_nt(k, spread_heads(q, ones))

    def softmax(n):
        s = w["s"][n % SLOTS_HELD] * scale + w["bias"][n % 2]
        s = jnp.exp2(s - jnp.max(s, axis=0, keepdims=True))
        w["p"][n] = (s * (1.0 / jnp.sum(s, axis=0, keepdims=True))).astype(bf16)

    def values(n):
        rows, lanes, g = unit_of(n)
        found = gather_heads(mm_tn(w["p"][n], w["packed"][rows, lanes(2)]), sel)
        w["ctx"][rows, lanes(0)] = found.astype(bf16)

    staged(w["p"].shape[0], scores, softmax, values)


def attention_back(w, beside):
    sel = lane_masks()
    ones = [m.astype(f32).astype(bf16) for m in sel]
    scale = HD ** (-0.5)

    def upstream(n):
        rows, lanes, g = unit_of(n)
        spread = spread_heads(w["dctx"][rows, lanes(0)], ones)
        w["gp"][rows, lanes(2)] = mm(w["p"][n], spread).astype(bf16)
        w["s"][n % SLOTS_HELD] = mm_nt(w["packed"][rows, lanes(2)], spread)

    def inward(n):
        p = w["p"][n].astype(f32)
        t = p * w["s"][n % SLOTS_HELD]
        ds = t - p * jnp.sum(t, axis=0, keepdims=True)
        w["d_bias"][n % 2] += ds
        w["ds"][n % SLOTS_HELD] = ds.astype(bf16)

    def outer(n):
        rows, lanes, g = unit_of(n)
        ds = w["ds"][n % SLOTS_HELD]
        q, k = w["packed"][rows, lanes(0)], w["packed"][rows, lanes(1)]
        w["gp"][rows, lanes(1)] = (mm(ds, spread_heads(q, ones)) * scale).astype(bf16)
        w["gp"][rows, lanes(0)] = (gather_heads(mm_tn(ds, k), sel) * scale).astype(bf16)

    staged(w["p"].shape[0], upstream, inward, outer, beside=beside)


def halves(rows):
    return slice(0, rows // 2), slice(rows // 2, rows)


def pieces_of(half):
    return [slice(r, r + 64) for r in range(half.start, half.stop, 64)]


def attend(x_ref, w):
    rows = x_ref.shape[0]
    gain1, gain2 = w["gain1"][...], w["gain2"][...]
    scales = {}

    def project(half):
        for at in pieces_of(half):
            w["normed"][at] = (norm(x_ref[at])[0] * gain1).astype(bf16)
        w["packed"][half] = mm(w["normed"][half], w["qkv"][...]).astype(bf16)

    def join(half):
        w["mixed"][half] = x_ref[half] + mm(w["ctx"][half], w["out"][...])
        for at in pieces_of(half):
            xhat, scales[at.start] = norm(w["mixed"][at])
            w["xhat"][at] = xhat
            w["normed2"][at] = (xhat * gain2).astype(bf16)

    project(slice(0, rows))
    attention(w)
    join(slice(0, rows))
    return scales


def block_forward(x_ref, w):
    attend(x_ref, w)
    rows = x_ref.shape[0]

    def start(c):
        w["a"][c % 2] = mm(w["normed2"][...], w["up"][:, 256 * c : 256 * c + 256])

    start(0)
    for c in range(FF // 256):
        cols = slice(256 * c, 256 * c + 256)
        if c < FF // 256 - 1:
            start(c + 1)
        for at in pieces(rows):
            active, slope = gelu_parts(w["a"][c % 2, at])
            w["active"][at, cols] = active.astype(bf16)
            w["slope"][at, cols] = slope.astype(bf16)
        before = w["mixed"] if c == 0 else w["xhat"]
        w["xhat"][...] = before[...] + mm(w["active"][:, cols], w["down"][cols, :])


def block_backward(x_ref, g_ref, w, fused, round_dn):
    rows = x_ref.shape[0]
    gain1, gain2 = w["gain1"][...], w["gain2"][...]
    if fused:
        scales = attend(x_ref, w)
    normed2_t = w["normed2"][...].T
    gb = g_ref[...].astype(bf16)
    gb_t = gb.T

    if fused:
        def start(c):
            cols = slice(256 * c, 256 * c + 256)
            if fused:
                w["a"][c % 2] = mm(w["normed2"][...], w["up"][:, cols])
            w["b"][c % 2] = mm_nt(gb, w["down"][cols, :])

        start(0)
        for c in range(FF // 256):
            cols = slice(256 * c, 256 * c + 256)
            if c < FF // 256 - 1:
                start(c + 1)
            for at in pieces(rows):
                if fused:
                    active, slope = gelu_parts(w["a"][c % 2, at])
                    w["active"][at, cols] = active.astype(bf16)
                else:
                    slope = w["slope"][at, cols].astype(f32)
                w["d_inner"][at, cols] = (w["b"][c % 2, at] * slope).astype(bf16)
            part = mm_nt(w["d_inner"][:, cols], w["up"][:, cols])
            w["dn"][...] = part if c == 0 else w["dn"][...] + part
            w["d_ff"][1024 + 256 * c : 1280 + 256 * c, :] += mm(gb_t, w["active"][:, cols])
            w["d_ff"][cols, :] += mm(normed2_t, w["d_inner"][:, cols])
            if fused:
                w["mixed"][...] += mm(w["active"][:, cols], w["down"][cols, :])
    else:
        for c in range(FF // 256):
            cols = slice(256 * c, 256 * c + 256)
            part = mm_nt(gb, w["down"][cols, :]) * w["slope"][:, cols].astype(f32)
            w["d_inner"][:, cols] = part.astype(bf16)
        w["dn"][...] = mm_nt(w["d_inner"][...], w["up"][...])
        for c in range(FF // 256):
            cols = slice(256 * c, 256 * c + 256)
            w["d_ff"][FF + 256 * c : FF + 256 * c + 256, :] += mm(gb_t, w["active"][:, cols])
            w["d_ff"][cols, :] += mm(normed2_t, w["d_inner"][:, cols])

    def into_heads(half):
        dgain = None
        for at in pieces_of(half):
            xhat, r = (w["xhat"][at], scales[at.start]) if fused else norm(w["mixed"][at])
            inward, part = norm_back(w["dn"][at], xhat, r, gain2)
            dgain = part if dgain is None else dgain + part
            d_mixed = g_ref[at] + inward
            g_ref[at] = d_mixed
            w["g_out"][at] = d_mixed.astype(bf16)
        w["d_small"][8:16, :] += dgain
        w["dctx"][half] = mm_nt(w["g_out"][half], w["out"][...]).astype(bf16)

    def d_out():
        w["d_at"][768:1024, :] += mm_tn(w["ctx"][...], w["g_out"][...])

    def out_of_heads(half):
        gp = w["gp"][half]
        w["dn"][half] = mm_nt(gp, w["qkv"][...])
        normed_t = w["normed"][half].T
        for c in range(3):
            cols = slice(256 * c, 256 * c + 256)
            w["d_at"][cols, :] += mm(normed_t, gp[:, cols])
        dgain = None
        for at in pieces_of(half):
            dn = w["dn"][at]
            if round_dn:
                dn = dn.astype(bf16).astype(f32)
            xhat, r = norm(x_ref[at])
            inward, part = norm_back(dn, xhat, r, gain1)
            dgain = part if dgain is None else dgain + part
            g_ref[at] = g_ref[at] + inward
        w["d_small"][0:8, :] += dgain

    one, two = halves(rows)
    units = rows // 64
    into_heads(one)
    beside = {2: [functools.partial(into_heads, two)], units: [d_out]}
    attention_back(w, beside)
    out_of_heads(slice(0, rows))


LIMIT = 56 * 1024 * 1024


def cost(us):
    return pl.CostEstimate(flops=int(us * 1.1e9), bytes_accessed=int(us * 3.6e6), transcendentals=0)


ANY = pl.BlockSpec(memory_space=pl.ANY)


def params(n):
    return pltpu.CompilerParams(
        dimension_semantics=("arbitrary",) * n, vmem_limit_bytes=LIMIT
    )


def latent_head(state, wl):
    center = mm_nt(state, wl[:ZC])
    squash = jnp.tanh(mm_nt(state, wl[ZC:]) * (1.0 / spread_bound))
    return center, squash, jnp.exp((0.5 * spread_bound) * squash)


def lanes_of_patch(width, back):
    lane = lax.broadcasted_iota(jnp.int32, (4 * 256, 4 * 64), 0)
    at = lax.broadcasted_iota(jnp.int32, (4 * 256, 4 * 64), 1)
    row, col = query_place(at & 63)
    want = 16 * (7 - row) + 7 - col if back else 16 * row + col
    return jnp.where(lane == (at >> 6) * 256 + want, 1.0, 0.0).astype(bf16)


def query_place(q):
    return (q >> 2) & 7, ((q >> 5) << 2) + (q & 3)


def table_lanes(back):
    a = lax.broadcasted_iota(jnp.int32, (256, 256), 0)
    b = lax.broadcasted_iota(jnp.int32, (256, 256), 1)
    side = 2 * WIN - 1
    if back:
        mirrored = 16 * (14 - (a >> 4)) + 14 - (a & 15)
        hit = ((a & 15) < side) & ((a >> 4) < side) & (b == (14 - (a >> 4)) * side + 14 - (a & 15))
    else:
        hit = ((b & 15) < side) & ((b >> 4) < side) & (a == (b >> 4) * side + (b & 15))
    return jnp.where(hit, 1.0, 0.0).astype(bf16)


def exactly(a, onehot):
    total = None
    for _ in range(3):
        term = a.astype(bf16)
        a = a - term.astype(f32)
        part = mm(term, onehot)
        total = part if total is None else total + part
    return total


def expand_bias(tables):
    spread = exactly(tables, table_lanes(False))
    choose = lanes_of_patch(64, False)
    out = []
    for n in range(4):
        heads = []
        for h in range(4 * n, 4 * n + 4):
            one = jnp.broadcast_to(spread[h : h + 1], (8, 256))
            heads.append(
                jnp.concatenate(
                    [
                        pltpu.roll(one, (16 * r + 137) % 256, 1, stride=1, stride_axis=0)
                        for r in range(WIN)
                    ]
                )
            )
        rows = exactly(jnp.concatenate(heads, axis=1), choose)
        out.append(to_halves(rows.reshape(WIN, WIN, 256)).reshape(64, 256))
    return out


def reduce_bias(grads):
    rows = from_halves(grads.reshape(2, HALF, 256)).reshape(64, 256).astype(bf16)
    lanes = lax.dot_general(
        rows, lanes_of_patch(64, True), (((1,), (1,)), ((), ())), preferred_element_type=f32
    )
    out = []
    for h in range(4):
        total = None
        for r in range(WIN):
            one = pltpu.roll(
                lanes[8 * r : 8 * r + 8, 256 * h : 256 * h + 256], 16 * r, 1, stride=1, stride_axis=0
            )
            total = one if total is None else total + one
        out.append(jnp.sum(total, axis=0, keepdims=True))
    return jnp.concatenate(out)


def prep_kernel(samples, cot, state, wl, tables, cot_h, state_h, kl, bias):
    @pl.when(pl.program_id(0) == 0)
    def _():
        padded = jnp.concatenate(
            [tables[...], jnp.zeros((16, 256 - tables.shape[1]), f32)], axis=1
        )
        for n, part in enumerate(expand_bias(padded * LOG2E)):
            bias[n // 2, n % 2] = part

    live = samples[0]
    for s in range(SLOTS):
        factor = jnp.where(s < live, 1.0, 0.0).astype(f32)
        cot_h[:, s] = (to_halves(cot[0, s].astype(f32)) * factor).astype(bf16)
    st = to_halves(state[0].astype(f32)).reshape(4, 64, D).astype(bf16)
    state_h[:, 0] = st
    center, squash, sigma = latent_head(st.reshape(4 * 64, D), wl[...])
    terms = 0.5 * (center * center + sigma * sigma - 1.0 - spread_bound * squash)

    @pl.when(pl.program_id(0) == 0)
    def _():
        kl[...] = jnp.zeros(kl.shape, f32)

    kl[:, :ZC] += jnp.sum(terms.reshape(-1, 8, ZC), axis=0)


def prep(samples, cot, state, wl, tables):
    bands = state.shape[1] // WIN
    nw = state.shape[2] // WIN
    return pl.pallas_call(
        prep_kernel,
        grid=(bands,),
        in_specs=[
            pl.BlockSpec(memory_space=pltpu.SMEM),
            pl.BlockSpec((1, SLOTS, WIN, nw * WIN, D), lambda i: (0, 0, i, 0, 0)),
            pl.BlockSpec((1, WIN, nw * WIN, D), lambda i: (0, i, 0, 0)),
            full(wl),
            full(tables),
        ],
        out_specs=[
            pl.BlockSpec((2 * nw, SLOTS, HALF, D), lambda i: (0, i, 0, 0)),
            pl.BlockSpec((nw, 1, 64, D), lambda i: (0, i, 0, 0)),
            pl.BlockSpec((8, D), lambda i: (0, 0)),
            pl.BlockSpec((2, 2, 64, 256), lambda i: (0, 0, 0, 0)),
        ],
        out_shape=[
            jax.ShapeDtypeStruct((2 * nw, bands * SLOTS, HALF, D), bf16),
            jax.ShapeDtypeStruct((nw, bands, 64, D), bf16),
            jax.ShapeDtypeStruct((8, D), f32),
            jax.ShapeDtypeStruct((2, 2, 64, 256), f32),
        ],
        compiler_params=params(1),
        cost_estimate=cost(4),
    )(samples, cot, state, wl, tables)


def noise_of(block):
    bands = block.shape[1] // WIN
    return jnp.stack(
        [
            jnp.stack(
                [to_halves(block[s, WIN * b : WIN * b + WIN]).reshape(64, ZC) for s in range(SLOTS)]
            )
            for b in range(bands)
        ]
    )


def noise_spec(bands, skip):
    return pl.BlockSpec((1, SLOTS, bands * WIN, WIN, ZC), lambda j: (0, 0, 0, j + skip, 0))


def cell_forward(state, noise, wl, ws, wn):
    bands = state.shape[0]
    flat = state.reshape(bands * 64, D)
    over = lambda x: x.reshape(bands, 1, 64, x.shape[-1])
    center, squash, sigma = latent_head(flat, wl)
    latent = (over(center) + over(sigma) * noise).reshape(-1, ZC).astype(bf16)
    mix = mm(latent, wn)
    half = 0.5 * (over(mm(flat, ws)) + mix[:, :D].reshape(bands, SLOTS, 64, D))
    gate = 0.5 + 0.5 * jnp.tanh(half)
    cand = jnp.tanh(mix[:, D:].reshape(bands, SLOTS, 64, D))
    hidden = gate * over(flat.astype(f32)) + (1.0 - gate) * cand
    return hidden.reshape(-1, D), center, squash, sigma, latent, gate, cand


def full(a):
    return pl.BlockSpec(a.shape, lambda *_: (0,) * a.ndim)


def block_specs(k):
    return [
        pl.BlockSpec((2, D), lambda *_: (0, 0)),
        pl.BlockSpec((1, D, 3 * D), lambda *_: (k, 0, 0)),
        pl.BlockSpec((1, 2, 64, 256), lambda *_: (k, 0, 0, 0)),
        pl.BlockSpec((1, D, D), lambda *_: (k, 0, 0)),
        pl.BlockSpec((2, D), lambda *_: (0, 0)),
        pl.BlockSpec((1, D, FF), lambda *_: (k, 0, 0)),
        pl.BlockSpec((1, FF, D), lambda *_: (k, 0, 0)),
    ]


NAMES = ("gain1", "qkv", "bias", "out", "gain2", "up", "down")


def named(refs, k):
    return {
        n: r.at[k : k + 1] if n.startswith("gain") else r.at[0] for n, r in zip(NAMES, refs)
    }


def saved_refs(rows):
    return [
        ("normed", (rows, D), bf16),
        ("packed", (rows, 3 * D), bf16),
        ("p", (rows // 32, 64, 256), bf16),
        ("ctx", (rows, D), bf16),
        ("mixed", (rows, D), f32),
        ("normed2", (rows, D), bf16),
        ("active", (rows, FF), bf16),
        ("slope", (rows, FF), bf16),
    ]


def forward_refs(rows):
    return [
        ("x", (rows, D), f32),
        ("s", (SLOTS_HELD, 64, 256), f32),
        ("xhat", (rows, D), f32),
        ("a", (2, rows, 256), f32),
    ]


def backward_refs(rows):
    return [
        ("x", (rows, D), f32),
        ("g", (rows, D), f32),
        ("s", (SLOTS_HELD, 64, 256), f32),
        ("b", (2, rows, 256), f32),
        ("d_inner", (rows, FF), bf16),
        ("dn", (rows, D), f32),
        ("g_out", (rows, D), bf16),
        ("dctx", (rows, D), bf16),
        ("ds", (SLOTS_HELD, 64, 256), bf16),
        ("gp", (rows, 3 * D), bf16),
    ]


def both_refs(rows):
    return saved_refs(rows) + forward_refs(rows)[2:] + backward_refs(rows)


def scratch(refs):
    return [pltpu.VMEM(shape, dtype) for _, shape, dtype in refs]


def names(refs):
    return [name for name, _, _ in refs]


def saved_specs(rows, skip):
    return [
        pl.BlockSpec((1,) + shape, lambda j, n=len(shape): (j + skip,) + (0,) * n)
        for _, shape, _ in saved_refs(rows)
    ]


N_SAVED, N_BACK, N_BOTH = len(saved_refs(64)), len(backward_refs(64)), len(both_refs(64))


GRAD_SHAPES = [(2048, D), (1024, D), (16, D), (2, 64, 256)]
GRAD_NAMES = ("d_ff", "d_at", "d_small", "d_bias")
GRAD_SCRATCH = [pltpu.VMEM(s, f32) for s in GRAD_SHAPES[:2]]
SMALL_SPECS = [pl.BlockSpec(s, lambda *_, n=len(s): (0,) * n) for s in GRAD_SHAPES[2:]]
SMALL_OUTS = [jax.ShapeDtypeStruct(s, f32) for s in GRAD_SHAPES[2:]]

ROWS_BLOCK = 3072
ROWS_CELL = 512
CHAINS = (((0, (ROWS_BLOCK + ROWS_CELL) // 2),), ((0, ROWS_BLOCK // 2),))
ALL_CHAINS = [(k, chain) for k in range(2) for chain in CHAINS[k]]


def first_kernel(state, noise, cot, wl, ws, wn, *rest, lead):
    w = named(rest[:7], 0)
    rest = rest[7:] if lead else rest[7 + 1 + N_SAVED :]
    h1, rest = rest[0], rest[1:]
    w.update((n, r.at[0]) for n, r in zip(names(saved_refs(64)), rest))
    rest = rest[N_SAVED:]
    if lead:
        halo, rest = rest[0], rest[1:]
    w.update(zip(names(forward_refs(64)), rest))
    w["x"][...] = cell_forward(state[0], noise_of(noise[0]), wl[...], ws[...], wn[...])[0]
    block_forward(w["x"], w)
    a, b = halves_of(w["xhat"][...])
    h1[0, 0] = a
    h1[0, 1] = b
    if lead:
        halo[0] = a.astype(bf16)
        halo[1] = cot[0]


def first(state_h, noise, cot_h, cell_w, block_w, before=None):
    nw, bands = state_h.shape[:2]
    half = (bands * SLOTS, HALF, D)
    rows = 64 * bands * SLOTS
    lead = before is None
    skip = 0 if lead else 1
    specs = [pl.BlockSpec((1, 2) + half, lambda j: (j + skip, 0, 0, 0, 0))] + saved_specs(rows, skip)
    shapes = [jax.ShapeDtypeStruct((nw, 2) + half, f32)] + [
        jax.ShapeDtypeStruct((nw,) + shape, dtype) for _, shape, dtype in saved_refs(rows)
    ]
    inputs = [state_h, noise, cot_h, *cell_w, *block_w]
    in_specs = [
        pl.BlockSpec((1, bands, 64, D), lambda j: (j + skip, 0, 0, 0)),
        noise_spec(bands, skip),
        pl.BlockSpec((1,) + half, lambda j: (0, 0, 0, 0)),
    ]
    in_specs += [full(a) for a in cell_w] + block_specs(0)
    aliases = {}
    if lead:
        specs.append(pl.BlockSpec((2,) + half, lambda j: (0, 0, 0, 0)))
        shapes.append(jax.ShapeDtypeStruct((2,) + half, bf16))
    else:
        aliases = {len(inputs) + n: n for n in range(len(before))}
        inputs += before
        in_specs += [pl.BlockSpec(memory_space=pl.ANY)] * len(before)
    return pl.pallas_call(
        functools.partial(first_kernel, lead=lead),
        grid=(1 if lead else nw - 1,),
        in_specs=in_specs,
        out_specs=specs,
        out_shape=shapes,
        input_output_aliases=aliases,
        scratch_shapes=scratch(forward_refs(rows)),
        compiler_params=params(1),
        cost_estimate=cost(6 if lead else 16),
    )(*inputs)


def zero_at_start(refs):
    @pl.when(pl.program_id(0) == 0)
    def _():
        for r in refs:
            r[...] = jnp.zeros(r.shape, r.dtype)


def halves_out(keep, send, parts):
    size = keep.shape[0]
    core = lax.axis_index("batch") & 1

    def write(low, high):
        first = 0
        for ref in parts:
            rows = ref.shape[0]
            cut = min(max(size - first, 0), rows)
            if cut:
                low[first : first + cut] = ref[:cut].astype(bf16)
            if cut < rows:
                high[first + cut - size : first + rows - size] = ref[cut:rows].astype(bf16)
            first += rows

    @pl.when(core == 0)
    def _():
        write(keep, send)

    @pl.when(core != 0)
    def _():
        write(send, keep)


def at_end():
    return pl.program_id(0) == pl.num_programs(0) - 1


def second_kernel(samples, ha, hb, ca, cb, *rest, lead):
    w = named(rest[:7], 1)
    grads1, small1, bias1 = (None,) * 3 if lead else rest[7:10]
    rest = rest[7:] if lead else rest[12:]
    act, dh, d_small, d_bias = rest[:4]
    if lead:
        packed_grads, back_halo = rest[4:6]
    else:
        keep, send = rest[4:6]
    rest = rest[6:]
    w.update(zip(names(both_refs(64)), rest))
    grads = rest[N_BOTH : N_BOTH + 2] + (d_small, d_bias)
    w.update(zip(GRAD_NAMES, grads))
    if lead:
        zero_at_start(grads)
    else:

        @pl.when(pl.program_id(0) == 0)
        def _():
            grads[0][...] = grads1[:2048].astype(f32)
            grads[1][...] = grads1[2048:].astype(f32)
            d_small[...] = small1[...]
            d_bias[...] = bias1[...]

    w["x"][...] = tile_of(ha[0, 0], hb[0].astype(f32) if lead else hb[0, 0])
    w["g"][...] = tile_of(ca[0].astype(f32), cb[0].astype(f32))
    block_backward(w["x"], w["g"], w, True, True)
    live = samples[0]
    a, b = halves_of(w["mixed"][...])
    factor = jnp.concatenate(
        [jnp.where(s % SLOTS < live, 1.0, 0.0) * jnp.ones((1, 1, D), f32) for s in range(a.shape[0])]
    )
    a, b = (a * factor).astype(bf16), (b * factor).astype(bf16)
    da, db = halves_of(w["g"][...])
    act[0, 0] = a
    act[0, 1] = b
    dh[0, 0] = da
    dh[0, 1] = db
    if lead:
        back_halo[0] = db.astype(bf16)
        back_halo[1] = b
        packed_grads[:2048] = grads[0][...].astype(bf16)
        packed_grads[2048:] = grads[1][...].astype(bf16)
    else:

        @pl.when(at_end())
        def _():
            halves_out(keep, send, [grads[0], grads[1]])


def second(samples, h1, cot_h, block_w, halo=None, before=None):
    nw = h1.shape[0]
    half = h1.shape[2:]
    lead = before is None
    if lead:
        tile, other = (lambda j: nw - 1), halo
        wide = [pl.BlockSpec((1,) + half, lambda j, n=n: (n, 0, 0, 0)) for n in range(2)]
    else:
        tile, other = (lambda j: j), cot_h
        wide = [
            pl.BlockSpec((1, 1) + half, lambda j: (j + 1, 0, 0, 0, 0)),
            pl.BlockSpec((1,) + half, lambda j: (2 * j + 2, 0, 0, 0)),
        ]
    inputs = [samples, h1, halo if lead else h1, cot_h, other, *block_w]
    in_specs = [
        pl.BlockSpec(memory_space=pltpu.SMEM),
        pl.BlockSpec((1, 1) + half, lambda j: (tile(j), 1, 0, 0, 0)),
        wide[0],
        pl.BlockSpec((1,) + half, lambda j: (2 * tile(j) + 1, 0, 0, 0)),
        wide[1],
    ]
    in_specs += block_specs(1)
    out_specs = [
        pl.BlockSpec((1, 2) + half, lambda j: (tile(j), 0, 0, 0, 0)),
        pl.BlockSpec((1, 2) + half, lambda j: (tile(j), 0, 0, 0, 0)),
    ] + SMALL_SPECS
    out_shape = [
        jax.ShapeDtypeStruct((nw, 2) + half, bf16),
        jax.ShapeDtypeStruct((nw, 2) + half, f32),
    ] + SMALL_OUTS
    aliases = {}
    if lead:
        out_specs.append(pl.BlockSpec((ROWS_BLOCK, D), lambda *_: (0, 0)))
        out_specs.append(pl.BlockSpec((2,) + half, lambda j: (0, 0, 0, 0)))
        out_shape.append(jax.ShapeDtypeStruct((ROWS_BLOCK, D), bf16))
        out_shape.append(jax.ShapeDtypeStruct((2,) + half, bf16))
    else:
        out_specs += [pl.BlockSpec((ROWS_BLOCK // 2, D), lambda *_: (0, 0))] * 2
        out_shape += [jax.ShapeDtypeStruct((ROWS_BLOCK // 2, D), bf16)] * 2
        act, dh, small1, bias1, grads1 = before
        sums = [grads1, small1, bias1]
        aliases = {len(inputs) + 3: 0, len(inputs) + 4: 1}
        inputs += sums + [act, dh]
        in_specs += [full(a) for a in sums] + [pl.BlockSpec(memory_space=pl.ANY)] * 2
    return pl.pallas_call(
        functools.partial(second_kernel, lead=lead),
        grid=(1 if lead else nw - 1,),
        in_specs=in_specs,
        out_specs=out_specs,
        out_shape=out_shape,
        input_output_aliases=aliases,
        scratch_shapes=scratch(both_refs(64 * half[0])) + GRAD_SCRATCH,
        compiler_params=params(1),
        cost_estimate=cost(9 if lead else 24),
    )(*inputs)


CELL_SHAPES = [(D, D), (2 * ZC, D), (2 * ZC, D), (2 * ZC, D)]


def divergence_parts(center, squash, sigma):
    return center.astype(bf16), (
        0.5 * (sigma * sigma - 1.0) * (1.0 - squash * squash)
    ).astype(bf16)


def third_kernel(state, noise, da, db, dhalo, small1, bias1, kl, wl, ws, wn, *rest):
    w = named(rest[:7], 0)
    w.update((n, r.at[0]) for n, r in zip(names(saved_refs(64)), rest[7:]))
    rest = rest[N_SAVED:]
    sg, keep, send = rest[7:10]
    w.update(zip(names(backward_refs(64)), rest[10:]))
    grads = rest[10 + N_BACK : 14 + N_BACK]
    d_ws, d_wn, d_wl, d_kl, d_rest = rest[14 + N_BACK :]
    cell_grads = (d_ws, d_wn, d_wl, d_kl)
    w.update(zip(GRAD_NAMES, grads))
    zero_at_start(grads + cell_grads)
    st = state[0]
    nz = noise_of(noise[0])
    bands = st.shape[0]
    hidden, center, squash, sigma, latent, gate, cand = cell_forward(
        st, nz, wl[...], ws[...], wn[...]
    )
    da_v = jnp.where(pl.program_id(0) == 0, dhalo[0].astype(f32), da[0, 0])
    w["x"][...] = hidden
    w["g"][...] = tile_of(da_v, db[0, 0])
    block_backward(w["x"], w["g"], w, False, False)
    dc = w["g"][...]
    over = lambda x: x.reshape(bands, 1, 64, x.shape[-1])
    flat = st.reshape(bands * 64, D)
    dc = dc.reshape(bands, SLOTS, 64, D)
    rest_gate = 1.0 - gate
    d_pre = dc * (over(flat.astype(f32)) - cand) * gate * rest_gate
    d_cand = dc * rest_gate * (1.0 - cand * cand)
    direct = jnp.sum(dc * gate, axis=1).reshape(-1, D)
    g_gate = jnp.sum(d_pre, axis=1).reshape(-1, D).astype(bf16)
    d_ws[...] += mm_tn(flat, g_gate)
    pre = d_pre.reshape(-1, D).astype(bf16)
    cnd = d_cand.reshape(-1, D).astype(bf16)
    d_wn[:ZC] += mm_tn(latent, pre)
    d_wn[ZC:] += mm_tn(latent, cnd)
    d_lat = mm_nt(pre, wn[:, :D]) + mm_nt(cnd, wn[:, D:])
    d_lat = d_lat.reshape(bands, SLOTS, 64, ZC)
    d_center = jnp.sum(d_lat, axis=1).reshape(-1, ZC)
    d_raw = jnp.sum(d_lat * nz, axis=1).reshape(-1, ZC) * 0.5 * sigma * (1.0 - squash * squash)
    d_center, d_raw = d_center.astype(bf16), d_raw.astype(bf16)
    d_wl[:ZC] += mm_tn(d_center, flat)
    d_wl[ZC:] += mm_tn(d_raw, flat)
    kl_center, kl_raw = divergence_parts(center, squash, sigma)
    d_kl[:ZC] += mm_tn(kl_center, flat)
    d_kl[ZC:] += mm_tn(kl_raw, flat)
    total = direct + mm_nt(g_gate, ws[...])
    total = total + mm(d_center, wl[:ZC]) + mm(d_raw, wl[ZC:])
    for b in range(bands):
        sg[0, WIN * b : WIN * b + WIN] = from_halves(
            total[64 * b : 64 * b + 64].reshape(2, HALF, D)
        )

    @pl.when(at_end())
    def _():
        d_small, d_bias = grads[2:]
        d_rest[:16] = jnp.concatenate(
            [reduce_bias(b) for b in (d_bias[0], d_bias[1], bias1[0], bias1[1])]
        )
        total = lambda x: jnp.sum(x, axis=0, keepdims=True)
        d_rest[16:] = jnp.concatenate(
            [total(d_small[:8]), total(d_small[8:]), total(small1[:8]), total(small1[8:])]
            + [total(kl[...]), jnp.zeros((43, D), f32)]
        )
        halves_out(keep, send, [grads[0], grads[1], *cell_grads, d_rest])


def third(state_h, noise, dh, halo, small1, bias1, kl, cell_w, block_w, saved):
    nw, bands = state_h.shape[:2]
    rows = 64 * bands * SLOTS
    half = dh.shape[2:]
    return pl.pallas_call(
        third_kernel,
        grid=(nw,),
        in_specs=[
            pl.BlockSpec((1, bands, 64, D), lambda j: (j, 0, 0, 0)),
            noise_spec(bands, 0),
            pl.BlockSpec((1, 1) + half, lambda j: (jnp.maximum(j - 1, 0), 1, 0, 0, 0)),
            pl.BlockSpec((1, 1) + half, lambda j: (j, 0, 0, 0, 0)),
            pl.BlockSpec((1,) + half, lambda j: (0, 0, 0, 0)),
        ]
        + [full(a) for a in (small1, bias1, kl)]
        + [full(a) for a in cell_w]
        + block_specs(0)
        + saved_specs(rows, 0),
        out_specs=[pl.BlockSpec((1, bands * WIN, WIN, D), lambda j: (0, 0, j, 0))]
        + [pl.BlockSpec(((ROWS_BLOCK + ROWS_CELL) // 2, D), lambda *_: (0, 0))] * 2,
        out_shape=[jax.ShapeDtypeStruct((1, bands * WIN, nw * WIN, D), f32)]
        + [jax.ShapeDtypeStruct(((ROWS_BLOCK + ROWS_CELL) // 2, D), bf16)] * 2,
        scratch_shapes=scratch(backward_refs(rows))
        + [pltpu.VMEM(s, f32) for s in GRAD_SHAPES + CELL_SHAPES + [(64, D)]],
        compiler_params=params(1),
        cost_estimate=cost(26),
    )(state_h, noise, dh, dh, halo, small1, bias1, kl, *cell_w, *block_w, *saved)


def place_kernel(act, halo, out):
    nw = act.shape[0]
    for s in range(SLOTS):
        halves = [halo[0, s].astype(f32)]
        for j in range(nw):
            halves.append(act[j, 0, s].astype(f32))
            if j < nw - 1:
                halves.append(act[j, 1, s].astype(f32))
        out[0, s] = from_halves(jnp.stack(halves)).astype(bf16)


def place(act, halo):
    nw = act.shape[0]
    bands = act.shape[2] // SLOTS
    return pl.pallas_call(
        place_kernel,
        grid=(bands,),
        in_specs=[
            pl.BlockSpec((nw, 2, SLOTS, HALF, D), lambda i: (0, 0, i, 0, 0)),
            pl.BlockSpec((1, SLOTS, HALF, D), lambda i: (1, i, 0, 0)),
        ],
        out_specs=pl.BlockSpec((1, SLOTS, WIN, nw * WIN, D), lambda i: (0, 0, i, 0, 0)),
        out_shape=jax.ShapeDtypeStruct((1, SLOTS, bands * WIN, nw * WIN, D), bf16),
        compiler_params=params(1),
        cost_estimate=cost(4),
    )(act, halo)


def finish_kernel(
    order, scalars, state, part, wl, *rest, cells, devices,
):
    n_blocks = 2 * len(ALL_CHAINS)
    blocks, rest = rest[:n_blocks], rest[n_blocks:]
    sg, div, o_wl, o_ws, o_wn, o_gain1, o_table, o_gain2, *large = rest[:12]
    sums, held = rest[12 : 12 + len(ALL_CHAINS)], rest[12 + len(ALL_CHAINS) : -6]
    o_qkv, o_out, o_up, o_down = stage = rest[-6:-2]
    in_sems, out_sems = rest[-2:]
    arrive = [pltpu.make_async_copy(b, h, in_sems.at[n]) for n, (b, h) in enumerate(zip(blocks, held))]
    leave = [
        [pltpu.make_async_copy(a.at[k], b.at[k], out_sems.at[4 * k + n]) for n, (a, b) in enumerate(zip(stage, large))]
        for k in range(2)
    ]
    for copy in arrive:
        copy.start()

    def assemble(k):
        for chain, (where, _) in enumerate(ALL_CHAINS):
            if where != k:
                continue
            whole = sums[chain]
            n = devices // 4
            count = whole.shape[0] // (2 * n)
            for at in range(2):
                arrive[2 * chain + at].wait()
                block = held[2 * chain + at]
                for i in range(n):
                    to = order[2 * chain, at] * n + jnp.bitwise_xor(order[2 * chain + 1, at], i)
                    whole[pl.ds(pl.multiple_of(to * count, 16), count)] = block[
                        count * i : count * i + count
                    ]

    def rows_of(k, first, count):
        size = CHAINS[k][-1][1]
        side, first = divmod(first, size)
        for (where, (low, high)), whole in zip(ALL_CHAINS, sums):
            if where == k and low <= first < high:
                first += side * whole.shape[0] // 2 - low
                return whole[first : first + count]

    def unpack(k):
        assemble(k)
        for c in range(3):
            cols = slice(256 * c, 256 * c + 256)
            o_qkv[k, :, cols] = rows_of(k, 2 * FF + 256 * c, 256).astype(f32)
        o_out[k] = rows_of(k, 2816, 256).astype(f32)
        leave[k][0].start()
        leave[k][1].start()
        for c in range(FF // 256):
            cols = slice(256 * c, 256 * c + 256)
            o_up[k, :, cols] = rows_of(k, 256 * c, 256).astype(f32)
        leave[k][2].start()
        for c in range(FF // 256):
            cols = slice(256 * c, 256 * c + 256)
            o_down[k, cols] = rows_of(k, FF + 256 * c, 256).astype(f32).T
        leave[k][3].start()

    unpack(0)
    unpack(1)
    cell_rows = lambda first, count: rows_of(0, ROWS_BLOCK + first, count)
    small = cell_rows(464, 16).astype(f32)
    kl_mean = small[4:5, :ZC] * (1.0 / cells)
    beta, floor = scalars[0], scalars[1]
    excess = sharpness * (kl_mean - floor)
    soft = jnp.maximum(excess, 0.0) + jnp.log(1.0 + jnp.exp(-jnp.abs(excess)))
    div[...] = beta * jnp.mean(floor + soft * (1.0 / sharpness), axis=-1, keepdims=True)
    amt = beta * jax.nn.sigmoid(excess) * (1.0 / (ZC * cells))

    rows = state.shape[1] * state.shape[2]
    center, squash, sigma = latent_head(state[0].reshape(rows, D), wl[...])
    kl_center, kl_raw = divergence_parts(center, squash, sigma)
    g_center = (kl_center.astype(f32) * amt).astype(bf16)
    g_raw = (kl_raw.astype(f32) * amt).astype(bf16)
    add = mm(g_center, wl[:ZC]) + mm(g_raw, wl[ZC:])
    sg[0] = part[0] + add.reshape(state.shape[1:])

    o_ws[...] = cell_rows(0, 256).astype(f32)
    wn = cell_rows(256, 64).astype(f32)
    o_wn[:, :D] = wn[:ZC]
    o_wn[:, D:] = wn[ZC:]
    at = lambda axis: lax.broadcasted_iota(jnp.int32, (ZC, ZC), axis)
    column = jnp.sum(jnp.where(at(0) == at(1), amt, 0.0), axis=1, keepdims=True)
    for h in range(2):
        o_wl[ZC * h : ZC * h + ZC] = (
            cell_rows(320 + ZC * h, ZC).astype(f32) + cell_rows(384 + ZC * h, ZC).astype(f32) * column
        )
    table = mm(cell_rows(448, 16), table_lanes(True))
    o_table[0] = table[:HEADS, : (2 * WIN - 1) ** 2]
    o_table[1] = table[HEADS:, : (2 * WIN - 1) ** 2]
    for k in range(2):
        o_gain1[k : k + 1] = small[2 * k : 2 * k + 1]
        o_gain2[k : k + 1] = small[2 * k + 1 : 2 * k + 2]
    for k in range(2):
        for copy in leave[k]:
            copy.wait()


def finish(order, scalars, state, part, wl, *blocks, cells, devices):
    small = [
        part.shape, (1, 1), (2 * ZC, D), (D, D), (ZC, 2 * D), (2, D),
        (2, HEADS, (2 * WIN - 1) ** 2), (2, D),
    ]
    large = [(2, D, 3 * D), (2, D, D), (2, D, FF), (2, FF, D)]
    smem, vmem = pl.BlockSpec(memory_space=pltpu.SMEM), pl.BlockSpec(memory_space=pltpu.VMEM)
    sg, div, wl, ws, wn, gain1, table, gain2, qkv, out, up, down = pl.pallas_call(
        functools.partial(finish_kernel, cells=cells, devices=devices),
        in_specs=[smem, smem] + [vmem] * 3 + [ANY] * len(blocks),
        out_specs=[vmem] * len(small) + [ANY] * len(large),
        out_shape=[jax.ShapeDtypeStruct(o, f32) for o in small + large],
        scratch_shapes=[pltpu.VMEM((2 * b.shape[0], D), bf16) for b in blocks[::2]]
        + [pltpu.VMEM(b.shape, bf16) for b in blocks]
        + [pltpu.VMEM(o, f32) for o in large]
        + [pltpu.SemaphoreType.DMA((len(blocks),)), pltpu.SemaphoreType.DMA((8,))],
        compiler_params=pltpu.CompilerParams(vmem_limit_bytes=40 * 1024 * 1024),
    )(order, scalars, state, part, wl, *blocks)
    return sg, div, wl, ws, wn, gain1, qkv, table, out, gain2, up, down


def shift_from(block, distance):
    n = lax.axis_size("lon")
    return lax.ppermute(block, "lon", [((i + distance) % n, i) for i in range(n)])


class Summation:
    def __init__(self, turn):
        n_lon, n_batch = lax.axis_size("lon"), lax.axis_size("batch")
        self.n = n = n_lon * n_batch
        me = lax.axis_index("lon") * n_batch + lax.axis_index("batch")
        bits = [1 << i for i in range(1, n.bit_length() - 1)]
        axes, rest = [bits[0], bits[-1]] + bits[1:2], bits[2:-1]
        axes = axes[: len(bits)]
        turned = lambda by: axes[by % len(axes) :] + axes[: by % len(axes)] + rest
        self.pairs = list(zip(turned(turn), turned(turn + 1)))
        self.core = me & 1
        self.bits = [self.core] + self.bits_of(me)
        places = [self.place(self.bits[1:-1]), self.place(self.bits_of(me ^ 1)[:-1])]
        self.order = jnp.stack([jnp.stack([self.core, 1 - self.core]), jnp.stack(places)])

    def bits_of(self, device):
        return [
            (jnp.bitwise_and(device, jnp.where(device & 1 == 0, a, b)) != 0).astype(jnp.int32)
            for a, b in self.pairs
        ]

    def place(self, bits):
        at = jnp.zeros((), jnp.int32)
        for bit in bits:
            at = 2 * at + bit
        return at

    def swap(self, block, step):
        pair = self.pairs[step - 1] if step else (1, 1)
        return lax.ppermute(
            block, ("lon", "batch"), [(i, i ^ pair[i & 1]) for i in range(self.n)]
        )

    def begin(self, keep, send):
        return self.add(keep, self.swap(send, 0))

    def add(self, a, b):
        return (a.astype(f32) + b.astype(f32)).astype(bf16)

    def plan(self):
        last = len(self.bits) - 1
        down, up = range(1, last), range(last - 1, 0, -1)
        return [("halve", n) for n in down] + [("both", last)] + [("double", n) for n in up]

    def pad(self, total):
        return jnp.pad(total, ((0, -total.shape[0] % (4 * self.n)), (0, 0)))

    def half(self, total, at):
        size = total.shape[0] // 2
        return lax.dynamic_slice_in_dim(total, at * size, size, 0)

    def exchange(self, total, kind, step):
        if kind == "halve":
            total = self.half(total, 1 - self.bits[step])
        return self.swap(total, step)

    def join(self, total, got, kind, step):
        if kind == "halve":
            total = self.half(total, self.bits[step])
        return jnp.concatenate([total, got]) if kind == "double" else self.add(total, got)


def in_turn(adders, totals, beside):
    tie = lax.optimization_barrier
    plain = [adder.pad(total) for adder, total in zip(adders, totals)]
    tied = list(plain)
    for n, move in enumerate(adders[0].plan()):
        got = [adder.exchange(total, *move) for adder, total in zip(adders, plain)]
        if n == 0:
            got[0], *beside = tie((got[0], *beside))
        got[0], tied[1] = tie((got[0], tied[1]))
        plain[0] = adders[0].join(tied[0], got[0], *move)
        got[1], tied[0] = tie((got[1], plain[0]))
        plain[1] = tied[1] = adders[1].join(tied[1], got[1], *move)
    blocks = []
    for adder, total in zip(adders, plain):
        blocks += [total, adder.swap(total, 0)]
    return blocks, beside


def body(
    state,
    noise,
    samples,
    step,
    kl_weight,
    floor,
    latent_weight,
    state_weight,
    noise_weight,
    attention_gain,
    query_key_value,
    offset_bias,
    output_weight,
    feedforward_gain,
    up_weight,
    down_weight,
    cotangent,
):
    items, height, breadth, width = state.shape
    cells = items * height * breadth * lax.axis_size("lon") * lax.axis_size("batch")
    cell_w = (latent_weight.T, state_weight, noise_weight)
    cot_h, state_h, kl, bias = prep(
        samples, cotangent, state, cell_w[0], offset_bias.reshape(2 * HEADS, -1)
    )
    block_w = (
        attention_gain,
        query_key_value,
        bias,
        output_weight,
        feedforward_gain,
        up_weight,
        down_weight,
    )
    adders = [Summation(turn) for turn in range(len(ALL_CHAINS))]
    add_up = adders[0]
    order = jnp.concatenate([adder.order for adder in adders])
    beta = kl_weight * (step + 1).astype(f32) / WARM
    scalars = jnp.stack([beta, floor])
    *ahead, halo = first(state_h, noise, cot_h, cell_w, block_w)
    halo = shift_from(halo, 1)
    h1, *saved = first(state_h, noise, cot_h, cell_w, block_w, ahead)
    *ahead, halo = second(samples, h1, cot_h, block_w, halo=halo)
    halo = shift_from(halo, -1)
    act, dh, small1, bias1, *grads1 = second(samples, h1, cot_h, block_w, before=ahead)
    part, *grads0 = third(
        state_h, noise, dh, halo, small1, bias1, kl, cell_w, block_w, saved
    )
    activations = place(act, halo)
    sum1 = add_up.begin(*grads1)
    sum0 = add_up.begin(*grads0)
    sum1, sum0 = lax.optimization_barrier((sum1, sum0))
    blocks, beside = in_turn(adders, (sum0, sum1), (activations, order, scalars))
    activations, order, scalars = beside
    state_gradient, divergence, *weights = finish(
        order, scalars, state, part, cell_w[0], *blocks, cells=cells, devices=add_up.n
    )
    return (activations, divergence.reshape(()), state_gradient, weights[0].T, *weights[1:])


def solution(mesh):
    return jax.shard_map(
        body,
        mesh=mesh,
        in_specs=(
            P("batch", None, "lon", None),
            P("batch", None, None, "lon", None),
            P("batch"),
            P(),
            P(),
            P(),
            P(),
            P(),
            P(),
            P(),
            P(),
            P(),
            P(),
            P(),
            P(),
            P(),
            P("batch", None, None, "lon", None),
        ),
        out_specs=(
            P("batch", None, None, "lon", None),
            P(),
            P("batch", None, "lon", None),
            P(),
            P(),
            P(),
            P(),
            P(),
            P(),
            P(),
            P(),
            P(),
            P(),
        ),
        check_vma=False,
    )
```

```python
import functools

import jax
import jax.numpy as jnp
from jax import lax
from jax.experimental import pallas as pl
from jax.experimental.pallas import tpu as pltpu
from jax.sharding import PartitionSpec as P

HEADS = 8
HD = 32
WIN = 8
WARM = 1000
SLOTS = 4
D = 256
FF = 1024
ZC = 32
HALF = WIN // 2 * WIN

eps_norm = 1e-05
sharpness = 8.0
spread_bound = 4.0
LOG2E = 1.4426950408889634
f32 = jnp.float32
bf16 = jnp.bfloat16


def mm(a, b):
    return lax.dot_general(a, b, (((1,), (0,)), ((), ())), preferred_element_type=f32)


def mm_nt(a, b):
    return lax.dot_general(a, b, (((1,), (1,)), ((), ())), preferred_element_type=f32)


def mm_tn(a, b):
    return lax.dot_general(a, b, (((0,), (0,)), ((), ())), preferred_element_type=f32)


def low_sublanes(shape):
    return lax.broadcasted_iota(jnp.int32, shape, len(shape) - 2) < 4


def to_halves(x):
    rows, cols, ch = x.shape
    n = cols // 8
    v = x.reshape(4, 2, n, 8, ch)
    a, b = v[:, 0], v[:, 1]
    low = low_sublanes(a.shape)
    first = jnp.where(low, a, pltpu.roll(b, 4, 2))
    second = jnp.where(low, pltpu.roll(a, 4, 2), b)
    first = first.transpose(1, 0, 2, 3)
    second = second.transpose(1, 0, 2, 3)
    return jnp.stack([first, second], axis=1).reshape(2 * n, HALF, ch)


def from_halves(x):
    n = x.shape[0] // 2
    ch = x.shape[-1]
    v = x.reshape(n, 2, 4, 8, ch)
    first, second = v[:, 0].transpose(1, 0, 2, 3), v[:, 1].transpose(1, 0, 2, 3)
    low = low_sublanes(first.shape)
    a = jnp.where(low, first, pltpu.roll(second, 4, 2))
    b = jnp.where(low, pltpu.roll(first, 4, 2), second)
    return jnp.stack([a, b], axis=1).reshape(8, 8 * n, ch)


def tile_of(first, second):
    return jnp.stack([first, second], axis=1).reshape(-1, first.shape[-1])


def halves_of(tile):
    v = tile.reshape(-1, 2, HALF, tile.shape[-1])
    return v[:, 0], v[:, 1]


def norm(x):
    c = x - jnp.mean(x, axis=-1, keepdims=True)
    r = lax.rsqrt(jnp.mean(c * c, axis=-1, keepdims=True) + eps_norm)
    return c * r, r


def norm_back(dy, xhat, r, gain):
    along = dy * gain
    inward = r * (
        along
        - jnp.mean(along, axis=-1, keepdims=True)
        - xhat * jnp.mean(along * xhat, axis=-1, keepdims=True)
    )
    return inward, jnp.sum((dy * xhat).reshape(-1, 8, D), axis=0)


ERF = (0.7978697122393114, 0.036392286377165226, -8.78266605765619e-05,
       -3.669342209361701e-05, 1.425004260912749e-06)


def gelu_parts(x):
    square = x * x
    p = ERF[-1]
    for c in ERF[-2::-1]:
        p = p * square + c
    erf = jnp.tanh(x * p)
    half = 0.5 * x
    density = jnp.exp2(square * (-0.5 * LOG2E))
    return half + half * erf, 0.5 + 0.5 * erf + x * density * 0.3989422804014327


def lane_masks():
    lane = lax.broadcasted_iota(jnp.int32, (1, 128), 1)
    return [(lane >= 32 * j) & (lane < 32 * j + 32) for j in range(4)]


def spread_heads(x, masks):
    return jnp.concatenate([x * m for m in masks], axis=0)


def gather_heads(x, masks):
    v = x.reshape(4, 64, 128)
    return jnp.where(masks[0], v[0], jnp.where(masks[1], v[1], jnp.where(masks[2], v[2], v[3])))


def pieces(rows):
    return [slice(r, r + 64) for r in range(0, rows, 64)]


LAG = 4
SLOTS_HELD = 2 * LAG


def staged(count, *stages, beside={}):
    for n in range(count + LAG * (len(stages) - 1)):
        for work in beside.get(n, ()):
            work()
        for late, stage in enumerate(stages):
            if 0 <= n - LAG * late < count:
                stage(n - LAG * late)


def unit_of(n):
    g = n % 2
    rows = slice(64 * (n // 2), 64 * (n // 2) + 64)
    return rows, lambda part: slice(256 * part + 128 * g, 256 * part + 128 * g + 128), g


def attention(w):
    sel = lane_masks()
    ones = [m.astype(f32).astype(bf16) for m in sel]
    scale = HD ** (-0.5) * LOG2E

    def scores(n):
        rows, lanes, g = unit_of(n)
        q, k = w["packed"][rows, lanes(0)], w["packed"][rows, lanes(1)]
        w["s"][n % SLOTS_HELD] = mm_nt(k, spread_heads(q, ones))

    def softmax(n):
        s = w["s"][n % SLOTS_HELD] * scale + w["bias"][n % 2]
        s = jnp.exp2(s - jnp.max(s, axis=0, keepdims=True))
        w["p"][n] = (s * (1.0 / jnp.sum(s, axis=0, keepdims=True))).astype(bf16)

    def values(n):
        rows, lanes, g = unit_of(n)
        found = gather_heads(mm_tn(w["p"][n], w["packed"][rows, lanes(2)]), sel)
        w["ctx"][rows, lanes(0)] = found.astype(bf16)

    staged(w["p"].shape[0], scores, softmax, values)


def attention_back(w, beside):
    sel = lane_masks()
    ones = [m.astype(f32).astype(bf16) for m in sel]
    scale = HD ** (-0.5)

    def upstream(n):
        rows, lanes, g = unit_of(n)
        spread = spread_heads(w["dctx"][rows, lanes(0)], ones)
        w["gp"][rows, lanes(2)] = mm(w["p"][n], spread).astype(bf16)
        w["s"][n % SLOTS_HELD] = mm_nt(w["packed"][rows, lanes(2)], spread)

    def inward(n):
        p = w["p"][n].astype(f32)
        t = p * w["s"][n % SLOTS_HELD]
        ds = t - p * jnp.sum(t, axis=0, keepdims=True)
        w["d_bias"][n % 2] += ds
        w["ds"][n % SLOTS_HELD] = ds.astype(bf16)

    def outer(n):
        rows, lanes, g = unit_of(n)
        ds = w["ds"][n % SLOTS_HELD]
        q, k = w["packed"][rows, lanes(0)], w["packed"][rows, lanes(1)]
        w["gp"][rows, lanes(1)] = (mm(ds, spread_heads(q, ones)) * scale).astype(bf16)
        w["gp"][rows, lanes(0)] = (gather_heads(mm_tn(ds, k), sel) * scale).astype(bf16)

    staged(w["p"].shape[0], upstream, inward, outer, beside=beside)


def halves(rows):
    return slice(0, rows // 2), slice(rows // 2, rows)


def pieces_of(half):
    return [slice(r, r + 64) for r in range(half.start, half.stop, 64)]


def attend(x_ref, w):
    rows = x_ref.shape[0]
    gain1, gain2 = w["gain1"][...], w["gain2"][...]
    scales = {}

    def project(half):
        for at in pieces_of(half):
            w["normed"][at] = (norm(x_ref[at])[0] * gain1).astype(bf16)
        w["packed"][half] = mm(w["normed"][half], w["qkv"][...]).astype(bf16)

    def join(half):
        w["mixed"][half] = x_ref[half] + mm(w["ctx"][half], w["out"][...])
        for at in pieces_of(half):
            xhat, scales[at.start] = norm(w["mixed"][at])
            w["xhat"][at] = xhat
            w["normed2"][at] = (xhat * gain2).astype(bf16)

    project(slice(0, rows))
    attention(w)
    join(slice(0, rows))
    return scales


def block_forward(x_ref, w):
    attend(x_ref, w)
    rows = x_ref.shape[0]

    def start(c):
        w["a"][c % 2] = mm(w["normed2"][...], w["up"][:, 256 * c : 256 * c + 256])

    start(0)
    for c in range(FF // 256):
        cols = slice(256 * c, 256 * c + 256)
        if c < FF // 256 - 1:
            start(c + 1)
        for at in pieces(rows):
            active, slope = gelu_parts(w["a"][c % 2, at])
            w["active"][at, cols] = active.astype(bf16)
            w["slope"][at, cols] = slope.astype(bf16)
        before = w["mixed"] if c == 0 else w["xhat"]
        w["xhat"][...] = before[...] + mm(w["active"][:, cols], w["down"][cols, :])


def block_backward(x_ref, g_ref, w, fused, round_dn):
    rows = x_ref.shape[0]
    gain1, gain2 = w["gain1"][...], w["gain2"][...]
    if fused:
        scales = attend(x_ref, w)
    normed2_t = w["normed2"][...].T
    gb = g_ref[...].astype(bf16)
    gb_t = gb.T

    if fused:
        def start(c):
            cols = slice(256 * c, 256 * c + 256)
            if fused:
                w["a"][c % 2] = mm(w["normed2"][...], w["up"][:, cols])
            w["b"][c % 2] = mm_nt(gb, w["down"][cols, :])

        start(0)
        for c in range(FF // 256):
            cols = slice(256 * c, 256 * c + 256)
            if c < FF // 256 - 1:
                start(c + 1)
            for at in pieces(rows):
                if fused:
                    active, slope = gelu_parts(w["a"][c % 2, at])
                    w["active"][at, cols] = active.astype(bf16)
                else:
                    slope = w["slope"][at, cols].astype(f32)
                w["d_inner"][at, cols] = (w["b"][c % 2, at] * slope).astype(bf16)
            part = mm_nt(w["d_inner"][:, cols], w["up"][:, cols])
            w["dn"][...] = part if c == 0 else w["dn"][...] + part
            w["d_ff"][1024 + 256 * c : 1280 + 256 * c, :] += mm(gb_t, w["active"][:, cols])
            w["d_ff"][cols, :] += mm(normed2_t, w["d_inner"][:, cols])
            if fused:
                w["mixed"][...] += mm(w["active"][:, cols], w["down"][cols, :])
    else:
        for c in range(FF // 256):
            cols = slice(256 * c, 256 * c + 256)
            part = mm_nt(gb, w["down"][cols, :]) * w["slope"][:, cols].astype(f32)
            w["d_inner"][:, cols] = part.astype(bf16)
        w["dn"][...] = mm_nt(w["d_inner"][...], w["up"][...])
        for c in range(FF // 256):
            cols = slice(256 * c, 256 * c + 256)
            w["d_ff"][FF + 256 * c : FF + 256 * c + 256, :] += mm(gb_t, w["active"][:, cols])
            w["d_ff"][cols, :] += mm(normed2_t, w["d_inner"][:, cols])

    def into_heads(half):
        dgain = None
        for at in pieces_of(half):
            xhat, r = (w["xhat"][at], scales[at.start]) if fused else norm(w["mixed"][at])
            inward, part = norm_back(w["dn"][at], xhat, r, gain2)
            dgain = part if dgain is None else dgain + part
            d_mixed = g_ref[at] + inward
            g_ref[at] = d_mixed
            w["g_out"][at] = d_mixed.astype(bf16)
        w["d_small"][8:16, :] += dgain
        w["dctx"][half] = mm_nt(w["g_out"][half], w["out"][...]).astype(bf16)

    def d_out():
        w["d_at"][768:1024, :] += mm_tn(w["ctx"][...], w["g_out"][...])

    def out_of_heads(half):
        gp = w["gp"][half]
        w["dn"][half] = mm_nt(gp, w["qkv"][...])
        normed_t = w["normed"][half].T
        for c in range(3):
            cols = slice(256 * c, 256 * c + 256)
            w["d_at"][cols, :] += mm(normed_t, gp[:, cols])
        dgain = None
        for at in pieces_of(half):
            dn = w["dn"][at]
            if round_dn:
                dn = dn.astype(bf16).astype(f32)
            xhat, r = norm(x_ref[at])
            inward, part = norm_back(dn, xhat, r, gain1)
            dgain = part if dgain is None else dgain + part
            g_ref[at] = g_ref[at] + inward
        w["d_small"][0:8, :] += dgain

    one, two = halves(rows)
    units = rows // 64
    into_heads(one)
    beside = {2: [functools.partial(into_heads, two)], units: [d_out]}
    attention_back(w, beside)
    out_of_heads(slice(0, rows))


LIMIT = 56 * 1024 * 1024


def cost(us):
    return pl.CostEstimate(flops=int(us * 1.1e9), bytes_accessed=int(us * 3.6e6), transcendentals=0)


ANY = pl.BlockSpec(memory_space=pl.ANY)


def params(n):
    return pltpu.CompilerParams(
        dimension_semantics=("arbitrary",) * n, vmem_limit_bytes=LIMIT
    )


def latent_head(state, wl):
    center = mm_nt(state, wl[:ZC])
    squash = jnp.tanh(mm_nt(state, wl[ZC:]) * (1.0 / spread_bound))
    return center, squash, jnp.exp((0.5 * spread_bound) * squash)


def lanes_of_patch(width, back):
    lane = lax.broadcasted_iota(jnp.int32, (4 * 256, 4 * 64), 0)
    at = lax.broadcasted_iota(jnp.int32, (4 * 256, 4 * 64), 1)
    row, col = query_place(at & 63)
    want = 16 * (7 - row) + 7 - col if back else 16 * row + col
    return jnp.where(lane == (at >> 6) * 256 + want, 1.0, 0.0).astype(bf16)


def query_place(q):
    return (q >> 2) & 7, ((q >> 5) << 2) + (q & 3)


def table_lanes(back):
    a = lax.broadcasted_iota(jnp.int32, (256, 256), 0)
    b = lax.broadcasted_iota(jnp.int32, (256, 256), 1)
    side = 2 * WIN - 1
    if back:
        mirrored = 16 * (14 - (a >> 4)) + 14 - (a & 15)
        hit = ((a & 15) < side) & ((a >> 4) < side) & (b == (14 - (a >> 4)) * side + 14 - (a & 15))
    else:
        hit = ((b & 15) < side) & ((b >> 4) < side) & (a == (b >> 4) * side + (b & 15))
    return jnp.where(hit, 1.0, 0.0).astype(bf16)


def exactly(a, onehot):
    total = None
    for _ in range(3):
        term = a.astype(bf16)
        a = a - term.astype(f32)
        part = mm(term, onehot)
        total = part if total is None else total + part
    return total


def expand_bias(tables):
    spread = exactly(tables, table_lanes(False))
    choose = lanes_of_patch(64, False)
    out = []
    for n in range(4):
        heads = []
        for h in range(4 * n, 4 * n + 4):
            one = jnp.broadcast_to(spread[h : h + 1], (8, 256))
            heads.append(
                jnp.concatenate(
                    [
                        pltpu.roll(one, (16 * r + 137) % 256, 1, stride=1, stride_axis=0)
                        for r in range(WIN)
                    ]
                )
            )
        rows = exactly(jnp.concatenate(heads, axis=1), choose)
        out.append(to_halves(rows.reshape(WIN, WIN, 256)).reshape(64, 256))
    return out


def reduce_bias(grads):
    rows = from_halves(grads.reshape(2, HALF, 256)).reshape(64, 256).astype(bf16)
    lanes = lax.dot_general(
        rows, lanes_of_patch(64, True), (((1,), (1,)), ((), ())), preferred_element_type=f32
    )
    out = []
    for h in range(4):
        total = None
        for r in range(WIN):
            one = pltpu.roll(
                lanes[8 * r : 8 * r + 8, 256 * h : 256 * h + 256], 16 * r, 1, stride=1, stride_axis=0
            )
            total = one if total is None else total + one
        out.append(jnp.sum(total, axis=0, keepdims=True))
    return jnp.concatenate(out)


def prep_kernel(samples, cot, state, wl, tables, cot_h, state_h, kl, bias):
    @pl.when(pl.program_id(0) == 0)
    def _():
        padded = jnp.concatenate(
            [tables[...], jnp.zeros((16, 256 - tables.shape[1]), f32)], axis=1
        )
        for n, part in enumerate(expand_bias(padded * LOG2E)):
            bias[n // 2, n % 2] = part

    live = samples[0]
    for s in range(SLOTS):
        factor = jnp.where(s < live, 1.0, 0.0).astype(f32)
        cot_h[:, s] = (to_halves(cot[0, s].astype(f32)) * factor).astype(bf16)
    st = to_halves(state[0].astype(f32)).reshape(4, 64, D).astype(bf16)
    state_h[:, 0] = st
    center, squash, sigma = latent_head(st.reshape(4 * 64, D), wl[...])
    terms = 0.5 * (center * center + sigma * sigma - 1.0 - spread_bound * squash)

    @pl.when(pl.program_id(0) == 0)
    def _():
        kl[...] = jnp.zeros(kl.shape, f32)

    kl[:, :ZC] += jnp.sum(terms.reshape(-1, 8, ZC), axis=0)


def prep(samples, cot, state, wl, tables):
    bands = state.shape[1] // WIN
    nw = state.shape[2] // WIN
    return pl.pallas_call(
        prep_kernel,
        grid=(bands,),
        in_specs=[
            pl.BlockSpec(memory_space=pltpu.SMEM),
            pl.BlockSpec((1, SLOTS, WIN, nw * WIN, D), lambda i: (0, 0, i, 0, 0)),
            pl.BlockSpec((1, WIN, nw * WIN, D), lambda i: (0, i, 0, 0)),
            full(wl),
            full(tables),
        ],
        out_specs=[
            pl.BlockSpec((2 * nw, SLOTS, HALF, D), lambda i: (0, i, 0, 0)),
            pl.BlockSpec((nw, 1, 64, D), lambda i: (0, i, 0, 0)),
            pl.BlockSpec((8, D), lambda i: (0, 0)),
            pl.BlockSpec((2, 2, 64, 256), lambda i: (0, 0, 0, 0)),
        ],
        out_shape=[
            jax.ShapeDtypeStruct((2 * nw, bands * SLOTS, HALF, D), bf16),
            jax.ShapeDtypeStruct((nw, bands, 64, D), bf16),
            jax.ShapeDtypeStruct((8, D), f32),
            jax.ShapeDtypeStruct((2, 2, 64, 256), f32),
        ],
        compiler_params=params(1),
        cost_estimate=cost(4),
    )(samples, cot, state, wl, tables)


def noise_of(block):
    bands = block.shape[1] // WIN
    return jnp.stack(
        [
            jnp.stack(
                [to_halves(block[s, WIN * b : WIN * b + WIN]).reshape(64, ZC) for s in range(SLOTS)]
            )
            for b in range(bands)
        ]
    )


def noise_spec(bands, skip):
    return pl.BlockSpec((1, SLOTS, bands * WIN, WIN, ZC), lambda j: (0, 0, 0, j + skip, 0))


def cell_forward(state, noise, wl, ws, wn):
    bands = state.shape[0]
    flat = state.reshape(bands * 64, D)
    over = lambda x: x.reshape(bands, 1, 64, x.shape[-1])
    center, squash, sigma = latent_head(flat, wl)
    latent = (over(center) + over(sigma) * noise).reshape(-1, ZC).astype(bf16)
    mix = mm(latent, wn)
    half = 0.5 * (over(mm(flat, ws)) + mix[:, :D].reshape(bands, SLOTS, 64, D))
    gate = 0.5 + 0.5 * jnp.tanh(half)
    cand = jnp.tanh(mix[:, D:].reshape(bands, SLOTS, 64, D))
    hidden = gate * over(flat.astype(f32)) + (1.0 - gate) * cand
    return hidden.reshape(-1, D), center, squash, sigma, latent, gate, cand


def full(a):
    return pl.BlockSpec(a.shape, lambda *_: (0,) * a.ndim)


def block_specs(k):
    return [
        pl.BlockSpec((2, D), lambda *_: (0, 0)),
        pl.BlockSpec((1, D, 3 * D), lambda *_: (k, 0, 0)),
        pl.BlockSpec((1, 2, 64, 256), lambda *_: (k, 0, 0, 0)),
        pl.BlockSpec((1, D, D), lambda *_: (k, 0, 0)),
        pl.BlockSpec((2, D), lambda *_: (0, 0)),
        pl.BlockSpec((1, D, FF), lambda *_: (k, 0, 0)),
        pl.BlockSpec((1, FF, D), lambda *_: (k, 0, 0)),
    ]


NAMES = ("gain1", "qkv", "bias", "out", "gain2", "up", "down")


def named(refs, k):
    return {
        n: r.at[k : k + 1] if n.startswith("gain") else r.at[0] for n, r in zip(NAMES, refs)
    }


def saved_refs(rows):
    return [
        ("normed", (rows, D), bf16),
        ("packed", (rows, 3 * D), bf16),
        ("p", (rows // 32, 64, 256), bf16),
        ("ctx", (rows, D), bf16),
        ("mixed", (rows, D), f32),
        ("normed2", (rows, D), bf16),
        ("active", (rows, FF), bf16),
        ("slope", (rows, FF), bf16),
    ]


def forward_refs(rows):
    return [
        ("x", (rows, D), f32),
        ("s", (SLOTS_HELD, 64, 256), f32),
        ("xhat", (rows, D), f32),
        ("a", (2, rows, 256), f32),
    ]


def backward_refs(rows):
    return [
        ("x", (rows, D), f32),
        ("g", (rows, D), f32),
        ("s", (SLOTS_HELD, 64, 256), f32),
        ("b", (2, rows, 256), f32),
        ("d_inner", (rows, FF), bf16),
        ("dn", (rows, D), f32),
        ("g_out", (rows, D), bf16),
        ("dctx", (rows, D), bf16),
        ("ds", (SLOTS_HELD, 64, 256), bf16),
        ("gp", (rows, 3 * D), bf16),
    ]


def both_refs(rows):
    return saved_refs(rows) + forward_refs(rows)[2:] + backward_refs(rows)


def scratch(refs):
    return [pltpu.VMEM(shape, dtype) for _, shape, dtype in refs]


def names(refs):
    return [name for name, _, _ in refs]


def saved_specs(rows, skip):
    return [
        pl.BlockSpec((1,) + shape, lambda j, n=len(shape): (j + skip,) + (0,) * n)
        for _, shape, _ in saved_refs(rows)
    ]


N_SAVED, N_BACK, N_BOTH = len(saved_refs(64)), len(backward_refs(64)), len(both_refs(64))


GRAD_SHAPES = [(2048, D), (1024, D), (16, D), (2, 64, 256)]
GRAD_NAMES = ("d_ff", "d_at", "d_small", "d_bias")
GRAD_SCRATCH = [pltpu.VMEM(s, f32) for s in GRAD_SHAPES[:2]]
SMALL_SPECS = [pl.BlockSpec(s, lambda *_, n=len(s): (0,) * n) for s in GRAD_SHAPES[2:]]
SMALL_OUTS = [jax.ShapeDtypeStruct(s, f32) for s in GRAD_SHAPES[2:]]

ROWS_BLOCK = 3072
ROWS_CELL = 512
CHAINS = (((0, (ROWS_BLOCK + ROWS_CELL) // 2),), ((0, ROWS_BLOCK // 2),))
ALL_CHAINS = [(k, chain) for k in range(2) for chain in CHAINS[k]]


def first_kernel(state, noise, cot, wl, ws, wn, *rest, lead):
    w = named(rest[:7], 0)
    rest = rest[7:] if lead else rest[7 + 1 + N_SAVED :]
    h1, rest = rest[0], rest[1:]
    w.update((n, r.at[0]) for n, r in zip(names(saved_refs(64)), rest))
    rest = rest[N_SAVED:]
    if lead:
        halo, rest = rest[0], rest[1:]
    w.update(zip(names(forward_refs(64)), rest))
    w["x"][...] = cell_forward(state[0], noise_of(noise[0]), wl[...], ws[...], wn[...])[0]
    block_forward(w["x"], w)
    a, b = halves_of(w["xhat"][...])
    h1[0, 0] = a
    h1[0, 1] = b
    if lead:
        halo[0] = a.astype(bf16)
        halo[1] = cot[0]


def first(state_h, noise, cot_h, cell_w, block_w, before=None):
    nw, bands = state_h.shape[:2]
    half = (bands * SLOTS, HALF, D)
    rows = 64 * bands * SLOTS
    lead = before is None
    skip = 0 if lead else 1
    specs = [pl.BlockSpec((1, 2) + half, lambda j: (j + skip, 0, 0, 0, 0))] + saved_specs(rows, skip)
    shapes = [jax.ShapeDtypeStruct((nw, 2) + half, f32)] + [
        jax.ShapeDtypeStruct((nw,) + shape, dtype) for _, shape, dtype in saved_refs(rows)
    ]
    inputs = [state_h, noise, cot_h, *cell_w, *block_w]
    in_specs = [
        pl.BlockSpec((1, bands, 64, D), lambda j: (j + skip, 0, 0, 0)),
        noise_spec(bands, skip),
        pl.BlockSpec((1,) + half, lambda j: (0, 0, 0, 0)),
    ]
    in_specs += [full(a) for a in cell_w] + block_specs(0)
    aliases = {}
    if lead:
        specs.append(pl.BlockSpec((2,) + half, lambda j: (0, 0, 0, 0)))
        shapes.append(jax.ShapeDtypeStruct((2,) + half, bf16))
    else:
        aliases = {len(inputs) + n: n for n in range(len(before))}
        inputs += before
        in_specs += [pl.BlockSpec(memory_space=pl.ANY)] * len(before)
    return pl.pallas_call(
        functools.partial(first_kernel, lead=lead),
        grid=(1 if lead else nw - 1,),
        in_specs=in_specs,
        out_specs=specs,
        out_shape=shapes,
        input_output_aliases=aliases,
        scratch_shapes=scratch(forward_refs(rows)),
        compiler_params=params(1),
        cost_estimate=cost(6 if lead else 16),
    )(*inputs)


def zero_at_start(refs):
    @pl.when(pl.program_id(0) == 0)
    def _():
        for r in refs:
            r[...] = jnp.zeros(r.shape, r.dtype)


def halves_out(keep, send, parts):
    size = keep.shape[0]
    core = lax.axis_index("batch") & 1

    def write(low, high):
        first = 0
        for ref in parts:
            rows = ref.shape[0]
            cut = min(max(size - first, 0), rows)
            if cut:
                low[first : first + cut] = ref[:cut].astype(bf16)
            if cut < rows:
                high[first + cut - size : first + rows - size] = ref[cut:rows].astype(bf16)
            first += rows

    @pl.when(core == 0)
    def _():
        write(keep, send)

    @pl.when(core != 0)
    def _():
        write(send, keep)


def at_end():
    return pl.program_id(0) == pl.num_programs(0) - 1


def second_kernel(samples, ha, hb, ca, cb, *rest, lead):
    w = named(rest[:7], 1)
    grads1, small1, bias1 = (None,) * 3 if lead else rest[7:10]
    rest = rest[7:] if lead else rest[12:]
    act, dh, d_small, d_bias = rest[:4]
    if lead:
        packed_grads, back_halo = rest[4:6]
    else:
        keep, send = rest[4:6]
    rest = rest[6:]
    w.update(zip(names(both_refs(64)), rest))
    grads = rest[N_BOTH : N_BOTH + 2] + (d_small, d_bias)
    w.update(zip(GRAD_NAMES, grads))
    if lead:
        zero_at_start(grads)
    else:

        @pl.when(pl.program_id(0) == 0)
        def _():
            grads[0][...] = grads1[:2048].astype(f32)
            grads[1][...] = grads1[2048:].astype(f32)
            d_small[...] = small1[...]
            d_bias[...] = bias1[...]

    w["x"][...] = tile_of(ha[0, 0], hb[0].astype(f32) if lead else hb[0, 0])
    w["g"][...] = tile_of(ca[0].astype(f32), cb[0].astype(f32))
    block_backward(w["x"], w["g"], w, True, True)
    live = samples[0]
    a, b = halves_of(w["mixed"][...])
    factor = jnp.concatenate(
        [jnp.where(s % SLOTS < live, 1.0, 0.0) * jnp.ones((1, 1, D), f32) for s in range(a.shape[0])]
    )
    a, b = (a * factor).astype(bf16), (b * factor).astype(bf16)
    da, db = halves_of(w["g"][...])
    act[0, 0] = a
    act[0, 1] = b
    dh[0, 0] = da
    dh[0, 1] = db
    if lead:
        back_halo[0] = db.astype(bf16)
        back_halo[1] = b
        packed_grads[:2048] = grads[0][...].astype(bf16)
        packed_grads[2048:] = grads[1][...].astype(bf16)
    else:

        @pl.when(at_end())
        def _():
            halves_out(keep, send, [grads[0], grads[1]])


def second(samples, h1, cot_h, block_w, halo=None, before=None):
    nw = h1.shape[0]
    half = h1.shape[2:]
    lead = before is None
    if lead:
        tile, other = (lambda j: nw - 1), halo
        wide = [pl.BlockSpec((1,) + half, lambda j, n=n: (n, 0, 0, 0)) for n in range(2)]
    else:
        tile, other = (lambda j: j), cot_h
        wide = [
            pl.BlockSpec((1, 1) + half, lambda j: (j + 1, 0, 0, 0, 0)),
            pl.BlockSpec((1,) + half, lambda j: (2 * j + 2, 0, 0, 0)),
        ]
    inputs = [samples, h1, halo if lead else h1, cot_h, other, *block_w]
    in_specs = [
        pl.BlockSpec(memory_space=pltpu.SMEM),
        pl.BlockSpec((1, 1) + half, lambda j: (tile(j), 1, 0, 0, 0)),
        wide[0],
        pl.BlockSpec((1,) + half, lambda j: (2 * tile(j) + 1, 0, 0, 0)),
        wide[1],
    ]
    in_specs += block_specs(1)
    out_specs = [
        pl.BlockSpec((1, 2) + half, lambda j: (tile(j), 0, 0, 0, 0)),
        pl.BlockSpec((1, 2) + half, lambda j: (tile(j), 0, 0, 0, 0)),
    ] + SMALL_SPECS
    out_shape = [
        jax.ShapeDtypeStruct((nw, 2) + half, bf16),
        jax.ShapeDtypeStruct((nw, 2) + half, f32),
    ] + SMALL_OUTS
    aliases = {}
    if lead:
        out_specs.append(pl.BlockSpec((ROWS_BLOCK, D), lambda *_: (0, 0)))
        out_specs.append(pl.BlockSpec((2,) + half, lambda j: (0, 0, 0, 0)))
        out_shape.append(jax.ShapeDtypeStruct((ROWS_BLOCK, D), bf16))
        out_shape.append(jax.ShapeDtypeStruct((2,) + half, bf16))
    else:
        out_specs += [pl.BlockSpec((ROWS_BLOCK // 2, D), lambda *_: (0, 0))] * 2
        out_shape += [jax.ShapeDtypeStruct((ROWS_BLOCK // 2, D), bf16)] * 2
        act, dh, small1, bias1, grads1 = before
        sums = [grads1, small1, bias1]
        aliases = {len(inputs) + 3: 0, len(inputs) + 4: 1}
        inputs += sums + [act, dh]
        in_specs += [full(a) for a in sums] + [pl.BlockSpec(memory_space=pl.ANY)] * 2
    return pl.pallas_call(
        functools.partial(second_kernel, lead=lead),
        grid=(1 if lead else nw - 1,),
        in_specs=in_specs,
        out_specs=out_specs,
        out_shape=out_shape,
        input_output_aliases=aliases,
        scratch_shapes=scratch(both_refs(64 * half[0])) + GRAD_SCRATCH,
        compiler_params=params(1),
        cost_estimate=cost(9 if lead else 24),
    )(*inputs)


CELL_SHAPES = [(D, D), (2 * ZC, D), (2 * ZC, D), (2 * ZC, D)]


def divergence_parts(center, squash, sigma):
    return center.astype(bf16), (
        0.5 * (sigma * sigma - 1.0) * (1.0 - squash * squash)
    ).astype(bf16)


def third_kernel(state, noise, da, db, dhalo, small1, bias1, kl, wl, ws, wn, *rest):
    w = named(rest[:7], 0)
    w.update((n, r.at[0]) for n, r in zip(names(saved_refs(64)), rest[7:]))
    rest = rest[N_SAVED:]
    sg, keep, send = rest[7:10]
    w.update(zip(names(backward_refs(64)), rest[10:]))
    grads = rest[10 + N_BACK : 14 + N_BACK]
    d_ws, d_wn, d_wl, d_kl, d_rest = rest[14 + N_BACK :]
    cell_grads = (d_ws, d_wn, d_wl, d_kl)
    w.update(zip(GRAD_NAMES, grads))
    zero_at_start(grads + cell_grads)
    st = state[0]
    nz = noise_of(noise[0])
    bands = st.shape[0]
    hidden, center, squash, sigma, latent, gate, cand = cell_forward(
        st, nz, wl[...], ws[...], wn[...]
    )
    da_v = jnp.where(pl.program_id(0) == 0, dhalo[0].astype(f32), da[0, 0])
    w["x"][...] = hidden
    w["g"][...] = tile_of(da_v, db[0, 0])
    block_backward(w["x"], w["g"], w, False, False)
    dc = w["g"][...]
    over = lambda x: x.reshape(bands, 1, 64, x.shape[-1])
    flat = st.reshape(bands * 64, D)
    dc = dc.reshape(bands, SLOTS, 64, D)
    rest_gate = 1.0 - gate
    d_pre = dc * (over(flat.astype(f32)) - cand) * gate * rest_gate
    d_cand = dc * rest_gate * (1.0 - cand * cand)
    direct = jnp.sum(dc * gate, axis=1).reshape(-1, D)
    g_gate = jnp.sum(d_pre, axis=1).reshape(-1, D).astype(bf16)
    d_ws[...] += mm_tn(flat, g_gate)
    pre = d_pre.reshape(-1, D).astype(bf16)
    cnd = d_cand.reshape(-1, D).astype(bf16)
    d_wn[:ZC] += mm_tn(latent, pre)
    d_wn[ZC:] += mm_tn(latent, cnd)
    d_lat = mm_nt(pre, wn[:, :D]) + mm_nt(cnd, wn[:, D:])
    d_lat = d_lat.reshape(bands, SLOTS, 64, ZC)
    d_center = jnp.sum(d_lat, axis=1).reshape(-1, ZC)
    d_raw = jnp.sum(d_lat * nz, axis=1).reshape(-1, ZC) * 0.5 * sigma * (1.0 - squash * squash)
    d_center, d_raw = d_center.astype(bf16), d_raw.astype(bf16)
    d_wl[:ZC] += mm_tn(d_center, flat)
    d_wl[ZC:] += mm_tn(d_raw, flat)
    kl_center, kl_raw = divergence_parts(center, squash, sigma)
    d_kl[:ZC] += mm_tn(kl_center, flat)
    d_kl[ZC:] += mm_tn(kl_raw, flat)
    total = direct + mm_nt(g_gate, ws[...])
    total = total + mm(d_center, wl[:ZC]) + mm(d_raw, wl[ZC:])
    for b in range(bands):
        sg[0, WIN * b : WIN * b + WIN] = from_halves(
            total[64 * b : 64 * b + 64].reshape(2, HALF, D)
        )

    @pl.when(at_end())
    def _():
        d_small, d_bias = grads[2:]
        d_rest[:16] = jnp.concatenate(
            [reduce_bias(b) for b in (d_bias[0], d_bias[1], bias1[0], bias1[1])]
        )
        total = lambda x: jnp.sum(x, axis=0, keepdims=True)
        d_rest[16:] = jnp.concatenate(
            [total(d_small[:8]), total(d_small[8:]), total(small1[:8]), total(small1[8:])]
            + [total(kl[...]), jnp.zeros((43, D), f32)]
        )
        halves_out(keep, send, [grads[0], grads[1], *cell_grads, d_rest])


def third(state_h, noise, dh, halo, small1, bias1, kl, cell_w, block_w, saved):
    nw, bands = state_h.shape[:2]
    rows = 64 * bands * SLOTS
    half = dh.shape[2:]
    return pl.pallas_call(
        third_kernel,
        grid=(nw,),
        in_specs=[
            pl.BlockSpec((1, bands, 64, D), lambda j: (j, 0, 0, 0)),
            noise_spec(bands, 0),
            pl.BlockSpec((1, 1) + half, lambda j: (jnp.maximum(j - 1, 0), 1, 0, 0, 0)),
            pl.BlockSpec((1, 1) + half, lambda j: (j, 0, 0, 0, 0)),
            pl.BlockSpec((1,) + half, lambda j: (0, 0, 0, 0)),
        ]
        + [full(a) for a in (small1, bias1, kl)]
        + [full(a) for a in cell_w]
        + block_specs(0)
        + saved_specs(rows, 0),
        out_specs=[pl.BlockSpec((1, bands * WIN, WIN, D), lambda j: (0, 0, j, 0))]
        + [pl.BlockSpec(((ROWS_BLOCK + ROWS_CELL) // 2, D), lambda *_: (0, 0))] * 2,
        out_shape=[jax.ShapeDtypeStruct((1, bands * WIN, nw * WIN, D), f32)]
        + [jax.ShapeDtypeStruct(((ROWS_BLOCK + ROWS_CELL) // 2, D), bf16)] * 2,
        scratch_shapes=scratch(backward_refs(rows))
        + [pltpu.VMEM(s, f32) for s in GRAD_SHAPES + CELL_SHAPES + [(64, D)]],
        compiler_params=params(1),
        cost_estimate=cost(26),
    )(state_h, noise, dh, dh, halo, small1, bias1, kl, *cell_w, *block_w, *saved)


def place_kernel(act, halo, out):
    nw = act.shape[0]
    for s in range(SLOTS):
        halves = [halo[0, s].astype(f32)]
        for j in range(nw):
            halves.append(act[j, 0, s].astype(f32))
            if j < nw - 1:
                halves.append(act[j, 1, s].astype(f32))
        out[0, s] = from_halves(jnp.stack(halves)).astype(bf16)


def place(act, halo):
    nw = act.shape[0]
    bands = act.shape[2] // SLOTS
    return pl.pallas_call(
        place_kernel,
        grid=(bands,),
        in_specs=[
            pl.BlockSpec((nw, 2, SLOTS, HALF, D), lambda i: (0, 0, i, 0, 0)),
            pl.BlockSpec((1, SLOTS, HALF, D), lambda i: (1, i, 0, 0)),
        ],
        out_specs=pl.BlockSpec((1, SLOTS, WIN, nw * WIN, D), lambda i: (0, 0, i, 0, 0)),
        out_shape=jax.ShapeDtypeStruct((1, SLOTS, bands * WIN, nw * WIN, D), bf16),
        compiler_params=params(1),
        cost_estimate=cost(4),
    )(act, halo)


def finish_kernel(
    order, scalars, state, part, wl, *rest, cells, devices,
):
    n_blocks = 2 * len(ALL_CHAINS)
    blocks, rest = rest[:n_blocks], rest[n_blocks:]
    sg, div, o_wl, o_ws, o_wn, o_gain1, o_table, o_gain2, *large = rest[:12]
    sums, held = rest[12 : 12 + len(ALL_CHAINS)], rest[12 + len(ALL_CHAINS) : -6]
    o_qkv, o_out, o_up, o_down = stage = rest[-6:-2]
    in_sems, out_sems = rest[-2:]
    arrive = [pltpu.make_async_copy(b, h, in_sems.at[n]) for n, (b, h) in enumerate(zip(blocks, held))]
    leave = [
        [pltpu.make_async_copy(a.at[k], b.at[k], out_sems.at[4 * k + n]) for n, (a, b) in enumerate(zip(stage, large))]
        for k in range(2)
    ]
    for copy in arrive:
        copy.start()

    def assemble(k):
        for chain, (where, _) in enumerate(ALL_CHAINS):
            if where != k:
                continue
            whole = sums[chain]
            n = devices // 4
            count = whole.shape[0] // (2 * n)
            for at in range(2):
                arrive[2 * chain + at].wait()
                block = held[2 * chain + at]
                for i in range(n):
                    to = order[2 * chain, at] * n + jnp.bitwise_xor(order[2 * chain + 1, at], i)
                    whole[pl.ds(pl.multiple_of(to * count, 16), count)] = block[
                        count * i : count * i + count
                    ]

    def rows_of(k, first, count):
        size = CHAINS[k][-1][1]
        side, first = divmod(first, size)
        for (where, (low, high)), whole in zip(ALL_CHAINS, sums):
            if where == k and low <= first < high:
                first += side * whole.shape[0] // 2 - low
                return whole[first : first + count]

    def unpack(k):
        assemble(k)
        for c in range(3):
            cols = slice(256 * c, 256 * c + 256)
            o_qkv[k, :, cols] = rows_of(k, 2 * FF + 256 * c, 256).astype(f32)
        o_out[k] = rows_of(k, 2816, 256).astype(f32)
        leave[k][0].start()
        leave[k][1].start()
        for c in range(FF // 256):
            cols = slice(256 * c, 256 * c + 256)
            o_up[k, :, cols] = rows_of(k, 256 * c, 256).astype(f32)
        leave[k][2].start()
        for c in range(FF // 256):
            cols = slice(256 * c, 256 * c + 256)
            o_down[k, cols] = rows_of(k, FF + 256 * c, 256).astype(f32).T
        leave[k][3].start()

    unpack(0)
    unpack(1)
    cell_rows = lambda first, count: rows_of(0, ROWS_BLOCK + first, count)
    small = cell_rows(464, 16).astype(f32)
    kl_mean = small[4:5, :ZC] * (1.0 / cells)
    beta, floor = scalars[0], scalars[1]
    excess = sharpness * (kl_mean - floor)
    soft = jnp.maximum(excess, 0.0) + jnp.log(1.0 + jnp.exp(-jnp.abs(excess)))
    div[...] = beta * jnp.mean(floor + soft * (1.0 / sharpness), axis=-1, keepdims=True)
    amt = beta * jax.nn.sigmoid(excess) * (1.0 / (ZC * cells))

    rows = state.shape[1] * state.shape[2]
    center, squash, sigma = latent_head(state[0].reshape(rows, D), wl[...])
    kl_center, kl_raw = divergence_parts(center, squash, sigma)
    g_center = (kl_center.astype(f32) * amt).astype(bf16)
    g_raw = (kl_raw.astype(f32) * amt).astype(bf16)
    add = mm(g_center, wl[:ZC]) + mm(g_raw, wl[ZC:])
    sg[0] = part[0] + add.reshape(state.shape[1:])

    o_ws[...] = cell_rows(0, 256).astype(f32)
    wn = cell_rows(256, 64).astype(f32)
    o_wn[:, :D] = wn[:ZC]
    o_wn[:, D:] = wn[ZC:]
    at = lambda axis: lax.broadcasted_iota(jnp.int32, (ZC, ZC), axis)
    column = jnp.sum(jnp.where(at(0) == at(1), amt, 0.0), axis=1, keepdims=True)
    for h in range(2):
        o_wl[ZC * h : ZC * h + ZC] = (
            cell_rows(320 + ZC * h, ZC).astype(f32) + cell_rows(384 + ZC * h, ZC).astype(f32) * column
        )
    table = mm(cell_rows(448, 16), table_lanes(True))
    o_table[0] = table[:HEADS, : (2 * WIN - 1) ** 2]
    o_table[1] = table[HEADS:, : (2 * WIN - 1) ** 2]
    for k in range(2):
        o_gain1[k : k + 1] = small[2 * k : 2 * k + 1]
        o_gain2[k : k + 1] = small[2 * k + 1 : 2 * k + 2]
    for k in range(2):
        for copy in leave[k]:
            copy.wait()


def finish(order, scalars, state, part, wl, *blocks, cells, devices):
    small = [
        part.shape, (1, 1), (2 * ZC, D), (D, D), (ZC, 2 * D), (2, D),
        (2, HEADS, (2 * WIN - 1) ** 2), (2, D),
    ]
    large = [(2, D, 3 * D), (2, D, D), (2, D, FF), (2, FF, D)]
    smem, vmem = pl.BlockSpec(memory_space=pltpu.SMEM), pl.BlockSpec(memory_space=pltpu.VMEM)
    sg, div, wl, ws, wn, gain1, table, gain2, qkv, out, up, down = pl.pallas_call(
        functools.partial(finish_kernel, cells=cells, devices=devices),
        in_specs=[smem, smem] + [vmem] * 3 + [ANY] * len(blocks),
        out_specs=[vmem] * len(small) + [ANY] * len(large),
        out_shape=[jax.ShapeDtypeStruct(o, f32) for o in small + large],
        scratch_shapes=[pltpu.VMEM((2 * b.shape[0], D), bf16) for b in blocks[::2]]
        + [pltpu.VMEM(b.shape, bf16) for b in blocks]
        + [pltpu.VMEM(o, f32) for o in large]
        + [pltpu.SemaphoreType.DMA((len(blocks),)), pltpu.SemaphoreType.DMA((8,))],
        compiler_params=pltpu.CompilerParams(vmem_limit_bytes=40 * 1024 * 1024),
    )(order, scalars, state, part, wl, *blocks)
    return sg, div, wl, ws, wn, gain1, qkv, table, out, gain2, up, down


def shift_from(block, distance):
    n = lax.axis_size("lon")
    return lax.ppermute(block, "lon", [((i + distance) % n, i) for i in range(n)])


class Summation:
    def __init__(self, turn):
        n_lon, n_batch = lax.axis_size("lon"), lax.axis_size("batch")
        self.n = n = n_lon * n_batch
        me = lax.axis_index("lon") * n_batch + lax.axis_index("batch")
        bits = [1 << i for i in range(1, n.bit_length() - 1)]
        axes, rest = [bits[0], bits[-1]] + bits[1:2], bits[2:-1]
        axes = axes[: len(bits)]
        turned = lambda by: axes[by % len(axes) :] + axes[: by % len(axes)] + rest
        self.pairs = list(zip(turned(turn), turned(turn + 1)))
        self.core = me & 1
        self.bits = [self.core] + self.bits_of(me)
        places = [self.place(self.bits[1:-1]), self.place(self.bits_of(me ^ 1)[:-1])]
        self.order = jnp.stack([jnp.stack([self.core, 1 - self.core]), jnp.stack(places)])

    def bits_of(self, device):
        return [
            (jnp.bitwise_and(device, jnp.where(device & 1 == 0, a, b)) != 0).astype(jnp.int32)
            for a, b in self.pairs
        ]

    def place(self, bits):
        at = jnp.zeros((), jnp.int32)
        for bit in bits:
            at = 2 * at + bit
        return at

    def swap(self, block, step):
        pair = self.pairs[step - 1] if step else (1, 1)
        return lax.ppermute(
            block, ("lon", "batch"), [(i, i ^ pair[i & 1]) for i in range(self.n)]
        )

    def begin(self, keep, send):
        return self.add(keep, self.swap(send, 0))

    def add(self, a, b):
        return (a.astype(f32) + b.astype(f32)).astype(bf16)

    def plan(self):
        last = len(self.bits) - 1
        down, up = range(1, last), range(last - 1, 0, -1)
        return [("halve", n) for n in down] + [("both", last)] + [("double", n) for n in up]

    def pad(self, total):
        return jnp.pad(total, ((0, -total.shape[0] % (4 * self.n)), (0, 0)))

    def half(self, total, at):
        size = total.shape[0] // 2
        return lax.dynamic_slice_in_dim(total, at * size, size, 0)

    def exchange(self, total, kind, step):
        if kind == "halve":
            total = self.half(total, 1 - self.bits[step])
        return self.swap(total, step)

    def join(self, total, got, kind, step):
        if kind == "halve":
            total = self.half(total, self.bits[step])
        return jnp.concatenate([total, got]) if kind == "double" else self.add(total, got)


def in_turn(adders, totals, beside):
    tie = lax.optimization_barrier
    plain = [adder.pad(total) for adder, total in zip(adders, totals)]
    tied = list(plain)
    for n, move in enumerate(adders[0].plan()):
        got = [adder.exchange(total, *move) for adder, total in zip(adders, plain)]
        if n == 0:
            got[0], *beside = tie((got[0], *beside))
        plain[0] = adders[0].join(tied[0], got[0], *move)
        got[1], tied[0] = tie((got[1], plain[0]))
        plain[1] = tied[1] = adders[1].join(tied[1], got[1], *move)
    blocks = []
    for adder, total in zip(adders, plain):
        blocks += [total, adder.swap(total, 0)]
    return blocks, beside


def body(
    state,
    noise,
    samples,
    step,
    kl_weight,
    floor,
    latent_weight,
    state_weight,
    noise_weight,
    attention_gain,
    query_key_value,
    offset_bias,
    output_weight,
    feedforward_gain,
    up_weight,
    down_weight,
    cotangent,
):
    items, height, breadth, width = state.shape
    cells = items * height * breadth * lax.axis_size("lon") * lax.axis_size("batch")
    cell_w = (latent_weight.T, state_weight, noise_weight)
    cot_h, state_h, kl, bias = prep(
        samples, cotangent, state, cell_w[0], offset_bias.reshape(2 * HEADS, -1)
    )
    block_w = (
        attention_gain,
        query_key_value,
        bias,
        output_weight,
        feedforward_gain,
        up_weight,
        down_weight,
    )
    adders = [Summation(turn) for turn in range(len(ALL_CHAINS))]
    add_up = adders[0]
    order = jnp.concatenate([adder.order for adder in adders])
    beta = kl_weight * (step + 1).astype(f32) / WARM
    scalars = jnp.stack([beta, floor])
    *ahead, halo = first(state_h, noise, cot_h, cell_w, block_w)
    halo = shift_from(halo, 1)
    h1, *saved = first(state_h, noise, cot_h, cell_w, block_w, ahead)
    *ahead, halo = second(samples, h1, cot_h, block_w, halo=halo)
    halo = shift_from(halo, -1)
    act, dh, small1, bias1, *grads1 = second(samples, h1, cot_h, block_w, before=ahead)
    part, *grads0 = third(
        state_h, noise, dh, halo, small1, bias1, kl, cell_w, block_w, saved
    )
    activations = place(act, halo)
    sum1 = add_up.begin(*grads1)
    sum0 = add_up.begin(*grads0)
    sum1, sum0 = lax.optimization_barrier((sum1, sum0))
    blocks, beside = in_turn(adders, (sum0, sum1), (activations, order, scalars))
    activations, order, scalars = beside
    state_gradient, divergence, *weights = finish(
        order, scalars, state, part, cell_w[0], *blocks, cells=cells, devices=add_up.n
    )
    return (activations, divergence.reshape(()), state_gradient, weights[0].T, *weights[1:])


def solution(mesh):
    return jax.shard_map(
        body,
        mesh=mesh,
        in_specs=(
            P("batch", None, "lon", None),
            P("batch", None, None, "lon", None),
            P("batch"),
            P(),
            P(),
            P(),
            P(),
            P(),
            P(),
            P(),
            P(),
            P(),
            P(),
            P(),
            P(),
            P(),
            P("batch", None, None, "lon", None),
        ),
        out_specs=(
            P("batch", None, None, "lon", None),
            P(),
            P("batch", None, "lon", None),
            P(),
            P(),
            P(),
            P(),
            P(),
            P(),
            P(),
            P(),
            P(),
            P(),
        ),
        check_vma=False,
    )
```

```python
import functools

import jax
import jax.numpy as jnp
from jax import lax
from jax.experimental import pallas as pl
from jax.experimental.pallas import tpu as pltpu
from jax.sharding import PartitionSpec as P

HEADS = 8
HD = 32
WIN = 8
WARM = 1000
SLOTS = 4
D = 256
FF = 1024
ZC = 32
HALF = WIN // 2 * WIN

eps_norm = 1e-05
sharpness = 8.0
spread_bound = 4.0
LOG2E = 1.4426950408889634
f32 = jnp.float32
bf16 = jnp.bfloat16


def mm(a, b):
    return lax.dot_general(a, b, (((1,), (0,)), ((), ())), preferred_element_type=f32)


def mm_nt(a, b):
    return lax.dot_general(a, b, (((1,), (1,)), ((), ())), preferred_element_type=f32)


def mm_tn(a, b):
    return lax.dot_general(a, b, (((0,), (0,)), ((), ())), preferred_element_type=f32)


def low_sublanes(shape):
    return lax.broadcasted_iota(jnp.int32, shape, len(shape) - 2) < 4


def to_halves(x):
    rows, cols, ch = x.shape
    n = cols // 8
    v = x.reshape(4, 2, n, 8, ch)
    a, b = v[:, 0], v[:, 1]
    low = low_sublanes(a.shape)
    first = jnp.where(low, a, pltpu.roll(b, 4, 2))
    second = jnp.where(low, pltpu.roll(a, 4, 2), b)
    first = first.transpose(1, 0, 2, 3)
    second = second.transpose(1, 0, 2, 3)
    return jnp.stack([first, second], axis=1).reshape(2 * n, HALF, ch)


def from_halves(x):
    n = x.shape[0] // 2
    ch = x.shape[-1]
    v = x.reshape(n, 2, 4, 8, ch)
    first, second = v[:, 0].transpose(1, 0, 2, 3), v[:, 1].transpose(1, 0, 2, 3)
    low = low_sublanes(first.shape)
    a = jnp.where(low, first, pltpu.roll(second, 4, 2))
    b = jnp.where(low, pltpu.roll(first, 4, 2), second)
    return jnp.stack([a, b], axis=1).reshape(8, 8 * n, ch)


def tile_of(first, second):
    return jnp.stack([first, second], axis=1).reshape(-1, first.shape[-1])


def halves_of(tile):
    v = tile.reshape(-1, 2, HALF, tile.shape[-1])
    return v[:, 0], v[:, 1]


def norm(x):
    c = x - jnp.mean(x, axis=-1, keepdims=True)
    r = lax.rsqrt(jnp.mean(c * c, axis=-1, keepdims=True) + eps_norm)
    return c * r, r


def norm_back(dy, xhat, r, gain):
    along = dy * gain
    inward = r * (
        along
        - jnp.mean(along, axis=-1, keepdims=True)
        - xhat * jnp.mean(along * xhat, axis=-1, keepdims=True)
    )
    return inward, jnp.sum((dy * xhat).reshape(-1, 8, D), axis=0)


ERF = (0.7978697122393114, 0.036392286377165226, -8.78266605765619e-05,
       -3.669342209361701e-05, 1.425004260912749e-06)


def gelu_parts(x):
    square = x * x
    p = ERF[-1]
    for c in ERF[-2::-1]:
        p = p * square + c
    erf = jnp.tanh(x * p)
    half = 0.5 * x
    density = jnp.exp2(square * (-0.5 * LOG2E))
    return half + half * erf, 0.5 + 0.5 * erf + x * density * 0.3989422804014327


def lane_masks():
    lane = lax.broadcasted_iota(jnp.int32, (1, 128), 1)
    return [(lane >= 32 * j) & (lane < 32 * j + 32) for j in range(4)]


def spread_heads(x, masks):
    return jnp.concatenate([x * m for m in masks], axis=0)


def gather_heads(x, masks):
    v = x.reshape(4, 64, 128)
    return jnp.where(masks[0], v[0], jnp.where(masks[1], v[1], jnp.where(masks[2], v[2], v[3])))


def pieces(rows):
    return [slice(r, r + 64) for r in range(0, rows, 64)]


LAG = 6
SLOTS_HELD = 2 * LAG


def staged(count, *stages, beside={}):
    for n in range(count + LAG * (len(stages) - 1)):
        for work in beside.get(n, ()):
            work()
        for late, stage in enumerate(stages):
            if 0 <= n - LAG * late < count:
                stage(n - LAG * late)


def unit_of(n):
    g = n % 2
    rows = slice(64 * (n // 2), 64 * (n // 2) + 64)
    return rows, lambda part: slice(256 * part + 128 * g, 256 * part + 128 * g + 128), g


def attention(w):
    sel = lane_masks()
    ones = [m.astype(f32).astype(bf16) for m in sel]
    scale = HD ** (-0.5) * LOG2E

    def scores(n):
        rows, lanes, g = unit_of(n)
        q, k = w["packed"][rows, lanes(0)], w["packed"][rows, lanes(1)]
        w["s"][n % SLOTS_HELD] = mm_nt(k, spread_heads(q, ones))

    def softmax(n):
        s = w["s"][n % SLOTS_HELD] * scale + w["bias"][n % 2]
        s = jnp.exp2(s - jnp.max(s, axis=0, keepdims=True))
        w["p"][n] = (s * (1.0 / jnp.sum(s, axis=0, keepdims=True))).astype(bf16)

    def values(n):
        rows, lanes, g = unit_of(n)
        found = gather_heads(mm_tn(w["p"][n], w["packed"][rows, lanes(2)]), sel)
        w["ctx"][rows, lanes(0)] = found.astype(bf16)

    staged(w["p"].shape[0], scores, softmax, values)


def attention_back(w, beside):
    sel = lane_masks()
    ones = [m.astype(f32).astype(bf16) for m in sel]
    scale = HD ** (-0.5)

    def upstream(n):
        rows, lanes, g = unit_of(n)
        spread = spread_heads(w["dctx"][rows, lanes(0)], ones)
        w["gp"][rows, lanes(2)] = mm(w["p"][n], spread).astype(bf16)
        w["s"][n % SLOTS_HELD] = mm_nt(w["packed"][rows, lanes(2)], spread)

    def inward(n):
        p = w["p"][n].astype(f32)
        t = p * w["s"][n % SLOTS_HELD]
        ds = t - p * jnp.sum(t, axis=0, keepdims=True)
        w["d_bias"][n % 2] += ds
        w["ds"][n % SLOTS_HELD] = ds.astype(bf16)

    def outer(n):
        rows, lanes, g = unit_of(n)
        ds = w["ds"][n % SLOTS_HELD]
        q, k = w["packed"][rows, lanes(0)], w["packed"][rows, lanes(1)]
        w["gp"][rows, lanes(1)] = (mm(ds, spread_heads(q, ones)) * scale).astype(bf16)
        w["gp"][rows, lanes(0)] = (gather_heads(mm_tn(ds, k), sel) * scale).astype(bf16)

    staged(w["p"].shape[0], upstream, inward, outer, beside=beside)


def halves(rows):
    return slice(0, rows // 2), slice(rows // 2, rows)


def pieces_of(half):
    return [slice(r, r + 64) for r in range(half.start, half.stop, 64)]


def attend(x_ref, w):
    rows = x_ref.shape[0]
    gain1, gain2 = w["gain1"][...], w["gain2"][...]
    scales = {}

    def project(half):
        for at in pieces_of(half):
            w["normed"][at] = (norm(x_ref[at])[0] * gain1).astype(bf16)
        w["packed"][half] = mm(w["normed"][half], w["qkv"][...]).astype(bf16)

    def join(half):
        w["mixed"][half] = x_ref[half] + mm(w["ctx"][half], w["out"][...])
        for at in pieces_of(half):
            xhat, scales[at.start] = norm(w["mixed"][at])
            w["xhat"][at] = xhat
            w["normed2"][at] = (xhat * gain2).astype(bf16)

    project(slice(0, rows))
    attention(w)
    join(slice(0, rows))
    return scales


def block_forward(x_ref, w):
    attend(x_ref, w)
    rows = x_ref.shape[0]

    def start(c):
        w["a"][c % 2] = mm(w["normed2"][...], w["up"][:, 256 * c : 256 * c + 256])

    start(0)
    for c in range(FF // 256):
        cols = slice(256 * c, 256 * c + 256)
        if c < FF // 256 - 1:
            start(c + 1)
        for at in pieces(rows):
            active, slope = gelu_parts(w["a"][c % 2, at])
            w["active"][at, cols] = active.astype(bf16)
            w["slope"][at, cols] = slope.astype(bf16)
        before = w["mixed"] if c == 0 else w["xhat"]
        w["xhat"][...] = before[...] + mm(w["active"][:, cols], w["down"][cols, :])


def block_backward(x_ref, g_ref, w, fused, round_dn):
    rows = x_ref.shape[0]
    gain1, gain2 = w["gain1"][...], w["gain2"][...]
    if fused:
        scales = attend(x_ref, w)
    normed2_t = w["normed2"][...].T
    gb = g_ref[...].astype(bf16)
    gb_t = gb.T

    if fused:
        def start(c):
            cols = slice(256 * c, 256 * c + 256)
            if fused:
                w["a"][c % 2] = mm(w["normed2"][...], w["up"][:, cols])
            w["b"][c % 2] = mm_nt(gb, w["down"][cols, :])

        start(0)
        for c in range(FF // 256):
            cols = slice(256 * c, 256 * c + 256)
            if c < FF // 256 - 1:
                start(c + 1)
            for at in pieces(rows):
                if fused:
                    active, slope = gelu_parts(w["a"][c % 2, at])
                    w["active"][at, cols] = active.astype(bf16)
                else:
                    slope = w["slope"][at, cols].astype(f32)
                w["d_inner"][at, cols] = (w["b"][c % 2, at] * slope).astype(bf16)
            part = mm_nt(w["d_inner"][:, cols], w["up"][:, cols])
            w["dn"][...] = part if c == 0 else w["dn"][...] + part
            w["d_ff"][1024 + 256 * c : 1280 + 256 * c, :] += mm(gb_t, w["active"][:, cols])
            w["d_ff"][cols, :] += mm(normed2_t, w["d_inner"][:, cols])
            if fused:
                w["mixed"][...] += mm(w["active"][:, cols], w["down"][cols, :])
    else:
        for c in range(FF // 256):
            cols = slice(256 * c, 256 * c + 256)
            part = mm_nt(gb, w["down"][cols, :]) * w["slope"][:, cols].astype(f32)
            w["d_inner"][:, cols] = part.astype(bf16)
        w["dn"][...] = mm_nt(w["d_inner"][...], w["up"][...])
        for c in range(FF // 256):
            cols = slice(256 * c, 256 * c + 256)
            w["d_ff"][FF + 256 * c : FF + 256 * c + 256, :] += mm(gb_t, w["active"][:, cols])
            w["d_ff"][cols, :] += mm(normed2_t, w["d_inner"][:, cols])

    def into_heads(half):
        dgain = None
        for at in pieces_of(half):
            xhat, r = (w["xhat"][at], scales[at.start]) if fused else norm(w["mixed"][at])
            inward, part = norm_back(w["dn"][at], xhat, r, gain2)
            dgain = part if dgain is None else dgain + part
            d_mixed = g_ref[at] + inward
            g_ref[at] = d_mixed
            w["g_out"][at] = d_mixed.astype(bf16)
        w["d_small"][8:16, :] += dgain
        w["dctx"][half] = mm_nt(w["g_out"][half], w["out"][...]).astype(bf16)

    def d_out():
        w["d_at"][768:1024, :] += mm_tn(w["ctx"][...], w["g_out"][...])

    def out_of_heads(half):
        gp = w["gp"][half]
        w["dn"][half] = mm_nt(gp, w["qkv"][...])
        normed_t = w["normed"][half].T
        for c in range(3):
            cols = slice(256 * c, 256 * c + 256)
            w["d_at"][cols, :] += mm(normed_t, gp[:, cols])
        dgain = None
        for at in pieces_of(half):
            dn = w["dn"][at]
            if round_dn:
                dn = dn.astype(bf16).astype(f32)
            xhat, r = norm(x_ref[at])
            inward, part = norm_back(dn, xhat, r, gain1)
            dgain = part if dgain is None else dgain + part
            g_ref[at] = g_ref[at] + inward
        w["d_small"][0:8, :] += dgain

    one, two = halves(rows)
    units = rows // 64
    into_heads(one)
    beside = {2: [functools.partial(into_heads, two)], units: [d_out]}
    attention_back(w, beside)
    out_of_heads(slice(0, rows))


LIMIT = 56 * 1024 * 1024


def cost(us):
    return pl.CostEstimate(flops=int(us * 1.1e9), bytes_accessed=int(us * 3.6e6), transcendentals=0)


ANY = pl.BlockSpec(memory_space=pl.ANY)


def params(n):
    return pltpu.CompilerParams(
        dimension_semantics=("arbitrary",) * n, vmem_limit_bytes=LIMIT
    )


def latent_head(state, wl):
    center = mm_nt(state, wl[:ZC])
    squash = jnp.tanh(mm_nt(state, wl[ZC:]) * (1.0 / spread_bound))
    return center, squash, jnp.exp((0.5 * spread_bound) * squash)


def lanes_of_patch(width, back):
    lane = lax.broadcasted_iota(jnp.int32, (4 * 256, 4 * 64), 0)
    at = lax.broadcasted_iota(jnp.int32, (4 * 256, 4 * 64), 1)
    row, col = query_place(at & 63)
    want = 16 * (7 - row) + 7 - col if back else 16 * row + col
    return jnp.where(lane == (at >> 6) * 256 + want, 1.0, 0.0).astype(bf16)


def query_place(q):
    return (q >> 2) & 7, ((q >> 5) << 2) + (q & 3)


def table_lanes(back):
    a = lax.broadcasted_iota(jnp.int32, (256, 256), 0)
    b = lax.broadcasted_iota(jnp.int32, (256, 256), 1)
    side = 2 * WIN - 1
    if back:
        mirrored = 16 * (14 - (a >> 4)) + 14 - (a & 15)
        hit = ((a & 15) < side) & ((a >> 4) < side) & (b == (14 - (a >> 4)) * side + 14 - (a & 15))
    else:
        hit = ((b & 15) < side) & ((b >> 4) < side) & (a == (b >> 4) * side + (b & 15))
    return jnp.where(hit, 1.0, 0.0).astype(bf16)


def exactly(a, onehot):
    total = None
    for _ in range(3):
        term = a.astype(bf16)
        a = a - term.astype(f32)
        part = mm(term, onehot)
        total = part if total is None else total + part
    return total


def expand_bias(tables):
    spread = exactly(tables, table_lanes(False))
    choose = lanes_of_patch(64, False)
    out = []
    for n in range(4):
        heads = []
        for h in range(4 * n, 4 * n + 4):
            one = jnp.broadcast_to(spread[h : h + 1], (8, 256))
            heads.append(
                jnp.concatenate(
                    [
                        pltpu.roll(one, (16 * r + 137) % 256, 1, stride=1, stride_axis=0)
                        for r in range(WIN)
                    ]
                )
            )
        rows = exactly(jnp.concatenate(heads, axis=1), choose)
        out.append(to_halves(rows.reshape(WIN, WIN, 256)).reshape(64, 256))
    return out


def reduce_bias(grads):
    rows = from_halves(grads.reshape(2, HALF, 256)).reshape(64, 256).astype(bf16)
    lanes = lax.dot_general(
        rows, lanes_of_patch(64, True), (((1,), (1,)), ((), ())), preferred_element_type=f32
    )
    out = []
    for h in range(4):
        total = None
        for r in range(WIN):
            one = pltpu.roll(
                lanes[8 * r : 8 * r + 8, 256 * h : 256 * h + 256], 16 * r, 1, stride=1, stride_axis=0
            )
            total = one if total is None else total + one
        out.append(jnp.sum(total, axis=0, keepdims=True))
    return jnp.concatenate(out)


def prep_kernel(samples, cot, state, wl, tables, cot_h, state_h, kl, bias):
    @pl.when(pl.program_id(0) == 0)
    def _():
        padded = jnp.concatenate(
            [tables[...], jnp.zeros((16, 256 - tables.shape[1]), f32)], axis=1
        )
        for n, part in enumerate(expand_bias(padded * LOG2E)):
            bias[n // 2, n % 2] = part

    live = samples[0]
    for s in range(SLOTS):
        factor = jnp.where(s < live, 1.0, 0.0).astype(f32)
        cot_h[:, s] = (to_halves(cot[0, s].astype(f32)) * factor).astype(bf16)
    st = to_halves(state[0].astype(f32)).reshape(4, 64, D).astype(bf16)
    state_h[:, 0] = st
    center, squash, sigma = latent_head(st.reshape(4 * 64, D), wl[...])
    terms = 0.5 * (center * center + sigma * sigma - 1.0 - spread_bound * squash)

    @pl.when(pl.program_id(0) == 0)
    def _():
        kl[...] = jnp.zeros(kl.shape, f32)

    kl[:, :ZC] += jnp.sum(terms.reshape(-1, 8, ZC), axis=0)


def prep(samples, cot, state, wl, tables):
    bands = state.shape[1] // WIN
    nw = state.shape[2] // WIN
    return pl.pallas_call(
        prep_kernel,
        grid=(bands,),
        in_specs=[
            pl.BlockSpec(memory_space=pltpu.SMEM),
            pl.BlockSpec((1, SLOTS, WIN, nw * WIN, D), lambda i: (0, 0, i, 0, 0)),
            pl.BlockSpec((1, WIN, nw * WIN, D), lambda i: (0, i, 0, 0)),
            full(wl),
            full(tables),
        ],
        out_specs=[
            pl.BlockSpec((2 * nw, SLOTS, HALF, D), lambda i: (0, i, 0, 0)),
            pl.BlockSpec((nw, 1, 64, D), lambda i: (0, i, 0, 0)),
            pl.BlockSpec((8, D), lambda i: (0, 0)),
            pl.BlockSpec((2, 2, 64, 256), lambda i: (0, 0, 0, 0)),
        ],
        out_shape=[
            jax.ShapeDtypeStruct((2 * nw, bands * SLOTS, HALF, D), bf16),
            jax.ShapeDtypeStruct((nw, bands, 64, D), bf16),
            jax.ShapeDtypeStruct((8, D), f32),
            jax.ShapeDtypeStruct((2, 2, 64, 256), f32),
        ],
        compiler_params=params(1),
        cost_estimate=cost(4),
    )(samples, cot, state, wl, tables)


def noise_of(block):
    bands = block.shape[1] // WIN
    return jnp.stack(
        [
            jnp.stack(
                [to_halves(block[s, WIN * b : WIN * b + WIN]).reshape(64, ZC) for s in range(SLOTS)]
            )
            for b in range(bands)
        ]
    )


def noise_spec(bands, skip):
    return pl.BlockSpec((1, SLOTS, bands * WIN, WIN, ZC), lambda j: (0, 0, 0, j + skip, 0))


def cell_forward(state, noise, wl, ws, wn):
    bands = state.shape[0]
    flat = state.reshape(bands * 64, D)
    over = lambda x: x.reshape(bands, 1, 64, x.shape[-1])
    center, squash, sigma = latent_head(flat, wl)
    latent = (over(center) + over(sigma) * noise).reshape(-1, ZC).astype(bf16)
    mix = mm(latent, wn)
    half = 0.5 * (over(mm(flat, ws)) + mix[:, :D].reshape(bands, SLOTS, 64, D))
    gate = 0.5 + 0.5 * jnp.tanh(half)
    cand = jnp.tanh(mix[:, D:].reshape(bands, SLOTS, 64, D))
    hidden = gate * over(flat.astype(f32)) + (1.0 - gate) * cand
    return hidden.reshape(-1, D), center, squash, sigma, latent, gate, cand


def full(a):
    return pl.BlockSpec(a.shape, lambda *_: (0,) * a.ndim)


def block_specs(k):
    return [
        pl.BlockSpec((2, D), lambda *_: (0, 0)),
        pl.BlockSpec((1, D, 3 * D), lambda *_: (k, 0, 0)),
        pl.BlockSpec((1, 2, 64, 256), lambda *_: (k, 0, 0, 0)),
        pl.BlockSpec((1, D, D), lambda *_: (k, 0, 0)),
        pl.BlockSpec((2, D), lambda *_: (0, 0)),
        pl.BlockSpec((1, D, FF), lambda *_: (k, 0, 0)),
        pl.BlockSpec((1, FF, D), lambda *_: (k, 0, 0)),
    ]


NAMES = ("gain1", "qkv", "bias", "out", "gain2", "up", "down")


def named(refs, k):
    return {
        n: r.at[k : k + 1] if n.startswith("gain") else r.at[0] for n, r in zip(NAMES, refs)
    }


def saved_refs(rows):
    return [
        ("normed", (rows, D), bf16),
        ("packed", (rows, 3 * D), bf16),
        ("p", (rows // 32, 64, 256), bf16),
        ("ctx", (rows, D), bf16),
        ("mixed", (rows, D), f32),
        ("normed2", (rows, D), bf16),
        ("active", (rows, FF), bf16),
        ("slope", (rows, FF), bf16),
    ]


def forward_refs(rows):
    return [
        ("x", (rows, D), f32),
        ("s", (SLOTS_HELD, 64, 256), f32),
        ("xhat", (rows, D), f32),
        ("a", (2, rows, 256), f32),
    ]


def backward_refs(rows):
    return [
        ("x", (rows, D), f32),
        ("g", (rows, D), f32),
        ("s", (SLOTS_HELD, 64, 256), f32),
        ("b", (2, rows, 256), f32),
        ("d_inner", (rows, FF), bf16),
        ("dn", (rows, D), f32),
        ("g_out", (rows, D), bf16),
        ("dctx", (rows, D), bf16),
        ("ds", (SLOTS_HELD, 64, 256), bf16),
        ("gp", (rows, 3 * D), bf16),
    ]


def both_refs(rows):
    return saved_refs(rows) + forward_refs(rows)[2:] + backward_refs(rows)


def scratch(refs):
    return [pltpu.VMEM(shape, dtype) for _, shape, dtype in refs]


def names(refs):
    return [name for name, _, _ in refs]


def saved_specs(rows, skip):
    return [
        pl.BlockSpec((1,) + shape, lambda j, n=len(shape): (j + skip,) + (0,) * n)
        for _, shape, _ in saved_refs(rows)
    ]


N_SAVED, N_BACK, N_BOTH = len(saved_refs(64)), len(backward_refs(64)), len(both_refs(64))


GRAD_SHAPES = [(2048, D), (1024, D), (16, D), (2, 64, 256)]
GRAD_NAMES = ("d_ff", "d_at", "d_small", "d_bias")
GRAD_SCRATCH = [pltpu.VMEM(s, f32) for s in GRAD_SHAPES[:2]]
SMALL_SPECS = [pl.BlockSpec(s, lambda *_, n=len(s): (0,) * n) for s in GRAD_SHAPES[2:]]
SMALL_OUTS = [jax.ShapeDtypeStruct(s, f32) for s in GRAD_SHAPES[2:]]

ROWS_BLOCK = 3072
ROWS_CELL = 512
CHAINS = (((0, (ROWS_BLOCK + ROWS_CELL) // 2),), ((0, ROWS_BLOCK // 2),))
ALL_CHAINS = [(k, chain) for k in range(2) for chain in CHAINS[k]]


def first_kernel(state, noise, cot, wl, ws, wn, *rest, lead):
    w = named(rest[:7], 0)
    rest = rest[7:] if lead else rest[7 + 1 + N_SAVED :]
    h1, rest = rest[0], rest[1:]
    w.update((n, r.at[0]) for n, r in zip(names(saved_refs(64)), rest))
    rest = rest[N_SAVED:]
    if lead:
        halo, rest = rest[0], rest[1:]
    w.update(zip(names(forward_refs(64)), rest))
    w["x"][...] = cell_forward(state[0], noise_of(noise[0]), wl[...], ws[...], wn[...])[0]
    block_forward(w["x"], w)
    a, b = halves_of(w["xhat"][...])
    h1[0, 0] = a
    h1[0, 1] = b
    if lead:
        halo[0] = a.astype(bf16)
        halo[1] = cot[0]


def first(state_h, noise, cot_h, cell_w, block_w, before=None):
    nw, bands = state_h.shape[:2]
    half = (bands * SLOTS, HALF, D)
    rows = 64 * bands * SLOTS
    lead = before is None
    skip = 0 if lead else 1
    specs = [pl.BlockSpec((1, 2) + half, lambda j: (j + skip, 0, 0, 0, 0))] + saved_specs(rows, skip)
    shapes = [jax.ShapeDtypeStruct((nw, 2) + half, f32)] + [
        jax.ShapeDtypeStruct((nw,) + shape, dtype) for _, shape, dtype in saved_refs(rows)
    ]
    inputs = [state_h, noise, cot_h, *cell_w, *block_w]
    in_specs = [
        pl.BlockSpec((1, bands, 64, D), lambda j: (j + skip, 0, 0, 0)),
        noise_spec(bands, skip),
        pl.BlockSpec((1,) + half, lambda j: (0, 0, 0, 0)),
    ]
    in_specs += [full(a) for a in cell_w] + block_specs(0)
    aliases = {}
    if lead:
        specs.append(pl.BlockSpec((2,) + half, lambda j: (0, 0, 0, 0)))
        shapes.append(jax.ShapeDtypeStruct((2,) + half, bf16))
    else:
        aliases = {len(inputs) + n: n for n in range(len(before))}
        inputs += before
        in_specs += [pl.BlockSpec(memory_space=pl.ANY)] * len(before)
    return pl.pallas_call(
        functools.partial(first_kernel, lead=lead),
        grid=(1 if lead else nw - 1,),
        in_specs=in_specs,
        out_specs=specs,
        out_shape=shapes,
        input_output_aliases=aliases,
        scratch_shapes=scratch(forward_refs(rows)),
        compiler_params=params(1),
        cost_estimate=cost(6 if lead else 16),
    )(*inputs)


def zero_at_start(refs):
    @pl.when(pl.program_id(0) == 0)
    def _():
        for r in refs:
            r[...] = jnp.zeros(r.shape, r.dtype)


def halves_out(keep, send, parts):
    size = keep.shape[0]
    core = lax.axis_index("batch") & 1

    def write(low, high):
        first = 0
        for ref in parts:
            rows = ref.shape[0]
            cut = min(max(size - first, 0), rows)
            if cut:
                low[first : first + cut] = ref[:cut].astype(bf16)
            if cut < rows:
                high[first + cut - size : first + rows - size] = ref[cut:rows].astype(bf16)
            first += rows

    @pl.when(core == 0)
    def _():
        write(keep, send)

    @pl.when(core != 0)
    def _():
        write(send, keep)


def at_end():
    return pl.program_id(0) == pl.num_programs(0) - 1


def second_kernel(samples, ha, hb, ca, cb, *rest, lead):
    w = named(rest[:7], 1)
    grads1, small1, bias1 = (None,) * 3 if lead else rest[7:10]
    rest = rest[7:] if lead else rest[12:]
    act, dh, d_small, d_bias = rest[:4]
    if lead:
        packed_grads, back_halo = rest[4:6]
    else:
        keep, send = rest[4:6]
    rest = rest[6:]
    w.update(zip(names(both_refs(64)), rest))
    grads = rest[N_BOTH : N_BOTH + 2] + (d_small, d_bias)
    w.update(zip(GRAD_NAMES, grads))
    if lead:
        zero_at_start(grads)
    else:

        @pl.when(pl.program_id(0) == 0)
        def _():
            grads[0][...] = grads1[:2048].astype(f32)
            grads[1][...] = grads1[2048:].astype(f32)
            d_small[...] = small1[...]
            d_bias[...] = bias1[...]

    w["x"][...] = tile_of(ha[0, 0], hb[0].astype(f32) if lead else hb[0, 0])
    w["g"][...] = tile_of(ca[0].astype(f32), cb[0].astype(f32))
    block_backward(w["x"], w["g"], w, True, True)
    live = samples[0]
    a, b = halves_of(w["mixed"][...])
    factor = jnp.concatenate(
        [jnp.where(s % SLOTS < live, 1.0, 0.0) * jnp.ones((1, 1, D), f32) for s in range(a.shape[0])]
    )
    a, b = (a * factor).astype(bf16), (b * factor).astype(bf16)
    da, db = halves_of(w["g"][...])
    act[0, 0] = a
    act[0, 1] = b
    dh[0, 0] = da
    dh[0, 1] = db
    if lead:
        back_halo[0] = db.astype(bf16)
        back_halo[1] = b
        packed_grads[:2048] = grads[0][...].astype(bf16)
        packed_grads[2048:] = grads[1][...].astype(bf16)
    else:

        @pl.when(at_end())
        def _():
            halves_out(keep, send, [grads[0], grads[1]])


def second(samples, h1, cot_h, block_w, halo=None, before=None):
    nw = h1.shape[0]
    half = h1.shape[2:]
    lead = before is None
    if lead:
        tile, other = (lambda j: nw - 1), halo
        wide = [pl.BlockSpec((1,) + half, lambda j, n=n: (n, 0, 0, 0)) for n in range(2)]
    else:
        tile, other = (lambda j: j), cot_h
        wide = [
            pl.BlockSpec((1, 1) + half, lambda j: (j + 1, 0, 0, 0, 0)),
            pl.BlockSpec((1,) + half, lambda j: (2 * j + 2, 0, 0, 0)),
        ]
    inputs = [samples, h1, halo if lead else h1, cot_h, other, *block_w]
    in_specs = [
        pl.BlockSpec(memory_space=pltpu.SMEM),
        pl.BlockSpec((1, 1) + half, lambda j: (tile(j), 1, 0, 0, 0)),
        wide[0],
        pl.BlockSpec((1,) + half, lambda j: (2 * tile(j) + 1, 0, 0, 0)),
        wide[1],
    ]
    in_specs += block_specs(1)
    out_specs = [
        pl.BlockSpec((1, 2) + half, lambda j: (tile(j), 0, 0, 0, 0)),
        pl.BlockSpec((1, 2) + half, lambda j: (tile(j), 0, 0, 0, 0)),
    ] + SMALL_SPECS
    out_shape = [
        jax.ShapeDtypeStruct((nw, 2) + half, bf16),
        jax.ShapeDtypeStruct((nw, 2) + half, f32),
    ] + SMALL_OUTS
    aliases = {}
    if lead:
        out_specs.append(pl.BlockSpec((ROWS_BLOCK, D), lambda *_: (0, 0)))
        out_specs.append(pl.BlockSpec((2,) + half, lambda j: (0, 0, 0, 0)))
        out_shape.append(jax.ShapeDtypeStruct((ROWS_BLOCK, D), bf16))
        out_shape.append(jax.ShapeDtypeStruct((2,) + half, bf16))
    else:
        out_specs += [pl.BlockSpec((ROWS_BLOCK // 2, D), lambda *_: (0, 0))] * 2
        out_shape += [jax.ShapeDtypeStruct((ROWS_BLOCK // 2, D), bf16)] * 2
        act, dh, small1, bias1, grads1 = before
        sums = [grads1, small1, bias1]
        aliases = {len(inputs) + 3: 0, len(inputs) + 4: 1}
        inputs += sums + [act, dh]
        in_specs += [full(a) for a in sums] + [pl.BlockSpec(memory_space=pl.ANY)] * 2
    return pl.pallas_call(
        functools.partial(second_kernel, lead=lead),
        grid=(1 if lead else nw - 1,),
        in_specs=in_specs,
        out_specs=out_specs,
        out_shape=out_shape,
        input_output_aliases=aliases,
        scratch_shapes=scratch(both_refs(64 * half[0])) + GRAD_SCRATCH,
        compiler_params=params(1),
        cost_estimate=cost(9 if lead else 24),
    )(*inputs)


CELL_SHAPES = [(D, D), (2 * ZC, D), (2 * ZC, D), (2 * ZC, D)]


def divergence_parts(center, squash, sigma):
    return center.astype(bf16), (
        0.5 * (sigma * sigma - 1.0) * (1.0 - squash * squash)
    ).astype(bf16)


def third_kernel(state, noise, da, db, dhalo, small1, bias1, kl, wl, ws, wn, *rest):
    w = named(rest[:7], 0)
    w.update((n, r.at[0]) for n, r in zip(names(saved_refs(64)), rest[7:]))
    rest = rest[N_SAVED:]
    sg, keep, send = rest[7:10]
    w.update(zip(names(backward_refs(64)), rest[10:]))
    grads = rest[10 + N_BACK : 14 + N_BACK]
    d_ws, d_wn, d_wl, d_kl, d_rest = rest[14 + N_BACK :]
    cell_grads = (d_ws, d_wn, d_wl, d_kl)
    w.update(zip(GRAD_NAMES, grads))
    zero_at_start(grads + cell_grads)
    st = state[0]
    nz = noise_of(noise[0])
    bands = st.shape[0]
    hidden, center, squash, sigma, latent, gate, cand = cell_forward(
        st, nz, wl[...], ws[...], wn[...]
    )
    da_v = jnp.where(pl.program_id(0) == 0, dhalo[0].astype(f32), da[0, 0])
    w["x"][...] = hidden
    w["g"][...] = tile_of(da_v, db[0, 0])
    block_backward(w["x"], w["g"], w, False, False)
    dc = w["g"][...]
    over = lambda x: x.reshape(bands, 1, 64, x.shape[-1])
    flat = st.reshape(bands * 64, D)
    dc = dc.reshape(bands, SLOTS, 64, D)
    rest_gate = 1.0 - gate
    d_pre = dc * (over(flat.astype(f32)) - cand) * gate * rest_gate
    d_cand = dc * rest_gate * (1.0 - cand * cand)
    direct = jnp.sum(dc * gate, axis=1).reshape(-1, D)
    g_gate = jnp.sum(d_pre, axis=1).reshape(-1, D).astype(bf16)
    d_ws[...] += mm_tn(flat, g_gate)
    pre = d_pre.reshape(-1, D).astype(bf16)
    cnd = d_cand.reshape(-1, D).astype(bf16)
    d_wn[:ZC] += mm_tn(latent, pre)
    d_wn[ZC:] += mm_tn(latent, cnd)
    d_lat = mm_nt(pre, wn[:, :D]) + mm_nt(cnd, wn[:, D:])
    d_lat = d_lat.reshape(bands, SLOTS, 64, ZC)
    d_center = jnp.sum(d_lat, axis=1).reshape(-1, ZC)
    d_raw = jnp.sum(d_lat * nz, axis=1).reshape(-1, ZC) * 0.5 * sigma * (1.0 - squash * squash)
    d_center, d_raw = d_center.astype(bf16), d_raw.astype(bf16)
    d_wl[:ZC] += mm_tn(d_center, flat)
    d_wl[ZC:] += mm_tn(d_raw, flat)
    kl_center, kl_raw = divergence_parts(center, squash, sigma)
    d_kl[:ZC] += mm_tn(kl_center, flat)
    d_kl[ZC:] += mm_tn(kl_raw, flat)
    total = direct + mm_nt(g_gate, ws[...])
    total = total + mm(d_center, wl[:ZC]) + mm(d_raw, wl[ZC:])
    for b in range(bands):
        sg[0, WIN * b : WIN * b + WIN] = from_halves(
            total[64 * b : 64 * b + 64].reshape(2, HALF, D)
        )

    @pl.when(at_end())
    def _():
        d_small, d_bias = grads[2:]
        d_rest[:16] = jnp.concatenate(
            [reduce_bias(b) for b in (d_bias[0], d_bias[1], bias1[0], bias1[1])]
        )
        total = lambda x: jnp.sum(x, axis=0, keepdims=True)
        d_rest[16:] = jnp.concatenate(
            [total(d_small[:8]), total(d_small[8:]), total(small1[:8]), total(small1[8:])]
            + [total(kl[...]), jnp.zeros((43, D), f32)]
        )
        halves_out(keep, send, [grads[0], grads[1], *cell_grads, d_rest])


def third(state_h, noise, dh, halo, small1, bias1, kl, cell_w, block_w, saved):
    nw, bands = state_h.shape[:2]
    rows = 64 * bands * SLOTS
    half = dh.shape[2:]
    return pl.pallas_call(
        third_kernel,
        grid=(nw,),
        in_specs=[
            pl.BlockSpec((1, bands, 64, D), lambda j: (j, 0, 0, 0)),
            noise_spec(bands, 0),
            pl.BlockSpec((1, 1) + half, lambda j: (jnp.maximum(j - 1, 0), 1, 0, 0, 0)),
            pl.BlockSpec((1, 1) + half, lambda j: (j, 0, 0, 0, 0)),
            pl.BlockSpec((1,) + half, lambda j: (0, 0, 0, 0)),
        ]
        + [full(a) for a in (small1, bias1, kl)]
        + [full(a) for a in cell_w]
        + block_specs(0)
        + saved_specs(rows, 0),
        out_specs=[pl.BlockSpec((1, bands * WIN, WIN, D), lambda j: (0, 0, j, 0))]
        + [pl.BlockSpec(((ROWS_BLOCK + ROWS_CELL) // 2, D), lambda *_: (0, 0))] * 2,
        out_shape=[jax.ShapeDtypeStruct((1, bands * WIN, nw * WIN, D), f32)]
        + [jax.ShapeDtypeStruct(((ROWS_BLOCK + ROWS_CELL) // 2, D), bf16)] * 2,
        scratch_shapes=scratch(backward_refs(rows))
        + [pltpu.VMEM(s, f32) for s in GRAD_SHAPES + CELL_SHAPES + [(64, D)]],
        compiler_params=params(1),
        cost_estimate=cost(26),
    )(state_h, noise, dh, dh, halo, small1, bias1, kl, *cell_w, *block_w, *saved)


def place_kernel(act, halo, out):
    nw = act.shape[0]
    for s in range(SLOTS):
        halves = [halo[0, s].astype(f32)]
        for j in range(nw):
            halves.append(act[j, 0, s].astype(f32))
            if j < nw - 1:
                halves.append(act[j, 1, s].astype(f32))
        out[0, s] = from_halves(jnp.stack(halves)).astype(bf16)


def place(act, halo):
    nw = act.shape[0]
    bands = act.shape[2] // SLOTS
    return pl.pallas_call(
        place_kernel,
        grid=(bands,),
        in_specs=[
            pl.BlockSpec((nw, 2, SLOTS, HALF, D), lambda i: (0, 0, i, 0, 0)),
            pl.BlockSpec((1, SLOTS, HALF, D), lambda i: (1, i, 0, 0)),
        ],
        out_specs=pl.BlockSpec((1, SLOTS, WIN, nw * WIN, D), lambda i: (0, 0, i, 0, 0)),
        out_shape=jax.ShapeDtypeStruct((1, SLOTS, bands * WIN, nw * WIN, D), bf16),
        compiler_params=params(1),
        cost_estimate=cost(4),
    )(act, halo)


def finish_kernel(
    order, scalars, state, part, wl, *rest, cells, devices,
):
    n_blocks = 2 * len(ALL_CHAINS)
    blocks, rest = rest[:n_blocks], rest[n_blocks:]
    sg, div, o_wl, o_ws, o_wn, o_gain1, o_table, o_gain2, *large = rest[:12]
    sums, held = rest[12 : 12 + len(ALL_CHAINS)], rest[12 + len(ALL_CHAINS) : -6]
    o_qkv, o_out, o_up, o_down = stage = rest[-6:-2]
    in_sems, out_sems = rest[-2:]
    arrive = [pltpu.make_async_copy(b, h, in_sems.at[n]) for n, (b, h) in enumerate(zip(blocks, held))]
    leave = [
        [pltpu.make_async_copy(a.at[k], b.at[k], out_sems.at[4 * k + n]) for n, (a, b) in enumerate(zip(stage, large))]
        for k in range(2)
    ]
    for copy in arrive:
        copy.start()

    def assemble(k):
        for chain, (where, _) in enumerate(ALL_CHAINS):
            if where != k:
                continue
            whole = sums[chain]
            n = devices // 4
            count = whole.shape[0] // (2 * n)
            for at in range(2):
                arrive[2 * chain + at].wait()
                block = held[2 * chain + at]
                for i in range(n):
                    to = order[2 * chain, at] * n + jnp.bitwise_xor(order[2 * chain + 1, at], i)
                    whole[pl.ds(pl.multiple_of(to * count, 16), count)] = block[
                        count * i : count * i + count
                    ]

    def rows_of(k, first, count):
        size = CHAINS[k][-1][1]
        side, first = divmod(first, size)
        for (where, (low, high)), whole in zip(ALL_CHAINS, sums):
            if where == k and low <= first < high:
                first += side * whole.shape[0] // 2 - low
                return whole[first : first + count]

    def unpack(k):
        assemble(k)
        for c in range(3):
            cols = slice(256 * c, 256 * c + 256)
            o_qkv[k, :, cols] = rows_of(k, 2 * FF + 256 * c, 256).astype(f32)
        o_out[k] = rows_of(k, 2816, 256).astype(f32)
        leave[k][0].start()
        leave[k][1].start()
        for c in range(FF // 256):
            cols = slice(256 * c, 256 * c + 256)
            o_up[k, :, cols] = rows_of(k, 256 * c, 256).astype(f32)
        leave[k][2].start()
        for c in range(FF // 256):
            cols = slice(256 * c, 256 * c + 256)
            o_down[k, cols] = rows_of(k, FF + 256 * c, 256).astype(f32).T
        leave[k][3].start()

    unpack(0)
    unpack(1)
    cell_rows = lambda first, count: rows_of(0, ROWS_BLOCK + first, count)
    small = cell_rows(464, 16).astype(f32)
    kl_mean = small[4:5, :ZC] * (1.0 / cells)
    beta, floor = scalars[0], scalars[1]
    excess = sharpness * (kl_mean - floor)
    soft = jnp.maximum(excess, 0.0) + jnp.log(1.0 + jnp.exp(-jnp.abs(excess)))
    div[...] = beta * jnp.mean(floor + soft * (1.0 / sharpness), axis=-1, keepdims=True)
    amt = beta * jax.nn.sigmoid(excess) * (1.0 / (ZC * cells))

    rows = state.shape[1] * state.shape[2]
    center, squash, sigma = latent_head(state[0].reshape(rows, D), wl[...])
    kl_center, kl_raw = divergence_parts(center, squash, sigma)
    g_center = (kl_center.astype(f32) * amt).astype(bf16)
    g_raw = (kl_raw.astype(f32) * amt).astype(bf16)
    add = mm(g_center, wl[:ZC]) + mm(g_raw, wl[ZC:])
    sg[0] = part[0] + add.reshape(state.shape[1:])

    o_ws[...] = cell_rows(0, 256).astype(f32)
    wn = cell_rows(256, 64).astype(f32)
    o_wn[:, :D] = wn[:ZC]
    o_wn[:, D:] = wn[ZC:]
    at = lambda axis: lax.broadcasted_iota(jnp.int32, (ZC, ZC), axis)
    column = jnp.sum(jnp.where(at(0) == at(1), amt, 0.0), axis=1, keepdims=True)
    for h in range(2):
        o_wl[ZC * h : ZC * h + ZC] = (
            cell_rows(320 + ZC * h, ZC).astype(f32) + cell_rows(384 + ZC * h, ZC).astype(f32) * column
        )
    table = mm(cell_rows(448, 16), table_lanes(True))
    o_table[0] = table[:HEADS, : (2 * WIN - 1) ** 2]
    o_table[1] = table[HEADS:, : (2 * WIN - 1) ** 2]
    for k in range(2):
        o_gain1[k : k + 1] = small[2 * k : 2 * k + 1]
        o_gain2[k : k + 1] = small[2 * k + 1 : 2 * k + 2]
    for k in range(2):
        for copy in leave[k]:
            copy.wait()


def finish(order, scalars, state, part, wl, *blocks, cells, devices):
    small = [
        part.shape, (1, 1), (2 * ZC, D), (D, D), (ZC, 2 * D), (2, D),
        (2, HEADS, (2 * WIN - 1) ** 2), (2, D),
    ]
    large = [(2, D, 3 * D), (2, D, D), (2, D, FF), (2, FF, D)]
    smem, vmem = pl.BlockSpec(memory_space=pltpu.SMEM), pl.BlockSpec(memory_space=pltpu.VMEM)
    sg, div, wl, ws, wn, gain1, table, gain2, qkv, out, up, down = pl.pallas_call(
        functools.partial(finish_kernel, cells=cells, devices=devices),
        in_specs=[smem, smem] + [vmem] * 3 + [ANY] * len(blocks),
        out_specs=[vmem] * len(small) + [ANY] * len(large),
        out_shape=[jax.ShapeDtypeStruct(o, f32) for o in small + large],
        scratch_shapes=[pltpu.VMEM((2 * b.shape[0], D), bf16) for b in blocks[::2]]
        + [pltpu.VMEM(b.shape, bf16) for b in blocks]
        + [pltpu.VMEM(o, f32) for o in large]
        + [pltpu.SemaphoreType.DMA((len(blocks),)), pltpu.SemaphoreType.DMA((8,))],
        compiler_params=pltpu.CompilerParams(vmem_limit_bytes=40 * 1024 * 1024),
    )(order, scalars, state, part, wl, *blocks)
    return sg, div, wl, ws, wn, gain1, qkv, table, out, gain2, up, down


def shift_from(block, distance):
    n = lax.axis_size("lon")
    return lax.ppermute(block, "lon", [((i + distance) % n, i) for i in range(n)])


class Summation:
    def __init__(self, turn):
        n_lon, n_batch = lax.axis_size("lon"), lax.axis_size("batch")
        self.n = n = n_lon * n_batch
        me = lax.axis_index("lon") * n_batch + lax.axis_index("batch")
        bits = [1 << i for i in range(1, n.bit_length() - 1)]
        axes, rest = [bits[0], bits[-1]] + bits[1:2], bits[2:-1]
        axes = axes[: len(bits)]
        turned = lambda by: axes[by % len(axes) :] + axes[: by % len(axes)] + rest
        self.pairs = list(zip(turned(turn), turned(turn + 1)))
        self.core = me & 1
        self.bits = [self.core] + self.bits_of(me)
        places = [self.place(self.bits[1:-1]), self.place(self.bits_of(me ^ 1)[:-1])]
        self.order = jnp.stack([jnp.stack([self.core, 1 - self.core]), jnp.stack(places)])

    def bits_of(self, device):
        return [
            (jnp.bitwise_and(device, jnp.where(device & 1 == 0, a, b)) != 0).astype(jnp.int32)
            for a, b in self.pairs
        ]

    def place(self, bits):
        at = jnp.zeros((), jnp.int32)
        for bit in bits:
            at = 2 * at + bit
        return at

    def swap(self, block, step):
        pair = self.pairs[step - 1] if step else (1, 1)
        return lax.ppermute(
            block, ("lon", "batch"), [(i, i ^ pair[i & 1]) for i in range(self.n)]
        )

    def begin(self, keep, send):
        return self.add(keep, self.swap(send, 0))

    def add(self, a, b):
        return (a.astype(f32) + b.astype(f32)).astype(bf16)

    def plan(self):
        last = len(self.bits) - 1
        down, up = range(1, last), range(last - 1, 0, -1)
        return [("halve", n) for n in down] + [("both", last)] + [("double", n) for n in up]

    def pad(self, total):
        return jnp.pad(total, ((0, -total.shape[0] % (4 * self.n)), (0, 0)))

    def half(self, total, at):
        size = total.shape[0] // 2
        return lax.dynamic_slice_in_dim(total, at * size, size, 0)

    def exchange(self, total, kind, step):
        if kind == "halve":
            total = self.half(total, 1 - self.bits[step])
        return self.swap(total, step)

    def join(self, total, got, kind, step):
        if kind == "halve":
            total = self.half(total, self.bits[step])
        return jnp.concatenate([total, got]) if kind == "double" else self.add(total, got)


def in_turn(adders, totals, beside):
    tie = lax.optimization_barrier
    plain = [adder.pad(total) for adder, total in zip(adders, totals)]
    tied = list(plain)
    for n, move in enumerate(adders[0].plan()):
        got = [adder.exchange(total, *move) for adder, total in zip(adders, plain)]
        if n == 0:
            got[0], *beside = tie((got[0], *beside))
        plain[0] = adders[0].join(tied[0], got[0], *move)
        got[1], tied[0] = tie((got[1], plain[0]))
        plain[1] = tied[1] = adders[1].join(tied[1], got[1], *move)
    blocks = []
    for adder, total in zip(adders, plain):
        blocks += [total, adder.swap(total, 0)]
    return blocks, beside


def body(
    state,
    noise,
    samples,
    step,
    kl_weight,
    floor,
    latent_weight,
    state_weight,
    noise_weight,
    attention_gain,
    query_key_value,
    offset_bias,
    output_weight,
    feedforward_gain,
    up_weight,
    down_weight,
    cotangent,
):
    items, height, breadth, width = state.shape
    cells = items * height * breadth * lax.axis_size("lon") * lax.axis_size("batch")
    cell_w = (latent_weight.T, state_weight, noise_weight)
    cot_h, state_h, kl, bias = prep(
        samples, cotangent, state, cell_w[0], offset_bias.reshape(2 * HEADS, -1)
    )
    block_w = (
        attention_gain,
        query_key_value,
        bias,
        output_weight,
        feedforward_gain,
        up_weight,
        down_weight,
    )
    adders = [Summation(turn) for turn in range(len(ALL_CHAINS))]
    add_up = adders[0]
    order = jnp.concatenate([adder.order for adder in adders])
    beta = kl_weight * (step + 1).astype(f32) / WARM
    scalars = jnp.stack([beta, floor])
    *ahead, halo = first(state_h, noise, cot_h, cell_w, block_w)
    halo = shift_from(halo, 1)
    h1, *saved = first(state_h, noise, cot_h, cell_w, block_w, ahead)
    *ahead, halo = second(samples, h1, cot_h, block_w, halo=halo)
    halo = shift_from(halo, -1)
    act, dh, small1, bias1, *grads1 = second(samples, h1, cot_h, block_w, before=ahead)
    part, *grads0 = third(
        state_h, noise, dh, halo, small1, bias1, kl, cell_w, block_w, saved
    )
    activations = place(act, halo)
    sum1 = add_up.begin(*grads1)
    sum0 = add_up.begin(*grads0)
    sum1, sum0 = lax.optimization_barrier((sum1, sum0))
    blocks, beside = in_turn(adders, (sum0, sum1), (activations, order, scalars))
    activations, order, scalars = beside
    state_gradient, divergence, *weights = finish(
        order, scalars, state, part, cell_w[0], *blocks, cells=cells, devices=add_up.n
    )
    return (activations, divergence.reshape(()), state_gradient, weights[0].T, *weights[1:])


def solution(mesh):
    return jax.shard_map(
        body,
        mesh=mesh,
        in_specs=(
            P("batch", None, "lon", None),
            P("batch", None, None, "lon", None),
            P("batch"),
            P(),
            P(),
            P(),
            P(),
            P(),
            P(),
            P(),
            P(),
            P(),
            P(),
            P(),
            P(),
            P(),
            P("batch", None, None, "lon", None),
        ),
        out_specs=(
            P("batch", None, None, "lon", None),
            P(),
            P("batch", None, "lon", None),
            P(),
            P(),
            P(),
            P(),
            P(),
            P(),
            P(),
            P(),
            P(),
            P(),
        ),
        check_vma=False,
    )
```
